32 devices in a mesh: seg: 8 (over z, x), pitch: 4 (over y, core).
Axes of the slice: x: 2, y: 2, z: 4, core: 2. Of those that a mesh axis runs over, the one named last changes fastest.
Arguments:
- state: float32 [128, 8, 5, 49, 128], P('seg', 'pitch'), may hold values from -6 to 6
- advect: float32 [128, 8, 5, 128], P('seg', 'pitch'), may hold values from 0.2 to 1
- viscous: float32 [128, 8, 5, 128], P('seg', 'pitch'), may hold values from 0.1 to 0.5
- inverse: bfloat16 [128, 8, 5, 5, 128], P('seg', 'pitch'), as said below
- lower: float32 [128, 8, 5, 5, 128], P('seg', 'pitch'), as said below
- upper: float32 [128, 8, 5, 5, 128], P('seg', 'pitch'), as said below
- blades: int32 [2], replicated, may hold values from 20 to 90
- harmonic: int32 [24], replicated, may hold values from 1 to 8, as said below
Outputs:
- update: float32 [128, 8, 5, 49, 128], P('seg', 'pitch')
The draws below stay inside these ranges and needn't reach their ends.
Inputs may be any that keep to these rules, and one draw needn't show every extreme that they name: inverse holds each cell's given block inverse. lower holds each cell's upstream coupling, already multiplied by the block inverse and negated. upper holds each cell's downstream coupling, already multiplied by the block inverse and negated. `harmonic`: the mode multiples are not all equal.
All inputs are finite; a program needn't handle non-finite values.
Results may differ from the reference program's by a relative error of at most 0.0003.
Values sent between devices are 32-bit elements; how exact they have to be, the bound alone decides.
No kernel may reach another device: no remote copies, remote signals or barrier semaphores. Data moves between devices by JAX's collectives and lax.ppermute only.
A program may use at most 128 MiB of HBM per device.

```python
import math
import jax
import jax.numpy as jnp
from jax import lax

SPANWISE_NODES = 128
HARM = 24
NT = 49
STREAMWISE_NODES = 128
BLADEWISE_NODES = 8


def product_block(left, right):
    return jnp.sum(left[..., :, :, None, :] * right[..., None, :, :, :], axis=-3)


def unit_inverse(nilpotent, identity):
    series_term = identity
    total = identity
    for order_id in range(4):
        series_term = product_block(series_term, -nilpotent)
        total = total + series_term
    return total


def coupling(key, orientation):
    stochastic_seeds = jax.random.split(key, 9)
    spread = 0.35
    slow_share = 0.5
    index_ids = jnp.arange(5)
    strict_low = (index_ids[:, None] > index_ids[None, :]).astype(jnp.float32)[None, :, :, None]
    strict_high = (index_ids[:, None] < index_ids[None, :]).astype(jnp.float32)[None, :, :, None]
    lower_mix = jax.random.uniform(stochastic_seeds[0], (BLADEWISE_NODES, 5, 5, SPANWISE_NODES), minval=-spread, maxval=spread) * strict_low
    upper_mix = jax.random.uniform(stochastic_seeds[7], (BLADEWISE_NODES, 5, 5, SPANWISE_NODES), minval=-spread, maxval=spread) * strict_high
    identity = jnp.eye(5, dtype=jnp.float32)[None, :, :, None] * jnp.ones((BLADEWISE_NODES, 1, 1, SPANWISE_NODES), jnp.float32)
    eigen_basis = product_block(identity + lower_mix, identity + upper_mix)
    inverse_basis = product_block(unit_inverse(upper_mix, identity), unit_inverse(lower_mix, identity))
    slow_mask = jax.random.uniform(stochastic_seeds[1], (BLADEWISE_NODES, 5, SPANWISE_NODES)) < slow_share
    slow_rate = math.log(10.0) * jax.random.uniform(stochastic_seeds[2], (BLADEWISE_NODES, 5, SPANWISE_NODES), minval=0.1, maxval=0.4) / STREAMWISE_NODES
    lengths = jnp.exp(jax.random.uniform(stochastic_seeds[3], (BLADEWISE_NODES, 5, SPANWISE_NODES), minval=math.log(4.0), maxval=math.log(30.0)))
    decay_rate = jnp.where(slow_mask, slow_rate, 1.0 / lengths)
    jitter = jax.random.uniform(stochastic_seeds[4], (STREAMWISE_NODES, BLADEWISE_NODES, 5, SPANWISE_NODES), minval=0.5, maxval=1.5)
    damping_multipliers = jnp.exp(-decay_rate[None] * jitter)
    spike_node_total = jax.random.randint(stochastic_seeds[5], (2, BLADEWISE_NODES, SPANWISE_NODES), 0, STREAMWISE_NODES)
    node_locations = jnp.arange(STREAMWISE_NODES)[:, None, None]
    spike_threshold = jax.random.uniform(stochastic_seeds[6], (2, BLADEWISE_NODES, 5, SPANWISE_NODES), minval=0.55, maxval=0.8)
    primary_strike = (node_locations == spike_node_total[0][None])[:, :, None, :]
    secondary_strike = (node_locations == spike_node_total[1][None])[:, :, None, :]
    damping_multipliers = damping_multipliers * jnp.where(primary_strike, spike_threshold[0][None], 1.0) * jnp.where(secondary_strike, spike_threshold[1][None], 1.0)
    unit = jnp.eye(5, dtype=jnp.float32)[None, None, :, :, None]
    mixing_field = jax.random.uniform(stochastic_seeds[8], (STREAMWISE_NODES, BLADEWISE_NODES, 5, 5, SPANWISE_NODES), minval=-1.0, maxval=1.0) * (1.0 - unit)
    inner_block = unit * damping_multipliers[:, :, :, None, :] + 0.2 * (1.0 - damping_multipliers)[:, :, :, None, :] * mixing_field
    inner_block = orientation * inner_block
    return jnp.einsum('pabr,zpbcr,pcdr->zpadr', eigen_basis, inner_block, inverse_basis).astype(jnp.float32)


def draw_lower(key, part):
    return coupling(jax.random.fold_in(key, 11), 1.0)


def draw_upper(key, part):
    return coupling(jax.random.fold_in(key, 23), -1.0)


def draw_harmonic(key, part):
    multiples = jax.random.randint(jax.random.fold_in(key, 53), (HARM,), 1, 9)
    second_value = 1 + jnp.mod(multiples[0], 8)
    position = jnp.arange(HARM)
    return jnp.where(position == 1, second_value, multiples).astype(jnp.int32)


def draw_inverse(key, part):
    stochastic_seeds = jax.random.split(jax.random.fold_in(key, 37), 2)
    diagonal = jnp.exp(jax.random.uniform(stochastic_seeds[0], (STREAMWISE_NODES, BLADEWISE_NODES, 5, SPANWISE_NODES), minval=math.log(0.5), maxval=math.log(2.0)))
    offdiag = jax.random.uniform(stochastic_seeds[1], (STREAMWISE_NODES, BLADEWISE_NODES, 5, 5, SPANWISE_NODES), minval=-0.3, maxval=0.3)
    unit = jnp.eye(5, dtype=jnp.float32)[None, None, :, :, None]
    whole = unit * diagonal[:, :, :, None, :] + (1.0 - unit) * offdiag
    scaling = 1.0 / math.sqrt(STREAMWISE_NODES)
    return (whole * scaling).astype(jnp.bfloat16)


def block_scale(own_key, extent, cuts, least, high):
    loudness, own = 1.0, jax.random.fold_in(own_key, 6)
    for dim, shards_of in cuts:
        steps = jnp.exp(jax.random.uniform(jax.random.fold_in(own, dim), (shards_of,), jnp.float32, least / len(cuts), high / len(cuts)))
        loudness = loudness * jnp.repeat(steps, extent[dim] // shards_of).reshape([-1 if axis == dim else 1 for axis in range(len(extent))])
    return loudness


def centred(stream_key, shape, scale, bound, cuts=(), kind=jnp.bfloat16):
    drawn = jax.random.normal(stream_key, shape, jnp.float32) * scale
    if len(cuts) > 0:
        drawn = block_scale(stream_key, shape, cuts, -0.22, 0.18) * drawn
    return jnp.clip(drawn, min=-bound, max=bound).astype(kind)


def setup_inputs(seed: int = 0) -> dict:
    key_list = jax.random.split(jax.random.key(seed), 9)
    return {
        "state": centred(key_list[0], (STREAMWISE_NODES, BLADEWISE_NODES, 5, NT, SPANWISE_NODES), 1.0, 6.0, ((0, 8), (1, 4)), jnp.float32),
        "advect": jnp.clip(jnp.exp(math.log(1.0) - 1.609438 * jax.random.uniform(key_list[1], (STREAMWISE_NODES, BLADEWISE_NODES, 5, SPANWISE_NODES), jnp.float32) ** block_scale(key_list[1], (STREAMWISE_NODES, BLADEWISE_NODES, 5, SPANWISE_NODES), ((0, 8), (1, 4)), -0.2, 0.2)), 0.2, 1.0),
        "viscous": jnp.clip(jnp.exp(math.log(0.5) - 1.609438 * jax.random.uniform(key_list[2], (STREAMWISE_NODES, BLADEWISE_NODES, 5, SPANWISE_NODES), jnp.float32) ** block_scale(key_list[2], (STREAMWISE_NODES, BLADEWISE_NODES, 5, SPANWISE_NODES), ((0, 8), (1, 4)), -0.2, 0.2)), 0.1, 0.5),
        "inverse": draw_inverse(jax.random.fold_in(key_list[8], 71), 0),
        "lower": draw_lower(jax.random.fold_in(key_list[8], 71), 0),
        "upper": draw_upper(jax.random.fold_in(key_list[8], 71), 0),
        "blades": jax.random.randint(key_list[6], (2,), 20, 91).astype(jnp.int32),
        "harmonic": draw_harmonic(jax.random.fold_in(key_list[8], 71), 0),
    }


def spectral_tables(blades, harmonic, fourier_components):
    sampled_moments = 2 * fourier_components + 1
    moment_number = jnp.arange(sampled_moments, dtype=jnp.int32)
    blade_spacing_displacement = moment_number[:, None] - moment_number[None, :]
    cyclic_folded = jnp.mod(blade_spacing_displacement, sampled_moments)
    parity = 1.0 - 2.0 * jnp.mod(blade_spacing_displacement, 2).astype(jnp.float32)
    protected_sinus = jnp.where(blade_spacing_displacement == 0, jnp.float32(1.0), jnp.sin(math.pi * blade_spacing_displacement.astype(jnp.float32) / sampled_moments))
    derive = jnp.where(blade_spacing_displacement == 0, jnp.float32(0.0), 0.5 * parity / protected_sinus)
    rotor_blades = blades[0].astype(jnp.float32)
    stator = blades[1].astype(jnp.float32)
    blade_ratio = stator / rotor_blades
    frequency = blade_ratio / fourier_components
    fourier_wavenumbers = jnp.arange(1, fourier_components + 1, dtype=jnp.int32)
    lag_amounts = 2.0 * math.pi * harmonic.astype(jnp.float32) * blade_ratio
    lag_radians = jnp.mod(fourier_wavenumbers[:, None, None] * cyclic_folded[None], sampled_moments).astype(jnp.float32) * (2.0 * math.pi / sampled_moments)
    forward_lag_angle = (1.0 + 2.0 * jnp.sum(jnp.cos(lag_radians + lag_amounts[:, None, None]), axis=0)) / sampled_moments
    rearward_displacement = (1.0 + 2.0 * jnp.sum(jnp.cos(lag_radians - lag_amounts[:, None, None]), axis=0)) / sampled_moments
    return derive, frequency, forward_lag_angle, rearward_displacement


def apply_block(left, right):
    return jnp.sum(left[..., :, :, None, :] * right[..., None, :, :, :], axis=-3)


def reference(state, advect, viscous, inverse, lower, upper, blades, harmonic):
    fourier_components = harmonic.shape[0]
    derive, frequency, forward_lag_angle, rearward_displacement = spectral_tables(blades, harmonic, fourier_components)
    exact = lax.Precision.HIGHEST
    ghost_low = jnp.einsum('nm,zvmr->zvnr', rearward_displacement, state[:, -1], precision=exact)
    ghost_high = jnp.einsum('nm,zvmr->zvnr', forward_lag_angle, state[:, 0], precision=exact)
    lowside = jnp.concatenate([ghost_low[:, None], state[:, :-1]], axis=1)
    highside = jnp.concatenate([state[:, 1:], ghost_high[:, None]], axis=1)
    zeros_rim = jnp.zeros_like(state[:1])
    upstream = jnp.concatenate([zeros_rim, state[:-1]], axis=0)
    downstream = jnp.concatenate([state[1:], zeros_rim], axis=0)
    axial_term = advect[:, :, :, None, :] * (upstream - downstream)
    pitch_term = viscous[:, :, :, None, :] * (lowside + highside - 2.0 * state)
    timing = frequency * jnp.einsum('nm,zpvmr->zpvnr', derive, state, precision=exact)
    residual = axial_term + pitch_term - timing

    def forward(current, pieces):
        inverse_cell, source_cell, coupling_cell = pieces
        current = apply_block(inverse_cell.astype(jnp.float32), source_cell) + apply_block(coupling_cell, current)
        return current, current

    initial = jnp.zeros_like(state[0])
    _, sweep_rows = lax.scan(forward, initial, (inverse, residual, lower))

    def backward(current, pieces):
        solved, coupling_cell = pieces
        current = solved + apply_block(coupling_cell, current)
        return current, current

    _, update = lax.scan(backward, initial, (sweep_rows, upper), reverse=True)
    return update
```

```python
import functools
import math

import jax
import jax.numpy as jnp
import numpy as np
from jax import lax
from jax.experimental import pallas as pl
from jax.experimental.pallas import tpu as pltpu
from jax.sharding import PartitionSpec as P

F32 = jnp.float32
BF16 = jnp.bfloat16
V = 5
NT = 49
PAD = 56
DEPTH = 64
LANES = 128
LEAD = 4
MB = 1 << 20

CHUNKS = (((0, 24), False), ((24, 40), True), ((40, 48), False))


def rows_of(chunk):
    (first, last), extra = chunk
    return last - first + (8 if extra else 0)


def padded_even(count):
    return (count + 7) // 8 * 8


def kernel_call(body, out_shapes, scratch=(), vmem=40, flops=1_000_000, moved=4_000_000, name=None):
    smem = pl.BlockSpec(memory_space=pltpu.SMEM)
    vmem_spec = pl.BlockSpec(memory_space=pltpu.VMEM)

    def run(flags, *arrays):
        return pl.pallas_call(
            body,
            out_shape=[jax.ShapeDtypeStruct(s, F32) for s in out_shapes],
            in_specs=[smem] + [vmem_spec] * len(arrays),
            out_specs=[vmem_spec] * len(out_shapes),
            scratch_shapes=list(scratch),
            compiler_params=pltpu.CompilerParams(vmem_limit_bytes=vmem * MB),
            cost_estimate=pl.CostEstimate(flops=flops, bytes_accessed=moved, transcendentals=0),
            name=name,
        )(flags, *arrays)

    return run


def coefficient(ref, z, a, b, p):
    return ref[pl.ds(((z * V + a) * V + b) * 2 + p, 1), :]


def split_left(matrix):
    high = matrix.astype(BF16).astype(F32)
    place = lax.broadcasted_iota(jnp.int32, matrix.shape, 1)
    return jnp.where(place < 2 * DEPTH, high, matrix - high).astype(BF16)


def over_instants(left, cells):
    whole = jnp.concatenate(cells, axis=1)
    if whole.shape[0] < DEPTH:
        whole = jnp.concatenate(
            [whole, jnp.zeros((DEPTH - whole.shape[0], whole.shape[1]), F32)], axis=0
        )
    high = whole.astype(BF16)
    low = (whole - high.astype(F32)).astype(BF16)
    product = jnp.dot(
        left, jnp.concatenate([high, low, high], axis=0), preferred_element_type=F32
    )
    return [product[:, i * LANES : (i + 1) * LANES] for i in range(len(cells))]


def prepare(flags, st, phase, xn, xf, *chunks):
    p = flags[0]
    wrap = flags[1]
    cells = xn.shape[0] // V
    left = split_left(phase[...])
    zeros = jnp.zeros((8, LANES), F32)

    def separate(z):
        for v in range(V):
            j = z * V + v
            for out, q in ((xn, 1 - p), (xf, p)):
                out[j, PAD - 8 : PAD, :] = zeros
                out[j, 0:NT, :] = st[pl.ds(j * 2 * NT + q, NT, stride=2), :]

    def lead(z, carry):
        separate(z)
        return carry

    lax.fori_loop(0, LEAD, lead, 0)

    def rest(z, carry):
        separate(z)
        raw = [xf[z * V + v] for v in range(V)]
        lagged = over_instants(left, raw)
        for v in range(V):
            value = jnp.where(wrap == 1, lagged[v], raw[v])
            j = (z - LEAD) * V + v
            for out, ((first, last), extra) in zip(chunks, CHUNKS):
                width = last - first
                out[pl.ds(pl.multiple_of(j * width, 8), width), :] = value[first:last]
                if extra:
                    out[pl.ds((cells - LEAD) * V * width + j, 1), :] = value[NT - 1 : NT]
        return carry

    lax.fori_loop(LEAD, cells, rest, 0)


def sweeps(source, g, fg, spans, p, inverse, lower, upper, cells):
    for first, last in spans:
        nothing = tuple(jnp.zeros((last - first, LANES), F32) for _ in range(V))

        def ahead(z, current, first=first, last=last):
            right = source(z, first, last)
            result = []
            for a in range(V):
                total = coefficient(inverse, z, a, 0, p) * right[0]
                for b in range(1, V):
                    total += coefficient(inverse, z, a, b, p) * right[b]
                for b in range(V):
                    total += coefficient(lower, z, a, b, p) * current[b]
                g[z * V + a, first:last, :] = total
                result.append(total)
            return tuple(result)

        out = lax.fori_loop(0, cells, ahead, nothing)
        for a in range(V):
            fg[a, first:last, :] = out[a]

        def back(i, current, first=first, last=last):
            z = cells - 1 - i
            result = []
            for a in range(V):
                total = g[z * V + a, first:last, :]
                for b in range(V):
                    total += coefficient(upper, z, a, b, p) * current[b]
                g[z * V + a, first:last, :] = total
                result.append(total)
            return tuple(result)

        out = lax.fori_loop(0, cells, back, nothing)
        for a in range(V):
            fg[V + a, first:last, :] = out[a]


def residuals(x, other, halo, edges, advect, viscous, left, p, cells, put):
    def one(z, above, below):
        here = [x[z * V + v] for v in range(V)]
        timing = over_instants(left, here)
        for v in range(V):
            j = z * V + v
            pitch = other[j] - 2.0 * here[v]
            if halo is not None:
                pitch += halo[j]
            put(
                j,
                advect[pl.ds(j * 2 + p, 1), :] * (above(z, v) - below(z, v))
                + viscous[pl.ds(j * 2 + p, 1), :] * pitch
                - timing[v],
            )

    inner_above = lambda z, v: x[(z - 1) * V + v]
    inner_below = lambda z, v: x[(z + 1) * V + v]
    one(0, lambda z, v: edges[v], inner_below)

    def step(z, carry):
        one(z, inner_above, inner_below)
        return carry

    lax.fori_loop(1, cells - 1, step, 0)
    one(cells - 1, inner_above, lambda z, v: edges[V + v])


def take_edges(edges, from_left, from_right, p):
    skip = from_left.shape[0] - V * NT * 2
    for v in range(V):
        edges[v, PAD - 8 : PAD, :] = jnp.zeros((8, LANES), F32)
        edges[v, 0:NT, :] = from_left[pl.ds(skip + v * 2 * NT + p, NT, stride=2), :]
        edges[V + v, PAD - 8 : PAD, :] = jnp.zeros((8, LANES), F32)
        edges[V + v, 0:NT, :] = from_right[pl.ds(v * 2 * NT + p, NT, stride=2), :]


def near_cell(
    flags, xn, xf, halo, from_left, from_right, advect, viscous, inverse, lower, upper, derive,
    g, fg, edges, right,
):
    p = 1 - flags[0]
    cells = xn.shape[0] // V
    take_edges(edges, from_left, from_right, p)

    def put(j, value):
        right[j] = value

    residuals(xn, xf, halo, edges, advect, viscous, split_left(derive[...]), p, cells, put)
    source = lambda z, first, last: [right[z * V + v, first:last, :] for v in range(V)]
    sweeps(source, g, fg, ((0, 32), (32, PAD)), p, inverse, lower, upper, cells)


def far_base(
    flags, xn, xf, from_left, from_right, slab, advect, viscous, derive, phase, base, edges, halo
):
    p = flags[0]
    wrap = flags[1]
    cells = xn.shape[0] // V
    take_edges(edges, from_left, from_right, p)

    def put(j, value):
        base[j] = value

    residuals(xf, xn, None, edges, advect, viscous, split_left(derive[...]), p, cells, put)
    left = split_left(phase[...])
    for z in range(LEAD):
        for v in range(V):
            halo[v, NT - 1 : PAD, :] = jnp.zeros((PAD - NT + 1, LANES), F32)
            halo[v, 0:NT, :] = slab[pl.ds((z * V + v) * NT, NT), :]
        raw = [halo[v] for v in range(V)]
        lagged = over_instants(left, raw)
        for v in range(V):
            j = z * V + v
            value = jnp.where(wrap == 1, lagged[v], raw[v])
            base[j] += viscous[pl.ds(j * 2 + p, 1), :] * value


def far_chunk(chunk, flags, base, halo, viscous, inverse, lower, upper, g, fg):
    (first, last), extra = chunk
    width = last - first
    p = flags[0]
    cells = base.shape[0] // V
    top = lax.broadcasted_iota(jnp.int32, (8, LANES), 0) == 0

    def source(z, start, stop):
        result = []
        for v in range(V):
            j = z * V + v
            value = base[j, first:last, :]
            if extra:
                value = jnp.concatenate([value, base[j, PAD - 8 : PAD, :]], axis=0)
            h = jnp.maximum(z - LEAD, 0) * V + v
            arrived = halo[pl.ds(pl.multiple_of(h * width, 8), width), :]
            if extra:
                row = halo[pl.ds((cells - LEAD) * V * width + h, 1), :]
                arrived = jnp.concatenate([arrived, jnp.where(top, row, 0.0)], axis=0)
            scale = jnp.where(z >= LEAD, viscous[pl.ds(j * 2 + p, 1), :], 0.0)
            result.append(value + scale * arrived)
        return result

    rows = rows_of(chunk)
    sweeps(source, g, fg, ((0, rows),), p, inverse, lower, upper, cells)


def times(matrix, vector):
    result = []
    for a in range(V):
        total = matrix(a, 0) * vector[0]
        for b in range(1, V):
            total += matrix(a, b) * vector[b]
        result.append(total)
    return result


def plus(one, two):
    return [a + b for a, b in zip(one, two)]


def tiles(ref, c, kind):
    return [ref[c, kind * V + a] for a in range(V)]


def rows(ref, c, kind):
    return lambda a, b: ref[c, kind * V + a, b : b + 1, :]


def unit(a):
    place = lax.broadcasted_iota(jnp.int32, (8, LANES), 0)
    return jnp.where(place == a, 1.0, 0.0).astype(F32)


def transfer(flags, lower, upper, blocks, group, forward):
    cells = blocks.shape[1] // V
    for c in range(2):
        p = 1 - flags[0] if c == 0 else flags[0]

        def ahead(z, current):
            result = times(lambda a, b: coefficient(lower, z, a, b, p), current)
            for a in range(V):
                forward[z * V + a] = result[a]
            return tuple(result)

        through = lax.fori_loop(0, cells, ahead, tuple(unit(a) for a in range(V)))

        def back(i, current):
            z = cells - 1 - i
            result = times(lambda a, b: coefficient(upper, z, a, b, p), current)
            for a in range(V):
                result[a] = result[a] + jnp.concatenate(
                    [forward[z * V + a], jnp.zeros((8, LANES), F32)], axis=0
                )
                blocks[c, z * V + a] = result[a]
            return tuple(result)

        start = tuple(
            jnp.concatenate([jnp.zeros((8, LANES), F32), unit(a)], axis=0) for a in range(V)
        )
        ends = lax.fori_loop(0, cells, back, start)
        for a in range(V):
            group[c, a] = ends[a][:8]
            group[c, V + a] = ends[a][8:]
            group[c, 2 * V + a] = through[a]


def merge_matrices(flags, bit, start, *refs):
    if start:
        group, other, mats, merged, share_out = refs
    else:
        group, other, share, mats, merged, share_out = refs
    right = flags[3 + bit] == 1
    for c in range(2):
        for a in range(V):
            for target, kind, own_if in ((0, 2, True), (1, 0, True), (2, 1, False)):
                mine, theirs = group[c, kind * V + a], other[c, kind * V + a]
                pick_own = right if own_if else jnp.logical_not(right)
                mats[c, target * V + a] = jnp.where(pick_own, mine, theirs)
        if start:
            own = [[unit(a) for a in range(V)], [jnp.zeros((8, LANES), F32)] * V, [unit(a) for a in range(V)]]
        else:
            own = [tiles(share, c, kind) for kind in range(3)]
        for a in range(V):
            mats[c, 3 * V + a] = jnp.where(right, own[0][a], 0.0)
            mats[c, 4 * V + a] = jnp.where(right, own[1][a], 0.0)
            mats[c, 5 * V + a] = jnp.where(right, 0.0, own[2][a])
        p_left = [jnp.where(right, other[c, 2 * V + a], group[c, 2 * V + a]) for a in range(V)]
        g_left = [jnp.where(right, other[c, a], group[c, a]) for a in range(V)]
        h_right = [jnp.where(right, group[c, V + a], other[c, V + a]) for a in range(V)]
        turned = times(rows(mats, c, 1), p_left)
        new_p = times(rows(mats, c, 0), p_left)
        new_g = plus(g_left, times(rows(mats, c, 2), turned))
        new_h = times(rows(mats, c, 2), h_right)
        for a in range(V):
            merged[c, a] = new_g[a]
            merged[c, V + a] = new_h[a]
            merged[c, 2 * V + a] = new_p[a]
        s0 = times(rows(mats, c, 3), p_left)
        s1 = times(rows(mats, c, 4), p_left)
        s1b = times(rows(mats, c, 5), turned)
        s2 = times(rows(mats, c, 5), h_right)
        for a in range(V):
            share_out[c, a] = jnp.where(right, s0[a], own[0][a])
            share_out[c, V + a] = jnp.where(right, s1[a], own[1][a] + s1b[a])
            share_out[c, 2 * V + a] = jnp.where(right, own[2][a], s2[a])


def merge_level(right, c, mats, mine, theirs, inflow):
    f_left = [jnp.where(right, theirs[a], mine[a]) for a in range(V)]
    g_right = [jnp.where(right, mine[V + a], theirs[V + a]) for a in range(V)]
    back = plus(g_right, times(rows(mats, c, 1), f_left))
    from_left = times(rows(mats, c, 3), f_left)
    from_right = plus(
        times(rows(mats, c, 4), f_left), times(rows(mats, c, 5), back)
    )
    if inflow is not None:
        from_left = plus(inflow[:V], from_left)
        from_right = plus(inflow[V:], from_right)
    return f_left, back, from_left + from_right


def merge_flows(bit, c, start, flags, mats, flows, other, *refs):
    if start:
        merged, inflow_out = refs
        inflow = None
    else:
        inflow_in, merged, inflow_out = refs
    right = flags[3 + bit] == 1
    count = flows.shape[1] // 8

    def tile(t, carry):
        span = pl.ds(pl.multiple_of(t * 8, 8), 8)
        mine = [flows[i, span, :] for i in range(2 * V)]
        theirs = [other[i, span, :] for i in range(2 * V)]
        known = None if start else [inflow_in[i, span, :] for i in range(2 * V)]
        f_left, back, total = merge_level(right, c, mats, mine, theirs, known)
        f_right = [jnp.where(right, mine[a], theirs[a]) for a in range(V)]
        g_left = [jnp.where(right, theirs[V + a], mine[V + a]) for a in range(V)]
        new_f = plus(f_right, times(rows(mats, c, 0), f_left))
        new_g = plus(g_left, times(rows(mats, c, 2), back))
        for i, value in enumerate(new_f + new_g):
            merged[i, span, :] = value
        for i, value in enumerate(total):
            inflow_out[i, span, :] = value
        return carry

    lax.fori_loop(0, count, tile, 0)


def last_flows(right, c, mats, flows, other, inflow_in, store):
    for t in range(flows.shape[1] // 8):
        span = slice(t * 8, t * 8 + 8)
        mine = [flows[i, span, :] for i in range(2 * V)]
        theirs = [other[i, span, :] for i in range(2 * V)]
        known = None if inflow_in is None else [inflow_in[i, span, :] for i in range(2 * V)]
        _, _, total = merge_level(right, c, mats, mine, theirs, known)
        for i, value in enumerate(total):
            store(i, span, value)


def corrected(c, z, a, first, last, g, blocks, inflow):
    total = g[z * V + a, first:last, :]
    for b in range(V):
        total += blocks[c, z * V + a, b : b + 1, :] * inflow[b]
        total += blocks[c, z * V + a, 8 + b : 9 + b, :] * inflow[V + b]
    return total


def correct(bit, c, flags, mats, flows, other, inflow_in, g, blocks, result, inflow):
    right = flags[3 + bit] == 1

    def store(i, span, value):
        inflow[i, span, :] = value

    last_flows(right, c, mats, flows, other, inflow_in, store)
    cells = g.shape[0] // V
    total = g.shape[1]
    spans = ((0, 32), (32, total)) if total > 32 else ((0, total),)
    for first, last in spans:
        known = tuple(inflow[i, first:last, :] for i in range(2 * V))

        def step(z, known, first=first, last=last):
            for a in range(V):
                result[z * V + a, first:last, :] = corrected(c, z, a, first, last, g, blocks, known)
            return known

        lax.fori_loop(0, cells, step, known)


def finish(bit, flags, mats, flows, other, inflow_in, g, blocks, near, *refs):
    done, out, inflow = refs[:-2], refs[-2], refs[-1]
    right = flags[3 + bit] == 1
    p = flags[0]

    @pl.when(pl.program_id(0) == 0)
    def _():
        def store(i, span, value):
            inflow[i, span, :] = value

        last_flows(right, 1, mats, flows, other, inflow_in, store)

    first_row, last_row = CHUNKS[-1][0]
    width = last_row - first_row
    known = tuple(inflow[i] for i in range(2 * V))

    def step(z, carry):
        for a in range(V):
            j = z * V + a
            row = j * 2 * NT
            out[pl.ds(row + 1 - p, NT, stride=2), :] = near[j, 0:NT, :]
            for ref, ((first, last), extra) in zip(done, CHUNKS):
                out[pl.ds(row + p + 2 * first, last - first, stride=2), :] = ref[j, 0 : last - first, :]
                if extra:
                    out[pl.ds(row + p + 2 * (NT - 1), 1), :] = ref[j, last - first : last - first + 1, :]
            out[pl.ds(row + p + 2 * first_row, width, stride=2), :] = corrected(1, z, a, 0, width, g, blocks, known)
        return carry

    lax.fori_loop(0, g.shape[0] // V, step, 0)


def phase_ahead(blades, harmonic):
    count = harmonic.shape[0]
    angle = 2.0 * math.pi * np.outer(np.arange(1, count + 1), np.arange(NT)) / NT
    cosine, sine = np.cos(angle).astype(np.float32), np.sin(angle).astype(np.float32)
    ratio = blades[1].astype(F32) / blades[0].astype(F32)
    lag = 2.0 * math.pi * harmonic.astype(F32) * ratio
    turn, cross = jnp.cos(lag)[:, None], jnp.sin(lag)[:, None]
    basis = np.concatenate([cosine, sine], axis=0)
    turned = jnp.concatenate([turn * cosine + cross * sine, turn * sine - cross * cosine], axis=0)
    total = jnp.einsum("kn,km->nm", basis, turned, precision=lax.Precision.HIGHEST)
    return (1.0 + 2.0 * total) / NT


def derivative(blades, harmonic):
    gap = np.arange(NT)[:, None] - np.arange(NT)[None, :]
    safe = np.where(gap == 0, 1.0, np.sin(np.pi * gap / NT))
    table = np.where(gap == 0, 0.0, 0.5 * (1.0 - 2.0 * np.mod(gap, 2)) / safe).astype(np.float32)
    ratio = blades[1].astype(F32) / blades[0].astype(F32)
    return ratio / harmonic.shape[0] * table


def thrice(matrix):
    wide = jnp.pad(matrix, ((0, PAD - NT), (0, DEPTH - NT)))
    return jnp.concatenate([wide] * 3, axis=1)


def local(state, advect, viscous, inverse, lower, upper, blades, harmonic):
    cells = state.shape[0]
    segs, slabs = lax.axis_size("seg"), lax.axis_size("pitch")
    levels = segs.bit_length() - 1
    slab, seg = lax.axis_index("pitch"), lax.axis_index("seg")
    side = slab % 2
    wrap = jnp.logical_or(slab == 0, slab == slabs - 1)
    bits = [(seg >> k) & 1 for k in range(levels)]
    flags = jnp.stack([side, wrap.astype(jnp.int32), seg, *bits]).astype(jnp.int32)
    far_pairs = [(i, (i - 1) % slabs if i % 2 == 0 else (i + 1) % slabs) for i in range(slabs)]
    near_pairs = [(i, i ^ 1) for i in range(slabs)]
    to_far = lambda x: lax.ppermute(x, "pitch", far_pairs)
    to_level = lambda x, k: lax.ppermute(x, "seg", [(i, i ^ (1 << k)) for i in range(segs)])

    st = state.transpose(0, 2, 3, 1, 4).reshape(cells * V * NT * 2, LANES)
    lead_rows = LEAD * V * NT
    slab_out = lax.dynamic_index_in_dim(
        st[: 2 * lead_rows].reshape(lead_rows, 2, LANES), side, axis=1, keepdims=False
    )
    slab_in = to_far(slab_out)

    flat = lambda x: x.transpose(0, 2, 3, 1, 4).reshape(cells * V * V * 2, LANES)
    inv, low, upp = flat(inverse.astype(F32)), flat(lower), flat(upper)
    adv = advect.transpose(0, 2, 1, 3).reshape(cells * V * 2, LANES)
    vis = viscous.transpose(0, 2, 1, 3).reshape(cells * V * 2, LANES)

    edge_rows = padded_even(V * NT * 2)
    from_left = lax.ppermute(st[-edge_rows:], "seg", [(i, i + 1) for i in range(segs - 1)])
    from_right = lax.ppermute(st[:edge_rows], "seg", [(i + 1, i) for i in range(segs - 1)])

    ahead = phase_ahead(blades, harmonic)
    sent = jnp.where(slab == 0, ahead, ahead.T)
    send_phase, take_phase = thrice(sent), thrice(sent.T)
    derive = thrice(derivative(blades, harmonic))

    rest = (cells - LEAD) * V
    chunk_shapes = [
        (rest * (last - first) + (padded_even(rest) if extra else 0), LANES)
        for (first, last), extra in CHUNKS
    ]
    x_shape = (cells * V, PAD, LANES)
    xn, xf, *chunks = kernel_call(
        prepare, [x_shape, x_shape, *chunk_shapes], vmem=24, moved=11_000_000, name="prepare"
    )(flags, st, send_phase)
    arrived = [to_far(chunk) for chunk in chunks]
    halo_near = lax.ppermute(xn, "pitch", near_pairs)

    blocks, group = kernel_call(
        transfer,
        [(2, cells * V, 16, LANES), (2, 3 * V, 8, LANES)],
        [pltpu.VMEM((cells * V, 8, LANES), F32)],
        vmem=16, name="transfer",
    )(flags, low, upp)
    mats, share = [], []
    mats_shape, group_shape = (2, 6 * V, 8, LANES), (2, 3 * V, 8, LANES)
    for k in range(levels):
        out = kernel_call(
            lambda flags, *refs, k=k: merge_matrices(flags, k, k == 0, *refs),
            [mats_shape, group_shape, group_shape], vmem=16, moved=500_000, name="merge_matrices",
        )(flags, group, to_level(group, k), *share)
        mats.append(out[0])
        group, share = out[1], [out[2]]

    def exchange(c, fg):
        inflow = []
        for k in range(levels - 1):
            shape = fg.shape
            fg, known = kernel_call(
                functools.partial(merge_flows, k, c, k == 0),
                [shape, shape], vmem=16, moved=500_000, name="merge_flows",
            )(flags, mats[k], fg, to_level(fg, k), *inflow)
            inflow = [known]
        return fg, to_level(fg, levels - 1), inflow[0]

    def settle(c, fg, g):
        flows = exchange(c, fg)
        return kernel_call(
            functools.partial(correct, levels - 1, c),
            [g.shape], [pltpu.VMEM((2 * V, g.shape[1], LANES), F32)], vmem=24, name="correct",
        )(flags, mats[-1], *flows, g, blocks)[0]

    g_near, fg_near = kernel_call(
        near_cell,
        [x_shape, (2 * V, PAD, LANES)],
        [pltpu.VMEM((2 * V, PAD, LANES), F32), pltpu.VMEM(x_shape, F32)],
        vmem=32, moved=12_000_000, name="near_cell",
    )(flags, xn, xf, halo_near, from_left, from_right, adv, vis, inv, low, upp, derive)
    base = kernel_call(
        far_base,
        [x_shape],
        [pltpu.VMEM((2 * V, PAD, LANES), F32), pltpu.VMEM((V, PAD, LANES), F32)],
        vmem=24, moved=8_000_000, name="far_base",
    )(flags, xn, xf, from_left, from_right, slab_in, adv, vis, derive, take_phase)[0]

    near = settle(0, fg_near, g_near)
    solved = []
    for chunk, halo in zip(CHUNKS, arrived):
        height = rows_of(chunk)
        solved.append(
            kernel_call(
                functools.partial(far_chunk, chunk),
                [(cells * V, height, LANES), (2 * V, height, LANES)], vmem=24, name="far_chunk",
            )(flags, base, halo, vis, inv, low, upp)
        )
    done = [settle(1, fg, g) for g, fg in solved[:-1]]
    g_last, fg_last = solved[-1]
    flows = exchange(1, fg_last)

    steps = 4
    part = cells // steps
    whole = lambda x: pl.BlockSpec(x.shape, lambda i: (0,) * x.ndim)
    by_cell = lambda x: pl.BlockSpec((part * V,) + x.shape[1:], lambda i: (i, 0, 0))
    height = rows_of(CHUNKS[-1])
    out = pl.pallas_call(
        functools.partial(finish, levels - 1),
        grid=(steps,),
        out_shape=jax.ShapeDtypeStruct(st.shape, F32),
        in_specs=[pl.BlockSpec(memory_space=pltpu.SMEM)]
        + [whole(x) for x in (mats[-1], *flows)]
        + [
            by_cell(g_last),
            pl.BlockSpec((2, part * V, 16, LANES), lambda i: (0, i, 0, 0)),
            by_cell(near),
        ]
        + [by_cell(x) for x in done],
        out_specs=pl.BlockSpec((part * V * NT * 2, LANES), lambda i: (i, 0)),
        scratch_shapes=[pltpu.VMEM((2 * V, height, LANES), F32)],
        compiler_params=pltpu.CompilerParams(vmem_limit_bytes=24 * MB),
        name="finish",
    )(flags, mats[-1], *flows, g_last, blocks, near, *done)
    return out.reshape(cells, V, NT, 2, LANES).transpose(0, 3, 1, 2, 4)


def solution(mesh):
    cell = P("seg", "pitch", None, None, None)
    return jax.shard_map(
        local,
        mesh=mesh,
        in_specs=(cell, P("seg", "pitch", None, None), P("seg", "pitch", None, None), cell, cell, cell, P(), P()),
        out_specs=cell,
        check_vma=False,
    )
```

```python
import functools
import math

import jax
import jax.numpy as jnp
import numpy as np
from jax import lax
from jax.experimental import pallas as pl
from jax.experimental.pallas import tpu as pltpu
from jax.sharding import PartitionSpec as P

F32 = jnp.float32
BF16 = jnp.bfloat16
V = 5
NT = 49
PAD = 56
DEPTH = 64
LANES = 128
LEAD = 4
MB = 1 << 20

CHUNKS = (((0, 24), False), ((24, 40), True), ((40, 48), False))


def rows_of(chunk):
    (first, last), extra = chunk
    return last - first + (8 if extra else 0)


def padded_even(count):
    return (count + 7) // 8 * 8


class Chain:
    def __init__(self, flags):
        self.flags = flags

    def after(self, array):
        self.flags, array = lax.optimization_barrier((self.flags, array))
        return array

    def __call__(self, body, out_shapes, arrays, scratch=(), vmem=24, name=None, grid=None, in_specs=None, out_specs=None):
        smem = pl.BlockSpec(memory_space=pltpu.SMEM)
        held = pl.BlockSpec(memory_space=pltpu.VMEM)
        extra = {} if grid is None else {"grid": grid}
        out = pl.pallas_call(
            body,
            out_shape=[jax.ShapeDtypeStruct(s, F32) for s in out_shapes],
            in_specs=[smem] + (in_specs or [held] * len(arrays)),
            out_specs=out_specs or [held] * len(out_shapes),
            scratch_shapes=list(scratch),
            compiler_params=pltpu.CompilerParams(vmem_limit_bytes=vmem * MB),
            cost_estimate=pl.CostEstimate(flops=1000, bytes_accessed=1000, transcendentals=0),
            name=name,
            **extra,
        )(self.flags, *arrays)
        out = list(out)
        out[0] = self.after(out[0])
        return out


def coefficient(ref, z, a, b, p):
    return ref[pl.ds(((z * V + a) * V + b) * 2 + p, 1), :]


def split_left(matrix):
    high = matrix.astype(BF16).astype(F32)
    place = lax.broadcasted_iota(jnp.int32, matrix.shape, 1)
    return jnp.where(place < 2 * DEPTH, high, matrix - high).astype(BF16)


def lag_matrix(basis, turned, trig, sign):
    half = turned.shape[0] // 2
    count = (half - 4) // 8 * 8
    cosine, sine = turned[:half], turned[half:]
    turn, cross = trig[:count, :1], trig[count : 2 * count, :1] * sign
    right = jnp.concatenate(
        [
            turn * cosine[:count] + cross * sine[:count],
            turn * sine[:count] - cross * cosine[:count],
            cosine[count:],
        ],
        axis=0,
    )
    return jnp.dot(basis, right, preferred_element_type=F32, precision=lax.Precision.HIGHEST)


def over_instants(left, cells):
    whole = jnp.concatenate(cells, axis=1)
    if whole.shape[0] < DEPTH:
        whole = jnp.concatenate(
            [whole, jnp.zeros((DEPTH - whole.shape[0], whole.shape[1]), F32)], axis=0
        )
    high = whole.astype(BF16)
    low = (whole - high.astype(F32)).astype(BF16)
    product = jnp.dot(
        left, jnp.concatenate([high, low, high], axis=0), preferred_element_type=F32
    )
    return [product[:, i * LANES : (i + 1) * LANES] for i in range(len(cells))]


def lead_cells(flags, st, slab):
    p = flags[0]
    width = 4 * NT

    def step(i, carry):
        slab[pl.ds(i * width, width), :] = st[pl.ds(i * 2 * width + p, width, stride=2), :]
        return carry

    lax.fori_loop(0, LEAD * V // 4, step, 0)


def prepare(flags, st, trig, basis, turned, xn, xf, first_cell, last_cell, *chunks):
    p = flags[0]
    wrap = flags[1]
    cells = xn.shape[0] // V
    sign = jnp.where(flags[2] == 1, 1.0, -1.0)
    left = split_left(lag_matrix(basis[...], turned[...], trig[...], sign))
    zeros = jnp.zeros((8, LANES), F32)

    def separate(z):
        for v in range(V):
            j = z * V + v
            for out, q in ((xn, 1 - p), (xf, p)):
                out[j, PAD - 8 : PAD, :] = zeros
                out[j, 0:NT, :] = st[pl.ds(j * 2 * NT + q, NT, stride=2), :]

    def lead(z, carry):
        separate(z)
        return carry

    lax.fori_loop(0, LEAD, lead, 0)

    def rest(z, carry):
        separate(z)
        raw = [xf[z * V + v] for v in range(V)]
        lagged = over_instants(left, raw)
        for v in range(V):
            value = jnp.where(wrap == 1, lagged[v], raw[v])
            j = (z - LEAD) * V + v
            for out, ((first, last), extra) in zip(chunks, CHUNKS):
                width = last - first
                out[pl.ds(pl.multiple_of(j * width, 8), width), :] = value[first:last]
                if extra:
                    out[pl.ds((cells - LEAD) * V * width + j, 1), :] = value[NT - 1 : NT]
        return carry

    lax.fori_loop(LEAD, cells, rest, 0)
    for v in range(V):
        first_cell[v] = xn[v]
        first_cell[V + v] = xf[v]
        last_cell[v] = xn[(cells - 1) * V + v]
        last_cell[V + v] = xf[(cells - 1) * V + v]


def keep_tiles(ref, kind, values, first, last, height):
    for a in range(V):
        for t in range(first // 8, last // 8):
            ref[(kind + a) * height + t] = values[a][t * 8 - first : t * 8 - first + 8]


def sweeps(source, g, fg, spans, p, inverse, lower, upper, cells):
    height = g.shape[1] // 8
    for first, last in spans:
        nothing = tuple(jnp.zeros((last - first, LANES), F32) for _ in range(V))

        def ahead(z, current, first=first, last=last):
            right = source(z, first, last)
            result = []
            for a in range(V):
                total = coefficient(inverse, z, a, 0, p) * right[0]
                for b in range(1, V):
                    total += coefficient(inverse, z, a, b, p) * right[b]
                for b in range(V):
                    total += coefficient(lower, z, a, b, p) * current[b]
                g[z * V + a, first:last, :] = total
                result.append(total)
            return tuple(result)

        out = lax.fori_loop(0, cells, ahead, nothing)
        keep_tiles(fg, 0, out, first, last, height)

        def back(i, current, first=first, last=last):
            z = cells - 1 - i
            result = []
            for a in range(V):
                total = g[z * V + a, first:last, :]
                for b in range(V):
                    total += coefficient(upper, z, a, b, p) * current[b]
                g[z * V + a, first:last, :] = total
                result.append(total)
            return tuple(result)

        out = lax.fori_loop(0, cells, back, nothing)
        keep_tiles(fg, V, out, first, last, height)


def residuals(x, other, halo, from_left, from_right, edge, advect, viscous, left, p, cells, put):
    def one(z, above, below):
        here = [x[z * V + v] for v in range(V)]
        timing = over_instants(left, here)
        for v in range(V):
            j = z * V + v
            pitch = other[j] - 2.0 * here[v]
            if halo is not None:
                pitch += halo[j]
            put(
                j,
                advect[pl.ds(j * 2 + p, 1), :] * (above(z, v) - below(z, v))
                + viscous[pl.ds(j * 2 + p, 1), :] * pitch
                - timing[v],
            )

    inner_above = lambda z, v: x[(z - 1) * V + v]
    inner_below = lambda z, v: x[(z + 1) * V + v]
    one(0, lambda z, v: from_left[edge + v], inner_below)

    def step(z, carry):
        one(z, inner_above, inner_below)
        return carry

    lax.fori_loop(1, cells - 1, step, 0)
    one(cells - 1, inner_above, lambda z, v: from_right[edge + v])


def timing_matrix(table, trig):
    return split_left(table[...] * trig[trig.shape[0] - 8 : trig.shape[0] - 7, :1])


def near_cell(
    flags, xn, xf, halo, from_left, from_right, advect, viscous, inverse, lower, upper, trig, table,
    group, g, flows, right,
):
    p = 1 - flags[0]
    cells = xn.shape[0] // V

    def put(j, value):
        right[j] = value

    residuals(xn, xf, halo, from_left, from_right, 0, advect, viscous, timing_matrix(table, trig), p, cells, put)
    source = lambda z, first, last: [right[z * V + v, first:last, :] for v in range(V)]
    sweeps(source, g, flows, ((0, 32), (32, PAD)), p, inverse, lower, upper, cells)
    for c in range(2):
        for i in range(3 * V):
            flows[NEAR_TILES + c * 3 * V + i] = group[c, i]


def far_base(
    flags, xn, xf, from_left, from_right, slab, advect, viscous, trig, table, basis, turned, base, halo
):
    p = flags[0]
    wrap = flags[1]
    cells = xn.shape[0] // V

    def put(j, value):
        base[j] = value

    residuals(xf, xn, None, from_left, from_right, V, advect, viscous, timing_matrix(table, trig), p, cells, put)
    sign = jnp.where(flags[2] == 1, -1.0, 1.0)
    left = split_left(lag_matrix(basis[...], turned[...], trig[...], sign))
    for z in range(LEAD):
        for v in range(V):
            halo[v, PAD - 8 : PAD, :] = jnp.zeros((8, LANES), F32)
            halo[v, 0:NT, :] = slab[pl.ds((z * V + v) * NT, NT), :]
        raw = [halo[v] for v in range(V)]
        lagged = over_instants(left, raw)
        for v in range(V):
            j = z * V + v
            value = jnp.where(wrap == 1, lagged[v], raw[v])
            base[j] += viscous[pl.ds(j * 2 + p, 1), :] * value


def far_chunk(chunk, flags, base, halo, viscous, inverse, lower, upper, g, fg):
    (first, last), extra = chunk
    width = last - first
    p = flags[0]
    cells = base.shape[0] // V
    top = lax.broadcasted_iota(jnp.int32, (8, LANES), 0) == 0

    def source(z, start, stop):
        result = []
        for v in range(V):
            j = z * V + v
            value = base[j, first:last, :]
            if extra:
                value = jnp.concatenate([value, base[j, PAD - 8 : PAD, :]], axis=0)
            h = jnp.maximum(z - LEAD, 0) * V + v
            arrived = halo[pl.ds(pl.multiple_of(h * width, 8), width), :]
            if extra:
                row = halo[pl.ds((cells - LEAD) * V * width + h, 1), :]
                arrived = jnp.concatenate([arrived, jnp.where(top, row, 0.0)], axis=0)
            scale = jnp.where(z >= LEAD, viscous[pl.ds(j * 2 + p, 1), :], 0.0)
            result.append(value + scale * arrived)
        return result

    rows = rows_of(chunk)
    sweeps(source, g, fg, ((0, rows),), p, inverse, lower, upper, cells)


def times(matrix, vector):
    result = []
    for a in range(V):
        total = matrix(a, 0) * vector[0]
        for b in range(1, V):
            total += matrix(a, b) * vector[b]
        result.append(total)
    return result


def plus(one, two):
    return [a + b for a, b in zip(one, two)]


def tiles(ref, c, kind):
    return [ref[c, kind * V + a] for a in range(V)]


def rows(ref, c, kind):
    return lambda a, b: ref[c, kind * V + a, b : b + 1, :]


def unit(a):
    place = lax.broadcasted_iota(jnp.int32, (8, LANES), 0)
    return jnp.where(place == a, 1.0, 0.0).astype(F32)


def transfer(flags, lower, upper, blocks, group, forward):
    cells = blocks.shape[1] // V
    for c in range(2):
        p = 1 - flags[0] if c == 0 else flags[0]

        def ahead(z, current):
            result = times(lambda a, b: coefficient(lower, z, a, b, p), current)
            for a in range(V):
                forward[z * V + a] = result[a]
            return tuple(result)

        through = lax.fori_loop(0, cells, ahead, tuple(unit(a) for a in range(V)))

        def back(i, current):
            z = cells - 1 - i
            result = times(lambda a, b: coefficient(upper, z, a, b, p), current)
            for a in range(V):
                result[a] = result[a] + jnp.concatenate(
                    [forward[z * V + a], jnp.zeros((8, LANES), F32)], axis=0
                )
                blocks[c, z * V + a] = result[a]
            return tuple(result)

        start = tuple(
            jnp.concatenate([jnp.zeros((8, LANES), F32), unit(a)], axis=0) for a in range(V)
        )
        ends = lax.fori_loop(0, cells, back, start)
        for a in range(V):
            group[c, a] = ends[a][:8]
            group[c, V + a] = ends[a][8:]
            group[c, 2 * V + a] = through[a]


def own_share(share, c):
    if share is None:
        nothing = [jnp.zeros((8, LANES), F32)] * V
        return [[unit(a) for a in range(V)], nothing, [unit(a) for a in range(V)]]
    return [tiles(share, c, kind) for kind in range(3)]


def merge_matrices(right, last_right, mine, other, share, mats, merged, share_out, last):
    for c in range(2):
        group = lambda ref, kind: [ref[NEAR_TILES + (c * 3 + kind) * V + a] for a in range(V)]
        pick = lambda kind, own: [jnp.where(own, m, t) for m, t in zip(group(mine, kind), group(other, kind))]
        left = jnp.logical_not(right)
        own = own_share(share, c)
        nothing = jnp.zeros((8, LANES), F32)
        for kind, values in (
            (0, pick(2, right)),
            (1, pick(0, right)),
            (2, pick(1, left)),
            (3, [jnp.where(right, x, nothing) for x in own[0]]),
            (4, [jnp.where(right, x, nothing) for x in own[1]]),
            (5, [jnp.where(right, nothing, x) for x in own[2]]),
        ):
            for a in range(V):
                mats[c, kind * V + a] = values[a]
        p_left, g_left, h_right = pick(2, left), pick(0, left), pick(1, right)
        turned = times(rows(mats, c, 1), p_left)
        new_g = plus(g_left, times(rows(mats, c, 2), turned))
        if last:
            for a in range(V):
                merged[NEAR_TILES // 2 + c * V + a] = new_g[a]
        else:
            new_h = times(rows(mats, c, 2), h_right)
            new_p = times(rows(mats, c, 0), p_left)
            for a in range(V):
                merged[NEAR_TILES + c * 3 * V + a] = new_g[a]
                merged[NEAR_TILES + (c * 3 + 1) * V + a] = new_h[a]
                merged[NEAR_TILES + (c * 3 + 2) * V + a] = new_p[a]
        s0 = times(rows(mats, c, 3), p_left)
        s1 = times(rows(mats, c, 4), p_left)
        s1b = times(rows(mats, c, 5), turned)
        s2 = times(rows(mats, c, 5), h_right)
        for a in range(V):
            share_out[c, a] = jnp.where(right, s0[a], own[0][a])
            share_out[c, V + a] = jnp.where(right, s1[a], own[1][a] + s1b[a])
            share_out[c, 2 * V + a] = jnp.where(right, own[2][a], s2[a])


def last_matrices(right, mine, other, share, mats):
    nothing = jnp.zeros((8, LANES), F32)
    for c in range(2):
        for a in range(V):
            i = NEAR_TILES // 2 + c * V + a
            mats[c, V + a] = jnp.where(right, mine[i], other[i])
            mats[c, 3 * V + a] = jnp.where(right, share[c, a], nothing)
            mats[c, 4 * V + a] = jnp.where(right, share[c, V + a], nothing)
            mats[c, 5 * V + a] = jnp.where(right, nothing, share[c, 2 * V + a])


def inflow_of(c, mats, f_left, g_right, known):
    back = plus(g_right, times(rows(mats, c, 1), f_left))
    from_left = times(rows(mats, c, 3), f_left)
    from_right = plus(times(rows(mats, c, 4), f_left), times(rows(mats, c, 5), back))
    total = from_left + from_right
    return back, total if known is None else plus(known, total)


def merge_flows(right, last_right, c, mats, flows, other, known, merged, inflow, height, last):
    def tile(t, carry):
        mine = [flows[i * height + t] for i in range(2 * V)]
        theirs = [other[i * height + t] for i in range(2 * V)]
        f_left = [jnp.where(right, y, x) for x, y in zip(mine[:V], theirs[:V])]
        f_right = [jnp.where(right, x, y) for x, y in zip(mine[:V], theirs[:V])]
        g_left = [jnp.where(right, y, x) for x, y in zip(mine[V:], theirs[V:])]
        g_right = [jnp.where(right, x, y) for x, y in zip(mine[V:], theirs[V:])]
        before = None if known is None else [known[i * height + t] for i in range(2 * V)]
        back, total = inflow_of(c, mats, f_left, g_right, before)
        new_f = plus(f_right, times(rows(mats, c, 0), f_left))
        new_g = plus(g_left, times(rows(mats, c, 2), back))
        if last:
            ends = [jnp.where(last_right, y, x) for x, y in zip(new_f, new_g)]
        else:
            ends = new_f + new_g
        for i, value in enumerate(ends):
            merged[i * height + t] = value
        for i, value in enumerate(total):
            inflow[i * height + t] = value
        return carry

    lax.fori_loop(0, height, tile, 0)


def merge_near(bit, levels, flags, *refs):
    start, last = bit == 0, bit == levels - 2
    if start:
        flows, other, mats, merged, share_out, inflow = refs
        share = known = None
    else:
        flows, other, share, known, mats, merged, share_out, inflow = refs
    right, last_right = flags[3 + bit] == 1, flags[2 + levels] == 1
    merge_matrices(right, last_right, flows, other, share, mats, merged, share_out, last)
    merge_flows(right, last_right, 0, mats, flows, other, known, merged, inflow, PAD // 8, last)


def merge_far(bit, levels, flags, mats, flows, other, *refs):
    known, merged, inflow = (None, *refs) if bit == 0 else refs
    right, last_right = flags[3 + bit] == 1, flags[2 + levels] == 1
    last = bit == levels - 2
    height = flows.shape[0] // (2 * V)
    merge_flows(right, last_right, 1, mats, flows, other, known, merged, inflow, height, last)


def last_inflow(right, c, mats, ends, other, known, height, store):
    for t in range(height):
        mine = [ends[a * height + t] for a in range(V)]
        theirs = [other[a * height + t] for a in range(V)]
        f_left = [jnp.where(right, y, x) for x, y in zip(mine, theirs)]
        g_right = [jnp.where(right, x, y) for x, y in zip(mine, theirs)]
        before = [known[i * height + t] for i in range(2 * V)]
        _, total = inflow_of(c, mats, f_left, g_right, before)
        for i, value in enumerate(total):
            store(i, t, value)


def corrected(c, z, a, first, last, g, blocks, inflow):
    total = g[z * V + a, first:last, :]
    for b in range(V):
        total += blocks[c, z * V + a, b : b + 1, :] * inflow[b]
        total += blocks[c, z * V + a, 8 + b : 9 + b, :] * inflow[V + b]
    return total


def correct(c, right, mats, ends, other, known, g, blocks, result, inflow):
    def store(i, t, value):
        inflow[i, t * 8 : t * 8 + 8, :] = value

    height = g.shape[1]
    last_inflow(right, c, mats, ends, other, known, height // 8, store)
    cells = g.shape[0] // V
    for first, last in ((0, 32), (32, height)) if height > 32 else ((0, height),):
        flow = tuple(inflow[i, first:last, :] for i in range(2 * V))

        def step(z, flow, first=first, last=last):
            for a in range(V):
                result[z * V + a, first:last, :] = corrected(c, z, a, first, last, g, blocks, flow)
            return flow

        lax.fori_loop(0, cells, step, flow)


def correct_near(levels, flags, ends, other, share, known, g, blocks, result, mats, inflow):
    right = flags[2 + levels] == 1
    last_matrices(right, ends, other, share, mats)
    correct(0, right, mats, ends, other, known, g, blocks, result, inflow)


def correct_far(levels, flags, mats, ends, other, known, g, blocks, result, inflow):
    correct(1, flags[2 + levels] == 1, mats, ends, other, known, g, blocks, result, inflow)


def finish(levels, flags, mats, ends, other, known, g, blocks, near, *refs):
    done, out, inflow = refs[:-2], refs[-2], refs[-1]
    right = flags[2 + levels] == 1
    p = flags[0]
    first_row, last_row = CHUNKS[-1][0]
    width = last_row - first_row

    @pl.when(pl.program_id(0) == 0)
    def _():
        def store(i, t, value):
            inflow[i, t * 8 : t * 8 + 8, :] = value

        last_inflow(right, 1, mats, ends, other, known, width // 8, store)

    flow = tuple(inflow[i] for i in range(2 * V))

    def step(z, carry):
        for a in range(V):
            j = z * V + a
            row = j * 2 * NT
            out[pl.ds(row + 1 - p, NT, stride=2), :] = near[j, 0:NT, :]
            for ref, ((first, last), extra) in zip(done, CHUNKS):
                out[pl.ds(row + p + 2 * first, last - first, stride=2), :] = ref[j, 0 : last - first, :]
                if extra:
                    out[pl.ds(row + p + 2 * (NT - 1), 1), :] = ref[j, last - first : last - first + 1, :]
            out[pl.ds(row + p + 2 * first_row, width, stride=2), :] = corrected(1, z, a, 0, width, g, blocks, flow)
        return carry

    lax.fori_loop(0, g.shape[0] // V, step, 0)


def phase_tables(count):
    angle = 2.0 * math.pi * np.outer(np.arange(1, count + 1), np.arange(NT)) / NT
    cosine, sine = np.cos(angle), np.sin(angle)
    basis = np.zeros((PAD, 2 * count + 8), np.float32)
    basis[:NT, :count], basis[:NT, count : 2 * count], basis[:NT, 2 * count] = cosine.T, sine.T, 0.5
    turned = np.zeros((2, count + 8, 3, DEPTH), np.float32)
    turned[0, :count, :, :NT], turned[1, :count, :, :NT] = cosine[:, None], sine[:, None]
    turned[0, count, :, :NT] = 1.0
    return (2.0 / NT * basis).astype(np.float32), turned.reshape(2 * (count + 8), 3 * DEPTH)


def derivative_table():
    gap = np.arange(NT)[:, None] - np.arange(NT)[None, :]
    safe = np.where(gap == 0, 1.0, np.sin(np.pi * gap / NT))
    table = np.where(gap == 0, 0.0, 0.5 * (1.0 - 2.0 * np.mod(gap, 2)) / safe)
    wide = np.zeros((PAD, 3, DEPTH), np.float32)
    wide[:NT, :, :NT] = table[:, None]
    return wide.reshape(PAD, 3 * DEPTH)


NEAR_TILES = 2 * V * (PAD // 8)


def local(state, advect, viscous, inverse, lower, upper, blades, harmonic):
    cells = state.shape[0]
    count = harmonic.shape[0]
    segs, slabs = lax.axis_size("seg"), lax.axis_size("pitch")
    levels = segs.bit_length() - 1
    slab, seg = lax.axis_index("pitch"), lax.axis_index("seg")
    side = slab % 2
    wrap = jnp.logical_or(slab == 0, slab == slabs - 1)
    bits = [(seg >> k) & 1 for k in range(levels)]
    run = Chain(
        jnp.stack(
            [side, wrap.astype(jnp.int32), (slab == 0).astype(jnp.int32), *bits]
        ).astype(jnp.int32)
    )
    far_pairs = [(i, (i - 1) % slabs if i % 2 == 0 else (i + 1) % slabs) for i in range(slabs)]
    near_pairs = [(i, i ^ 1) for i in range(slabs)]
    to_far = lambda x: lax.ppermute(x, "pitch", far_pairs)
    to_level = lambda x, k: lax.ppermute(x, "seg", [(i, i ^ (1 << k)) for i in range(segs)])
    x_shape = (cells * V, PAD, LANES)

    st = state.transpose(0, 2, 3, 1, 4).reshape(cells * V * NT * 2, LANES)
    lead_rows = LEAD * V * NT
    slab_in = to_far(
        run(
            lead_cells, [(lead_rows, LANES)], [st], grid=(1,), name="lead_cells",
            in_specs=[pl.BlockSpec((2 * lead_rows, LANES), lambda i: (0, 0))],
            out_specs=[pl.BlockSpec((lead_rows, LANES), lambda i: (0, 0))],
        )[0]
    )

    ratio = blades[1].astype(F32) / blades[0].astype(F32)
    lag = 2.0 * math.pi * harmonic.astype(F32) * ratio
    trig = jnp.concatenate([jnp.cos(lag), jnp.sin(lag), jnp.full((8,), ratio / count)])
    trig = jnp.broadcast_to(trig[:, None], (2 * count + 8, LANES))
    basis, turned = phase_tables(count)
    table = derivative_table()

    rest = (cells - LEAD) * V
    chunk_shapes = [
        (rest * (last - first) + (padded_even(rest) if extra else 0), LANES)
        for (first, last), extra in CHUNKS
    ]
    edge_shape = (2 * V, PAD, LANES)
    xn, xf, first_cell, last_cell, *chunks = run(
        prepare, [x_shape, x_shape, edge_shape, edge_shape, *chunk_shapes], [st, trig, basis, turned],
        name="prepare",
    )
    halo_near = lax.ppermute(xn, "pitch", near_pairs)
    from_left = lax.ppermute(last_cell, "seg", [(i, i + 1) for i in range(segs - 1)])
    from_right = lax.ppermute(first_cell, "seg", [(i + 1, i) for i in range(segs - 1)])
    arrived, before = [], slab_in
    for chunk in chunks:
        if arrived:
            chunk, before = lax.optimization_barrier((chunk, before))
            if len(arrived) == 1:
                slab_in = before
            else:
                arrived[-2] = before
            before = arrived[-1]
        arrived.append(to_far(chunk))

    flat = lambda x: x.transpose(0, 2, 3, 1, 4).reshape(cells * V * V * 2, LANES)
    inv, low, upp = flat(inverse.astype(F32)), flat(lower), flat(upper)
    adv = advect.transpose(0, 2, 1, 3).reshape(cells * V * 2, LANES)
    vis = viscous.transpose(0, 2, 1, 3).reshape(cells * V * 2, LANES)

    blocks, group = run(
        transfer, [(2, cells * V, 16, LANES), (2, 3 * V, 8, LANES)], [low, upp],
        scratch=[pltpu.VMEM((cells * V, 8, LANES), F32)], name="transfer",
    )
    g_near, flows_near = run(
        near_cell, [x_shape, (NEAR_TILES + 6 * V, 8, LANES)],
        [xn, xf, halo_near, from_left, from_right, adv, vis, inv, low, upp, trig, table, group],
        scratch=[pltpu.VMEM(x_shape, F32)], name="near_cell",
    )
    base = run(
        far_base, [x_shape],
        [xn, xf, from_left, from_right, slab_in, adv, vis, trig, table, basis, turned],
        scratch=[pltpu.VMEM((V, PAD, LANES), F32)], name="far_base",
    )[0]

    mats, near_state = [], []
    mats_shape, share_shape = (2, 6 * V, 8, LANES), (2, 3 * V, 8, LANES)

    def near_level(k):
        nonlocal flows_near, near_state
        shape = (NEAR_TILES + 6 * V if k < levels - 2 else NEAR_TILES // 2 + 2 * V, 8, LANES)
        out = run(
            functools.partial(merge_near, k, levels),
            [mats_shape, shape, share_shape, (NEAR_TILES, 8, LANES)],
            [flows_near, to_level(flows_near, k), *near_state], name="merge_near",
        )
        mats.append(out[0])
        flows_near, near_state = out[1], out[2:]

    def far_solve(i):
        height = rows_of(CHUNKS[i])
        g, flows = run(
            functools.partial(far_chunk, CHUNKS[i]),
            [(cells * V, height, LANES), (2 * V * height // 8, 8, LANES)],
            [base, arrived[i], vis, inv, low, upp], name="far_chunk",
        )
        return [g, flows, None]

    def far_level(k, item):
        g, flows, known = item
        count = flows.shape[0]
        out = run(
            functools.partial(merge_far, k, levels),
            [(count if k < levels - 2 else count // 2, 8, LANES), (count, 8, LANES)],
            [mats[k], flows, to_level(flows, k)] + ([] if known is None else [known]), name="merge_far",
        )
        return [g, out[0], out[1]]

    def settle_far(item):
        g, ends, known = item
        return run(
            functools.partial(correct_far, levels), [g.shape],
            [mats[-1], ends, to_level(ends, levels - 1), known, g, blocks],
            scratch=[pltpu.VMEM((2 * V, g.shape[1], LANES), F32)], name="correct_far",
        )[0]

    near_level(0)
    one = far_solve(0)
    for k in range(1, levels - 1):
        near_level(k)
    for k in range(levels - 1):
        one = far_level(k, one)
    near, last = run(
        functools.partial(correct_near, levels), [x_shape, mats_shape],
        [flows_near, to_level(flows_near, levels - 1), *near_state, g_near, blocks],
        scratch=[pltpu.VMEM((2 * V, PAD, LANES), F32)], name="correct_near",
    )
    mats.append(last)
    two = far_solve(1)
    two = far_level(0, two)
    done = [settle_far(one)]
    three = far_solve(2)
    for k in range(1, levels - 1):
        two = far_level(k, two)
    three = far_level(0, three)
    done.append(settle_far(two))
    for k in range(1, levels - 1):
        three = far_level(k, three)
    g_last, ends, known = three

    steps = 4
    part = cells // steps
    whole = lambda x: pl.BlockSpec(x.shape, lambda i: (0,) * x.ndim)
    by_cell = lambda x: pl.BlockSpec((part * V,) + x.shape[1:], lambda i: (i, 0, 0))
    small = [mats[-1], ends, to_level(ends, levels - 1), known]
    out = run(
        functools.partial(finish, levels), [st.shape], [*small, g_last, blocks, near, *done],
        grid=(steps,),
        in_specs=[whole(x) for x in small]
        + [by_cell(g_last), pl.BlockSpec((2, part * V, 16, LANES), lambda i: (0, i, 0, 0))]
        + [by_cell(x) for x in (near, *done)],
        out_specs=[pl.BlockSpec((part * V * NT * 2, LANES), lambda i: (i, 0))],
        scratch=[pltpu.VMEM((2 * V, rows_of(CHUNKS[-1]), LANES), F32)], name="finish",
    )[0]
    return out.reshape(cells, V, NT, 2, LANES).transpose(0, 3, 1, 2, 4)


def solution(mesh):
    cell = P("seg", "pitch", None, None, None)
    return jax.shard_map(
        local,
        mesh=mesh,
        in_specs=(cell, P("seg", "pitch", None, None), P("seg", "pitch", None, None), cell, cell, cell, P(), P()),
        out_specs=cell,
        check_vma=False,
    )
```

```python
import functools
import math

import jax
import jax.numpy as jnp
import numpy as np
from jax import lax
from jax.experimental import pallas as pl
from jax.experimental.pallas import tpu as pltpu
from jax.sharding import PartitionSpec as P

F32 = jnp.float32
BF16 = jnp.bfloat16
V = 5
NT = 49
PAD = 56
DEPTH = 64
LANES = 128
LEAD = 4
MB = 1 << 20

CHUNKS = (((0, 8), False), ((8, 24), False), ((24, 40), True), ((40, 48), False))


def rows_of(chunk):
    (first, last), extra = chunk
    return last - first + (8 if extra else 0)


def padded_even(count):
    return (count + 7) // 8 * 8


class Chain:
    def __init__(self, flags):
        self.flags = flags

    def after(self, array):
        self.flags, array = lax.optimization_barrier((self.flags, array))
        return array

    def __call__(self, body, out_shapes, arrays, scratch=(), vmem=24, name=None, grid=None, in_specs=None, out_specs=None, scalars=()):
        smem = pl.BlockSpec(memory_space=pltpu.SMEM)
        held = pl.BlockSpec(memory_space=pltpu.VMEM)
        extra = {} if grid is None else {"grid": grid}
        out = pl.pallas_call(
            body,
            out_shape=[jax.ShapeDtypeStruct(s, F32) for s in out_shapes],
            in_specs=[smem] * (1 + len(scalars)) + (in_specs or [held] * len(arrays)),
            out_specs=out_specs or [held] * len(out_shapes),
            scratch_shapes=list(scratch),
            compiler_params=pltpu.CompilerParams(vmem_limit_bytes=vmem * MB),
            cost_estimate=pl.CostEstimate(flops=1000, bytes_accessed=1000, transcendentals=0),
            name=name,
            **extra,
        )(self.flags, *scalars, *arrays)
        out = list(out)
        out[0] = self.after(out[0])
        return out


def coefficient(ref, z, a, b, p):
    return ref[pl.ds(((z * V + a) * V + b) * 2 + p, 1), :]


def split_left(matrix):
    high = matrix.astype(BF16).astype(F32)
    place = lax.broadcasted_iota(jnp.int32, matrix.shape, 1)
    return jnp.where(place < 2 * DEPTH, high, matrix - high).astype(BF16)


def lag_matrix(basis, turned, trig, sign):
    half = turned.shape[0] // 2
    count = (half - 4) // 8 * 8
    cosine, sine = turned[:half], turned[half:]
    turn, cross = trig[:count, :1], trig[count : 2 * count, :1] * sign
    right = jnp.concatenate(
        [
            turn * cosine[:count] + cross * sine[:count],
            turn * sine[:count] - cross * cosine[:count],
            cosine[count:],
        ],
        axis=0,
    )
    return jnp.dot(basis, right, preferred_element_type=F32, precision=lax.Precision.HIGHEST)


def over_instants(left, cells):
    whole = jnp.concatenate(cells, axis=1)
    if whole.shape[0] < DEPTH:
        whole = jnp.concatenate(
            [whole, jnp.zeros((DEPTH - whole.shape[0], whole.shape[1]), F32)], axis=0
        )
    high = whole.astype(BF16)
    low = (whole - high.astype(F32)).astype(BF16)
    product = jnp.dot(
        left, jnp.concatenate([high, low, high], axis=0), preferred_element_type=F32
    )
    return [product[:, i * LANES : (i + 1) * LANES] for i in range(len(cells))]


def split_cells(st, slab, first_cell, last_cell, xn, xf):
    p = lax.axis_index("pitch") % 2
    edge = first_cell.shape[0]
    zeros = jnp.zeros((8, LANES), F32)
    width = 4 * NT

    def step(i, carry):
        slab[pl.ds(i * width, width), :] = st[pl.ds(i * 2 * width + p, width, stride=2), :]
        return carry

    lax.fori_loop(0, LEAD * V // 4, step, 0)
    first_cell[...] = st[0:edge, :]
    last_cell[...] = st[st.shape[0] - edge :, :]

    def separate(z, carry):
        for v in range(V):
            j = z * V + v
            for out, q in ((xn, 1 - p), (xf, p)):
                out[j, PAD - 8 : PAD, :] = zeros
                out[j, 0:NT, :] = st[pl.ds(j * 2 * NT + q, NT, stride=2), :]
        return carry

    lax.fori_loop(0, xn.shape[0] // V, separate, 0)


def lags(blades, harmonic, trig):
    count = harmonic.shape[0]
    rotor = jnp.full(harmonic.shape, blades[0]).astype(F32)
    stator = jnp.full(harmonic.shape, blades[1]).astype(F32)
    turns = harmonic[...] * stator
    lag = (turns - rotor * jnp.floor(turns / rotor)) / rotor * (2.0 * math.pi)
    trig[0:count, :] = jnp.cos(lag)
    trig[count : 2 * count, :] = jnp.sin(lag)
    trig[2 * count : 2 * count + 8, :] = (stator / rotor / count)[:8]


def prepare(flags, blades, xf, harmonic, basis, turned, trig, *chunks):
    lags(blades, harmonic, trig)
    wrap = flags[1]
    cells = xf.shape[0] // V
    sign = jnp.where(flags[2] == 1, 1.0, -1.0)
    left = split_left(lag_matrix(basis[...], turned[...], trig[...], sign))

    def step(z, carry):
        raw = [xf[z * V + v] for v in range(V)]
        lagged = over_instants(left, raw)
        for v in range(V):
            value = jnp.where(wrap == 1, lagged[v], raw[v])
            j = (z - LEAD) * V + v
            for out, ((first, last), extra) in zip(chunks, CHUNKS):
                width = last - first
                out[pl.ds(pl.multiple_of(j * width, 8), width), :] = value[first:last]
                if extra:
                    out[pl.ds((cells - LEAD) * V * width + j, 1), :] = value[NT - 1 : NT]
        return carry

    lax.fori_loop(LEAD, cells, step, 0)


def keep_tiles(ref, offset, values, first, last, height):
    for a in range(V):
        for t in range(first // 8, last // 8):
            ref[offset + a * height + t] = values[a][t * 8 - first : t * 8 - first + 8]


def sweeps(source, g, fg, offset, spans, p, inverse, lower, upper, cells):
    height = g.shape[1] // 8
    for first, last in spans:
        nothing = tuple(jnp.zeros((last - first, LANES), F32) for _ in range(V))

        def ahead(z, current, first=first, last=last):
            right = source(z, first, last)
            result = []
            for a in range(V):
                total = coefficient(inverse, z, a, 0, p) * right[0]
                for b in range(1, V):
                    total += coefficient(inverse, z, a, b, p) * right[b]
                for b in range(V):
                    total += coefficient(lower, z, a, b, p) * current[b]
                g[z * V + a, first:last, :] = total
                result.append(total)
            return tuple(result)

        out = lax.fori_loop(0, cells, ahead, nothing)
        keep_tiles(fg, offset, out, first, last, height)

        def back(i, current, first=first, last=last):
            z = cells - 1 - i
            result = []
            for a in range(V):
                total = g[z * V + a, first:last, :]
                for b in range(V):
                    total += coefficient(upper, z, a, b, p) * current[b]
                g[z * V + a, first:last, :] = total
                result.append(total)
            return tuple(result)

        out = lax.fori_loop(0, cells, back, nothing)
        keep_tiles(fg, offset + V * height, out, first, last, height)


def take_edges(edges, from_left, from_right, p):
    skip = from_left.shape[0] - V * NT * 2
    for v in range(V):
        edges[v, PAD - 8 : PAD, :] = jnp.zeros((8, LANES), F32)
        edges[v, 0:NT, :] = from_left[pl.ds(skip + v * 2 * NT + p, NT, stride=2), :]
        edges[V + v, PAD - 8 : PAD, :] = jnp.zeros((8, LANES), F32)
        edges[V + v, 0:NT, :] = from_right[pl.ds(v * 2 * NT + p, NT, stride=2), :]


def residuals(x, other, halo, edges, advect, viscous, left, p, cells, put):
    def one(z, above, below):
        here = [x[z * V + v] for v in range(V)]
        timing = over_instants(left, here)
        for v in range(V):
            j = z * V + v
            pitch = other[j] - 2.0 * here[v]
            if halo is not None:
                pitch += halo[j]
            put(
                j,
                advect[pl.ds(j * 2 + p, 1), :] * (above(z, v) - below(z, v))
                + viscous[pl.ds(j * 2 + p, 1), :] * pitch
                - timing[v],
            )

    inner_above = lambda z, v: x[(z - 1) * V + v]
    inner_below = lambda z, v: x[(z + 1) * V + v]
    one(0, lambda z, v: edges[v], inner_below)

    def step(z, carry):
        one(z, inner_above, inner_below)
        return carry

    lax.fori_loop(1, cells - 1, step, 0)
    one(cells - 1, inner_above, lambda z, v: edges[V + v])


def timing_matrix(table, trig):
    return split_left(table[...] * trig[trig.shape[0] - 8 : trig.shape[0] - 7, :1])


def near_cell(
    flags, xn, xf, halo, from_left, from_right, advect, viscous, inverse, lower, upper, trig, table,
    g, flows, right, edges,
):
    p = 1 - flags[0]
    cells = xn.shape[0] // V
    take_edges(edges, from_left, from_right, p)

    def put(j, value):
        right[j] = value

    residuals(xn, xf, halo, edges, advect, viscous, timing_matrix(table, trig), p, cells, put)
    source = lambda z, first, last: [right[z * V + v, first:last, :] for v in range(V)]
    sweeps(source, g, flows, 0, ((0, 32), (32, PAD)), p, inverse, lower, upper, cells)


def far_base(flags, xn, xf, from_left, from_right, advect, viscous, trig, table, base, edges):
    p = flags[0]
    cells = xn.shape[0] // V
    take_edges(edges, from_left, from_right, p)

    def put(j, value):
        base[j] = value

    residuals(xf, xn, None, edges, advect, viscous, timing_matrix(table, trig), p, cells, put)


def far_lead(flags, slab, trig, basis, turned, lead, halo):
    wrap = flags[1]
    sign = jnp.where(flags[2] == 1, -1.0, 1.0)
    left = split_left(lag_matrix(basis[...], turned[...], trig[...], sign))
    for z in range(LEAD):
        for v in range(V):
            halo[v, PAD - 8 : PAD, :] = jnp.zeros((8, LANES), F32)
            halo[v, 0:NT, :] = slab[pl.ds((z * V + v) * NT, NT), :]
        raw = [halo[v] for v in range(V)]
        lagged = over_instants(left, raw)
        for v in range(V):
            lead[z * V + v] = jnp.where(wrap == 1, lagged[v], raw[v])


def far_chunk(chunk, flags, base, lead, halo, viscous, inverse, lower, upper, *refs):
    others, (g, fg) = refs[:-2], refs[-2:]
    (first, last), extra = chunk
    width = last - first
    p = flags[0]
    cells = base.shape[0] // V
    top = lax.broadcasted_iota(jnp.int32, (8, LANES), 0) == 0
    offset = 0
    for other in others:
        fg[0 : other.shape[0]] = other[...]
        offset = other.shape[0]

    def pieces(ref, j, rows):
        value = ref[j, first:last, :]
        return jnp.concatenate([value, ref[j, PAD - 8 : PAD, :]], axis=0) if extra else value

    def source(z, start, stop):
        result = []
        for v in range(V):
            j = z * V + v
            h = jnp.maximum(z - LEAD, 0) * V + v
            arrived = halo[pl.ds(pl.multiple_of(h * width, 8), width), :]
            if extra:
                row = halo[pl.ds((cells - LEAD) * V * width + h, 1), :]
                arrived = jnp.concatenate([arrived, jnp.where(top, row, 0.0)], axis=0)
            early = pieces(lead, jnp.minimum(z, LEAD - 1) * V + v, rows)
            arrived = jnp.where(z >= LEAD, arrived, early)
            result.append(pieces(base, j, rows) + viscous[pl.ds(j * 2 + p, 1), :] * arrived)
        return result

    height = rows_of(chunk)
    sweeps(source, g, fg, offset, ((0, height),), p, inverse, lower, upper, cells)


def times(matrix, vector):
    result = []
    for a in range(V):
        total = matrix(a, 0) * vector[0]
        for b in range(1, V):
            total += matrix(a, b) * vector[b]
        result.append(total)
    return result


def plus(one, two):
    return [a + b for a, b in zip(one, two)]


def tiles(ref, c, kind):
    return [ref[c, kind * V + a] for a in range(V)]


def rows(ref, c, kind):
    return lambda a, b: ref[c, kind * V + a, b : b + 1, :]


def unit(a):
    place = lax.broadcasted_iota(jnp.int32, (8, LANES), 0)
    return jnp.where(place == a, 1.0, 0.0).astype(F32)


def transfer(flags, lower, upper, blocks, group, forward):
    cells = blocks.shape[1] // V
    for c in range(2):
        p = 1 - flags[0] if c == 0 else flags[0]

        def ahead(z, current):
            result = times(lambda a, b: coefficient(lower, z, a, b, p), current)
            for a in range(V):
                forward[z * V + a] = result[a]
            return tuple(result)

        through = lax.fori_loop(0, cells, ahead, tuple(unit(a) for a in range(V)))

        def back(i, current):
            z = cells - 1 - i
            result = times(lambda a, b: coefficient(upper, z, a, b, p), current)
            for a in range(V):
                result[a] = result[a] + jnp.concatenate(
                    [forward[z * V + a], jnp.zeros((8, LANES), F32)], axis=0
                )
                blocks[c, z * V + a] = result[a]
            return tuple(result)

        start = tuple(
            jnp.concatenate([jnp.zeros((8, LANES), F32), unit(a)], axis=0) for a in range(V)
        )
        ends = lax.fori_loop(0, cells, back, start)
        for a in range(V):
            group[c, a] = ends[a][:8]
            group[c, V + a] = ends[a][8:]
            group[c, 2 * V + a] = through[a]


def merge_matrices(bit, levels, flags, *refs):
    start, last = bit == 0, bit == levels - 1
    refs = list(refs)
    mine, other = refs.pop(0), refs.pop(0)
    share = None if start else refs.pop(0)
    mats = refs.pop(0)
    merged, share_out = (None, None) if last else refs
    right = flags[3 + bit] == 1
    left = jnp.logical_not(right)
    nothing = jnp.zeros((8, LANES), F32)
    for c in range(2):
        pick = lambda kind, own: [jnp.where(own, m, t) for m, t in zip(tiles(mine, c, kind), tiles(other, c, kind))]
        if start:
            own = [[unit(a) for a in range(V)], [nothing] * V, [unit(a) for a in range(V)]]
        else:
            own = [tiles(share, c, kind) for kind in range(3)]
        found = [
            (1, pick(0, right)),
            (3, [jnp.where(right, x, nothing) for x in own[0]]),
            (4, [jnp.where(right, x, nothing) for x in own[1]]),
            (5, [jnp.where(right, nothing, x) for x in own[2]]),
        ]
        if not last:
            found += [(0, pick(2, right)), (2, pick(1, left))]
        for kind, values in found:
            for a in range(V):
                mats[c, kind * V + a] = values[a]
        if last:
            continue
        p_left, g_left, h_right = pick(2, left), pick(0, left), pick(1, right)
        turned = times(rows(mats, c, 1), p_left)
        new = [plus(g_left, times(rows(mats, c, 2), turned))]
        if bit < levels - 2:
            new += [times(rows(mats, c, 2), h_right), times(rows(mats, c, 0), p_left)]
        for kind, values in enumerate(new):
            for a in range(V):
                merged[c, kind * V + a] = values[a]
        s0 = times(rows(mats, c, 3), p_left)
        s1 = times(rows(mats, c, 4), p_left)
        s1b = times(rows(mats, c, 5), turned)
        s2 = times(rows(mats, c, 5), h_right)
        for a in range(V):
            share_out[c, a] = jnp.where(right, s0[a], own[0][a])
            share_out[c, V + a] = jnp.where(right, s1[a], own[1][a] + s1b[a])
            share_out[c, 2 * V + a] = jnp.where(right, own[2][a], s2[a])


def inflow_of(c, mats, f_left, g_right, known):
    back = plus(g_right, times(rows(mats, c, 1), f_left))
    from_left = times(rows(mats, c, 3), f_left)
    from_right = plus(times(rows(mats, c, 4), f_left), times(rows(mats, c, 5), back))
    total = from_left + from_right
    return back, total if known is None else plus(known, total)


def merge_flows(parts, bit, levels, flags, mats, flows, other, *refs):
    known, merged, inflow = (None, *refs) if bit == 0 else refs
    right, last_right = flags[3 + bit] == 1, flags[2 + levels] == 1
    last = bit == levels - 2
    start = 0
    for c, height in parts:

        def tile(t, carry, c=c, height=height, start=start):
            at = lambda i: start * 2 * V + i * height + t
            mine = [flows[at(i)] for i in range(2 * V)]
            theirs = [other[at(i)] for i in range(2 * V)]
            f_left = [jnp.where(right, y, x) for x, y in zip(mine[:V], theirs[:V])]
            f_right = [jnp.where(right, x, y) for x, y in zip(mine[:V], theirs[:V])]
            g_left = [jnp.where(right, y, x) for x, y in zip(mine[V:], theirs[V:])]
            g_right = [jnp.where(right, x, y) for x, y in zip(mine[V:], theirs[V:])]
            before = None if known is None else [known[at(i)] for i in range(2 * V)]
            back, total = inflow_of(c, mats, f_left, g_right, before)
            new_f = plus(f_right, times(rows(mats, c, 0), f_left))
            new_g = plus(g_left, times(rows(mats, c, 2), back))
            if last:
                for i in range(V):
                    end = jnp.where(last_right, new_g[i], new_f[i])
                    merged[start * V + i * height + t] = end
            else:
                for i, value in enumerate(new_f + new_g):
                    merged[at(i)] = value
            for i, value in enumerate(total):
                inflow[at(i)] = value
            return carry

        lax.fori_loop(0, height, tile, 0)
        start += height


def last_inflow(right, c, mats, ends, other, known, start, height, inflow):
    for t in range(height):
        mine = [ends[start * V + a * height + t] for a in range(V)]
        theirs = [other[start * V + a * height + t] for a in range(V)]
        f_left = [jnp.where(right, y, x) for x, y in zip(mine, theirs)]
        g_right = [jnp.where(right, x, y) for x, y in zip(mine, theirs)]
        before = [known[start * 2 * V + i * height + t] for i in range(2 * V)]
        _, total = inflow_of(c, mats, f_left, g_right, before)
        for i, value in enumerate(total):
            inflow[i, t * 8 : t * 8 + 8, :] = value


def corrected(c, z, a, first, last, g, blocks, inflow):
    total = g[z * V + a, first:last, :]
    for b in range(V):
        total += blocks[c, z * V + a, b : b + 1, :] * inflow[b]
        total += blocks[c, z * V + a, 8 + b : 9 + b, :] * inflow[V + b]
    return total


def correct(parts, levels, flags, mats, ends, other, known, blocks, *refs):
    solved, results, inflow = refs[: len(parts)], refs[len(parts) : -1], refs[-1]
    right = flags[2 + levels] == 1
    start = 0
    for (c, tall), g, result in zip(parts, solved, results):
        last_inflow(right, c, mats, ends, other, known, start, tall, inflow)
        start += tall
        height = tall * 8
        for first, last in ((0, 32), (32, height)) if height > 32 else ((0, height),):
            flow = tuple(inflow[i, first:last, :] for i in range(2 * V))

            def step(z, flow, c=c, first=first, last=last, g=g, result=result):
                for a in range(V):
                    result[z * V + a, first:last, :] = corrected(c, z, a, first, last, g, blocks, flow)
                return flow

            lax.fori_loop(0, g.shape[0] // V, step, flow)


def finish(levels, flags, mats, ends, other, known, g, blocks, near, *refs):
    done, out, inflow = refs[:-2], refs[-2], refs[-1]
    right = flags[2 + levels] == 1
    p = flags[0]
    first_row, last_row = CHUNKS[-1][0]
    width = last_row - first_row

    @pl.when(pl.program_id(0) == 0)
    def _():
        last_inflow(right, 1, mats, ends, other, known, 0, width // 8, inflow)

    flow = tuple(inflow[i] for i in range(2 * V))

    def step(z, carry):
        for a in range(V):
            j = z * V + a
            row = j * 2 * NT
            out[pl.ds(row + 1 - p, NT, stride=2), :] = near[j, 0:NT, :]
            for ref, ((first, last), extra) in zip(done, CHUNKS):
                out[pl.ds(row + p + 2 * first, last - first, stride=2), :] = ref[j, 0 : last - first, :]
                if extra:
                    out[pl.ds(row + p + 2 * (NT - 1), 1), :] = ref[j, last - first : last - first + 1, :]
            out[pl.ds(row + p + 2 * first_row, width, stride=2), :] = corrected(1, z, a, 0, width, g, blocks, flow)
        return carry

    lax.fori_loop(0, g.shape[0] // V, step, 0)


def phase_tables(count):
    angle = 2.0 * math.pi * np.outer(np.arange(1, count + 1), np.arange(NT)) / NT
    cosine, sine = np.cos(angle), np.sin(angle)
    basis = np.zeros((PAD, 2 * count + 8), np.float32)
    basis[:NT, :count], basis[:NT, count : 2 * count], basis[:NT, 2 * count] = cosine.T, sine.T, 0.5
    turned = np.zeros((2, count + 8, 3, DEPTH), np.float32)
    turned[0, :count, :, :NT], turned[1, :count, :, :NT] = cosine[:, None], sine[:, None]
    turned[0, count, :, :NT] = 1.0
    return (2.0 / NT * basis).astype(np.float32), turned.reshape(2 * (count + 8), 3 * DEPTH)


def derivative_table():
    gap = np.arange(NT)[:, None] - np.arange(NT)[None, :]
    safe = np.where(gap == 0, 1.0, np.sin(np.pi * gap / NT))
    table = np.where(gap == 0, 0.0, 0.5 * (1.0 - 2.0 * np.mod(gap, 2)) / safe)
    wide = np.zeros((PAD, 3, DEPTH), np.float32)
    wide[:NT, :, :NT] = table[:, None]
    return wide.reshape(PAD, 3 * DEPTH)


def local(state, advect, viscous, inverse, lower, upper, blades, harmonic):
    cells = state.shape[0]
    count = harmonic.shape[0]
    segs, slabs = lax.axis_size("seg"), lax.axis_size("pitch")
    levels = segs.bit_length() - 1
    far_pairs = [(i, (i - 1) % slabs if i % 2 == 0 else (i + 1) % slabs) for i in range(slabs)]
    near_pairs = [(i, i ^ 1) for i in range(slabs)]
    to_far = lambda x: lax.ppermute(x, "pitch", far_pairs)
    to_level = lambda x, k: lax.ppermute(x, "seg", [(i, i ^ (1 << k)) for i in range(segs)])
    x_shape = (cells * V, PAD, LANES)

    st = state.transpose(0, 2, 3, 1, 4).reshape(cells * V * NT * 2, LANES)
    lead_rows, edge_rows = LEAD * V * NT, padded_even(V * NT * 2)
    held = pl.BlockSpec(memory_space=pltpu.VMEM)
    shapes = [(lead_rows, LANES), (edge_rows, LANES), (edge_rows, LANES), x_shape, x_shape]
    slab_out, first_cell, last_cell, xn, xf = pl.pallas_call(
        split_cells,
        out_shape=[jax.ShapeDtypeStruct(x, F32) for x in shapes],
        in_specs=[held],
        out_specs=[held] * 5,
        compiler_params=pltpu.CompilerParams(vmem_limit_bytes=16 * MB),
        name="split_cells",
    )(st)
    halo_near = lax.ppermute(xn, "pitch", near_pairs)
    slab_in = to_far(slab_out)
    from_left = lax.ppermute(last_cell, "seg", [(i, i + 1) for i in range(segs - 1)])
    from_right = lax.ppermute(first_cell, "seg", [(i + 1, i) for i in range(segs - 1)])

    slab, seg = lax.axis_index("pitch"), lax.axis_index("seg")
    side = slab % 2
    wrap = jnp.logical_or(slab == 0, slab == slabs - 1)
    bits = [(seg >> k) & 1 for k in range(levels)]
    run = Chain(
        jnp.stack(
            [side, wrap.astype(jnp.int32), (slab == 0).astype(jnp.int32), *bits]
        ).astype(jnp.int32)
    )
    run.after(slab_out)
    basis, turned = phase_tables(count)
    table = derivative_table()
    wide_harmonic = jnp.broadcast_to(harmonic.astype(F32)[:, None], (count, LANES))

    rest = (cells - LEAD) * V
    chunk_shapes = [
        (rest * (last - first) + (padded_even(rest) if extra else 0), LANES)
        for (first, last), extra in CHUNKS
    ]
    trig, *chunks = run(
        prepare, [(2 * count + 8, LANES), *chunk_shapes], [xf, wide_harmonic, basis, turned],
        scalars=[blades], name="prepare",
    )
    chunks[0], halo_near = lax.optimization_barrier((chunks[0], halo_near))
    arrived = [slab_in]
    for chunk in chunks:
        if len(arrived) >= 2:
            chunk, arrived[-2] = lax.optimization_barrier((chunk, arrived[-2]))
        arrived.append(to_far(chunk))
    slab_in, *arrived = arrived

    flat = lambda x: x.transpose(0, 2, 3, 1, 4).reshape(cells * V * V * 2, LANES)
    inv, low, upp = flat(inverse.astype(F32)), flat(lower), flat(upper)
    adv = advect.transpose(0, 2, 1, 3).reshape(cells * V * 2, LANES)
    vis = viscous.transpose(0, 2, 1, 3).reshape(cells * V * 2, LANES)
    edges = pltpu.VMEM((2 * V, PAD, LANES), F32)

    mats, group, share = [], None, []
    mats_shape = (2, 6 * V, 8, LANES)

    def merge_group(k):
        nonlocal group, share
        shapes = [mats_shape]
        if k < levels - 1:
            shapes += [(2, 3 * V if k < levels - 2 else V, 8, LANES), (2, 3 * V, 8, LANES)]
        out = run(
            functools.partial(merge_matrices, k, levels), shapes,
            [group, to_level(group, k), *share], name="merge_matrices",
        )
        mats.append(out[0])
        if k < levels - 1:
            group, share = out[1], [out[2]]

    def solve_chunk(i, others=()):
        height = rows_of(CHUNKS[i])
        tall = 2 * V * height // 8 + sum(x.shape[0] for x in others)
        g, flows = run(
            functools.partial(far_chunk, CHUNKS[i]), [(cells * V, height, LANES), (tall, 8, LANES)],
            [base, lead, arrived[i], vis, inv, low, upp, *others], name="far_chunk",
        )
        return g, flows

    class Exchange:
        def __init__(self, parts, flows, solved):
            self.parts = [(c, g.shape[1] // 8) for c, g in zip(parts, solved)]
            self.flows, self.known, self.solved, self.level = flows, [], solved, 0

        def step(self):
            tall = sum(h for _, h in self.parts)
            k = self.level
            out = run(
                functools.partial(merge_flows, self.parts, k, levels),
                [((2 if k < levels - 2 else 1) * V * tall, 8, LANES), (2 * V * tall, 8, LANES)],
                [mats[k], self.flows, to_level(self.flows, k), *self.known], name="merge_flows",
            )
            self.flows, self.known, self.level = out[0], [out[1]], k + 1

        def last(self):
            return [mats[-1], self.flows, to_level(self.flows, levels - 1), *self.known]

        def correct(self):
            tall = max(h for _, h in self.parts)
            return run(
                functools.partial(correct, self.parts, levels), [g.shape for g in self.solved],
                [*self.last(), blocks, *self.solved],
                scratch=[pltpu.VMEM((2 * V, tall * 8, LANES), F32)], name="correct",
            )

    blocks, group = run(
        transfer, [(2, cells * V, 16, LANES), (2, 3 * V, 8, LANES)], [low, upp],
        scratch=[pltpu.VMEM((cells * V, 8, LANES), F32)], name="transfer",
    )
    base = run(
        far_base, [x_shape], [xn, xf, from_left, from_right, adv, vis, trig, table],
        scratch=[edges], name="far_base",
    )[0]
    lead = run(
        far_lead, [(LEAD * V, PAD, LANES)], [slab_in, trig, basis, turned],
        scratch=[pltpu.VMEM((V, PAD, LANES), F32)], name="far_lead",
    )[0]
    g_near, flows_near = run(
        near_cell, [x_shape, (2 * V * PAD // 8, 8, LANES)],
        [xn, xf, halo_near, from_left, from_right, adv, vis, inv, low, upp, trig, table],
        scratch=[pltpu.VMEM(x_shape, F32), edges], name="near_cell",
    )
    g_first, flows = solve_chunk(0, [flows_near])
    first = Exchange([0, 1], flows, [g_near, g_first])
    for k in range(levels):
        merge_group(k)
    first.step()
    g, flows = solve_chunk(1)
    second = Exchange([1], flows, [g])
    first.step()
    second.step()
    g, flows = solve_chunk(2)
    third = Exchange([1], flows, [g])
    second.step()
    g, flows = solve_chunk(3)
    fourth = Exchange([1], flows, [g])
    third.step()
    for k in range(levels - 3):
        first.step()
        second.step()
    done_first = first.correct()
    fourth.step()
    done_second = second.correct()
    third.step()
    fourth.step()
    done_third = third.correct()
    for k in range(levels - 3):
        third.step()
        fourth.step()
    near, *done = [*done_first, *done_second, *done_third]
    g_last = fourth.solved[0]

    steps = 4
    part = cells // steps
    whole = lambda x: pl.BlockSpec(x.shape, lambda i: (0,) * x.ndim)
    by_cell = lambda x: pl.BlockSpec((part * V,) + x.shape[1:], lambda i: (i, 0, 0))
    small = fourth.last()
    out = run(
        functools.partial(finish, levels), [st.shape], [*small, g_last, blocks, near, *done],
        grid=(steps,),
        in_specs=[whole(x) for x in small]
        + [by_cell(g_last), pl.BlockSpec((2, part * V, 16, LANES), lambda i: (0, i, 0, 0))]
        + [by_cell(x) for x in (near, *done)],
        out_specs=[pl.BlockSpec((part * V * NT * 2, LANES), lambda i: (i, 0))],
        scratch=[pltpu.VMEM((2 * V, rows_of(CHUNKS[-1]), LANES), F32)], name="finish",
    )[0]
    return out.reshape(cells, V, NT, 2, LANES).transpose(0, 3, 1, 2, 4)


def solution(mesh):
    cell = P("seg", "pitch", None, None, None)
    return jax.shard_map(
        local,
        mesh=mesh,
        in_specs=(cell, P("seg", "pitch", None, None), P("seg", "pitch", None, None), cell, cell, cell, P(), P()),
        out_specs=cell,
        check_vma=False,
    )
```

```python
import functools
import math

import jax
import jax.numpy as jnp
import numpy as np
from jax import lax
from jax.experimental import pallas as pl
from jax.experimental.pallas import tpu as pltpu
from jax.sharding import PartitionSpec as P

F32 = jnp.float32
BF16 = jnp.bfloat16
V = 5
NT = 49
PAD = 56
DEPTH = 64
LANES = 128
LEAD = 4
MB = 1 << 20

CHUNKS = (((0, 32), False), ((32, 48), True))


def rows_of(chunk):
    (first, last), extra = chunk
    return last - first + (8 if extra else 0)


def padded_even(count):
    return (count + 7) // 8 * 8


class Chain:
    def __init__(self, flags):
        self.flags = flags

    def after(self, array):
        self.flags, array = lax.optimization_barrier((self.flags, array))
        return array

    def __call__(self, body, out_shapes, arrays, scratch=(), vmem=24, name=None, grid=None, in_specs=None, out_specs=None, scalars=(), flops=1000):
        smem = pl.BlockSpec(memory_space=pltpu.SMEM)
        held = pl.BlockSpec(memory_space=pltpu.VMEM)
        extra = {} if grid is None else {"grid": grid}
        out = pl.pallas_call(
            body,
            out_shape=[jax.ShapeDtypeStruct(s, F32) for s in out_shapes],
            in_specs=[smem] * (1 + len(scalars)) + (in_specs or [held] * len(arrays)),
            out_specs=out_specs or [held] * len(out_shapes),
            scratch_shapes=list(scratch),
            compiler_params=pltpu.CompilerParams(vmem_limit_bytes=vmem * MB),
            cost_estimate=pl.CostEstimate(flops=flops, bytes_accessed=1000, transcendentals=0),
            name=name,
            **extra,
        )(self.flags, *scalars, *arrays)
        out = list(out)
        out[0] = self.after(out[0])
        return out


def coefficient(ref, z, a, b, p):
    return ref[pl.ds(((z * V + a) * V + b) * 2 + p, 1), :]


def split_left(matrix):
    high = matrix.astype(BF16).astype(F32)
    place = lax.broadcasted_iota(jnp.int32, matrix.shape, 1)
    return jnp.where(place < 2 * DEPTH, high, matrix - high).astype(BF16)


def lag_matrix(basis, turned, trig, sign):
    half = turned.shape[0] // 2
    count = (half - 4) // 8 * 8
    cosine, sine = turned[:half], turned[half:]
    turn, cross = trig[:count, :1], trig[count : 2 * count, :1] * sign
    right = jnp.concatenate(
        [
            turn * cosine[:count] + cross * sine[:count],
            turn * sine[:count] - cross * cosine[:count],
            cosine[count:],
        ],
        axis=0,
    )
    return jnp.dot(basis, right, preferred_element_type=F32, precision=lax.Precision.HIGHEST)


def over_instants(left, cells):
    whole = jnp.concatenate(cells, axis=1)
    if whole.shape[0] < DEPTH:
        whole = jnp.concatenate(
            [whole, jnp.zeros((DEPTH - whole.shape[0], whole.shape[1]), F32)], axis=0
        )
    high = whole.astype(BF16)
    low = (whole - high.astype(F32)).astype(BF16)
    product = jnp.dot(
        left, jnp.concatenate([high, low, high], axis=0), preferred_element_type=F32
    )
    return [product[:, i * LANES : (i + 1) * LANES] for i in range(len(cells))]


def split_cells(st, slab, first_cell, last_cell, xn, xf):
    p = lax.axis_index("pitch") % 2
    edge = first_cell.shape[0]
    zeros = jnp.zeros((8, LANES), F32)
    width = 4 * NT

    def step(i, carry):
        slab[pl.ds(i * width, width), :] = st[pl.ds(i * 2 * width + p, width, stride=2), :]
        return carry

    lax.fori_loop(0, LEAD * V // 4, step, 0)
    first_cell[...] = st[0:edge, :]
    last_cell[...] = st[st.shape[0] - edge :, :]

    def separate(z, carry):
        for v in range(V):
            j = z * V + v
            for out, q in ((xn, 1 - p), (xf, p)):
                out[j, PAD - 8 : PAD, :] = zeros
                out[j, 0:NT, :] = st[pl.ds(j * 2 * NT + q, NT, stride=2), :]
        return carry

    lax.fori_loop(0, xn.shape[0] // V, separate, 0)


def lags(blades, harmonic, trig):
    count = harmonic.shape[0]
    rotor = jnp.full(harmonic.shape, blades[0]).astype(F32)
    stator = jnp.full(harmonic.shape, blades[1]).astype(F32)
    turns = harmonic[...] * stator
    lag = (turns - rotor * jnp.floor(turns / rotor)) / rotor * (2.0 * math.pi)
    trig[0:count, :] = jnp.cos(lag)
    trig[count : 2 * count, :] = jnp.sin(lag)
    trig[2 * count : 2 * count + 8, :] = (stator / rotor / count)[:8]


def prepare(flags, blades, xf, harmonic, basis, turned, trig, *chunks):
    lags(blades, harmonic, trig)
    wrap = flags[1]
    cells = xf.shape[0] // V
    sign = jnp.where(flags[2] == 1, 1.0, -1.0)
    left = split_left(lag_matrix(basis[...], turned[...], trig[...], sign))

    def step(z, carry):
        raw = [xf[z * V + v] for v in range(V)]
        lagged = over_instants(left, raw)
        for v in range(V):
            value = jnp.where(wrap == 1, lagged[v], raw[v])
            j = (z - LEAD) * V + v
            for out, ((first, last), extra) in zip(chunks, CHUNKS):
                width = last - first
                out[pl.ds(pl.multiple_of(j * width, 8), width), :] = value[first:last]
                if extra:
                    out[pl.ds((cells - LEAD) * V * width + j, 1), :] = value[NT - 1 : NT]
        return carry

    lax.fori_loop(LEAD, cells, step, 0)


def keep_tiles(ref, offset, values, first, last, height):
    for a in range(V):
        for t in range(first // 8, last // 8):
            ref[offset + a * height + t] = values[a][t * 8 - first : t * 8 - first + 8]


def sweeps(source, g, fg, offset, spans, p, inverse, lower, upper, cells):
    height = g.shape[1] // 8
    for first, last in spans:
        nothing = tuple(jnp.zeros((last - first, LANES), F32) for _ in range(V))

        def ahead(z, current, first=first, last=last):
            right = source(z, first, last)
            result = []
            for a in range(V):
                total = coefficient(inverse, z, a, 0, p) * right[0]
                for b in range(1, V):
                    total += coefficient(inverse, z, a, b, p) * right[b]
                for b in range(V):
                    total += coefficient(lower, z, a, b, p) * current[b]
                g[z * V + a, first:last, :] = total
                result.append(total)
            return tuple(result)

        out = lax.fori_loop(0, cells, ahead, nothing)
        keep_tiles(fg, offset, out, first, last, height)

        def back(i, current, first=first, last=last):
            z = cells - 1 - i
            result = []
            for a in range(V):
                total = g[z * V + a, first:last, :]
                for b in range(V):
                    total += coefficient(upper, z, a, b, p) * current[b]
                g[z * V + a, first:last, :] = total
                result.append(total)
            return tuple(result)

        out = lax.fori_loop(0, cells, back, nothing)
        keep_tiles(fg, offset + V * height, out, first, last, height)


def take_edges(edges, from_left, from_right, p):
    skip = from_left.shape[0] - V * NT * 2
    for v in range(V):
        edges[v, PAD - 8 : PAD, :] = jnp.zeros((8, LANES), F32)
        edges[v, 0:NT, :] = from_left[pl.ds(skip + v * 2 * NT + p, NT, stride=2), :]
        edges[V + v, PAD - 8 : PAD, :] = jnp.zeros((8, LANES), F32)
        edges[V + v, 0:NT, :] = from_right[pl.ds(v * 2 * NT + p, NT, stride=2), :]


def residuals(x, other, halo, edges, advect, viscous, left, p, cells, put):
    def one(z, above, below):
        here = [x[z * V + v] for v in range(V)]
        timing = over_instants(left, here)
        for v in range(V):
            j = z * V + v
            pitch = other[j] - 2.0 * here[v]
            if halo is not None:
                pitch += halo[j]
            put(
                j,
                advect[pl.ds(j * 2 + p, 1), :] * (above(z, v) - below(z, v))
                + viscous[pl.ds(j * 2 + p, 1), :] * pitch
                - timing[v],
            )

    inner_above = lambda z, v: x[(z - 1) * V + v]
    inner_below = lambda z, v: x[(z + 1) * V + v]
    one(0, lambda z, v: edges[v], inner_below)

    def step(z, carry):
        one(z, inner_above, inner_below)
        return carry

    lax.fori_loop(1, cells - 1, step, 0)
    one(cells - 1, inner_above, lambda z, v: edges[V + v])


def timing_matrix(table, trig):
    return split_left(table[...] * trig[trig.shape[0] - 8 : trig.shape[0] - 7, :1])


def near_cell(
    flags, xn, xf, halo, from_left, from_right, advect, viscous, inverse, lower, upper, trig, table,
    group, g, flows, right, edges,
):
    p = 1 - flags[0]
    cells = xn.shape[0] // V
    take_edges(edges, from_left, from_right, p)

    def put(j, value):
        right[j] = value

    residuals(xn, xf, halo, edges, advect, viscous, timing_matrix(table, trig), p, cells, put)
    source = lambda z, first, last: [right[z * V + v, first:last, :] for v in range(V)]
    sweeps(source, g, flows, 0, ((0, 32), (32, PAD)), p, inverse, lower, upper, cells)
    for c in range(2):
        for i in range(3 * V):
            flows[2 * V * PAD // 8 + c * 3 * V + i] = group[c, i]


def far_base(flags, xn, xf, from_left, from_right, advect, viscous, trig, table, base, edges):
    p = flags[0]
    cells = xn.shape[0] // V
    take_edges(edges, from_left, from_right, p)

    def put(j, value):
        base[j] = value

    residuals(xf, xn, None, edges, advect, viscous, timing_matrix(table, trig), p, cells, put)


def far_lead(flags, slab, trig, basis, turned, lead, halo):
    wrap = flags[1]
    sign = jnp.where(flags[2] == 1, -1.0, 1.0)
    left = split_left(lag_matrix(basis[...], turned[...], trig[...], sign))
    for z in range(LEAD):
        for v in range(V):
            halo[v, PAD - 8 : PAD, :] = jnp.zeros((8, LANES), F32)
            halo[v, 0:NT, :] = slab[pl.ds((z * V + v) * NT, NT), :]
        raw = [halo[v] for v in range(V)]
        lagged = over_instants(left, raw)
        for v in range(V):
            lead[z * V + v] = jnp.where(wrap == 1, lagged[v], raw[v])


def far_chunk(chunk, flags, base, lead, halo, viscous, inverse, lower, upper, g, fg):
    (first, last), extra = chunk
    width = last - first
    p = flags[0]
    cells = base.shape[0] // V
    top = lax.broadcasted_iota(jnp.int32, (8, LANES), 0) == 0

    def pieces(ref, j, rows):
        value = ref[j, first:last, :]
        return jnp.concatenate([value, ref[j, PAD - 8 : PAD, :]], axis=0) if extra else value

    def source(z, start, stop):
        result = []
        for v in range(V):
            j = z * V + v
            h = jnp.maximum(z - LEAD, 0) * V + v
            arrived = halo[pl.ds(pl.multiple_of(h * width, 8), width), :]
            if extra:
                row = halo[pl.ds((cells - LEAD) * V * width + h, 1), :]
                arrived = jnp.concatenate([arrived, jnp.where(top, row, 0.0)], axis=0)
            early = pieces(lead, jnp.minimum(z, LEAD - 1) * V + v, rows)
            arrived = jnp.where(z >= LEAD, arrived, early)
            result.append(pieces(base, j, rows) + viscous[pl.ds(j * 2 + p, 1), :] * arrived)
        return result

    height = rows_of(chunk)
    sweeps(source, g, fg, 0, ((0, height),), p, inverse, lower, upper, cells)


def times(matrix, vector):
    result = []
    for a in range(V):
        total = matrix(a, 0) * vector[0]
        for b in range(1, V):
            total += matrix(a, b) * vector[b]
        result.append(total)
    return result


def plus(one, two):
    return [a + b for a, b in zip(one, two)]


def tiles(ref, c, kind):
    return [ref[c, kind * V + a] for a in range(V)]


def rows(ref, c, kind):
    return lambda a, b: ref[c, kind * V + a, b : b + 1, :]


def unit(a):
    place = lax.broadcasted_iota(jnp.int32, (8, LANES), 0)
    return jnp.where(place == a, 1.0, 0.0).astype(F32)


def transfer(flags, lower, upper, blocks, group, forward):
    cells = blocks.shape[1] // V
    for c in range(2):
        p = 1 - flags[0] if c == 0 else flags[0]

        def ahead(z, current):
            result = times(lambda a, b: coefficient(lower, z, a, b, p), current)
            for a in range(V):
                forward[z * V + a] = result[a]
            return tuple(result)

        through = lax.fori_loop(0, cells, ahead, tuple(unit(a) for a in range(V)))

        def back(i, current):
            z = cells - 1 - i
            result = times(lambda a, b: coefficient(upper, z, a, b, p), current)
            for a in range(V):
                result[a] = result[a] + jnp.concatenate(
                    [forward[z * V + a], jnp.zeros((8, LANES), F32)], axis=0
                )
                blocks[c, z * V + a] = result[a]
            return tuple(result)

        start = tuple(
            jnp.concatenate([jnp.zeros((8, LANES), F32), unit(a)], axis=0) for a in range(V)
        )
        ends = lax.fori_loop(0, cells, back, start)
        for a in range(V):
            group[c, a] = ends[a][:8]
            group[c, V + a] = ends[a][8:]
            group[c, 2 * V + a] = through[a]


def merge_matrices(bit, levels, flags, mine, other, share, mats, merged, share_out, offset, new_offset):
    start, last = bit == 0, bit == levels - 1
    right = flags[3 + bit] == 1
    left = jnp.logical_not(right)
    nothing = jnp.zeros((8, LANES), F32)
    for c in range(2):
        kinds = 1 if last else 3
        at = lambda ref, kind: [ref[offset + (c * kinds + kind) * V + a] for a in range(V)]
        pick = lambda kind, own: [jnp.where(own, m, t) for m, t in zip(at(mine, kind), at(other, kind))]
        if start:
            own = [[unit(a) for a in range(V)], [nothing] * V, [unit(a) for a in range(V)]]
        else:
            own = [tiles(share, c, kind) for kind in range(3)]
        found = [
            (1, pick(0, right)),
            (3, [jnp.where(right, x, nothing) for x in own[0]]),
            (4, [jnp.where(right, x, nothing) for x in own[1]]),
            (5, [jnp.where(right, nothing, x) for x in own[2]]),
        ]
        if not last:
            found += [(0, pick(2, right)), (2, pick(1, left))]
        for kind, values in found:
            for a in range(V):
                mats[c, kind * V + a] = values[a]
        if last:
            continue
        p_left, g_left, h_right = pick(2, left), pick(0, left), pick(1, right)
        turned = times(rows(mats, c, 1), p_left)
        new = [plus(g_left, times(rows(mats, c, 2), turned))]
        if bit < levels - 2:
            new += [times(rows(mats, c, 2), h_right), times(rows(mats, c, 0), p_left)]
        for kind, values in enumerate(new):
            for a in range(V):
                merged[new_offset + (c * len(new) + kind) * V + a] = values[a]
        s0 = times(rows(mats, c, 3), p_left)
        s1 = times(rows(mats, c, 4), p_left)
        s1b = times(rows(mats, c, 5), turned)
        s2 = times(rows(mats, c, 5), h_right)
        for a in range(V):
            share_out[c, a] = jnp.where(right, s0[a], own[0][a])
            share_out[c, V + a] = jnp.where(right, s1[a], own[1][a] + s1b[a])
            share_out[c, 2 * V + a] = jnp.where(right, own[2][a], s2[a])


def inflow_of(c, mats, f_left, g_right, known):
    back = plus(g_right, times(rows(mats, c, 1), f_left))
    from_left = times(rows(mats, c, 3), f_left)
    from_right = plus(times(rows(mats, c, 4), f_left), times(rows(mats, c, 5), back))
    total = from_left + from_right
    return back, total if known is None else plus(known, total)


def merge_all(parts, bit, levels, flags, flows, other, *refs):
    share, known, mats, merged, share_out, inflow = (None, None, *refs) if bit == 0 else refs
    tall = sum(height for _, height in parts) * V
    new_offset = tall * (1 if bit == levels - 2 else 2)
    merge_matrices(bit, levels, flags, flows, other, share, mats, merged, share_out, 2 * tall, new_offset)
    merge_flows(parts, bit, levels, flags, mats, flows, other, *([] if known is None else [known]), merged, inflow)


def merge_flows(parts, bit, levels, flags, mats, flows, other, *refs):
    known, merged, inflow = (None, *refs) if bit == 0 else refs
    right, last_right = flags[3 + bit] == 1, flags[2 + levels] == 1
    last = bit == levels - 2
    start = 0
    for c, height in parts:

        def tile(t, carry, c=c, height=height, start=start):
            at = lambda i: start * 2 * V + i * height + t
            mine = [flows[at(i)] for i in range(2 * V)]
            theirs = [other[at(i)] for i in range(2 * V)]
            f_left = [jnp.where(right, y, x) for x, y in zip(mine[:V], theirs[:V])]
            f_right = [jnp.where(right, x, y) for x, y in zip(mine[:V], theirs[:V])]
            g_left = [jnp.where(right, y, x) for x, y in zip(mine[V:], theirs[V:])]
            g_right = [jnp.where(right, x, y) for x, y in zip(mine[V:], theirs[V:])]
            before = None if known is None else [known[at(i)] for i in range(2 * V)]
            back, total = inflow_of(c, mats, f_left, g_right, before)
            new_f = plus(f_right, times(rows(mats, c, 0), f_left))
            new_g = plus(g_left, times(rows(mats, c, 2), back))
            if last:
                for i in range(V):
                    end = jnp.where(last_right, new_g[i], new_f[i])
                    merged[start * V + i * height + t] = end
            else:
                for i, value in enumerate(new_f + new_g):
                    merged[at(i)] = value
            for i, value in enumerate(total):
                inflow[at(i)] = value
            return carry

        lax.fori_loop(0, height, tile, 0)
        start += height


def last_inflow(right, c, mats, ends, other, known, start, height, inflow):
    for t in range(height):
        mine = [ends[start * V + a * height + t] for a in range(V)]
        theirs = [other[start * V + a * height + t] for a in range(V)]
        f_left = [jnp.where(right, y, x) for x, y in zip(mine, theirs)]
        g_right = [jnp.where(right, x, y) for x, y in zip(mine, theirs)]
        before = [known[start * 2 * V + i * height + t] for i in range(2 * V)]
        _, total = inflow_of(c, mats, f_left, g_right, before)
        for i, value in enumerate(total):
            inflow[i, t * 8 : t * 8 + 8, :] = value


def corrected(c, z, a, first, last, g, blocks, inflow):
    total = g[z * V + a, first:last, :]
    for b in range(V):
        total += blocks[c, z * V + a, b : b + 1, :] * inflow[b]
        total += blocks[c, z * V + a, 8 + b : 9 + b, :] * inflow[V + b]
    return total


def correct(parts, levels, flags, mats, ends, other, known, blocks, *refs):
    solved, results, inflow = refs[: len(parts)], refs[len(parts) : -1], refs[-1]
    right = flags[2 + levels] == 1
    start = 0
    for (c, tall), g, result in zip(parts, solved, results):
        last_inflow(right, c, mats, ends, other, known, start, tall, inflow)
        start += tall
        height = tall * 8
        for first, last in ((0, 32), (32, height)) if height > 32 else ((0, height),):
            flow = tuple(inflow[i, first:last, :] for i in range(2 * V))

            def step(z, flow, c=c, first=first, last=last, g=g, result=result):
                for a in range(V):
                    result[z * V + a, first:last, :] = corrected(c, z, a, first, last, g, blocks, flow)
                return flow

            lax.fori_loop(0, g.shape[0] // V, step, flow)


def correct_all(parts, levels, flags, ends, other, share, known, blocks, *refs):
    count = len(parts)
    solved, results, mats, inflow = refs[:count], refs[count : 2 * count], refs[-2], refs[-1]
    tall = sum(height for _, height in parts) * V
    merge_matrices(levels - 1, levels, flags, ends, other, share, mats, None, None, tall, 0)
    correct(parts, levels, flags, mats, ends, other, known, blocks, *solved, *results, inflow)


def finish(levels, flags, mats, ends, other, known, g, blocks, near, *refs):
    done, out, inflow = refs[:-2], refs[-2], refs[-1]
    right = flags[2 + levels] == 1
    p = flags[0]
    (first_row, last_row), last_extra = CHUNKS[-1]
    width, height = last_row - first_row, rows_of(CHUNKS[-1])

    @pl.when(pl.program_id(0) == 0)
    def _():
        last_inflow(right, 1, mats, ends, other, known, 0, height // 8, inflow)

    flow = tuple(inflow[i] for i in range(2 * V))

    def step(z, carry):
        for a in range(V):
            j = z * V + a
            row = j * 2 * NT
            out[pl.ds(row + 1 - p, NT, stride=2), :] = near[j, 0:NT, :]
            for ref, ((first, last), extra) in zip(done, CHUNKS):
                out[pl.ds(row + p + 2 * first, last - first, stride=2), :] = ref[j, 0 : last - first, :]
                if extra:
                    out[pl.ds(row + p + 2 * (NT - 1), 1), :] = ref[j, last - first : last - first + 1, :]
            value = corrected(1, z, a, 0, height, g, blocks, flow)
            out[pl.ds(row + p + 2 * first_row, width, stride=2), :] = value[:width]
            if last_extra:
                out[pl.ds(row + p + 2 * (NT - 1), 1), :] = value[width : width + 1]
        return carry

    lax.fori_loop(0, g.shape[0] // V, step, 0)


def phase_tables(count):
    angle = 2.0 * math.pi * np.outer(np.arange(1, count + 1), np.arange(NT)) / NT
    cosine, sine = np.cos(angle), np.sin(angle)
    basis = np.zeros((PAD, 2 * count + 8), np.float32)
    basis[:NT, :count], basis[:NT, count : 2 * count], basis[:NT, 2 * count] = cosine.T, sine.T, 0.5
    turned = np.zeros((2, count + 8, 3, DEPTH), np.float32)
    turned[0, :count, :, :NT], turned[1, :count, :, :NT] = cosine[:, None], sine[:, None]
    turned[0, count, :, :NT] = 1.0
    return (2.0 / NT * basis).astype(np.float32), turned.reshape(2 * (count + 8), 3 * DEPTH)


def derivative_table():
    gap = np.arange(NT)[:, None] - np.arange(NT)[None, :]
    safe = np.where(gap == 0, 1.0, np.sin(np.pi * gap / NT))
    table = np.where(gap == 0, 0.0, 0.5 * (1.0 - 2.0 * np.mod(gap, 2)) / safe)
    wide = np.zeros((PAD, 3, DEPTH), np.float32)
    wide[:NT, :, :NT] = table[:, None]
    return wide.reshape(PAD, 3 * DEPTH)


def local(state, advect, viscous, inverse, lower, upper, blades, harmonic):
    cells = state.shape[0]
    count = harmonic.shape[0]
    segs, slabs = lax.axis_size("seg"), lax.axis_size("pitch")
    levels = segs.bit_length() - 1
    far_pairs = [(i, (i - 1) % slabs if i % 2 == 0 else (i + 1) % slabs) for i in range(slabs)]
    near_pairs = [(i, i ^ 1) for i in range(slabs)]
    to_far = lambda x: lax.ppermute(x, "pitch", far_pairs)
    to_level = lambda x, k: lax.ppermute(x, "seg", [(i, i ^ (1 << k)) for i in range(segs)])
    x_shape = (cells * V, PAD, LANES)

    st = state.transpose(0, 2, 3, 1, 4).reshape(cells * V * NT * 2, LANES)
    lead_rows, edge_rows = LEAD * V * NT, padded_even(V * NT * 2)
    held = pl.BlockSpec(memory_space=pltpu.VMEM)
    shapes = [(lead_rows, LANES), (edge_rows, LANES), (edge_rows, LANES), x_shape, x_shape]
    slab_out, first_cell, last_cell, xn, xf = pl.pallas_call(
        split_cells,
        out_shape=[jax.ShapeDtypeStruct(x, F32) for x in shapes],
        in_specs=[held],
        out_specs=[held] * 5,
        compiler_params=pltpu.CompilerParams(vmem_limit_bytes=16 * MB),
        name="split_cells",
    )(st)
    halo_near = lax.ppermute(xn, "pitch", near_pairs)
    slab_in = to_far(slab_out)
    from_left = lax.ppermute(last_cell, "seg", [(i, i + 1) for i in range(segs - 1)])
    from_right = lax.ppermute(first_cell, "seg", [(i + 1, i) for i in range(segs - 1)])

    slab, seg = lax.axis_index("pitch"), lax.axis_index("seg")
    side = slab % 2
    wrap = jnp.logical_or(slab == 0, slab == slabs - 1)
    bits = [(seg >> k) & 1 for k in range(levels)]
    run = Chain(
        jnp.stack(
            [side, wrap.astype(jnp.int32), (slab == 0).astype(jnp.int32), *bits]
        ).astype(jnp.int32)
    )
    run.after(slab_out)
    basis, turned = phase_tables(count)
    table = derivative_table()
    wide_harmonic = jnp.broadcast_to(harmonic.astype(F32)[:, None], (count, LANES))

    rest = (cells - LEAD) * V
    chunk_shapes = [
        (rest * (last - first) + (padded_even(rest) if extra else 0), LANES)
        for (first, last), extra in CHUNKS
    ]
    trig, *chunks = run(
        prepare, [(2 * count + 8, LANES), *chunk_shapes], [xf, wide_harmonic, basis, turned],
        scalars=[blades], name="prepare",
    )
    arrived = [slab_in]
    for chunk in chunks:
        if len(arrived) >= 2:
            chunk, arrived[-2] = lax.optimization_barrier((chunk, arrived[-2]))
        arrived.append(to_far(chunk))
    slab_in, *arrived = arrived

    flat = lambda x: x.transpose(0, 2, 3, 1, 4).reshape(cells * V * V * 2, LANES)
    inv, low, upp = flat(inverse.astype(F32)), flat(lower), flat(upper)
    adv = advect.transpose(0, 2, 1, 3).reshape(cells * V * 2, LANES)
    vis = viscous.transpose(0, 2, 1, 3).reshape(cells * V * 2, LANES)
    edges = pltpu.VMEM((2 * V, PAD, LANES), F32)

    mats = []
    mats_shape = (2, 6 * V, 8, LANES)

    def solve_chunk(i):
        height = rows_of(CHUNKS[i])
        return run(
            functools.partial(far_chunk, CHUNKS[i]),
            [(cells * V, height, LANES), (2 * V * height // 8, 8, LANES)],
            [base, lead, arrived[i], vis, inv, low, upp], name="far_chunk",
        )

    class Exchange:
        def __init__(self, c, g, flows, leads=False):
            self.parts, self.leads = [(c, g.shape[1] // 8)], leads
            self.flows, self.known, self.solved, self.level = flows, [], g, 0
            self.scratch = [pltpu.VMEM((2 * V, g.shape[1], LANES), F32)]

        def step(self):
            tall, k = self.parts[0][1], self.level
            shape = ((2 if k < levels - 2 else 1) * V * tall, 8, LANES)
            inflow = (2 * V * tall, 8, LANES)
            other = to_level(self.flows, k)
            if self.leads:
                shape = (shape[0] + (6 * V if k < levels - 2 else 2 * V),) + shape[1:]
                out = run(
                    functools.partial(merge_all, self.parts, k, levels),
                    [mats_shape, shape, (2, 3 * V, 8, LANES), inflow],
                    [self.flows, other, *self.known], name="merge_all",
                )
                mats.append(out[0])
                self.flows, self.known = out[1], out[2:]
            else:
                out = run(
                    functools.partial(merge_flows, self.parts, k, levels), [shape, inflow],
                    [mats[k], self.flows, other, *self.known], name="merge_flows",
                )
                self.flows, self.known = out[0], out[1:]
            self.level = k + 1

        def last(self):
            return [self.flows, to_level(self.flows, levels - 1), *self.known]

        def correct(self):
            if self.leads:
                result, last = run(
                    functools.partial(correct_all, self.parts, levels), [self.solved.shape, mats_shape],
                    [*self.last(), blocks, self.solved], scratch=self.scratch, name="correct_all",
                )
                mats.append(last)
                return result
            return run(
                functools.partial(correct, self.parts, levels), [self.solved.shape],
                [mats[-1], *self.last(), blocks, self.solved], scratch=self.scratch, name="correct",
            )[0]

    blocks, group = run(
        transfer, [(2, cells * V, 16, LANES), (2, 3 * V, 8, LANES)], [low, upp],
        scratch=[pltpu.VMEM((cells * V, 8, LANES), F32)], name="transfer",
    )
    base = run(
        far_base, [x_shape], [xn, xf, from_left, from_right, adv, vis, trig, table],
        scratch=[edges], name="far_base",
    )[0]
    lead = run(
        far_lead, [(LEAD * V, PAD, LANES)], [slab_in, trig, basis, turned],
        scratch=[pltpu.VMEM((V, PAD, LANES), F32)], name="far_lead",
    )[0]
    g_near, flows_near = run(
        near_cell, [x_shape, (2 * V * PAD // 8 + 6 * V, 8, LANES)],
        [xn, xf, halo_near, from_left, from_right, adv, vis, inv, low, upp, trig, table, group],
        scratch=[pltpu.VMEM(x_shape, F32), edges], name="near_cell", flops=6_000_000_000,
    )
    first = Exchange(0, g_near, flows_near, leads=True)
    second = Exchange(1, *solve_chunk(0))
    first.step()
    second.step()
    for k in range(1, levels - 1):
        first.step()
    third = Exchange(1, *solve_chunk(1))
    for k in range(1, levels - 1):
        second.step()
    third.step()
    near = first.correct()
    for k in range(1, levels - 1):
        third.step()
    done = [second.correct()]
    g_last = third.solved
    small = [mats[-1], *third.last()]

    steps = 4
    part = cells // steps
    whole = lambda x: pl.BlockSpec(x.shape, lambda i: (0,) * x.ndim)
    by_cell = lambda x: pl.BlockSpec((part * V,) + x.shape[1:], lambda i: (i, 0, 0))
    out = run(
        functools.partial(finish, levels), [st.shape], [*small, g_last, blocks, near, *done],
        grid=(steps,),
        in_specs=[whole(x) for x in small]
        + [by_cell(g_last), pl.BlockSpec((2, part * V, 16, LANES), lambda i: (0, i, 0, 0))]
        + [by_cell(x) for x in (near, *done)],
        out_specs=[pl.BlockSpec((part * V * NT * 2, LANES), lambda i: (i, 0))],
        scratch=[pltpu.VMEM((2 * V, rows_of(CHUNKS[-1]), LANES), F32)], name="finish",
    )[0]
    return out.reshape(cells, V, NT, 2, LANES).transpose(0, 3, 1, 2, 4)


def solution(mesh):
    cell = P("seg", "pitch", None, None, None)
    return jax.shard_map(
        local,
        mesh=mesh,
        in_specs=(cell, P("seg", "pitch", None, None), P("seg", "pitch", None, None), cell, cell, cell, P(), P()),
        out_specs=cell,
        check_vma=False,
    )
```

```python
import functools
import math

import jax
import jax.numpy as jnp
import numpy as np
from jax import lax
from jax.experimental import pallas as pl
from jax.experimental.pallas import tpu as pltpu
from jax.sharding import PartitionSpec as P

F32 = jnp.float32
BF16 = jnp.bfloat16
V = 5
NT = 49
PAD = 56
DEPTH = 64
LANES = 128
LEAD = 4
MB = 1 << 20

CHUNKS = (((0, 24), False), ((24, 40), True), ((40, 48), False))


def rows_of(chunk):
    (first, last), extra = chunk
    return last - first + (8 if extra else 0)


def padded_even(count):
    return (count + 7) // 8 * 8


class Chain:
    def __init__(self, flags):
        self.flags = flags

    def after(self, array):
        self.flags, array = lax.optimization_barrier((self.flags, array))
        return array

    def __call__(self, body, out_shapes, arrays, scratch=(), vmem=24, name=None, grid=None, in_specs=None, out_specs=None, scalars=(), flops=1000):
        smem = pl.BlockSpec(memory_space=pltpu.SMEM)
        held = pl.BlockSpec(memory_space=pltpu.VMEM)
        extra = {} if grid is None else {"grid": grid}
        out = pl.pallas_call(
            body,
            out_shape=[jax.ShapeDtypeStruct(s, F32) for s in out_shapes],
            in_specs=[smem] * (1 + len(scalars)) + (in_specs or [held] * len(arrays)),
            out_specs=out_specs or [held] * len(out_shapes),
            scratch_shapes=list(scratch),
            compiler_params=pltpu.CompilerParams(vmem_limit_bytes=vmem * MB),
            cost_estimate=pl.CostEstimate(flops=flops, bytes_accessed=1000, transcendentals=0),
            name=name,
            **extra,
        )(self.flags, *scalars, *arrays)
        out = list(out)
        out[0] = self.after(out[0])
        return out


def coefficient(ref, z, a, b, p):
    return ref[pl.ds(((z * V + a) * V + b) * 2 + p, 1), :]


def split_left(matrix):
    high = matrix.astype(BF16).astype(F32)
    place = lax.broadcasted_iota(jnp.int32, matrix.shape, 1)
    return jnp.where(place < 2 * DEPTH, high, matrix - high).astype(BF16)


def lag_matrix(basis, turned, trig, sign):
    half = turned.shape[0] // 2
    count = (half - 4) // 8 * 8
    cosine, sine = turned[:half], turned[half:]
    turn, cross = trig[:count, :1], trig[count : 2 * count, :1] * sign
    right = jnp.concatenate(
        [
            turn * cosine[:count] + cross * sine[:count],
            turn * sine[:count] - cross * cosine[:count],
            cosine[count:],
        ],
        axis=0,
    )
    return jnp.dot(basis, right, preferred_element_type=F32, precision=lax.Precision.HIGHEST)


def over_instants(lefts, cells):
    whole = jnp.concatenate(cells, axis=1)
    if whole.shape[0] < DEPTH:
        whole = jnp.concatenate(
            [whole, jnp.zeros((DEPTH - whole.shape[0], whole.shape[1]), F32)], axis=0
        )
    high = whole.astype(BF16)
    low = (whole - high.astype(F32)).astype(BF16)
    right = jnp.concatenate([high, low, high], axis=0)
    products = [jnp.dot(left, right, preferred_element_type=F32) for left in lefts]
    return [[x[:, i * LANES : (i + 1) * LANES] for i in range(len(cells))] for x in products]


def split_cells(st, slab, first_cell, last_cell, xn, xf):
    p = lax.axis_index("pitch") % 2
    edge = first_cell.shape[0]
    zeros = jnp.zeros((8, LANES), F32)
    width = 4 * NT

    def step(i, carry):
        slab[pl.ds(i * width, width), :] = st[pl.ds(i * 2 * width + p, width, stride=2), :]
        return carry

    lax.fori_loop(0, LEAD * V // 4, step, 0)
    first_cell[...] = st[0:edge, :]
    last_cell[...] = st[st.shape[0] - edge :, :]

    def separate(z, carry):
        for v in range(V):
            j = z * V + v
            for out, q in ((xn, 1 - p), (xf, p)):
                out[j, PAD - 8 : PAD, :] = zeros
                out[j, 0:NT, :] = st[pl.ds(j * 2 * NT + q, NT, stride=2), :]
        return carry

    lax.fori_loop(0, xn.shape[0] // V, separate, 0)


def lags(blades, harmonic, trig):
    count = harmonic.shape[0]
    rotor = jnp.full(harmonic.shape, blades[0]).astype(F32)
    stator = jnp.full(harmonic.shape, blades[1]).astype(F32)
    turns = harmonic[...] * stator
    lag = (turns - rotor * jnp.floor(turns / rotor)) / rotor * (2.0 * math.pi)
    trig[0:count, :] = jnp.cos(lag)
    trig[count : 2 * count, :] = jnp.sin(lag)
    trig[2 * count : 2 * count + 8, :] = (stator / rotor / count)[:8]


def own_terms(z, x, other, advect, viscous, p, timing, above, below, base):
    for v in range(V):
        j = z * V + v
        total = viscous[pl.ds(j * 2 + p, 1), :] * (other[j] - 2.0 * x[j]) - timing[v]
        rate = advect[pl.ds(j * 2 + p, 1), :]
        if above and below:
            total += rate * (x[j - V] - x[j + V])
        else:
            total += rate * (x[j - V] if above else -x[j + V])
        base[j] = total


def timing_matrix(table, trig):
    return split_left(table[...] * trig[trig.shape[0] - 8 : trig.shape[0] - 7, :1])


def prepare(flags, blades, xn, xf, harmonic, basis, turned, advect, viscous, table, trig, base, *chunks):
    lags(blades, harmonic, trig)
    p, wrap = flags[0], flags[1]
    cells = xf.shape[0] // V
    sign = jnp.where(flags[2] == 1, 1.0, -1.0)
    lag = split_left(lag_matrix(basis[...], turned[...], trig[...], sign))
    derive = timing_matrix(table, trig)

    def one(z, above=True, below=True, sends=True):
        raw = [xf[z * V + v] for v in range(V)]
        timing, *lagged = over_instants([derive, lag] if sends else [derive], raw)
        own_terms(z, xf, xn, advect, viscous, p, timing, above, below, base)
        if not sends:
            return
        for v in range(V):
            value = jnp.where(wrap == 1, lagged[0][v], raw[v])
            j = (z - LEAD) * V + v
            for out, ((first, last), extra) in zip(chunks, CHUNKS):
                width = last - first
                out[pl.ds(pl.multiple_of(j * width, 8), width), :] = value[first:last]
                if extra:
                    out[pl.ds((cells - LEAD) * V * width + j, 1), :] = value[NT - 1 : NT]

    def early(z, carry):
        one(z, sends=False)
        return carry

    def late(z, carry):
        one(z)
        return carry

    one(0, above=False, sends=False)
    lax.fori_loop(1, LEAD, early, 0)
    lax.fori_loop(LEAD, cells - 1, late, 0)
    one(cells - 1, below=False)


def near_base(flags, xn, xf, advect, viscous, table, trig, base):
    p = 1 - flags[0]
    cells = xn.shape[0] // V
    derive = timing_matrix(table, trig)

    def one(z, above=True, below=True):
        (timing,) = over_instants([derive], [xn[z * V + v] for v in range(V)])
        own_terms(z, xn, xf, advect, viscous, p, timing, above, below, base)

    def inner(z, carry):
        one(z)
        return carry

    one(0, above=False)
    lax.fori_loop(1, cells - 1, inner, 0)
    one(cells - 1, below=False)


def keep_tiles(ref, offset, values, first, last, height):
    for a in range(V):
        for t in range(first // 8, last // 8):
            ref[offset + a * height + t] = values[a][t * 8 - first : t * 8 - first + 8]


def sweeps(source, g, fg, offset, spans, p, inverse, lower, upper, cells):
    height = g.shape[1] // 8
    for first, last in spans:
        nothing = tuple(jnp.zeros((last - first, LANES), F32) for _ in range(V))

        def ahead(z, current, first=first, last=last):
            right = source(z, first, last)
            result = []
            for a in range(V):
                total = coefficient(inverse, z, a, 0, p) * right[0]
                for b in range(1, V):
                    total += coefficient(inverse, z, a, b, p) * right[b]
                for b in range(V):
                    total += coefficient(lower, z, a, b, p) * current[b]
                g[z * V + a, first:last, :] = total
                result.append(total)
            return tuple(result)

        out = lax.fori_loop(1, cells - 1, ahead, ahead(0, nothing))
        out = ahead(cells - 1, out)
        keep_tiles(fg, offset, out, first, last, height)

        def back(i, current, first=first, last=last):
            z = cells - 1 - i
            result = []
            for a in range(V):
                total = g[z * V + a, first:last, :]
                for b in range(V):
                    total += coefficient(upper, z, a, b, p) * current[b]
                g[z * V + a, first:last, :] = total
                result.append(total)
            return tuple(result)

        out = lax.fori_loop(0, cells, back, nothing)
        keep_tiles(fg, offset + V * height, out, first, last, height)


def take_edges(edges, from_left, from_right, p):
    skip = from_left.shape[0] - V * NT * 2
    for v in range(V):
        edges[v, PAD - 8 : PAD, :] = jnp.zeros((8, LANES), F32)
        edges[v, 0:NT, :] = from_left[pl.ds(skip + v * 2 * NT + p, NT, stride=2), :]
        edges[V + v, PAD - 8 : PAD, :] = jnp.zeros((8, LANES), F32)
        edges[V + v, 0:NT, :] = from_right[pl.ds(v * 2 * NT + p, NT, stride=2), :]


def edge_terms(z, cells, values, edges, advect, p, first, last):
    if not isinstance(z, int):
        return values
    return [
        value
        + (1.0 if z == 0 else -1.0)
        * advect[pl.ds((z * V + v) * 2 + p, 1), :]
        * edges[v if z == 0 else V + v, first:last, :]
        for v, value in enumerate(values)
    ]


def near_cell(
    flags, base, halo, from_left, from_right, advect, viscous, inverse, lower, upper, g, flows, edges
):
    p = 1 - flags[0]
    cells = base.shape[0] // V
    take_edges(edges, from_left, from_right, p)

    def source(z, first, last):
        values = []
        for v in range(V):
            j = z * V + v
            values.append(base[j, first:last, :] + viscous[pl.ds(j * 2 + p, 1), :] * halo[j, first:last, :])
        return edge_terms(z, cells, values, edges, advect, p, first, last)

    sweeps(source, g, flows, 0, ((0, 32), (32, PAD)), p, inverse, lower, upper, cells)


def far_lead(flags, slab, trig, basis, turned, lead, halo):
    wrap = flags[1]
    sign = jnp.where(flags[2] == 1, -1.0, 1.0)
    left = split_left(lag_matrix(basis[...], turned[...], trig[...], sign))
    for z in range(LEAD):
        for v in range(V):
            halo[v, PAD - 8 : PAD, :] = jnp.zeros((8, LANES), F32)
            halo[v, 0:NT, :] = slab[pl.ds((z * V + v) * NT, NT), :]
        raw = [halo[v] for v in range(V)]
        (lagged,) = over_instants([left], raw)
        for v in range(V):
            lead[z * V + v] = jnp.where(wrap == 1, lagged[v], raw[v])


def far_chunk(chunk, flags, base, lead, halo, from_left, from_right, advect, viscous, inverse, lower, upper, g, fg, edges):
    (first, last), extra = chunk
    width = last - first
    p = flags[0]
    cells = base.shape[0] // V
    top = lax.broadcasted_iota(jnp.int32, (8, LANES), 0) == 0
    take_edges(edges, from_left, from_right, p)

    def pieces(ref, j):
        value = ref[j, first:last, :]
        return jnp.concatenate([value, ref[j, PAD - 8 : PAD, :]], axis=0) if extra else value

    def source(z, start, stop):
        result = []
        for v in range(V):
            j = z * V + v
            h = jnp.maximum(z - LEAD, 0) * V + v
            arrived = halo[pl.ds(pl.multiple_of(h * width, 8), width), :]
            if extra:
                row = halo[pl.ds((cells - LEAD) * V * width + h, 1), :]
                arrived = jnp.concatenate([arrived, jnp.where(top, row, 0.0)], axis=0)
            early = pieces(lead, jnp.minimum(z, LEAD - 1) * V + v)
            arrived = jnp.where(z >= LEAD, arrived, early)
            value = pieces(base, j) + viscous[pl.ds(j * 2 + p, 1), :] * arrived
            if isinstance(z, int):
                rate = advect[pl.ds(j * 2 + p, 1), :]
                edge = pieces(edges, v if z == 0 else V + v)
                value += rate * edge if z == 0 else -rate * edge
            result.append(value)
        return result

    height = rows_of(chunk)
    sweeps(source, g, fg, 0, ((0, height),), p, inverse, lower, upper, cells)


def times(matrix, vector):
    result = []
    for a in range(V):
        total = matrix(a, 0) * vector[0]
        for b in range(1, V):
            total += matrix(a, b) * vector[b]
        result.append(total)
    return result


def plus(one, two):
    return [a + b for a, b in zip(one, two)]


def tiles(ref, c, kind):
    return [ref[c, kind * V + a] for a in range(V)]


def rows(ref, c, kind):
    return lambda a, b: ref[c, kind * V + a, b : b + 1, :]


def unit(a):
    place = lax.broadcasted_iota(jnp.int32, (8, LANES), 0)
    return jnp.where(place == a, 1.0, 0.0).astype(F32)


def transfer(flags, lower, upper, blocks, group, forward):
    cells = blocks.shape[1] // V
    for c in range(2):
        p = 1 - flags[0] if c == 0 else flags[0]

        def ahead(z, current):
            result = times(lambda a, b: coefficient(lower, z, a, b, p), current)
            for a in range(V):
                forward[z * V + a] = result[a]
            return tuple(result)

        through = lax.fori_loop(0, cells, ahead, tuple(unit(a) for a in range(V)))

        def back(i, current):
            z = cells - 1 - i
            result = times(lambda a, b: coefficient(upper, z, a, b, p), current)
            for a in range(V):
                result[a] = result[a] + jnp.concatenate(
                    [forward[z * V + a], jnp.zeros((8, LANES), F32)], axis=0
                )
                blocks[c, z * V + a] = result[a]
            return tuple(result)

        start = tuple(
            jnp.concatenate([jnp.zeros((8, LANES), F32), unit(a)], axis=0) for a in range(V)
        )
        ends = lax.fori_loop(0, cells, back, start)
        for a in range(V):
            group[c * 3 * V + a] = ends[a][:8]
            group[(c * 3 + 1) * V + a] = ends[a][8:]
            group[(c * 3 + 2) * V + a] = through[a]


def merge_matrices(bit, levels, flags, mine, other, *refs):
    start, last = bit == 0, bit == levels - 1
    share, refs = (None, refs) if start else (refs[0], refs[1:])
    mats, merged, share_out = (refs[0], None, None) if last else refs
    right = flags[3 + bit] == 1
    left = jnp.logical_not(right)
    nothing = jnp.zeros((8, LANES), F32)
    for c in range(2):
        kinds = 1 if last else 3
        at = lambda ref, kind: [ref[(c * kinds + kind) * V + a] for a in range(V)]
        pick = lambda kind, own: [jnp.where(own, m, t) for m, t in zip(at(mine, kind), at(other, kind))]
        if start:
            own = [[unit(a) for a in range(V)], [nothing] * V, [unit(a) for a in range(V)]]
        else:
            own = [tiles(share, c, kind) for kind in range(3)]
        found = [
            (1, pick(0, right)),
            (3, [jnp.where(right, x, nothing) for x in own[0]]),
            (4, [jnp.where(right, x, nothing) for x in own[1]]),
            (5, [jnp.where(right, nothing, x) for x in own[2]]),
        ]
        if not last:
            found += [(0, pick(2, right)), (2, pick(1, left))]
        for kind, values in found:
            for a in range(V):
                mats[c, kind * V + a] = values[a]
        if last:
            continue
        p_left, g_left, h_right = pick(2, left), pick(0, left), pick(1, right)
        turned = times(rows(mats, c, 1), p_left)
        new = [plus(g_left, times(rows(mats, c, 2), turned))]
        if bit < levels - 2:
            new += [times(rows(mats, c, 2), h_right), times(rows(mats, c, 0), p_left)]
        for kind, values in enumerate(new):
            for a in range(V):
                merged[(c * len(new) + kind) * V + a] = values[a]
        s0 = times(rows(mats, c, 3), p_left)
        s1 = times(rows(mats, c, 4), p_left)
        s1b = times(rows(mats, c, 5), turned)
        s2 = times(rows(mats, c, 5), h_right)
        for a in range(V):
            share_out[c, a] = jnp.where(right, s0[a], own[0][a])
            share_out[c, V + a] = jnp.where(right, s1[a], own[1][a] + s1b[a])
            share_out[c, 2 * V + a] = jnp.where(right, own[2][a], s2[a])


def inflow_of(c, mats, f_left, g_right, known):
    back = plus(g_right, times(rows(mats, c, 1), f_left))
    from_left = times(rows(mats, c, 3), f_left)
    from_right = plus(times(rows(mats, c, 4), f_left), times(rows(mats, c, 5), back))
    total = from_left + from_right
    return back, total if known is None else plus(known, total)


def merge_flows(parts, bit, levels, flags, mats, flows, other, *refs):
    known, merged, inflow = (None, *refs) if bit == 0 else refs
    right, last_right = flags[3 + bit] == 1, flags[2 + levels] == 1
    last = bit == levels - 2
    start = 0
    for c, height in parts:

        def tile(t, carry, c=c, height=height, start=start):
            at = lambda i: start * 2 * V + i * height + t
            mine = [flows[at(i)] for i in range(2 * V)]
            theirs = [other[at(i)] for i in range(2 * V)]
            f_left = [jnp.where(right, y, x) for x, y in zip(mine[:V], theirs[:V])]
            f_right = [jnp.where(right, x, y) for x, y in zip(mine[:V], theirs[:V])]
            g_left = [jnp.where(right, y, x) for x, y in zip(mine[V:], theirs[V:])]
            g_right = [jnp.where(right, x, y) for x, y in zip(mine[V:], theirs[V:])]
            before = None if known is None else [known[at(i)] for i in range(2 * V)]
            back, total = inflow_of(c, mats, f_left, g_right, before)
            new_f = plus(f_right, times(rows(mats, c, 0), f_left))
            new_g = plus(g_left, times(rows(mats, c, 2), back))
            if last:
                for i in range(V):
                    end = jnp.where(last_right, new_g[i], new_f[i])
                    merged[start * V + i * height + t] = end
            else:
                for i, value in enumerate(new_f + new_g):
                    merged[at(i)] = value
            for i, value in enumerate(total):
                inflow[at(i)] = value
            return carry

        lax.fori_loop(0, height, tile, 0)
        start += height


def last_inflow(right, c, mats, ends, other, known, start, height, inflow):
    for t in range(height):
        mine = [ends[start * V + a * height + t] for a in range(V)]
        theirs = [other[start * V + a * height + t] for a in range(V)]
        f_left = [jnp.where(right, y, x) for x, y in zip(mine, theirs)]
        g_right = [jnp.where(right, x, y) for x, y in zip(mine, theirs)]
        before = [known[start * 2 * V + i * height + t] for i in range(2 * V)]
        _, total = inflow_of(c, mats, f_left, g_right, before)
        for i, value in enumerate(total):
            inflow[i, t * 8 : t * 8 + 8, :] = value


def corrected(c, z, a, first, last, g, blocks, inflow):
    total = g[z * V + a, first:last, :]
    for b in range(V):
        total += blocks[c, z * V + a, b : b + 1, :] * inflow[b]
        total += blocks[c, z * V + a, 8 + b : 9 + b, :] * inflow[V + b]
    return total


def correct(parts, levels, flags, mats, ends, other, known, blocks, *refs):
    solved, results, inflow = refs[: len(parts)], refs[len(parts) : -1], refs[-1]
    right = flags[2 + levels] == 1
    start = 0
    for (c, tall), g, result in zip(parts, solved, results):
        last_inflow(right, c, mats, ends, other, known, start, tall, inflow)
        start += tall
        height = tall * 8
        for first, last in ((0, 32), (32, height)) if height > 32 else ((0, height),):
            flow = tuple(inflow[i, first:last, :] for i in range(2 * V))

            def step(z, flow, c=c, first=first, last=last, g=g, result=result):
                for a in range(V):
                    result[z * V + a, first:last, :] = corrected(c, z, a, first, last, g, blocks, flow)
                return flow

            lax.fori_loop(0, g.shape[0] // V, step, flow)


def finish(levels, flags, mats, ends, other, known, g, blocks, near, *refs):
    done, out, inflow = refs[:-2], refs[-2], refs[-1]
    right = flags[2 + levels] == 1
    p = flags[0]
    (first_row, last_row), last_extra = CHUNKS[-1]
    width, height = last_row - first_row, rows_of(CHUNKS[-1])

    @pl.when(pl.program_id(0) == 0)
    def _():
        last_inflow(right, 1, mats, ends, other, known, 0, height // 8, inflow)

    flow = tuple(inflow[i] for i in range(2 * V))

    def step(z, carry):
        for a in range(V):
            j = z * V + a
            row = j * 2 * NT
            out[pl.ds(row + 1 - p, NT, stride=2), :] = near[j, 0:NT, :]
            for ref, ((first, last), extra) in zip(done, CHUNKS):
                out[pl.ds(row + p + 2 * first, last - first, stride=2), :] = ref[j, 0 : last - first, :]
                if extra:
                    out[pl.ds(row + p + 2 * (NT - 1), 1), :] = ref[j, last - first : last - first + 1, :]
            value = corrected(1, z, a, 0, height, g, blocks, flow)
            out[pl.ds(row + p + 2 * first_row, width, stride=2), :] = value[:width]
            if last_extra:
                out[pl.ds(row + p + 2 * (NT - 1), 1), :] = value[width : width + 1]
        return carry

    lax.fori_loop(0, g.shape[0] // V, step, 0)


def phase_tables(count):
    angle = 2.0 * math.pi * np.outer(np.arange(1, count + 1), np.arange(NT)) / NT
    cosine, sine = np.cos(angle), np.sin(angle)
    basis = np.zeros((PAD, 2 * count + 8), np.float32)
    basis[:NT, :count], basis[:NT, count : 2 * count], basis[:NT, 2 * count] = cosine.T, sine.T, 0.5
    turned = np.zeros((2, count + 8, 3, DEPTH), np.float32)
    turned[0, :count, :, :NT], turned[1, :count, :, :NT] = cosine[:, None], sine[:, None]
    turned[0, count, :, :NT] = 1.0
    return (2.0 / NT * basis).astype(np.float32), turned.reshape(2 * (count + 8), 3 * DEPTH)


def derivative_table():
    gap = np.arange(NT)[:, None] - np.arange(NT)[None, :]
    safe = np.where(gap == 0, 1.0, np.sin(np.pi * gap / NT))
    table = np.where(gap == 0, 0.0, 0.5 * (1.0 - 2.0 * np.mod(gap, 2)) / safe)
    wide = np.zeros((PAD, 3, DEPTH), np.float32)
    wide[:NT, :, :NT] = table[:, None]
    return wide.reshape(PAD, 3 * DEPTH)


COSTS = (0, 0, 6_000_000_000, 0)


def local(state, advect, viscous, inverse, lower, upper, blades, harmonic):
    cells = state.shape[0]
    count = harmonic.shape[0]
    segs, slabs = lax.axis_size("seg"), lax.axis_size("pitch")
    levels = segs.bit_length() - 1
    far_pairs = [(i, (i - 1) % slabs if i % 2 == 0 else (i + 1) % slabs) for i in range(slabs)]
    near_pairs = [(i, i ^ 1) for i in range(slabs)]
    to_far = lambda x: lax.ppermute(x, "pitch", far_pairs)
    to_level = lambda x, k: lax.ppermute(x, "seg", [(i, i ^ (1 << k)) for i in range(segs)])
    x_shape = (cells * V, PAD, LANES)

    st = state.transpose(0, 2, 3, 1, 4).reshape(cells * V * NT * 2, LANES)
    lead_rows, edge_rows = LEAD * V * NT, padded_even(V * NT * 2)
    held = pl.BlockSpec(memory_space=pltpu.VMEM)
    shapes = [(lead_rows, LANES), (edge_rows, LANES), (edge_rows, LANES), x_shape, x_shape]
    slab_out, first_cell, last_cell, xn, xf = pl.pallas_call(
        split_cells,
        out_shape=[jax.ShapeDtypeStruct(x, F32) for x in shapes],
        in_specs=[held],
        out_specs=[held] * 5,
        compiler_params=pltpu.CompilerParams(vmem_limit_bytes=16 * MB),
        name="split_cells",
    )(st)
    halo_near = lax.ppermute(xn, "pitch", near_pairs)
    slab_in = to_far(slab_out)
    from_left = lax.ppermute(last_cell, "seg", [(i, i + 1) for i in range(segs - 1)])
    from_right = lax.ppermute(first_cell, "seg", [(i + 1, i) for i in range(segs - 1)])

    slab, seg = lax.axis_index("pitch"), lax.axis_index("seg")
    side = slab % 2
    wrap = jnp.logical_or(slab == 0, slab == slabs - 1)
    bits = [(seg >> k) & 1 for k in range(levels)]
    run = Chain(
        jnp.stack(
            [side, wrap.astype(jnp.int32), (slab == 0).astype(jnp.int32), *bits]
        ).astype(jnp.int32)
    )
    run.after(slab_out)
    basis, turned = phase_tables(count)
    table = derivative_table()
    wide_harmonic = jnp.broadcast_to(harmonic.astype(F32)[:, None], (count, LANES))

    rest = (cells - LEAD) * V
    chunk_shapes = [
        (rest * (last - first) + (padded_even(rest) if extra else 0), LANES)
        for (first, last), extra in CHUNKS
    ]
    adv = advect.transpose(0, 2, 1, 3).reshape(cells * V * 2, LANES)
    vis = viscous.transpose(0, 2, 1, 3).reshape(cells * V * 2, LANES)
    trig, base, *chunks = run(
        prepare, [(2 * count + 8, LANES), x_shape, *chunk_shapes],
        [xn, xf, wide_harmonic, basis, turned, adv, vis, table], scalars=[blades], name="prepare",
    )
    arrived = [slab_in]
    for chunk in chunks:
        if len(arrived) >= 2:
            chunk, arrived[-2] = lax.optimization_barrier((chunk, arrived[-2]))
        arrived.append(to_far(chunk))
    slab_in, *arrived = arrived

    flat = lambda x: x.transpose(0, 2, 3, 1, 4).reshape(cells * V * V * 2, LANES)
    inv, low, upp = flat(inverse.astype(F32)), flat(lower), flat(upper)
    edges = pltpu.VMEM((2 * V, PAD, LANES), F32)

    mats, group, share = [], None, []

    def merge_group(k):
        nonlocal group, share
        shapes = [(2, 6 * V, 8, LANES)]
        if k < levels - 1:
            shapes += [((6 if k < levels - 2 else 2) * V, 8, LANES), (2, 3 * V, 8, LANES)]
        out = run(
            functools.partial(merge_matrices, k, levels), shapes,
            [group, to_level(group, k), *share], name="merge_matrices",
        )
        mats.append(out[0])
        if k < levels - 1:
            group, share = out[1], [out[2]]

    def solve_chunk(i):
        height = rows_of(CHUNKS[i])
        return run(
            functools.partial(far_chunk, CHUNKS[i]),
            [(cells * V, height, LANES), (2 * V * height // 8, 8, LANES)],
            [base, lead, arrived[i], from_left, from_right, adv, vis, inv, low, upp],
            scratch=[edges], name="far_chunk",
        )

    class Exchange:
        def __init__(self, c, g, flows):
            self.parts = [(c, g.shape[1] // 8)]
            self.flows, self.known, self.solved, self.level = flows, [], g, 0

        def step(self):
            tall, k = self.parts[0][1], self.level
            shape = ((2 if k < levels - 2 else 1) * V * tall, 8, LANES)
            out = run(
                functools.partial(merge_flows, self.parts, k, levels),
                [shape, (2 * V * tall, 8, LANES)],
                [mats[k], self.flows, to_level(self.flows, k), *self.known], name="merge_flows",
            )
            self.flows, self.known, self.level = out[0], out[1:], k + 1

        def last(self):
            return [mats[-1], self.flows, to_level(self.flows, levels - 1), *self.known]

        def correct(self):
            return run(
                functools.partial(correct, self.parts, levels), [self.solved.shape],
                [*self.last(), blocks, self.solved],
                scratch=[pltpu.VMEM((2 * V, self.solved.shape[1], LANES), F32)], name="correct",
            )[0]

    base_near = run(
        near_base, [x_shape], [xn, xf, adv, vis, table, trig], name="near_base", flops=COSTS[0]
    )[0]
    blocks, group = run(
        transfer, [(2, cells * V, 16, LANES), (6 * V, 8, LANES)], [low, upp],
        scratch=[pltpu.VMEM((cells * V, 8, LANES), F32)], name="transfer", flops=COSTS[1],
    )
    first = Exchange(
        0,
        *run(
            near_cell, [x_shape, (2 * V * PAD // 8, 8, LANES)],
            [base_near, halo_near, from_left, from_right, adv, vis, inv, low, upp],
            scratch=[edges], name="near_cell", flops=COSTS[2],
        )
    )
    lead = run(
        far_lead, [(LEAD * V, PAD, LANES)], [slab_in, trig, basis, turned],
        scratch=[pltpu.VMEM((V, PAD, LANES), F32)], name="far_lead", flops=COSTS[3],
    )[0]
    second = Exchange(1, *solve_chunk(0))
    merge_group(0)
    first.step()
    second.step()
    for k in range(1, levels):
        merge_group(k)
    third = Exchange(1, *solve_chunk(1))
    for k in range(1, levels - 1):
        second.step()
        first.step()
    fourth = Exchange(1, *solve_chunk(2))
    third.step()
    done = [second.correct()]
    fourth.step()
    for k in range(1, levels - 1):
        third.step()
    near = first.correct()
    for k in range(1, levels - 1):
        fourth.step()
    done.append(third.correct())
    g_last = fourth.solved
    small = fourth.last()

    steps = 4
    part = cells // steps
    whole = lambda x: pl.BlockSpec(x.shape, lambda i: (0,) * x.ndim)
    by_cell = lambda x: pl.BlockSpec((part * V,) + x.shape[1:], lambda i: (i, 0, 0))
    out = run(
        functools.partial(finish, levels), [st.shape], [*small, g_last, blocks, near, *done],
        grid=(steps,),
        in_specs=[whole(x) for x in small]
        + [by_cell(g_last), pl.BlockSpec((2, part * V, 16, LANES), lambda i: (0, i, 0, 0))]
        + [by_cell(x) for x in (near, *done)],
        out_specs=[pl.BlockSpec((part * V * NT * 2, LANES), lambda i: (i, 0))],
        scratch=[pltpu.VMEM((2 * V, rows_of(CHUNKS[-1]), LANES), F32)], name="finish",
    )[0]
    return out.reshape(cells, V, NT, 2, LANES).transpose(0, 3, 1, 2, 4)


def solution(mesh):
    cell = P("seg", "pitch", None, None, None)
    return jax.shard_map(
        local,
        mesh=mesh,
        in_specs=(cell, P("seg", "pitch", None, None), P("seg", "pitch", None, None), cell, cell, cell, P(), P()),
        out_specs=cell,
        check_vma=False,
    )
```

```python
import functools
import math

import jax
import jax.numpy as jnp
import numpy as np
from jax import lax
from jax.experimental import pallas as pl
from jax.experimental.pallas import tpu as pltpu
from jax.sharding import PartitionSpec as P

F32 = jnp.float32
BF16 = jnp.bfloat16
V = 5
NT = 49
PAD = 56
DEPTH = 64
LANES = 128
LEAD = 4
MB = 1 << 20

CHUNKS = (((0, 32), True), ((32, 48), False))


def rows_of(chunk):
    (first, last), extra = chunk
    return last - first + (8 if extra else 0)


def padded_even(count):
    return (count + 7) // 8 * 8


class Chain:
    def __init__(self, flags):
        self.flags = flags

    def before(self, array):
        return lax.optimization_barrier((self.flags, array))[1]

    def after(self, array):
        self.flags, array = lax.optimization_barrier((self.flags, array))
        return array

    def __call__(self, body, out_shapes, arrays, scratch=(), vmem=16, name=None, grid=None, in_specs=None, out_specs=None, scalars=(), flops=1000):
        smem = pl.BlockSpec(memory_space=pltpu.SMEM)
        held = pl.BlockSpec(memory_space=pltpu.VMEM)
        extra = {} if grid is None else {"grid": grid}
        out = pl.pallas_call(
            body,
            out_shape=[jax.ShapeDtypeStruct(s, F32) for s in out_shapes],
            in_specs=[smem] * (1 + len(scalars)) + (in_specs or [held] * len(arrays)),
            out_specs=out_specs or [held] * len(out_shapes),
            scratch_shapes=list(scratch),
            compiler_params=pltpu.CompilerParams(vmem_limit_bytes=vmem * MB),
            cost_estimate=pl.CostEstimate(flops=flops, bytes_accessed=1000, transcendentals=0),
            name=name,
            **extra,
        )(self.flags, *scalars, *arrays)
        out = list(out)
        out[0] = self.after(out[0])
        return out


def coefficient(ref, z, a, b, p):
    return ref[pl.ds(((z * V + a) * V + b) * 2 + p, 1), :]


def split_left(matrix):
    high = matrix.astype(BF16).astype(F32)
    place = lax.broadcasted_iota(jnp.int32, matrix.shape, 1)
    return jnp.where(place < 2 * DEPTH, high, matrix - high).astype(BF16)


def lag_matrix(basis, turned, trig, sign):
    half = turned.shape[0] // 2
    count = (half - 4) // 8 * 8
    cosine, sine = turned[:half], turned[half:]
    turn, cross = trig[:count, :1], trig[count : 2 * count, :1] * sign
    right = jnp.concatenate(
        [
            turn * cosine[:count] + cross * sine[:count],
            turn * sine[:count] - cross * cosine[:count],
            cosine[count:],
        ],
        axis=0,
    )
    return jnp.dot(basis, right, preferred_element_type=F32, precision=lax.Precision.HIGHEST)


def over_instants(lefts, cells):
    whole = jnp.concatenate(cells, axis=1)
    if whole.shape[0] < DEPTH:
        whole = jnp.concatenate(
            [whole, jnp.zeros((DEPTH - whole.shape[0], whole.shape[1]), F32)], axis=0
        )
    high = whole.astype(BF16)
    low = (whole - high.astype(F32)).astype(BF16)
    right = jnp.concatenate([high, low, high], axis=0)
    products = [jnp.dot(left, right, preferred_element_type=F32) for left in lefts]
    return [[x[:, i * LANES : (i + 1) * LANES] for i in range(len(cells))] for x in products]


def split_cells(st, slab, first_cell, last_cell, xn, xf):
    p = lax.axis_index("pitch") % 2
    edge = first_cell.shape[0]
    zeros = jnp.zeros((8, LANES), F32)
    width = 4 * NT

    def step(i, carry):
        slab[pl.ds(i * width, width), :] = st[pl.ds(i * 2 * width + p, width, stride=2), :]
        return carry

    lax.fori_loop(0, LEAD * V // 4, step, 0)
    first_cell[...] = st[0:edge, :]
    last_cell[...] = st[st.shape[0] - edge :, :]

    def separate(z, carry):
        for v in range(V):
            j = z * V + v
            for out, q in ((xn, 1 - p), (xf, p)):
                out[j, PAD - 8 : PAD, :] = zeros
                out[j, 0:NT, :] = st[pl.ds(j * 2 * NT + q, NT, stride=2), :]
        return carry

    lax.fori_loop(0, xn.shape[0] // V, separate, 0)


def lags(blades, harmonic, trig):
    count = harmonic.shape[0]
    rotor = jnp.full(harmonic.shape, blades[0]).astype(F32)
    stator = jnp.full(harmonic.shape, blades[1]).astype(F32)
    turns = harmonic[...] * stator
    lag = (turns - rotor * jnp.floor(turns / rotor)) / rotor * (2.0 * math.pi)
    trig[0:count, :] = jnp.cos(lag)
    trig[count : 2 * count, :] = jnp.sin(lag)
    trig[2 * count : 2 * count + 8, :] = (stator / rotor / count)[:8]


def own_terms(z, x, other, advect, viscous, p, timing, above, below, base):
    for v in range(V):
        j = z * V + v
        total = viscous[pl.ds(j * 2 + p, 1), :] * (other[j] - 2.0 * x[j]) - timing[v]
        rate = advect[pl.ds(j * 2 + p, 1), :]
        if above and below:
            total += rate * (x[j - V] - x[j + V])
        else:
            total += rate * (x[j - V] if above else -x[j + V])
        base[j] = total


def timing_matrix(table, trig):
    return split_left(table[...] * trig[trig.shape[0] - 8 : trig.shape[0] - 7, :1])


def prepare(flags, blades, xn, xf, harmonic, basis, turned, advect, viscous, table, trig, base, *chunks):
    lags(blades, harmonic, trig)
    p, wrap = flags[0], flags[1]
    cells = xf.shape[0] // V
    sign = jnp.where(flags[2] == 1, 1.0, -1.0)
    lag = split_left(lag_matrix(basis[...], turned[...], trig[...], sign))
    derive = timing_matrix(table, trig)

    def one(z, above=True, below=True, sends=True):
        raw = [xf[z * V + v] for v in range(V)]
        timing, *lagged = over_instants([derive, lag] if sends else [derive], raw)
        own_terms(z, xf, xn, advect, viscous, p, timing, above, below, base)
        if not sends:
            return
        for v in range(V):
            value = jnp.where(wrap == 1, lagged[0][v], raw[v])
            j = (z - LEAD) * V + v
            for out, ((first, last), extra) in zip(chunks, CHUNKS):
                width = last - first
                out[pl.ds(pl.multiple_of(j * width, 8), width), :] = value[first:last]
                if extra:
                    out[pl.ds((cells - LEAD) * V * width + j, 1), :] = value[NT - 1 : NT]

    def early(z, carry):
        one(z, sends=False)
        return carry

    def late(z, carry):
        one(z)
        return carry

    one(0, above=False, sends=False)
    lax.fori_loop(1, LEAD, early, 0)
    lax.fori_loop(LEAD, cells - 1, late, 0)
    one(cells - 1, below=False)


def near_base(flags, xn, xf, advect, viscous, table, trig, base):
    p = 1 - flags[0]
    cells = xn.shape[0] // V
    derive = timing_matrix(table, trig)

    def one(z, above=True, below=True):
        (timing,) = over_instants([derive], [xn[z * V + v] for v in range(V)])
        own_terms(z, xn, xf, advect, viscous, p, timing, above, below, base)

    def inner(z, carry):
        one(z)
        return carry

    one(0, above=False)
    lax.fori_loop(1, cells - 1, inner, 0)
    one(cells - 1, below=False)


def keep_tiles(ref, offset, values, first, last, height):
    for a in range(V):
        for t in range(first // 8, last // 8):
            ref[offset + a * height + t] = values[a][t * 8 - first : t * 8 - first + 8]


def sweeps(source, g, fg, offset, spans, p, inverse, lower, upper, cells):
    height = g.shape[1] // 8
    for first, last in spans:
        nothing = tuple(jnp.zeros((last - first, LANES), F32) for _ in range(V))

        def ahead(z, current, first=first, last=last):
            right = source(z, first, last)
            result = []
            for a in range(V):
                total = coefficient(inverse, z, a, 0, p) * right[0]
                for b in range(1, V):
                    total += coefficient(inverse, z, a, b, p) * right[b]
                for b in range(V):
                    total += coefficient(lower, z, a, b, p) * current[b]
                g[z * V + a, first:last, :] = total
                result.append(total)
            return tuple(result)

        out = lax.fori_loop(1, cells - 1, ahead, ahead(0, nothing))
        out = ahead(cells - 1, out)
        keep_tiles(fg, offset, out, first, last, height)

        def back(i, current, first=first, last=last):
            z = cells - 1 - i
            result = []
            for a in range(V):
                total = g[z * V + a, first:last, :]
                for b in range(V):
                    total += coefficient(upper, z, a, b, p) * current[b]
                g[z * V + a, first:last, :] = total
                result.append(total)
            return tuple(result)

        out = lax.fori_loop(0, cells, back, nothing)
        keep_tiles(fg, offset + V * height, out, first, last, height)


def take_edges(edges, from_left, from_right, p):
    skip = from_left.shape[0] - V * NT * 2
    for v in range(V):
        edges[v, PAD - 8 : PAD, :] = jnp.zeros((8, LANES), F32)
        edges[v, 0:NT, :] = from_left[pl.ds(skip + v * 2 * NT + p, NT, stride=2), :]
        edges[V + v, PAD - 8 : PAD, :] = jnp.zeros((8, LANES), F32)
        edges[V + v, 0:NT, :] = from_right[pl.ds(v * 2 * NT + p, NT, stride=2), :]


def edge_terms(z, cells, values, edges, advect, p, first, last):
    if not isinstance(z, int):
        return values
    return [
        value
        + (1.0 if z == 0 else -1.0)
        * advect[pl.ds((z * V + v) * 2 + p, 1), :]
        * edges[v if z == 0 else V + v, first:last, :]
        for v, value in enumerate(values)
    ]


def near_cell(
    flags, base, halo, from_left, from_right, advect, viscous, inverse, lower, upper, g, flows, edges
):
    p = 1 - flags[0]
    cells = base.shape[0] // V
    take_edges(edges, from_left, from_right, p)

    def source(z, first, last):
        values = []
        for v in range(V):
            j = z * V + v
            values.append(base[j, first:last, :] + viscous[pl.ds(j * 2 + p, 1), :] * halo[j, first:last, :])
        return edge_terms(z, cells, values, edges, advect, p, first, last)

    sweeps(source, g, flows, 0, ((0, 32), (32, PAD)), p, inverse, lower, upper, cells)


def far_lead(flags, slab, trig, basis, turned, lead, halo):
    wrap = flags[1]
    sign = jnp.where(flags[2] == 1, -1.0, 1.0)
    left = split_left(lag_matrix(basis[...], turned[...], trig[...], sign))
    for z in range(LEAD):
        for v in range(V):
            halo[v, PAD - 8 : PAD, :] = jnp.zeros((8, LANES), F32)
            halo[v, 0:NT, :] = slab[pl.ds((z * V + v) * NT, NT), :]
        raw = [halo[v] for v in range(V)]
        (lagged,) = over_instants([left], raw)
        for v in range(V):
            lead[z * V + v] = jnp.where(wrap == 1, lagged[v], raw[v])


def far_chunk(chunk, flags, base, lead, halo, from_left, from_right, advect, viscous, inverse, lower, upper, g, fg, edges):
    (first, last), extra = chunk
    width = last - first
    p = flags[0]
    cells = base.shape[0] // V
    top = lax.broadcasted_iota(jnp.int32, (8, LANES), 0) == 0
    take_edges(edges, from_left, from_right, p)

    def pieces(ref, j):
        value = ref[j, first:last, :]
        return jnp.concatenate([value, ref[j, PAD - 8 : PAD, :]], axis=0) if extra else value

    def source(z, start, stop):
        result = []
        for v in range(V):
            j = z * V + v
            h = jnp.maximum(z - LEAD, 0) * V + v
            arrived = halo[pl.ds(pl.multiple_of(h * width, 8), width), :]
            if extra:
                row = halo[pl.ds((cells - LEAD) * V * width + h, 1), :]
                arrived = jnp.concatenate([arrived, jnp.where(top, row, 0.0)], axis=0)
            early = pieces(lead, jnp.minimum(z, LEAD - 1) * V + v)
            arrived = jnp.where(z >= LEAD, arrived, early)
            value = pieces(base, j) + viscous[pl.ds(j * 2 + p, 1), :] * arrived
            if isinstance(z, int):
                rate = advect[pl.ds(j * 2 + p, 1), :]
                edge = pieces(edges, v if z == 0 else V + v)
                value += rate * edge if z == 0 else -rate * edge
            result.append(value)
        return result

    height = rows_of(chunk)
    sweeps(source, g, fg, 0, ((0, height),), p, inverse, lower, upper, cells)


def times(matrix, vector):
    result = []
    for a in range(V):
        total = matrix(a, 0) * vector[0]
        for b in range(1, V):
            total += matrix(a, b) * vector[b]
        result.append(total)
    return result


def plus(one, two):
    return [a + b for a, b in zip(one, two)]


def tiles(ref, c, kind):
    return [ref[c, kind * V + a] for a in range(V)]


def rows(ref, c, kind):
    return lambda a, b: ref[c, kind * V + a, b : b + 1, :]


def unit(a):
    place = lax.broadcasted_iota(jnp.int32, (8, LANES), 0)
    return jnp.where(place == a, 1.0, 0.0).astype(F32)


def transfer(flags, lower, upper, blocks, group, forward):
    cells = blocks.shape[1] // V
    for c in range(2):
        p = 1 - flags[0] if c == 0 else flags[0]

        def ahead(z, current):
            result = times(lambda a, b: coefficient(lower, z, a, b, p), current)
            for a in range(V):
                forward[z * V + a] = result[a]
            return tuple(result)

        through = lax.fori_loop(0, cells, ahead, tuple(unit(a) for a in range(V)))

        def back(i, current):
            z = cells - 1 - i
            result = times(lambda a, b: coefficient(upper, z, a, b, p), current)
            for a in range(V):
                result[a] = result[a] + jnp.concatenate(
                    [forward[z * V + a], jnp.zeros((8, LANES), F32)], axis=0
                )
                blocks[c, z * V + a] = result[a]
            return tuple(result)

        start = tuple(
            jnp.concatenate([jnp.zeros((8, LANES), F32), unit(a)], axis=0) for a in range(V)
        )
        ends = lax.fori_loop(0, cells, back, start)
        for a in range(V):
            group[c * 3 * V + a] = ends[a][:8]
            group[(c * 3 + 1) * V + a] = ends[a][8:]
            group[(c * 3 + 2) * V + a] = through[a]


def merge_matrices(bit, levels, flags, mine, other, *refs):
    start, last = bit == 0, bit == levels - 1
    share, refs = (None, refs) if start else (refs[0], refs[1:])
    mats, merged, share_out = (refs[0], None, None) if last else refs
    right = flags[3 + bit] == 1
    left = jnp.logical_not(right)
    nothing = jnp.zeros((8, LANES), F32)
    for c in range(2):
        kinds = 1 if last else 3
        at = lambda ref, kind: [ref[(c * kinds + kind) * V + a] for a in range(V)]
        pick = lambda kind, own: [jnp.where(own, m, t) for m, t in zip(at(mine, kind), at(other, kind))]
        if start:
            own = [[unit(a) for a in range(V)], [nothing] * V, [unit(a) for a in range(V)]]
        else:
            own = [tiles(share, c, kind) for kind in range(3)]
        found = [
            (1, pick(0, right)),
            (3, [jnp.where(right, x, nothing) for x in own[0]]),
            (4, [jnp.where(right, x, nothing) for x in own[1]]),
            (5, [jnp.where(right, nothing, x) for x in own[2]]),
        ]
        if not last:
            found += [(0, pick(2, right)), (2, pick(1, left))]
        for kind, values in found:
            for a in range(V):
                mats[c, kind * V + a] = values[a]
        if last:
            continue
        p_left, g_left, h_right = pick(2, left), pick(0, left), pick(1, right)
        turned = times(rows(mats, c, 1), p_left)
        new = [plus(g_left, times(rows(mats, c, 2), turned))]
        if bit < levels - 2:
            new += [times(rows(mats, c, 2), h_right), times(rows(mats, c, 0), p_left)]
        for kind, values in enumerate(new):
            for a in range(V):
                merged[(c * len(new) + kind) * V + a] = values[a]
        s0 = times(rows(mats, c, 3), p_left)
        s1 = times(rows(mats, c, 4), p_left)
        s1b = times(rows(mats, c, 5), turned)
        s2 = times(rows(mats, c, 5), h_right)
        for a in range(V):
            share_out[c, a] = jnp.where(right, s0[a], own[0][a])
            share_out[c, V + a] = jnp.where(right, s1[a], own[1][a] + s1b[a])
            share_out[c, 2 * V + a] = jnp.where(right, own[2][a], s2[a])


def inflow_of(c, mats, f_left, g_right, known):
    back = plus(g_right, times(rows(mats, c, 1), f_left))
    from_left = times(rows(mats, c, 3), f_left)
    from_right = plus(times(rows(mats, c, 4), f_left), times(rows(mats, c, 5), back))
    total = from_left + from_right
    return back, total if known is None else plus(known, total)


def merge_flows(parts, bit, levels, flags, mats, flows, other, *refs):
    known, merged, inflow = (None, *refs) if bit == 0 else refs
    right, last_right = flags[3 + bit] == 1, flags[2 + levels] == 1
    last = bit == levels - 2
    start = 0
    for c, height in parts:

        def tile(t, carry, c=c, height=height, start=start):
            at = lambda i: start * 2 * V + i * height + t
            mine = [flows[at(i)] for i in range(2 * V)]
            theirs = [other[at(i)] for i in range(2 * V)]
            f_left = [jnp.where(right, y, x) for x, y in zip(mine[:V], theirs[:V])]
            f_right = [jnp.where(right, x, y) for x, y in zip(mine[:V], theirs[:V])]
            g_left = [jnp.where(right, y, x) for x, y in zip(mine[V:], theirs[V:])]
            g_right = [jnp.where(right, x, y) for x, y in zip(mine[V:], theirs[V:])]
            before = None if known is None else [known[at(i)] for i in range(2 * V)]
            back, total = inflow_of(c, mats, f_left, g_right, before)
            new_f = plus(f_right, times(rows(mats, c, 0), f_left))
            new_g = plus(g_left, times(rows(mats, c, 2), back))
            if last:
                for i in range(V):
                    end = jnp.where(last_right, new_g[i], new_f[i])
                    merged[start * V + i * height + t] = end
            else:
                for i, value in enumerate(new_f + new_g):
                    merged[at(i)] = value
            for i, value in enumerate(total):
                inflow[at(i)] = value
            return carry

        lax.fori_loop(0, height, tile, 0)
        start += height


def last_inflow(right, c, mats, ends, other, known, start, height, inflow):
    for t in range(height):
        mine = [ends[start * V + a * height + t] for a in range(V)]
        theirs = [other[start * V + a * height + t] for a in range(V)]
        f_left = [jnp.where(right, y, x) for x, y in zip(mine, theirs)]
        g_right = [jnp.where(right, x, y) for x, y in zip(mine, theirs)]
        before = [known[start * 2 * V + i * height + t] for i in range(2 * V)]
        _, total = inflow_of(c, mats, f_left, g_right, before)
        for i, value in enumerate(total):
            inflow[i, t * 8 : t * 8 + 8, :] = value


def corrected(c, z, a, first, last, g, blocks, inflow):
    total = g[z * V + a, first:last, :]
    for b in range(V):
        total += blocks[c, z * V + a, b : b + 1, :] * inflow[b]
        total += blocks[c, z * V + a, 8 + b : 9 + b, :] * inflow[V + b]
    return total


def correct(parts, levels, flags, mats, ends, other, known, blocks, *refs):
    solved, results, inflow = refs[: len(parts)], refs[len(parts) : -1], refs[-1]
    right = flags[2 + levels] == 1
    start = 0
    for (c, tall), g, result in zip(parts, solved, results):
        last_inflow(right, c, mats, ends, other, known, start, tall, inflow)
        start += tall
        height = tall * 8
        for first, last in ((0, 32), (32, height)) if height > 32 else ((0, height),):
            flow = tuple(inflow[i, first:last, :] for i in range(2 * V))

            def step(z, flow, c=c, first=first, last=last, g=g, result=result):
                for a in range(V):
                    result[z * V + a, first:last, :] = corrected(c, z, a, first, last, g, blocks, flow)
                return flow

            lax.fori_loop(0, g.shape[0] // V, step, flow)


def finish(levels, flags, mats, ends, other, known, g, blocks, near, *refs):
    done, out, inflow = refs[:-2], refs[-2], refs[-1]
    right = flags[2 + levels] == 1
    p = flags[0]
    (first_row, last_row), last_extra = CHUNKS[-1]
    width, height = last_row - first_row, rows_of(CHUNKS[-1])

    @pl.when(pl.program_id(0) == 0)
    def _():
        last_inflow(right, 1, mats, ends, other, known, 0, height // 8, inflow)

    flow = tuple(inflow[i] for i in range(2 * V))

    def step(z, carry):
        for a in range(V):
            j = z * V + a
            row = j * 2 * NT
            out[pl.ds(row + 1 - p, NT, stride=2), :] = near[j, 0:NT, :]
            for ref, ((first, last), extra) in zip(done, CHUNKS):
                out[pl.ds(row + p + 2 * first, last - first, stride=2), :] = ref[j, 0 : last - first, :]
                if extra:
                    out[pl.ds(row + p + 2 * (NT - 1), 1), :] = ref[j, last - first : last - first + 1, :]
            value = corrected(1, z, a, 0, height, g, blocks, flow)
            out[pl.ds(row + p + 2 * first_row, width, stride=2), :] = value[:width]
            if last_extra:
                out[pl.ds(row + p + 2 * (NT - 1), 1), :] = value[width : width + 1]
        return carry

    lax.fori_loop(0, g.shape[0] // V, step, 0)


def phase_tables(count):
    angle = 2.0 * math.pi * np.outer(np.arange(1, count + 1), np.arange(NT)) / NT
    cosine, sine = np.cos(angle), np.sin(angle)
    basis = np.zeros((PAD, 2 * count + 8), np.float32)
    basis[:NT, :count], basis[:NT, count : 2 * count], basis[:NT, 2 * count] = cosine.T, sine.T, 0.5
    turned = np.zeros((2, count + 8, 3, DEPTH), np.float32)
    turned[0, :count, :, :NT], turned[1, :count, :, :NT] = cosine[:, None], sine[:, None]
    turned[0, count, :, :NT] = 1.0
    return (2.0 / NT * basis).astype(np.float32), turned.reshape(2 * (count + 8), 3 * DEPTH)


def derivative_table():
    gap = np.arange(NT)[:, None] - np.arange(NT)[None, :]
    safe = np.where(gap == 0, 1.0, np.sin(np.pi * gap / NT))
    table = np.where(gap == 0, 0.0, 0.5 * (1.0 - 2.0 * np.mod(gap, 2)) / safe)
    wide = np.zeros((PAD, 3, DEPTH), np.float32)
    wide[:NT, :, :NT] = table[:, None]
    return wide.reshape(PAD, 3 * DEPTH)


COSTS = (0, 0, 6_000_000_000, 0)


def local(state, advect, viscous, inverse, lower, upper, blades, harmonic):
    cells = state.shape[0]
    count = harmonic.shape[0]
    segs, slabs = lax.axis_size("seg"), lax.axis_size("pitch")
    levels = segs.bit_length() - 1
    far_pairs = [(i, (i - 1) % slabs if i % 2 == 0 else (i + 1) % slabs) for i in range(slabs)]
    near_pairs = [(i, i ^ 1) for i in range(slabs)]
    to_far = lambda x: lax.ppermute(x, "pitch", far_pairs)
    to_level = lambda x, k: lax.ppermute(x, "seg", [(i, i ^ (1 << k)) for i in range(segs)])
    x_shape = (cells * V, PAD, LANES)

    slab, seg = lax.axis_index("pitch"), lax.axis_index("seg")
    side = slab % 2
    wrap = jnp.logical_or(slab == 0, slab == slabs - 1)
    bits = [(seg >> k) & 1 for k in range(levels)]
    run = Chain(
        jnp.stack(
            [side, wrap.astype(jnp.int32), (slab == 0).astype(jnp.int32), *bits]
        ).astype(jnp.int32)
    )
    flat = lambda x: x.transpose(0, 2, 3, 1, 4).reshape(cells * V * V * 2, LANES)
    inv, low, upp = flat(inverse.astype(F32)), flat(lower), flat(upper)
    blocks, group = run(
        transfer, [(2, cells * V, 16, LANES), (6 * V, 8, LANES)], [low, upp],
        scratch=[pltpu.VMEM((cells * V, 8, LANES), F32)], name="transfer", flops=COSTS[1],
    )
    st = state.transpose(0, 2, 3, 1, 4).reshape(cells * V * NT * 2, LANES)
    lead_rows, edge_rows = LEAD * V * NT, padded_even(V * NT * 2)
    held = pl.BlockSpec(memory_space=pltpu.VMEM)
    shapes = [(lead_rows, LANES), (edge_rows, LANES), (edge_rows, LANES), x_shape, x_shape]
    slab_out, first_cell, last_cell, xn, xf = pl.pallas_call(
        split_cells,
        out_shape=[jax.ShapeDtypeStruct(x, F32) for x in shapes],
        in_specs=[held],
        out_specs=[held] * 5,
        compiler_params=pltpu.CompilerParams(vmem_limit_bytes=16 * MB),
        name="split_cells",
    )(run.before(st))
    halo_near = lax.ppermute(xn, "pitch", near_pairs)
    slab_in = to_far(slab_out)
    from_left = lax.ppermute(last_cell, "seg", [(i, i + 1) for i in range(segs - 1)])
    from_right = lax.ppermute(first_cell, "seg", [(i + 1, i) for i in range(segs - 1)])

    basis, turned = phase_tables(count)
    table = derivative_table()
    wide_harmonic = jnp.broadcast_to(harmonic.astype(F32)[:, None], (count, LANES))

    rest = (cells - LEAD) * V
    chunk_shapes = [
        (rest * (last - first) + (padded_even(rest) if extra else 0), LANES)
        for (first, last), extra in CHUNKS
    ]
    adv = advect.transpose(0, 2, 1, 3).reshape(cells * V * 2, LANES)
    vis = viscous.transpose(0, 2, 1, 3).reshape(cells * V * 2, LANES)
    trig, base, *chunks = run(
        prepare, [(2 * count + 8, LANES), x_shape, *chunk_shapes],
        [xn, xf, wide_harmonic, basis, turned, adv, vis, table], scalars=[blades], name="prepare",
    )
    arrived = [slab_in]
    for chunk in chunks:
        if len(arrived) >= 2:
            chunk, arrived[-2] = lax.optimization_barrier((chunk, arrived[-2]))
        arrived.append(to_far(chunk))
    slab_in, *arrived = arrived

    edges = pltpu.VMEM((2 * V, PAD, LANES), F32)

    mats, share = [], []

    def merge_group(k):
        nonlocal group, share
        shapes = [(2, 6 * V, 8, LANES)]
        if k < levels - 1:
            shapes += [((6 if k < levels - 2 else 2) * V, 8, LANES), (2, 3 * V, 8, LANES)]
        out = run(
            functools.partial(merge_matrices, k, levels), shapes,
            [group, to_level(group, k), *share], name="merge_matrices",
        )
        mats.append(out[0])
        if k < levels - 1:
            group, share = out[1], [out[2]]

    def solve_chunk(i):
        height = rows_of(CHUNKS[i])
        return run(
            functools.partial(far_chunk, CHUNKS[i]),
            [(cells * V, height, LANES), (2 * V * height // 8, 8, LANES)],
            [base, lead, arrived[i], from_left, from_right, adv, vis, inv, low, upp],
            scratch=[edges], name="far_chunk",
        )

    class Exchange:
        def __init__(self, c, g, flows):
            self.parts = [(c, g.shape[1] // 8)]
            self.flows, self.known, self.solved, self.level = flows, [], g, 0

        def step(self):
            tall, k = self.parts[0][1], self.level
            shape = ((2 if k < levels - 2 else 1) * V * tall, 8, LANES)
            out = run(
                functools.partial(merge_flows, self.parts, k, levels),
                [shape, (2 * V * tall, 8, LANES)],
                [mats[k], self.flows, to_level(self.flows, k), *self.known], name="merge_flows",
            )
            self.flows, self.known, self.level = out[0], out[1:], k + 1

        def last(self):
            return [mats[-1], self.flows, to_level(self.flows, levels - 1), *self.known]

        def correct(self):
            return run(
                functools.partial(correct, self.parts, levels), [self.solved.shape],
                [*self.last(), blocks, self.solved],
                scratch=[pltpu.VMEM((2 * V, self.solved.shape[1], LANES), F32)], name="correct",
            )[0]

    group, halo_near = lax.optimization_barrier((group, halo_near))
    base_near = run(
        near_base, [x_shape], [xn, xf, adv, vis, table, trig], name="near_base", flops=COSTS[0]
    )[0]
    merge_group(0)
    lead = run(
        far_lead, [(LEAD * V, PAD, LANES)], [slab_in, trig, basis, turned],
        scratch=[pltpu.VMEM((V, PAD, LANES), F32)], name="far_lead", flops=COSTS[3],
    )[0]
    first = Exchange(
        0,
        *run(
            near_cell, [x_shape, (2 * V * PAD // 8, 8, LANES)],
            [base_near, halo_near, from_left, from_right, adv, vis, inv, low, upp],
            scratch=[edges], name="near_cell", flops=COSTS[2],
        )
    )
    for k in range(1, levels):
        merge_group(k)
    first.step()
    second = Exchange(1, *solve_chunk(0))
    for k in range(1, levels - 1):
        second.step()
        first.step()
    second.step()
    third = Exchange(1, *solve_chunk(1))
    third.step()
    near = first.correct()
    for k in range(1, levels - 1):
        third.step()
    done = [second.correct()]
    g_last = third.solved
    small = third.last()

    steps = 4
    part = cells // steps
    whole = lambda x: pl.BlockSpec(x.shape, lambda i: (0,) * x.ndim)
    by_cell = lambda x: pl.BlockSpec((part * V,) + x.shape[1:], lambda i: (i, 0, 0))
    out = run(
        functools.partial(finish, levels), [st.shape], [*small, g_last, blocks, near, *done],
        grid=(steps,),
        in_specs=[whole(x) for x in small]
        + [by_cell(g_last), pl.BlockSpec((2, part * V, 16, LANES), lambda i: (0, i, 0, 0))]
        + [by_cell(x) for x in (near, *done)],
        out_specs=[pl.BlockSpec((part * V * NT * 2, LANES), lambda i: (i, 0))],
        scratch=[pltpu.VMEM((2 * V, rows_of(CHUNKS[-1]), LANES), F32)], name="finish",
    )[0]
    return out.reshape(cells, V, NT, 2, LANES).transpose(0, 3, 1, 2, 4)


def solution(mesh):
    cell = P("seg", "pitch", None, None, None)
    return jax.shard_map(
        local,
        mesh=mesh,
        in_specs=(cell, P("seg", "pitch", None, None), P("seg", "pitch", None, None), cell, cell, cell, P(), P()),
        out_specs=cell,
        check_vma=False,
    )
```

```python
import functools
import math

import jax
import jax.numpy as jnp
import numpy as np
from jax import lax
from jax.experimental import pallas as pl
from jax.experimental.pallas import tpu as pltpu
from jax.sharding import PartitionSpec as P

F32 = jnp.float32
BF16 = jnp.bfloat16
V = 5
NT = 49
PAD = 56
DEPTH = 64
LANES = 128
LEAD = 4
MB = 1 << 20

CHUNKS = (((0, 32), True), ((32, 48), False))


def rows_of(chunk):
    (first, last), extra = chunk
    return last - first + (8 if extra else 0)


def padded_even(count):
    return (count + 7) // 8 * 8


class Chain:
    def __init__(self, flags):
        self.flags = flags

    def before(self, array):
        return lax.optimization_barrier((self.flags, array))[1]

    def after(self, array):
        self.flags, array = lax.optimization_barrier((self.flags, array))
        return array

    def __call__(self, body, out_shapes, arrays, scratch=(), vmem=16, name=None, grid=None, in_specs=None, out_specs=None, scalars=(), flops=1000):
        smem = pl.BlockSpec(memory_space=pltpu.SMEM)
        held = pl.BlockSpec(memory_space=pltpu.VMEM)
        extra = {} if grid is None else {"grid": grid}
        out = pl.pallas_call(
            body,
            out_shape=[jax.ShapeDtypeStruct(s, F32) for s in out_shapes],
            in_specs=[smem] * (1 + len(scalars)) + (in_specs or [held] * len(arrays)),
            out_specs=out_specs or [held] * len(out_shapes),
            scratch_shapes=list(scratch),
            compiler_params=pltpu.CompilerParams(vmem_limit_bytes=vmem * MB),
            cost_estimate=pl.CostEstimate(flops=flops, bytes_accessed=1000, transcendentals=0),
            name=name,
            **extra,
        )(self.flags, *scalars, *arrays)
        out = list(out)
        out[0] = self.after(out[0])
        return out


def coefficient(ref, z, a, b, p):
    return ref[pl.ds(((z * V + a) * V + b) * 2 + p, 1), :]


def split_left(matrix):
    high = matrix.astype(BF16).astype(F32)
    place = lax.broadcasted_iota(jnp.int32, matrix.shape, 1)
    return jnp.where(place < 2 * DEPTH, high, matrix - high).astype(BF16)


def lag_matrix(basis, turned, trig, sign):
    half = turned.shape[0] // 2
    count = (half - 4) // 8 * 8
    cosine, sine = turned[:half], turned[half:]
    turn, cross = trig[:count, :1], trig[count : 2 * count, :1] * sign
    right = jnp.concatenate(
        [
            turn * cosine[:count] + cross * sine[:count],
            turn * sine[:count] - cross * cosine[:count],
            cosine[count:],
        ],
        axis=0,
    )
    return jnp.dot(basis, right, preferred_element_type=F32, precision=lax.Precision.HIGHEST)


def over_instants(lefts, cells):
    whole = jnp.concatenate(cells, axis=1)
    if whole.shape[0] < DEPTH:
        whole = jnp.concatenate(
            [whole, jnp.zeros((DEPTH - whole.shape[0], whole.shape[1]), F32)], axis=0
        )
    high = whole.astype(BF16)
    low = (whole - high.astype(F32)).astype(BF16)
    right = jnp.concatenate([high, low, high], axis=0)
    products = [jnp.dot(left, right, preferred_element_type=F32) for left in lefts]
    return [[x[:, i * LANES : (i + 1) * LANES] for i in range(len(cells))] for x in products]


def split_cells(st, slab, first_cell, last_cell, xn, xf):
    p = lax.axis_index("pitch") % 2
    edge = first_cell.shape[0]
    zeros = jnp.zeros((8, LANES), F32)
    width = 4 * NT

    def step(i, carry):
        slab[pl.ds(i * width, width), :] = st[pl.ds(i * 2 * width + p, width, stride=2), :]
        return carry

    lax.fori_loop(0, LEAD * V // 4, step, 0)
    first_cell[...] = st[0:edge, :]
    last_cell[...] = st[st.shape[0] - edge :, :]

    def separate(z, carry):
        for v in range(V):
            j = z * V + v
            for out, q in ((xn, 1 - p), (xf, p)):
                out[j, PAD - 8 : PAD, :] = zeros
                out[j, 0:NT, :] = st[pl.ds(j * 2 * NT + q, NT, stride=2), :]
        return carry

    lax.fori_loop(0, xn.shape[0] // V, separate, 0)


def lags(blades, harmonic, trig):
    count = harmonic.shape[0]
    rotor = jnp.full(harmonic.shape, blades[0]).astype(F32)
    stator = jnp.full(harmonic.shape, blades[1]).astype(F32)
    turns = harmonic[...] * stator
    lag = (turns - rotor * jnp.floor(turns / rotor)) / rotor * (2.0 * math.pi)
    trig[0:count, :] = jnp.cos(lag)
    trig[count : 2 * count, :] = jnp.sin(lag)
    trig[2 * count : 2 * count + 8, :] = (stator / rotor / count)[:8]


def own_terms(z, x, other, advect, viscous, p, timing, above, below, base):
    for v in range(V):
        j = z * V + v
        total = viscous[pl.ds(j * 2 + p, 1), :] * (other[j] - 2.0 * x[j]) - timing[v]
        rate = advect[pl.ds(j * 2 + p, 1), :]
        if above and below:
            total += rate * (x[j - V] - x[j + V])
        else:
            total += rate * (x[j - V] if above else -x[j + V])
        base[j] = total


def timing_matrix(table, trig):
    return split_left(table[...] * trig[trig.shape[0] - 8 : trig.shape[0] - 7, :1])


def prepare(flags, blades, xn, xf, harmonic, basis, turned, advect, viscous, table, trig, base, *chunks):
    lags(blades, harmonic, trig)
    p, wrap = flags[0], flags[1]
    cells = xf.shape[0] // V
    sign = jnp.where(flags[2] == 1, 1.0, -1.0)
    lag = split_left(lag_matrix(basis[...], turned[...], trig[...], sign))
    derive = timing_matrix(table, trig)

    def one(z, above=True, below=True, sends=True):
        raw = [xf[z * V + v] for v in range(V)]
        timing, *lagged = over_instants([derive, lag] if sends else [derive], raw)
        own_terms(z, xf, xn, advect, viscous, p, timing, above, below, base)
        if not sends:
            return
        for v in range(V):
            value = jnp.where(wrap == 1, lagged[0][v], raw[v])
            j = (z - LEAD) * V + v
            for out, ((first, last), extra) in zip(chunks, CHUNKS):
                width = last - first
                out[pl.ds(pl.multiple_of(j * width, 8), width), :] = value[first:last]
                if extra:
                    out[pl.ds((cells - LEAD) * V * width + j, 1), :] = value[NT - 1 : NT]

    def early(z, carry):
        one(z, sends=False)
        return carry

    def late(z, carry):
        one(z)
        return carry

    one(0, above=False, sends=False)
    lax.fori_loop(1, LEAD, early, 0)
    lax.fori_loop(LEAD, cells - 1, late, 0)
    one(cells - 1, below=False)


def near_base(flags, xn, xf, advect, viscous, table, trig, base):
    p = 1 - flags[0]
    cells = xn.shape[0] // V
    derive = timing_matrix(table, trig)

    def one(z, above=True, below=True):
        (timing,) = over_instants([derive], [xn[z * V + v] for v in range(V)])
        own_terms(z, xn, xf, advect, viscous, p, timing, above, below, base)

    def inner(z, carry):
        one(z)
        return carry

    one(0, above=False)
    lax.fori_loop(1, cells - 1, inner, 0)
    one(cells - 1, below=False)


def keep_tiles(ref, offset, values, first, last, height):
    for a in range(V):
        for t in range(first // 8, last // 8):
            ref[offset + a * height + t] = values[a][t * 8 - first : t * 8 - first + 8]


def sweeps(source, g, fg, offset, spans, p, inverse, lower, upper, cells):
    height = g.shape[1] // 8
    for first, last in spans:
        nothing = tuple(jnp.zeros((last - first, LANES), F32) for _ in range(V))

        def ahead(z, current, first=first, last=last):
            right = source(z, first, last)
            result = []
            for a in range(V):
                total = coefficient(inverse, z, a, 0, p) * right[0]
                for b in range(1, V):
                    total += coefficient(inverse, z, a, b, p) * right[b]
                for b in range(V):
                    total += coefficient(lower, z, a, b, p) * current[b]
                g[z * V + a, first:last, :] = total
                result.append(total)
            return tuple(result)

        out = lax.fori_loop(1, cells - 1, ahead, ahead(0, nothing))
        out = ahead(cells - 1, out)
        keep_tiles(fg, offset, out, first, last, height)

        def back(i, current, first=first, last=last):
            z = cells - 1 - i
            result = []
            for a in range(V):
                total = g[z * V + a, first:last, :]
                for b in range(V):
                    total += coefficient(upper, z, a, b, p) * current[b]
                g[z * V + a, first:last, :] = total
                result.append(total)
            return tuple(result)

        out = lax.fori_loop(0, cells, back, nothing)
        keep_tiles(fg, offset + V * height, out, first, last, height)


def take_edges(edges, from_left, from_right, p):
    skip = from_left.shape[0] - V * NT * 2
    for v in range(V):
        edges[v, PAD - 8 : PAD, :] = jnp.zeros((8, LANES), F32)
        edges[v, 0:NT, :] = from_left[pl.ds(skip + v * 2 * NT + p, NT, stride=2), :]
        edges[V + v, PAD - 8 : PAD, :] = jnp.zeros((8, LANES), F32)
        edges[V + v, 0:NT, :] = from_right[pl.ds(v * 2 * NT + p, NT, stride=2), :]


def edge_terms(z, cells, values, edges, advect, p, first, last):
    if not isinstance(z, int):
        return values
    return [
        value
        + (1.0 if z == 0 else -1.0)
        * advect[pl.ds((z * V + v) * 2 + p, 1), :]
        * edges[v if z == 0 else V + v, first:last, :]
        for v, value in enumerate(values)
    ]


def near_cell(
    flags, base, halo, from_left, from_right, advect, viscous, inverse, lower, upper, group,
    g, flows, edges,
):
    p = 1 - flags[0]
    cells = base.shape[0] // V
    take_edges(edges, from_left, from_right, p)

    def source(z, first, last):
        values = []
        for v in range(V):
            j = z * V + v
            values.append(base[j, first:last, :] + viscous[pl.ds(j * 2 + p, 1), :] * halo[j, first:last, :])
        return edge_terms(z, cells, values, edges, advect, p, first, last)

    sweeps(source, g, flows, 0, ((0, 32), (32, PAD)), p, inverse, lower, upper, cells)
    flows[2 * V * PAD // 8 :] = group[...]


def far_lead(flags, slab, trig, basis, turned, lead, halo):
    wrap = flags[1]
    sign = jnp.where(flags[2] == 1, -1.0, 1.0)
    left = split_left(lag_matrix(basis[...], turned[...], trig[...], sign))
    for z in range(LEAD):
        for v in range(V):
            halo[v, PAD - 8 : PAD, :] = jnp.zeros((8, LANES), F32)
            halo[v, 0:NT, :] = slab[pl.ds((z * V + v) * NT, NT), :]
        raw = [halo[v] for v in range(V)]
        (lagged,) = over_instants([left], raw)
        for v in range(V):
            lead[z * V + v] = jnp.where(wrap == 1, lagged[v], raw[v])


def far_chunk(chunk, flags, base, lead, halo, from_left, from_right, advect, viscous, inverse, lower, upper, g, fg, edges):
    (first, last), extra = chunk
    width = last - first
    p = flags[0]
    cells = base.shape[0] // V
    top = lax.broadcasted_iota(jnp.int32, (8, LANES), 0) == 0
    take_edges(edges, from_left, from_right, p)

    def pieces(ref, j):
        value = ref[j, first:last, :]
        return jnp.concatenate([value, ref[j, PAD - 8 : PAD, :]], axis=0) if extra else value

    def source(z, start, stop):
        result = []
        for v in range(V):
            j = z * V + v
            h = jnp.maximum(z - LEAD, 0) * V + v
            arrived = halo[pl.ds(pl.multiple_of(h * width, 8), width), :]
            if extra:
                row = halo[pl.ds((cells - LEAD) * V * width + h, 1), :]
                arrived = jnp.concatenate([arrived, jnp.where(top, row, 0.0)], axis=0)
            early = pieces(lead, jnp.minimum(z, LEAD - 1) * V + v)
            arrived = jnp.where(z >= LEAD, arrived, early)
            value = pieces(base, j) + viscous[pl.ds(j * 2 + p, 1), :] * arrived
            if isinstance(z, int):
                rate = advect[pl.ds(j * 2 + p, 1), :]
                edge = pieces(edges, v if z == 0 else V + v)
                value += rate * edge if z == 0 else -rate * edge
            result.append(value)
        return result

    height = rows_of(chunk)
    sweeps(source, g, fg, 0, ((0, height),), p, inverse, lower, upper, cells)


def times(matrix, vector):
    result = []
    for a in range(V):
        total = matrix(a, 0) * vector[0]
        for b in range(1, V):
            total += matrix(a, b) * vector[b]
        result.append(total)
    return result


def plus(one, two):
    return [a + b for a, b in zip(one, two)]


def tiles(ref, c, kind):
    return [ref[c, kind * V + a] for a in range(V)]


def rows(ref, c, kind):
    return lambda a, b: ref[c, kind * V + a, b : b + 1, :]


def unit(a):
    place = lax.broadcasted_iota(jnp.int32, (8, LANES), 0)
    return jnp.where(place == a, 1.0, 0.0).astype(F32)


def transfer(flags, lower, upper, blocks, group, forward):
    cells = blocks.shape[1] // V
    for c in range(2):
        p = 1 - flags[0] if c == 0 else flags[0]

        def ahead(z, current):
            result = times(lambda a, b: coefficient(lower, z, a, b, p), current)
            for a in range(V):
                forward[z * V + a] = result[a]
            return tuple(result)

        through = lax.fori_loop(0, cells, ahead, tuple(unit(a) for a in range(V)))

        def back(i, current):
            z = cells - 1 - i
            result = times(lambda a, b: coefficient(upper, z, a, b, p), current)
            for a in range(V):
                result[a] = result[a] + jnp.concatenate(
                    [forward[z * V + a], jnp.zeros((8, LANES), F32)], axis=0
                )
                blocks[c, z * V + a] = result[a]
            return tuple(result)

        start = tuple(
            jnp.concatenate([jnp.zeros((8, LANES), F32), unit(a)], axis=0) for a in range(V)
        )
        ends = lax.fori_loop(0, cells, back, start)
        for a in range(V):
            group[c * 3 * V + a] = ends[a][:8]
            group[(c * 3 + 1) * V + a] = ends[a][8:]
            group[(c * 3 + 2) * V + a] = through[a]


def merge_matrices(bit, levels, flags, mine, other, share, mats, merged, share_out, offset, new_offset):
    start, last = bit == 0, bit == levels - 1
    right = flags[3 + bit] == 1
    left = jnp.logical_not(right)
    nothing = jnp.zeros((8, LANES), F32)
    for c in range(2):
        kinds = 1 if last else 3
        at = lambda ref, kind: [ref[offset + (c * kinds + kind) * V + a] for a in range(V)]
        pick = lambda kind, own: [jnp.where(own, m, t) for m, t in zip(at(mine, kind), at(other, kind))]
        if start:
            own = [[unit(a) for a in range(V)], [nothing] * V, [unit(a) for a in range(V)]]
        else:
            own = [tiles(share, c, kind) for kind in range(3)]
        found = [
            (1, pick(0, right)),
            (3, [jnp.where(right, x, nothing) for x in own[0]]),
            (4, [jnp.where(right, x, nothing) for x in own[1]]),
            (5, [jnp.where(right, nothing, x) for x in own[2]]),
        ]
        if not last:
            found += [(0, pick(2, right)), (2, pick(1, left))]
        for kind, values in found:
            for a in range(V):
                mats[c, kind * V + a] = values[a]
        if last:
            continue
        p_left, g_left, h_right = pick(2, left), pick(0, left), pick(1, right)
        turned = times(rows(mats, c, 1), p_left)
        new = [plus(g_left, times(rows(mats, c, 2), turned))]
        if bit < levels - 2:
            new += [times(rows(mats, c, 2), h_right), times(rows(mats, c, 0), p_left)]
        for kind, values in enumerate(new):
            for a in range(V):
                merged[new_offset + (c * len(new) + kind) * V + a] = values[a]
        s0 = times(rows(mats, c, 3), p_left)
        s1 = times(rows(mats, c, 4), p_left)
        s1b = times(rows(mats, c, 5), turned)
        s2 = times(rows(mats, c, 5), h_right)
        for a in range(V):
            share_out[c, a] = jnp.where(right, s0[a], own[0][a])
            share_out[c, V + a] = jnp.where(right, s1[a], own[1][a] + s1b[a])
            share_out[c, 2 * V + a] = jnp.where(right, own[2][a], s2[a])


def inflow_of(c, mats, f_left, g_right, known):
    back = plus(g_right, times(rows(mats, c, 1), f_left))
    from_left = times(rows(mats, c, 3), f_left)
    from_right = plus(times(rows(mats, c, 4), f_left), times(rows(mats, c, 5), back))
    total = from_left + from_right
    return back, total if known is None else plus(known, total)


def merge_all(parts, bit, levels, flags, flows, other, *refs):
    share, known, mats, merged, share_out, inflow = (None, None, *refs) if bit == 0 else refs
    tall = sum(height for _, height in parts) * V
    new_offset = tall * (1 if bit == levels - 2 else 2)
    merge_matrices(bit, levels, flags, flows, other, share, mats, merged, share_out, 2 * tall, new_offset)
    merge_flows(parts, bit, levels, flags, mats, flows, other, *([] if known is None else [known]), merged, inflow)


def merge_flows(parts, bit, levels, flags, mats, flows, other, *refs):
    known, merged, inflow = (None, *refs) if bit == 0 else refs
    right, last_right = flags[3 + bit] == 1, flags[2 + levels] == 1
    last = bit == levels - 2
    start = 0
    for c, height in parts:

        def tile(t, carry, c=c, height=height, start=start):
            at = lambda i: start * 2 * V + i * height + t
            mine = [flows[at(i)] for i in range(2 * V)]
            theirs = [other[at(i)] for i in range(2 * V)]
            f_left = [jnp.where(right, y, x) for x, y in zip(mine[:V], theirs[:V])]
            f_right = [jnp.where(right, x, y) for x, y in zip(mine[:V], theirs[:V])]
            g_left = [jnp.where(right, y, x) for x, y in zip(mine[V:], theirs[V:])]
            g_right = [jnp.where(right, x, y) for x, y in zip(mine[V:], theirs[V:])]
            before = None if known is None else [known[at(i)] for i in range(2 * V)]
            back, total = inflow_of(c, mats, f_left, g_right, before)
            new_f = plus(f_right, times(rows(mats, c, 0), f_left))
            new_g = plus(g_left, times(rows(mats, c, 2), back))
            if last:
                for i in range(V):
                    end = jnp.where(last_right, new_g[i], new_f[i])
                    merged[start * V + i * height + t] = end
            else:
                for i, value in enumerate(new_f + new_g):
                    merged[at(i)] = value
            for i, value in enumerate(total):
                inflow[at(i)] = value
            return carry

        lax.fori_loop(0, height, tile, 0)
        start += height


def last_inflow(right, c, mats, ends, other, known, start, height, inflow):
    for t in range(height):
        mine = [ends[start * V + a * height + t] for a in range(V)]
        theirs = [other[start * V + a * height + t] for a in range(V)]
        f_left = [jnp.where(right, y, x) for x, y in zip(mine, theirs)]
        g_right = [jnp.where(right, x, y) for x, y in zip(mine, theirs)]
        before = [known[start * 2 * V + i * height + t] for i in range(2 * V)]
        _, total = inflow_of(c, mats, f_left, g_right, before)
        for i, value in enumerate(total):
            inflow[i, t * 8 : t * 8 + 8, :] = value


def corrected(c, z, a, first, last, g, blocks, inflow):
    total = g[z * V + a, first:last, :]
    for b in range(V):
        total += blocks[c, z * V + a, b : b + 1, :] * inflow[b]
        total += blocks[c, z * V + a, 8 + b : 9 + b, :] * inflow[V + b]
    return total


def correct(parts, levels, flags, mats, ends, other, known, blocks, *refs):
    solved, results, inflow = refs[: len(parts)], refs[len(parts) : -1], refs[-1]
    right = flags[2 + levels] == 1
    start = 0
    for (c, tall), g, result in zip(parts, solved, results):
        last_inflow(right, c, mats, ends, other, known, start, tall, inflow)
        start += tall
        height = tall * 8
        for first, last in ((0, 32), (32, height)) if height > 32 else ((0, height),):
            flow = tuple(inflow[i, first:last, :] for i in range(2 * V))

            def step(z, flow, c=c, first=first, last=last, g=g, result=result):
                for a in range(V):
                    result[z * V + a, first:last, :] = corrected(c, z, a, first, last, g, blocks, flow)
                return flow

            lax.fori_loop(0, g.shape[0] // V, step, flow)


def correct_all(parts, levels, flags, ends, other, share, known, blocks, *refs):
    count = len(parts)
    solved, results, mats, inflow = refs[:count], refs[count : 2 * count], refs[-2], refs[-1]
    tall = sum(height for _, height in parts) * V
    merge_matrices(levels - 1, levels, flags, ends, other, share, mats, None, None, tall, 0)
    correct(parts, levels, flags, mats, ends, other, known, blocks, *solved, *results, inflow)


def finish(levels, flags, mats, ends, other, known, g, blocks, near, *refs):
    done, (out, inflow, held, sems) = refs[:-4], refs[-4:]
    right = flags[2 + levels] == 1
    p = flags[0]
    (first_row, last_row), last_extra = CHUNKS[-1]
    width, height = last_row - first_row, rows_of(CHUNKS[-1])
    last_inflow(right, 1, mats, ends, other, known, 0, height // 8, inflow)
    flow = tuple(inflow[i] for i in range(2 * V))

    def step(z, carry):
        for a in range(V):
            j = z * V + a
            row = j * 2 * NT
            held[pl.ds(row + 1 - p, NT, stride=2), :] = near[j, 0:NT, :]
            for ref, ((first, last), extra) in zip(done, CHUNKS):
                held[pl.ds(row + p + 2 * first, last - first, stride=2), :] = ref[j, 0 : last - first, :]
                if extra:
                    held[pl.ds(row + p + 2 * (NT - 1), 1), :] = ref[j, last - first : last - first + 1, :]
            value = corrected(1, z, a, 0, height, g, blocks, flow)
            held[pl.ds(row + p + 2 * first_row, width, stride=2), :] = value[:width]
            if last_extra:
                held[pl.ds(row + p + 2 * (NT - 1), 1), :] = value[width : width + 1]
        return carry

    parts = sems.shape[0]
    cells = g.shape[0] // V // parts
    size = held.shape[0] // parts
    copies = []
    for i in range(parts):
        lax.fori_loop(i * cells, (i + 1) * cells, step, 0)
        span = pl.ds(i * size, size)
        copies.append(pltpu.make_async_copy(held.at[span, :], out.at[span, :], sems.at[i]))
        copies[-1].start()
    for copy in copies:
        copy.wait()


def phase_tables(count):
    angle = 2.0 * math.pi * np.outer(np.arange(1, count + 1), np.arange(NT)) / NT
    cosine, sine = np.cos(angle), np.sin(angle)
    basis = np.zeros((PAD, 2 * count + 8), np.float32)
    basis[:NT, :count], basis[:NT, count : 2 * count], basis[:NT, 2 * count] = cosine.T, sine.T, 0.5
    turned = np.zeros((2, count + 8, 3, DEPTH), np.float32)
    turned[0, :count, :, :NT], turned[1, :count, :, :NT] = cosine[:, None], sine[:, None]
    turned[0, count, :, :NT] = 1.0
    return (2.0 / NT * basis).astype(np.float32), turned.reshape(2 * (count + 8), 3 * DEPTH)


def derivative_table():
    gap = np.arange(NT)[:, None] - np.arange(NT)[None, :]
    safe = np.where(gap == 0, 1.0, np.sin(np.pi * gap / NT))
    table = np.where(gap == 0, 0.0, 0.5 * (1.0 - 2.0 * np.mod(gap, 2)) / safe)
    wide = np.zeros((PAD, 3, DEPTH), np.float32)
    wide[:NT, :, :NT] = table[:, None]
    return wide.reshape(PAD, 3 * DEPTH)


COSTS = (0, 0, 6_000_000_000, 0)


def local(state, advect, viscous, inverse, lower, upper, blades, harmonic):
    cells = state.shape[0]
    count = harmonic.shape[0]
    segs, slabs = lax.axis_size("seg"), lax.axis_size("pitch")
    levels = segs.bit_length() - 1
    far_pairs = [(i, (i - 1) % slabs if i % 2 == 0 else (i + 1) % slabs) for i in range(slabs)]
    near_pairs = [(i, i ^ 1) for i in range(slabs)]
    to_far = lambda x: lax.ppermute(x, "pitch", far_pairs)
    to_level = lambda x, k: lax.ppermute(x, "seg", [(i, i ^ (1 << k)) for i in range(segs)])
    x_shape = (cells * V, PAD, LANES)

    slab, seg = lax.axis_index("pitch"), lax.axis_index("seg")
    side = slab % 2
    wrap = jnp.logical_or(slab == 0, slab == slabs - 1)
    bits = [(seg >> k) & 1 for k in range(levels)]
    run = Chain(
        jnp.stack(
            [side, wrap.astype(jnp.int32), (slab == 0).astype(jnp.int32), *bits]
        ).astype(jnp.int32)
    )
    flat = lambda x: x.transpose(0, 2, 3, 1, 4).reshape(cells * V * V * 2, LANES)
    inv, low, upp = flat(inverse.astype(F32)), flat(lower), flat(upper)
    st = state.transpose(0, 2, 3, 1, 4).reshape(cells * V * NT * 2, LANES)
    lead_rows, edge_rows = LEAD * V * NT, padded_even(V * NT * 2)
    held = pl.BlockSpec(memory_space=pltpu.VMEM)
    shapes = [(lead_rows, LANES), (edge_rows, LANES), (edge_rows, LANES), x_shape, x_shape]
    slab_out, first_cell, last_cell, xn, xf = pl.pallas_call(
        split_cells,
        out_shape=[jax.ShapeDtypeStruct(x, F32) for x in shapes],
        in_specs=[held],
        out_specs=[held] * 5,
        compiler_params=pltpu.CompilerParams(vmem_limit_bytes=16 * MB),
        name="split_cells",
    )(st)
    halo_near = lax.ppermute(xn, "pitch", near_pairs)
    slab_in = to_far(slab_out)
    from_left = lax.ppermute(last_cell, "seg", [(i, i + 1) for i in range(segs - 1)])
    from_right = lax.ppermute(first_cell, "seg", [(i + 1, i) for i in range(segs - 1)])

    basis, turned = phase_tables(count)
    table = derivative_table()
    wide_harmonic = jnp.broadcast_to(harmonic.astype(F32)[:, None], (count, LANES))

    rest = (cells - LEAD) * V
    chunk_shapes = [
        (rest * (last - first) + (padded_even(rest) if extra else 0), LANES)
        for (first, last), extra in CHUNKS
    ]
    adv = advect.transpose(0, 2, 1, 3).reshape(cells * V * 2, LANES)
    vis = viscous.transpose(0, 2, 1, 3).reshape(cells * V * 2, LANES)
    trig, base, *chunks = run(
        prepare, [(2 * count + 8, LANES), x_shape, *chunk_shapes],
        [xn, xf, wide_harmonic, basis, turned, adv, vis, table], scalars=[blades], name="prepare",
    )
    arrived = [slab_in]
    for chunk in chunks:
        if len(arrived) >= 2:
            chunk, arrived[-2] = lax.optimization_barrier((chunk, arrived[-2]))
        arrived.append(to_far(chunk))
    slab_in, *arrived = arrived

    edges = pltpu.VMEM((2 * V, PAD, LANES), F32)

    mats = []
    mats_shape = (2, 6 * V, 8, LANES)

    def solve_chunk(i):
        height = rows_of(CHUNKS[i])
        return run(
            functools.partial(far_chunk, CHUNKS[i]),
            [(cells * V, height, LANES), (2 * V * height // 8, 8, LANES)],
            [base, lead, arrived[i], from_left, from_right, adv, vis, inv, low, upp],
            scratch=[edges], name="far_chunk",
        )

    class Exchange:
        def __init__(self, c, g, flows, leads=False):
            self.parts, self.leads = [(c, g.shape[1] // 8)], leads
            self.flows, self.known, self.solved, self.level = flows, [], g, 0
            self.scratch = [pltpu.VMEM((2 * V, g.shape[1], LANES), F32)]

        def step(self):
            tall, k = self.parts[0][1], self.level
            shape = ((2 if k < levels - 2 else 1) * V * tall, 8, LANES)
            inflow = (2 * V * tall, 8, LANES)
            other = to_level(self.flows, k)
            if self.leads:
                shape = (shape[0] + (6 * V if k < levels - 2 else 2 * V),) + shape[1:]
                out = run(
                    functools.partial(merge_all, self.parts, k, levels),
                    [mats_shape, shape, (2, 3 * V, 8, LANES), inflow],
                    [self.flows, other, *self.known], name="merge_all",
                )
                mats.append(out[0])
                self.flows, self.known = out[1], out[2:]
            else:
                out = run(
                    functools.partial(merge_flows, self.parts, k, levels), [shape, inflow],
                    [mats[k], self.flows, other, *self.known], name="merge_flows",
                )
                self.flows, self.known = out[0], out[1:]
            self.level = k + 1

        def last(self):
            return [self.flows, to_level(self.flows, levels - 1), *self.known]

        def correct(self):
            if self.leads:
                result, last = run(
                    functools.partial(correct_all, self.parts, levels), [self.solved.shape, mats_shape],
                    [*self.last(), blocks, self.solved], scratch=self.scratch, name="correct_all",
                )
                mats.append(last)
                return result
            return run(
                functools.partial(correct, self.parts, levels), [self.solved.shape],
                [mats[-1], *self.last(), blocks, self.solved], scratch=self.scratch, name="correct",
            )[0]

    base_near = run(
        near_base, [x_shape], [xn, xf, adv, vis, table, trig], name="near_base", flops=COSTS[0]
    )[0]
    blocks, group = run(
        transfer, [(2, cells * V, 16, LANES), (6 * V, 8, LANES)], [low, upp],
        scratch=[pltpu.VMEM((cells * V, 8, LANES), F32)], name="transfer", flops=COSTS[1],
    )
    lead = run(
        far_lead, [(LEAD * V, PAD, LANES)], [slab_in, trig, basis, turned],
        scratch=[pltpu.VMEM((V, PAD, LANES), F32)], name="far_lead", flops=COSTS[3],
    )[0]
    first = Exchange(
        0,
        *run(
            near_cell, [x_shape, (2 * V * PAD // 8 + 6 * V, 8, LANES)],
            [base_near, halo_near, from_left, from_right, adv, vis, inv, low, upp, group],
            scratch=[edges], name="near_cell", flops=COSTS[2],
        ),
        leads=True,
    )
    first.step()
    second = Exchange(1, *solve_chunk(0))
    second.step()
    for k in range(1, levels - 1):
        first.step()
    third = Exchange(1, *solve_chunk(1))
    for k in range(1, levels - 1):
        second.step()
    third.step()
    near = first.correct()
    for k in range(1, levels - 1):
        third.step()
    done = [second.correct()]
    g_last = third.solved
    small = [mats[-1], *third.last()]

    out = run(
        functools.partial(finish, levels), [st.shape], [*small, g_last, blocks, near, *done],
        out_specs=[pl.BlockSpec(memory_space=pltpu.HBM)],
        scratch=[
            pltpu.VMEM((2 * V, rows_of(CHUNKS[-1]), LANES), F32),
            pltpu.VMEM(st.shape, F32),
            pltpu.SemaphoreType.DMA((4,)),
        ],
        name="finish",
    )[0]
    return out.reshape(cells, V, NT, 2, LANES).transpose(0, 3, 1, 2, 4)


def solution(mesh):
    cell = P("seg", "pitch", None, None, None)
    return jax.shard_map(
        local,
        mesh=mesh,
        in_specs=(cell, P("seg", "pitch", None, None), P("seg", "pitch", None, None), cell, cell, cell, P(), P()),
        out_specs=cell,
        check_vma=False,
    )
```

```python
import functools
import math

import jax
import jax.numpy as jnp
import numpy as np
from jax import lax
from jax.experimental import pallas as pl
from jax.experimental.pallas import tpu as pltpu
from jax.sharding import PartitionSpec as P

F32 = jnp.float32
BF16 = jnp.bfloat16
V = 5
NT = 49
PAD = 56
DEPTH = 64
LANES = 128
LEAD = 4
MB = 1 << 20

CHUNKS = (((0, 32), True), ((32, 48), False))


def rows_of(chunk):
    (first, last), extra = chunk
    return last - first + (8 if extra else 0)


def padded_even(count):
    return (count + 7) // 8 * 8


class Chain:
    def __init__(self, flags):
        self.flags = flags

    def before(self, array):
        return lax.optimization_barrier((self.flags, array))[1]

    def after(self, array):
        self.flags, array = lax.optimization_barrier((self.flags, array))
        return array

    def __call__(self, body, out_shapes, arrays, scratch=(), vmem=16, name=None, grid=None, in_specs=None, out_specs=None, scalars=(), flops=1000):
        smem = pl.BlockSpec(memory_space=pltpu.SMEM)
        held = pl.BlockSpec(memory_space=pltpu.VMEM)
        extra = {} if grid is None else {"grid": grid}
        out = pl.pallas_call(
            body,
            out_shape=[jax.ShapeDtypeStruct(s, F32) for s in out_shapes],
            in_specs=[smem] * (1 + len(scalars)) + (in_specs or [held] * len(arrays)),
            out_specs=out_specs or [held] * len(out_shapes),
            scratch_shapes=list(scratch),
            compiler_params=pltpu.CompilerParams(vmem_limit_bytes=vmem * MB),
            cost_estimate=pl.CostEstimate(flops=flops, bytes_accessed=1000, transcendentals=0),
            name=name,
            **extra,
        )(self.flags, *scalars, *arrays)
        out = list(out)
        out[0] = self.after(out[0])
        return out


def coefficient(ref, z, a, b, p):
    return ref[pl.ds(((z * V + a) * V + b) * 2 + p, 1), :]


def split_left(matrix):
    high = matrix.astype(BF16).astype(F32)
    place = lax.broadcasted_iota(jnp.int32, matrix.shape, 1)
    return jnp.where(place < 2 * DEPTH, high, matrix - high).astype(BF16)


def lag_matrix(basis, turned, trig, sign):
    half = turned.shape[0] // 2
    count = (half - 4) // 8 * 8
    cosine, sine = turned[:half], turned[half:]
    turn, cross = trig[:count, :1], trig[count : 2 * count, :1] * sign
    right = jnp.concatenate(
        [
            turn * cosine[:count] + cross * sine[:count],
            turn * sine[:count] - cross * cosine[:count],
            cosine[count:],
        ],
        axis=0,
    )
    return jnp.dot(basis, right, preferred_element_type=F32, precision=lax.Precision.HIGHEST)


def over_instants(lefts, cells):
    whole = jnp.concatenate(cells, axis=1)
    if whole.shape[0] < DEPTH:
        whole = jnp.concatenate(
            [whole, jnp.zeros((DEPTH - whole.shape[0], whole.shape[1]), F32)], axis=0
        )
    high = whole.astype(BF16)
    low = (whole - high.astype(F32)).astype(BF16)
    right = jnp.concatenate([high, low, high], axis=0)
    products = [jnp.dot(left, right, preferred_element_type=F32) for left in lefts]
    return [[x[:, i * LANES : (i + 1) * LANES] for i in range(len(cells))] for x in products]


def split_cells(st, slab, first_cell, last_cell, xn, xf):
    p = lax.axis_index("pitch") % 2
    edge = first_cell.shape[0]
    zeros = jnp.zeros((8, LANES), F32)
    width = 4 * NT

    def step(i, carry):
        slab[pl.ds(i * width, width), :] = st[pl.ds(i * 2 * width + p, width, stride=2), :]
        return carry

    lax.fori_loop(0, LEAD * V // 4, step, 0)
    first_cell[...] = st[0:edge, :]
    last_cell[...] = st[st.shape[0] - edge :, :]

    def separate(z, carry):
        for v in range(V):
            j = z * V + v
            for out, q in ((xn, 1 - p), (xf, p)):
                out[j, PAD - 8 : PAD, :] = zeros
                out[j, 0:NT, :] = st[pl.ds(j * 2 * NT + q, NT, stride=2), :]
        return carry

    lax.fori_loop(0, xn.shape[0] // V, separate, 0)


def lags(blades, harmonic, trig):
    count = harmonic.shape[0]
    rotor = jnp.full(harmonic.shape, blades[0]).astype(F32)
    stator = jnp.full(harmonic.shape, blades[1]).astype(F32)
    turns = harmonic[...] * stator
    lag = (turns - rotor * jnp.floor(turns / rotor)) / rotor * (2.0 * math.pi)
    trig[0:count, :] = jnp.cos(lag)
    trig[count : 2 * count, :] = jnp.sin(lag)
    trig[2 * count : 2 * count + 8, :] = (stator / rotor / count)[:8]


def own_terms(z, x, other, advect, viscous, p, timing, above, below, base):
    for v in range(V):
        j = z * V + v
        total = viscous[pl.ds(j * 2 + p, 1), :] * (other[j] - 2.0 * x[j]) - timing[v]
        rate = advect[pl.ds(j * 2 + p, 1), :]
        if above and below:
            total += rate * (x[j - V] - x[j + V])
        else:
            total += rate * (x[j - V] if above else -x[j + V])
        base[j] = total


def timing_matrix(table, trig):
    return split_left(table[...] * trig[trig.shape[0] - 8 : trig.shape[0] - 7, :1])


def prepare(flags, blades, xn, xf, harmonic, basis, turned, advect, viscous, table, trig, base, *chunks):
    lags(blades, harmonic, trig)
    p, wrap = flags[0], flags[1]
    cells = xf.shape[0] // V
    sign = jnp.where(flags[2] == 1, 1.0, -1.0)
    lag = split_left(lag_matrix(basis[...], turned[...], trig[...], sign))
    derive = timing_matrix(table, trig)

    def one(z, above=True, below=True, sends=True):
        raw = [xf[z * V + v] for v in range(V)]
        timing, *lagged = over_instants([derive, lag] if sends else [derive], raw)
        own_terms(z, xf, xn, advect, viscous, p, timing, above, below, base)
        if not sends:
            return
        for v in range(V):
            value = jnp.where(wrap == 1, lagged[0][v], raw[v])
            j = (z - LEAD) * V + v
            for out, ((first, last), extra) in zip(chunks, CHUNKS):
                width = last - first
                out[pl.ds(pl.multiple_of(j * width, 8), width), :] = value[first:last]
                if extra:
                    out[pl.ds((cells - LEAD) * V * width + j, 1), :] = value[NT - 1 : NT]

    def early(z, carry):
        one(z, sends=False)
        return carry

    def late(z, carry):
        one(z)
        return carry

    one(0, above=False, sends=False)
    lax.fori_loop(1, LEAD, early, 0)
    lax.fori_loop(LEAD, cells - 1, late, 0)
    one(cells - 1, below=False)


def near_base(flags, xn, xf, advect, viscous, table, trig, base):
    p = 1 - flags[0]
    cells = xn.shape[0] // V
    derive = timing_matrix(table, trig)

    def one(z, above=True, below=True):
        (timing,) = over_instants([derive], [xn[z * V + v] for v in range(V)])
        own_terms(z, xn, xf, advect, viscous, p, timing, above, below, base)

    def inner(z, carry):
        one(z)
        return carry

    one(0, above=False)
    lax.fori_loop(1, cells - 1, inner, 0)
    one(cells - 1, below=False)


def keep_tiles(ref, offset, values, first, last, height):
    for a in range(V):
        for t in range(first // 8, last // 8):
            ref[offset + a * height + t] = values[a][t * 8 - first : t * 8 - first + 8]


def sweeps(source, g, fg, offset, spans, p, inverse, lower, upper, cells):
    height = g.shape[1] // 8
    for first, last in spans:
        nothing = tuple(jnp.zeros((last - first, LANES), F32) for _ in range(V))

        def ahead(z, current, first=first, last=last):
            right = source(z, first, last)
            result = []
            for a in range(V):
                total = coefficient(inverse, z, a, 0, p) * right[0]
                for b in range(1, V):
                    total += coefficient(inverse, z, a, b, p) * right[b]
                for b in range(V):
                    total += coefficient(lower, z, a, b, p) * current[b]
                g[z * V + a, first:last, :] = total
                result.append(total)
            return tuple(result)

        out = lax.fori_loop(1, cells - 1, ahead, ahead(0, nothing))
        out = ahead(cells - 1, out)
        keep_tiles(fg, offset, out, first, last, height)

        def back(i, current, first=first, last=last):
            z = cells - 1 - i
            result = []
            for a in range(V):
                total = g[z * V + a, first:last, :]
                for b in range(V):
                    total += coefficient(upper, z, a, b, p) * current[b]
                g[z * V + a, first:last, :] = total
                result.append(total)
            return tuple(result)

        out = lax.fori_loop(0, cells, back, nothing)
        keep_tiles(fg, offset + V * height, out, first, last, height)


def take_edges(edges, from_left, from_right, p):
    skip = from_left.shape[0] - V * NT * 2
    for v in range(V):
        edges[v, PAD - 8 : PAD, :] = jnp.zeros((8, LANES), F32)
        edges[v, 0:NT, :] = from_left[pl.ds(skip + v * 2 * NT + p, NT, stride=2), :]
        edges[V + v, PAD - 8 : PAD, :] = jnp.zeros((8, LANES), F32)
        edges[V + v, 0:NT, :] = from_right[pl.ds(v * 2 * NT + p, NT, stride=2), :]


def edge_terms(z, cells, values, edges, advect, p, first, last):
    if not isinstance(z, int):
        return values
    return [
        value
        + (1.0 if z == 0 else -1.0)
        * advect[pl.ds((z * V + v) * 2 + p, 1), :]
        * edges[v if z == 0 else V + v, first:last, :]
        for v, value in enumerate(values)
    ]


def near_cell(
    flags, base, halo, from_left, from_right, advect, viscous, inverse, lower, upper, group,
    g, flows, edges,
):
    p = 1 - flags[0]
    cells = base.shape[0] // V
    take_edges(edges, from_left, from_right, p)

    def source(z, first, last):
        values = []
        for v in range(V):
            j = z * V + v
            values.append(base[j, first:last, :] + viscous[pl.ds(j * 2 + p, 1), :] * halo[j, first:last, :])
        return edge_terms(z, cells, values, edges, advect, p, first, last)

    sweeps(source, g, flows, 0, ((0, 32), (32, PAD)), p, inverse, lower, upper, cells)
    flows[2 * V * PAD // 8 :] = group[...]


def far_lead(flags, slab, trig, basis, turned, lead, halo):
    wrap = flags[1]
    sign = jnp.where(flags[2] == 1, -1.0, 1.0)
    left = split_left(lag_matrix(basis[...], turned[...], trig[...], sign))
    for z in range(LEAD):
        for v in range(V):
            halo[v, PAD - 8 : PAD, :] = jnp.zeros((8, LANES), F32)
            halo[v, 0:NT, :] = slab[pl.ds((z * V + v) * NT, NT), :]
        raw = [halo[v] for v in range(V)]
        (lagged,) = over_instants([left], raw)
        for v in range(V):
            lead[z * V + v] = jnp.where(wrap == 1, lagged[v], raw[v])


def far_chunk(chunk, flags, base, lead, halo, from_left, from_right, advect, viscous, inverse, lower, upper, g, fg, edges):
    (first, last), extra = chunk
    width = last - first
    p = flags[0]
    cells = base.shape[0] // V
    top = lax.broadcasted_iota(jnp.int32, (8, LANES), 0) == 0
    take_edges(edges, from_left, from_right, p)

    def pieces(ref, j):
        value = ref[j, first:last, :]
        return jnp.concatenate([value, ref[j, PAD - 8 : PAD, :]], axis=0) if extra else value

    def source(z, start, stop):
        result = []
        for v in range(V):
            j = z * V + v
            h = jnp.maximum(z - LEAD, 0) * V + v
            arrived = halo[pl.ds(pl.multiple_of(h * width, 8), width), :]
            if extra:
                row = halo[pl.ds((cells - LEAD) * V * width + h, 1), :]
                arrived = jnp.concatenate([arrived, jnp.where(top, row, 0.0)], axis=0)
            early = pieces(lead, jnp.minimum(z, LEAD - 1) * V + v)
            arrived = jnp.where(z >= LEAD, arrived, early)
            value = pieces(base, j) + viscous[pl.ds(j * 2 + p, 1), :] * arrived
            if isinstance(z, int):
                rate = advect[pl.ds(j * 2 + p, 1), :]
                edge = pieces(edges, v if z == 0 else V + v)
                value += rate * edge if z == 0 else -rate * edge
            result.append(value)
        return result

    height = rows_of(chunk)
    sweeps(source, g, fg, 0, ((0, height),), p, inverse, lower, upper, cells)


def times(matrix, vector):
    result = []
    for a in range(V):
        total = matrix(a, 0) * vector[0]
        for b in range(1, V):
            total += matrix(a, b) * vector[b]
        result.append(total)
    return result


def plus(one, two):
    return [a + b for a, b in zip(one, two)]


def tiles(ref, c, kind):
    return [ref[c, kind * V + a] for a in range(V)]


def rows(ref, c, kind):
    return lambda a, b: ref[c, kind * V + a, b : b + 1, :]


def unit(a):
    place = lax.broadcasted_iota(jnp.int32, (8, LANES), 0)
    return jnp.where(place == a, 1.0, 0.0).astype(F32)


def transfer(flags, lower, upper, blocks, group, forward):
    cells = blocks.shape[1] // V
    for c in range(2):
        p = 1 - flags[0] if c == 0 else flags[0]

        def ahead(z, current):
            result = times(lambda a, b: coefficient(lower, z, a, b, p), current)
            for a in range(V):
                forward[z * V + a] = result[a]
            return tuple(result)

        through = lax.fori_loop(0, cells, ahead, tuple(unit(a) for a in range(V)))

        def back(i, current):
            z = cells - 1 - i
            result = times(lambda a, b: coefficient(upper, z, a, b, p), current)
            for a in range(V):
                result[a] = result[a] + jnp.concatenate(
                    [forward[z * V + a], jnp.zeros((8, LANES), F32)], axis=0
                )
                blocks[c, z * V + a] = result[a]
            return tuple(result)

        start = tuple(
            jnp.concatenate([jnp.zeros((8, LANES), F32), unit(a)], axis=0) for a in range(V)
        )
        ends = lax.fori_loop(0, cells, back, start)
        for a in range(V):
            group[c * 3 * V + a] = ends[a][:8]
            group[(c * 3 + 1) * V + a] = ends[a][8:]
            group[(c * 3 + 2) * V + a] = through[a]


def merge_matrices(bit, levels, flags, mine, other, share, mats, merged, share_out, offset, new_offset):
    start, last = bit == 0, bit == levels - 1
    right = flags[3 + bit] == 1
    left = jnp.logical_not(right)
    nothing = jnp.zeros((8, LANES), F32)
    for c in range(2):
        kinds = 1 if last else 3
        at = lambda ref, kind: [ref[offset + (c * kinds + kind) * V + a] for a in range(V)]
        pick = lambda kind, own: [jnp.where(own, m, t) for m, t in zip(at(mine, kind), at(other, kind))]
        if start:
            own = [[unit(a) for a in range(V)], [nothing] * V, [unit(a) for a in range(V)]]
        else:
            own = [tiles(share, c, kind) for kind in range(3)]
        found = [
            (1, pick(0, right)),
            (3, [jnp.where(right, x, nothing) for x in own[0]]),
            (4, [jnp.where(right, x, nothing) for x in own[1]]),
            (5, [jnp.where(right, nothing, x) for x in own[2]]),
        ]
        if not last:
            found += [(0, pick(2, right)), (2, pick(1, left))]
        for kind, values in found:
            for a in range(V):
                mats[c, kind * V + a] = values[a]
        if last:
            continue
        p_left, g_left, h_right = pick(2, left), pick(0, left), pick(1, right)
        turned = times(rows(mats, c, 1), p_left)
        new = [plus(g_left, times(rows(mats, c, 2), turned))]
        if bit < levels - 2:
            new += [times(rows(mats, c, 2), h_right), times(rows(mats, c, 0), p_left)]
        for kind, values in enumerate(new):
            for a in range(V):
                merged[new_offset + (c * len(new) + kind) * V + a] = values[a]
        s0 = times(rows(mats, c, 3), p_left)
        s1 = times(rows(mats, c, 4), p_left)
        s1b = times(rows(mats, c, 5), turned)
        s2 = times(rows(mats, c, 5), h_right)
        for a in range(V):
            share_out[c, a] = jnp.where(right, s0[a], own[0][a])
            share_out[c, V + a] = jnp.where(right, s1[a], own[1][a] + s1b[a])
            share_out[c, 2 * V + a] = jnp.where(right, own[2][a], s2[a])


def inflow_of(c, mats, f_left, g_right, known):
    back = plus(g_right, times(rows(mats, c, 1), f_left))
    from_left = times(rows(mats, c, 3), f_left)
    from_right = plus(times(rows(mats, c, 4), f_left), times(rows(mats, c, 5), back))
    total = from_left + from_right
    return back, total if known is None else plus(known, total)


def merge_all(parts, bit, levels, flags, flows, other, *refs):
    share, known, mats, merged, share_out, inflow = (None, None, *refs) if bit == 0 else refs
    tall = sum(height for _, height in parts) * V
    new_offset = tall * (1 if bit == levels - 2 else 2)
    merge_matrices(bit, levels, flags, flows, other, share, mats, merged, share_out, 2 * tall, new_offset)
    merge_flows(parts, bit, levels, flags, mats, flows, other, *([] if known is None else [known]), merged, inflow)


def merge_flows(parts, bit, levels, flags, mats, flows, other, *refs):
    known, merged, inflow = (None, *refs) if bit == 0 else refs
    right, last_right = flags[3 + bit] == 1, flags[2 + levels] == 1
    last = bit == levels - 2
    start = 0
    for c, height in parts:

        def tile(t, carry, c=c, height=height, start=start):
            at = lambda i: start * 2 * V + i * height + t
            mine = [flows[at(i)] for i in range(2 * V)]
            theirs = [other[at(i)] for i in range(2 * V)]
            f_left = [jnp.where(right, y, x) for x, y in zip(mine[:V], theirs[:V])]
            f_right = [jnp.where(right, x, y) for x, y in zip(mine[:V], theirs[:V])]
            g_left = [jnp.where(right, y, x) for x, y in zip(mine[V:], theirs[V:])]
            g_right = [jnp.where(right, x, y) for x, y in zip(mine[V:], theirs[V:])]
            before = None if known is None else [known[at(i)] for i in range(2 * V)]
            back, total = inflow_of(c, mats, f_left, g_right, before)
            new_f = plus(f_right, times(rows(mats, c, 0), f_left))
            new_g = plus(g_left, times(rows(mats, c, 2), back))
            if last:
                for i in range(V):
                    end = jnp.where(last_right, new_g[i], new_f[i])
                    merged[start * V + i * height + t] = end
            else:
                for i, value in enumerate(new_f + new_g):
                    merged[at(i)] = value
            for i, value in enumerate(total):
                inflow[at(i)] = value
            return carry

        lax.fori_loop(0, height, tile, 0)
        start += height


def last_inflow(right, c, mats, ends, other, known, start, height, inflow):
    for t in range(height):
        mine = [ends[start * V + a * height + t] for a in range(V)]
        theirs = [other[start * V + a * height + t] for a in range(V)]
        f_left = [jnp.where(right, y, x) for x, y in zip(mine, theirs)]
        g_right = [jnp.where(right, x, y) for x, y in zip(mine, theirs)]
        before = [known[start * 2 * V + i * height + t] for i in range(2 * V)]
        _, total = inflow_of(c, mats, f_left, g_right, before)
        for i, value in enumerate(total):
            inflow[i, t * 8 : t * 8 + 8, :] = value


def corrected(c, z, a, first, last, g, blocks, inflow):
    total = g[z * V + a, first:last, :]
    for b in range(V):
        total += blocks[c, z * V + a, b : b + 1, :] * inflow[b]
        total += blocks[c, z * V + a, 8 + b : 9 + b, :] * inflow[V + b]
    return total


def correct(parts, levels, flags, mats, ends, other, known, blocks, *refs):
    solved, results, inflow = refs[: len(parts)], refs[len(parts) : -1], refs[-1]
    right = flags[2 + levels] == 1
    start = 0
    for (c, tall), g, result in zip(parts, solved, results):
        last_inflow(right, c, mats, ends, other, known, start, tall, inflow)
        start += tall
        height = tall * 8
        for first, last in ((0, 32), (32, height)) if height > 32 else ((0, height),):
            flow = tuple(inflow[i, first:last, :] for i in range(2 * V))

            def step(z, flow, c=c, first=first, last=last, g=g, result=result):
                for a in range(V):
                    result[z * V + a, first:last, :] = corrected(c, z, a, first, last, g, blocks, flow)
                return flow

            lax.fori_loop(0, g.shape[0] // V, step, flow)


def correct_all(parts, levels, flags, ends, other, share, known, blocks, *refs):
    count = len(parts)
    solved, results, mats, inflow = refs[:count], refs[count : 2 * count], refs[-2], refs[-1]
    tall = sum(height for _, height in parts) * V
    merge_matrices(levels - 1, levels, flags, ends, other, share, mats, None, None, tall, 0)
    correct(parts, levels, flags, mats, ends, other, known, blocks, *solved, *results, inflow)


def finish(levels, flags, mats, ends, other, known, g, blocks, near, *refs):
    done, (out, inflow, held, sems) = refs[:-4], refs[-4:]
    right = flags[2 + levels] == 1
    p = flags[0]
    (first_row, last_row), last_extra = CHUNKS[-1]
    width, height = last_row - first_row, rows_of(CHUNKS[-1])
    last_inflow(right, 1, mats, ends, other, known, 0, height // 8, inflow)
    flow = tuple(inflow[i] for i in range(2 * V))

    def step(z, carry):
        for a in range(V):
            j = z * V + a
            row = j * 2 * NT
            held[pl.ds(row + 1 - p, NT, stride=2), :] = near[j, 0:NT, :]
            for ref, ((first, last), extra) in zip(done, CHUNKS):
                held[pl.ds(row + p + 2 * first, last - first, stride=2), :] = ref[j, 0 : last - first, :]
                if extra:
                    held[pl.ds(row + p + 2 * (NT - 1), 1), :] = ref[j, last - first : last - first + 1, :]
            value = corrected(1, z, a, 0, height, g, blocks, flow)
            held[pl.ds(row + p + 2 * first_row, width, stride=2), :] = value[:width]
            if last_extra:
                held[pl.ds(row + p + 2 * (NT - 1), 1), :] = value[width : width + 1]
        return carry

    parts = sems.shape[0]
    cells = g.shape[0] // V // parts
    size = held.shape[0] // parts
    copies = []
    for i in range(parts):
        lax.fori_loop(i * cells, (i + 1) * cells, step, 0)
        span = pl.ds(i * size, size)
        copies.append(pltpu.make_async_copy(held.at[span, :], out.at[span, :], sems.at[i]))
        copies[-1].start()
    for copy in copies:
        copy.wait()


def phase_tables(count):
    angle = 2.0 * math.pi * np.outer(np.arange(1, count + 1), np.arange(NT)) / NT
    cosine, sine = np.cos(angle), np.sin(angle)
    basis = np.zeros((PAD, 2 * count + 8), np.float32)
    basis[:NT, :count], basis[:NT, count : 2 * count], basis[:NT, 2 * count] = cosine.T, sine.T, 0.5
    turned = np.zeros((2, count + 8, 3, DEPTH), np.float32)
    turned[0, :count, :, :NT], turned[1, :count, :, :NT] = cosine[:, None], sine[:, None]
    turned[0, count, :, :NT] = 1.0
    return (2.0 / NT * basis).astype(np.float32), turned.reshape(2 * (count + 8), 3 * DEPTH)


def derivative_table():
    gap = np.arange(NT)[:, None] - np.arange(NT)[None, :]
    safe = np.where(gap == 0, 1.0, np.sin(np.pi * gap / NT))
    table = np.where(gap == 0, 0.0, 0.5 * (1.0 - 2.0 * np.mod(gap, 2)) / safe)
    wide = np.zeros((PAD, 3, DEPTH), np.float32)
    wide[:NT, :, :NT] = table[:, None]
    return wide.reshape(PAD, 3 * DEPTH)


COSTS = (0, 0, 6_000_000_000, 0)


def local(state, advect, viscous, inverse, lower, upper, blades, harmonic):
    cells = state.shape[0]
    count = harmonic.shape[0]
    segs, slabs = lax.axis_size("seg"), lax.axis_size("pitch")
    levels = segs.bit_length() - 1
    far_pairs = [(i, (i - 1) % slabs if i % 2 == 0 else (i + 1) % slabs) for i in range(slabs)]
    near_pairs = [(i, i ^ 1) for i in range(slabs)]
    to_far = lambda x: lax.ppermute(x, "pitch", far_pairs)
    to_level = lambda x, k: lax.ppermute(x, "seg", [(i, i ^ (1 << k)) for i in range(segs)])
    x_shape = (cells * V, PAD, LANES)

    slab, seg = lax.axis_index("pitch"), lax.axis_index("seg")
    side = slab % 2
    wrap = jnp.logical_or(slab == 0, slab == slabs - 1)
    bits = [(seg >> k) & 1 for k in range(levels)]
    run = Chain(
        jnp.stack(
            [side, wrap.astype(jnp.int32), (slab == 0).astype(jnp.int32), *bits]
        ).astype(jnp.int32)
    )
    flat = lambda x: x.transpose(0, 2, 3, 1, 4).reshape(cells * V * V * 2, LANES)
    inv, low, upp = flat(inverse.astype(F32)), flat(lower), flat(upper)
    st = state.transpose(0, 2, 3, 1, 4).reshape(cells * V * NT * 2, LANES)
    lead_rows, edge_rows = LEAD * V * NT, padded_even(V * NT * 2)
    held = pl.BlockSpec(memory_space=pltpu.VMEM)
    shapes = [(lead_rows, LANES), (edge_rows, LANES), (edge_rows, LANES), x_shape, x_shape]
    slab_out, first_cell, last_cell, xn, xf = pl.pallas_call(
        split_cells,
        out_shape=[jax.ShapeDtypeStruct(x, F32) for x in shapes],
        in_specs=[held],
        out_specs=[held] * 5,
        compiler_params=pltpu.CompilerParams(vmem_limit_bytes=16 * MB),
        name="split_cells",
    )(run.before(st))
    halo_near = lax.ppermute(xn, "pitch", near_pairs)
    slab_in = to_far(slab_out)
    from_left = lax.ppermute(last_cell, "seg", [(i, i + 1) for i in range(segs - 1)])
    from_right = lax.ppermute(first_cell, "seg", [(i + 1, i) for i in range(segs - 1)])

    basis, turned = phase_tables(count)
    table = derivative_table()
    wide_harmonic = jnp.broadcast_to(harmonic.astype(F32)[:, None], (count, LANES))

    rest = (cells - LEAD) * V
    chunk_shapes = [
        (rest * (last - first) + (padded_even(rest) if extra else 0), LANES)
        for (first, last), extra in CHUNKS
    ]
    adv = advect.transpose(0, 2, 1, 3).reshape(cells * V * 2, LANES)
    vis = viscous.transpose(0, 2, 1, 3).reshape(cells * V * 2, LANES)
    trig, base, *chunks = run(
        prepare, [(2 * count + 8, LANES), x_shape, *chunk_shapes],
        [xn, xf, wide_harmonic, basis, turned, adv, vis, table], scalars=[blades], name="prepare",
    )
    arrived = [slab_in]
    for chunk in chunks:
        if len(arrived) >= 2:
            chunk, arrived[-2] = lax.optimization_barrier((chunk, arrived[-2]))
        arrived.append(to_far(chunk))
    slab_in, *arrived = arrived

    edges = pltpu.VMEM((2 * V, PAD, LANES), F32)

    mats = []
    mats_shape = (2, 6 * V, 8, LANES)

    def solve_chunk(i):
        height = rows_of(CHUNKS[i])
        return run(
            functools.partial(far_chunk, CHUNKS[i]),
            [(cells * V, height, LANES), (2 * V * height // 8, 8, LANES)],
            [base, lead, arrived[i], from_left, from_right, adv, vis, inv, low, upp],
            scratch=[edges], name="far_chunk",
        )

    class Exchange:
        def __init__(self, c, g, flows, leads=False):
            self.parts, self.leads = [(c, g.shape[1] // 8)], leads
            self.flows, self.known, self.solved, self.level = flows, [], g, 0
            self.scratch = [pltpu.VMEM((2 * V, g.shape[1], LANES), F32)]

        def step(self):
            tall, k = self.parts[0][1], self.level
            shape = ((2 if k < levels - 2 else 1) * V * tall, 8, LANES)
            inflow = (2 * V * tall, 8, LANES)
            other = to_level(self.flows, k)
            if self.leads:
                shape = (shape[0] + (6 * V if k < levels - 2 else 2 * V),) + shape[1:]
                out = run(
                    functools.partial(merge_all, self.parts, k, levels),
                    [mats_shape, shape, (2, 3 * V, 8, LANES), inflow],
                    [self.flows, other, *self.known], name="merge_all",
                )
                mats.append(out[0])
                self.flows, self.known = out[1], out[2:]
            else:
                out = run(
                    functools.partial(merge_flows, self.parts, k, levels), [shape, inflow],
                    [mats[k], self.flows, other, *self.known], name="merge_flows",
                )
                self.flows, self.known = out[0], out[1:]
            self.level = k + 1

        def last(self):
            return [self.flows, to_level(self.flows, levels - 1), *self.known]

        def correct(self):
            if self.leads:
                result, last = run(
                    functools.partial(correct_all, self.parts, levels), [self.solved.shape, mats_shape],
                    [*self.last(), blocks, self.solved], scratch=self.scratch, name="correct_all",
                )
                mats.append(last)
                return result
            return run(
                functools.partial(correct, self.parts, levels), [self.solved.shape],
                [mats[-1], *self.last(), blocks, self.solved], scratch=self.scratch, name="correct",
            )[0]

    base_near = run(
        near_base, [x_shape], [xn, xf, adv, vis, table, trig], name="near_base", flops=COSTS[0]
    )[0]
    blocks, group = run(
        transfer, [(2, cells * V, 16, LANES), (6 * V, 8, LANES)], [low, upp],
        scratch=[pltpu.VMEM((cells * V, 8, LANES), F32)], name="transfer", flops=COSTS[1],
    )
    lead = run(
        far_lead, [(LEAD * V, PAD, LANES)], [slab_in, trig, basis, turned],
        scratch=[pltpu.VMEM((V, PAD, LANES), F32)], name="far_lead", flops=COSTS[3],
    )[0]
    first = Exchange(
        0,
        *run(
            near_cell, [x_shape, (2 * V * PAD // 8 + 6 * V, 8, LANES)],
            [base_near, halo_near, from_left, from_right, adv, vis, inv, low, upp, group],
            scratch=[edges], name="near_cell", flops=COSTS[2],
        ),
        leads=True,
    )
    first.step()
    second = Exchange(1, *solve_chunk(0))
    second.step()
    for k in range(1, levels - 1):
        first.step()
    third = Exchange(1, *solve_chunk(1))
    for k in range(1, levels - 1):
        second.step()
    third.step()
    near = first.correct()
    for k in range(1, levels - 1):
        third.step()
    done = [second.correct()]
    g_last = third.solved
    small = [mats[-1], *third.last()]

    out = run(
        functools.partial(finish, levels), [st.shape], [*small, g_last, blocks, near, *done],
        out_specs=[pl.BlockSpec(memory_space=pltpu.HBM)],
        scratch=[
            pltpu.VMEM((2 * V, rows_of(CHUNKS[-1]), LANES), F32),
            pltpu.VMEM(st.shape, F32),
            pltpu.SemaphoreType.DMA((4,)),
        ],
        name="finish",
    )[0]
    return out.reshape(cells, V, NT, 2, LANES).transpose(0, 3, 1, 2, 4)


def solution(mesh):
    cell = P("seg", "pitch", None, None, None)
    return jax.shard_map(
        local,
        mesh=mesh,
        in_specs=(cell, P("seg", "pitch", None, None), P("seg", "pitch", None, None), cell, cell, cell, P(), P()),
        out_specs=cell,
        check_vma=False,
    )
```

```python
import functools
import math

import jax
import jax.numpy as jnp
import numpy as np
from jax import lax
from jax.experimental import pallas as pl
from jax.experimental.pallas import tpu as pltpu
from jax.sharding import PartitionSpec as P

F32 = jnp.float32
BF16 = jnp.bfloat16
V = 5
NT = 49
PAD = 56
DEPTH = 64
LANES = 128
LEAD = 4
MB = 1 << 20

CHUNKS = (((0, 32), True), ((32, 48), False))


def rows_of(chunk):
    (first, last), extra = chunk
    return last - first + (8 if extra else 0)


def padded_even(count):
    return (count + 7) // 8 * 8


class Chain:
    def __init__(self, flags):
        self.flags = flags

    def before(self, array):
        return lax.optimization_barrier((self.flags, array))[1]

    def after(self, array):
        self.flags, array = lax.optimization_barrier((self.flags, array))
        return array

    def __call__(self, body, out_shapes, arrays, scratch=(), vmem=16, name=None, grid=None, in_specs=None, out_specs=None, scalars=(), flops=1000):
        smem = pl.BlockSpec(memory_space=pltpu.SMEM)
        held = pl.BlockSpec(memory_space=pltpu.VMEM)
        extra = {} if grid is None else {"grid": grid}
        out = pl.pallas_call(
            body,
            out_shape=[jax.ShapeDtypeStruct(s, F32) for s in out_shapes],
            in_specs=[smem] * (1 + len(scalars)) + (in_specs or [held] * len(arrays)),
            out_specs=out_specs or [held] * len(out_shapes),
            scratch_shapes=list(scratch),
            compiler_params=pltpu.CompilerParams(vmem_limit_bytes=vmem * MB),
            cost_estimate=pl.CostEstimate(flops=flops, bytes_accessed=1000, transcendentals=0),
            name=name,
            **extra,
        )(self.flags, *scalars, *arrays)
        out = list(out)
        out[0] = self.after(out[0])
        return out


def coefficient(ref, z, a, b, p):
    return ref[pl.ds(((z * V + a) * V + b) * 2 + p, 1), :]


def split_left(matrix):
    high = matrix.astype(BF16).astype(F32)
    place = lax.broadcasted_iota(jnp.int32, matrix.shape, 1)
    return jnp.where(place < 2 * DEPTH, high, matrix - high).astype(BF16)


def lag_matrix(basis, turned, trig, sign):
    half = turned.shape[0] // 2
    count = (half - 4) // 8 * 8
    cosine, sine = turned[:half], turned[half:]
    turn, cross = trig[:count, :1], trig[count : 2 * count, :1] * sign
    right = jnp.concatenate(
        [
            turn * cosine[:count] + cross * sine[:count],
            turn * sine[:count] - cross * cosine[:count],
            cosine[count:],
        ],
        axis=0,
    )
    return jnp.dot(basis, right, preferred_element_type=F32, precision=lax.Precision.HIGHEST)


def over_instants(lefts, cells):
    whole = jnp.concatenate(cells, axis=1)
    if whole.shape[0] < DEPTH:
        whole = jnp.concatenate(
            [whole, jnp.zeros((DEPTH - whole.shape[0], whole.shape[1]), F32)], axis=0
        )
    high = whole.astype(BF16)
    low = (whole - high.astype(F32)).astype(BF16)
    right = jnp.concatenate([high, low, high], axis=0)
    products = [jnp.dot(left, right, preferred_element_type=F32) for left in lefts]
    return [[x[:, i * LANES : (i + 1) * LANES] for i in range(len(cells))] for x in products]


def split_cells(st, slab, first_cell, last_cell, xn, xf):
    p = lax.axis_index("pitch") % 2
    edge = first_cell.shape[0]
    zeros = jnp.zeros((8, LANES), F32)
    width = 4 * NT

    def step(i, carry):
        slab[pl.ds(i * width, width), :] = st[pl.ds(i * 2 * width + p, width, stride=2), :]
        return carry

    lax.fori_loop(0, LEAD * V // 4, step, 0)
    first_cell[...] = st[0:edge, :]
    last_cell[...] = st[st.shape[0] - edge :, :]

    def separate(z, carry):
        for v in range(V):
            j = z * V + v
            for out, q in ((xn, 1 - p), (xf, p)):
                out[j, PAD - 8 : PAD, :] = zeros
                out[j, 0:NT, :] = st[pl.ds(j * 2 * NT + q, NT, stride=2), :]
        return carry

    lax.fori_loop(0, xn.shape[0] // V, separate, 0)


def lags(blades, harmonic, trig):
    count = harmonic.shape[0]
    rotor = jnp.full(harmonic.shape, blades[0]).astype(F32)
    stator = jnp.full(harmonic.shape, blades[1]).astype(F32)
    turns = harmonic[...] * stator
    lag = (turns - rotor * jnp.floor(turns / rotor)) / rotor * (2.0 * math.pi)
    trig[0:count, :] = jnp.cos(lag)
    trig[count : 2 * count, :] = jnp.sin(lag)
    trig[2 * count : 2 * count + 8, :] = (stator / rotor / count)[:8]


def own_terms(z, x, other, advect, viscous, p, timing, above, below, base):
    for v in range(V):
        j = z * V + v
        total = viscous[pl.ds(j * 2 + p, 1), :] * (other[j] - 2.0 * x[j]) - timing[v]
        rate = advect[pl.ds(j * 2 + p, 1), :]
        if above and below:
            total += rate * (x[j - V] - x[j + V])
        else:
            total += rate * (x[j - V] if above else -x[j + V])
        base[j] = total


def timing_matrix(table, trig):
    return split_left(table[...] * trig[trig.shape[0] - 8 : trig.shape[0] - 7, :1])


def prepare(flags, blades, xn, xf, harmonic, basis, turned, advect, viscous, table, trig, base, *chunks):
    lags(blades, harmonic, trig)
    p, wrap = flags[0], flags[1]
    cells = xf.shape[0] // V
    sign = jnp.where(flags[2] == 1, 1.0, -1.0)
    lag = split_left(lag_matrix(basis[...], turned[...], trig[...], sign))
    derive = timing_matrix(table, trig)

    def one(z, above=True, below=True, sends=True):
        raw = [xf[z * V + v] for v in range(V)]
        timing, *lagged = over_instants([derive, lag] if sends else [derive], raw)
        own_terms(z, xf, xn, advect, viscous, p, timing, above, below, base)
        if not sends:
            return
        for v in range(V):
            value = jnp.where(wrap == 1, lagged[0][v], raw[v])
            j = (z - LEAD) * V + v
            for out, ((first, last), extra) in zip(chunks, CHUNKS):
                width = last - first
                out[pl.ds(pl.multiple_of(j * width, 8), width), :] = value[first:last]
                if extra:
                    out[pl.ds((cells - LEAD) * V * width + j, 1), :] = value[NT - 1 : NT]

    def early(z, carry):
        one(z, sends=False)
        return carry

    def late(z, carry):
        one(z)
        return carry

    one(0, above=False, sends=False)
    lax.fori_loop(1, LEAD, early, 0)
    lax.fori_loop(LEAD, cells - 1, late, 0)
    one(cells - 1, below=False)


def near_base(flags, xn, xf, advect, viscous, table, trig, base):
    p = 1 - flags[0]
    cells = xn.shape[0] // V
    derive = timing_matrix(table, trig)

    def one(z, above=True, below=True):
        (timing,) = over_instants([derive], [xn[z * V + v] for v in range(V)])
        own_terms(z, xn, xf, advect, viscous, p, timing, above, below, base)

    def inner(z, carry):
        one(z)
        return carry

    one(0, above=False)
    lax.fori_loop(1, cells - 1, inner, 0)
    one(cells - 1, below=False)


def split_height(rows_high, extra):
    return rows_high // 8 - (1 if extra else 0)


def packed_rows(count, height, extra):
    return count * height * 8 + (padded_even(count) if extra else 0)


def vector_rows(count, i, t, height):
    if isinstance(t, int) and t == height:
        return pl.ds(count * height * 8 + i, 1)
    return pl.ds(pl.multiple_of((i * height + t) * 8, 8), 8)


def over_tiles(height, extra, tile):
    lax.fori_loop(0, height, lambda t, carry: (tile(t), carry)[1], 0)
    if extra:
        tile(height)


def keep_tiles(ref, kind, values, first, last, height, extra):
    for a in range(V):
        for t in range(first // 8, last // 8):
            place = vector_rows(2 * V, kind + a, t, height)
            ref[place, :] = values[a][t * 8 - first : t * 8 - first + (1 if t == height else 8)]


def sweeps(source, g, fg, extra, spans, p, inverse, lower, upper, cells):
    height = split_height(g.shape[1], extra)
    for first, last in spans:
        nothing = tuple(jnp.zeros((last - first, LANES), F32) for _ in range(V))

        def ahead(z, current, first=first, last=last):
            right = source(z, first, last)
            result = []
            for a in range(V):
                total = coefficient(inverse, z, a, 0, p) * right[0]
                for b in range(1, V):
                    total += coefficient(inverse, z, a, b, p) * right[b]
                for b in range(V):
                    total += coefficient(lower, z, a, b, p) * current[b]
                g[z * V + a, first:last, :] = total
                result.append(total)
            return tuple(result)

        out = lax.fori_loop(1, cells - 1, ahead, ahead(0, nothing))
        out = ahead(cells - 1, out)
        keep_tiles(fg, 0, out, first, last, height, extra)

        def back(i, current, first=first, last=last):
            z = cells - 1 - i
            result = []
            for a in range(V):
                total = g[z * V + a, first:last, :]
                for b in range(V):
                    total += coefficient(upper, z, a, b, p) * current[b]
                g[z * V + a, first:last, :] = total
                result.append(total)
            return tuple(result)

        out = lax.fori_loop(0, cells, back, nothing)
        keep_tiles(fg, V, out, first, last, height, extra)


def take_edges(edges, from_left, from_right, p):
    skip = from_left.shape[0] - V * NT * 2
    for v in range(V):
        edges[v, PAD - 8 : PAD, :] = jnp.zeros((8, LANES), F32)
        edges[v, 0:NT, :] = from_left[pl.ds(skip + v * 2 * NT + p, NT, stride=2), :]
        edges[V + v, PAD - 8 : PAD, :] = jnp.zeros((8, LANES), F32)
        edges[V + v, 0:NT, :] = from_right[pl.ds(v * 2 * NT + p, NT, stride=2), :]


def edge_terms(z, cells, values, edges, advect, p, first, last):
    if not isinstance(z, int):
        return values
    return [
        value
        + (1.0 if z == 0 else -1.0)
        * advect[pl.ds((z * V + v) * 2 + p, 1), :]
        * edges[v if z == 0 else V + v, first:last, :]
        for v, value in enumerate(values)
    ]


def near_cell(
    flags, base, halo, from_left, from_right, advect, viscous, inverse, lower, upper, group,
    g, flows, edges,
):
    p = 1 - flags[0]
    cells = base.shape[0] // V
    take_edges(edges, from_left, from_right, p)

    def source(z, first, last):
        values = []
        for v in range(V):
            j = z * V + v
            values.append(base[j, first:last, :] + viscous[pl.ds(j * 2 + p, 1), :] * halo[j, first:last, :])
        return edge_terms(z, cells, values, edges, advect, p, first, last)

    sweeps(source, g, flows, True, ((0, 32), (32, PAD)), p, inverse, lower, upper, cells)
    flows[flows.shape[0] - group.shape[0] :, :] = group[...]


def far_lead(flags, slab, trig, basis, turned, lead, halo):
    wrap = flags[1]
    sign = jnp.where(flags[2] == 1, -1.0, 1.0)
    left = split_left(lag_matrix(basis[...], turned[...], trig[...], sign))
    for z in range(LEAD):
        for v in range(V):
            halo[v, PAD - 8 : PAD, :] = jnp.zeros((8, LANES), F32)
            halo[v, 0:NT, :] = slab[pl.ds((z * V + v) * NT, NT), :]
        raw = [halo[v] for v in range(V)]
        (lagged,) = over_instants([left], raw)
        for v in range(V):
            lead[z * V + v] = jnp.where(wrap == 1, lagged[v], raw[v])


def far_chunk(chunk, flags, base, lead, halo, from_left, from_right, advect, viscous, inverse, lower, upper, g, fg, edges):
    (first, last), extra = chunk
    width = last - first
    p = flags[0]
    cells = base.shape[0] // V
    top = lax.broadcasted_iota(jnp.int32, (8, LANES), 0) == 0
    take_edges(edges, from_left, from_right, p)

    def pieces(ref, j):
        value = ref[j, first:last, :]
        return jnp.concatenate([value, ref[j, PAD - 8 : PAD, :]], axis=0) if extra else value

    def source(z, start, stop):
        result = []
        for v in range(V):
            j = z * V + v
            h = jnp.maximum(z - LEAD, 0) * V + v
            arrived = halo[pl.ds(pl.multiple_of(h * width, 8), width), :]
            if extra:
                row = halo[pl.ds((cells - LEAD) * V * width + h, 1), :]
                arrived = jnp.concatenate([arrived, jnp.where(top, row, 0.0)], axis=0)
            early = pieces(lead, jnp.minimum(z, LEAD - 1) * V + v)
            arrived = jnp.where(z >= LEAD, arrived, early)
            value = pieces(base, j) + viscous[pl.ds(j * 2 + p, 1), :] * arrived
            if isinstance(z, int):
                rate = advect[pl.ds(j * 2 + p, 1), :]
                edge = pieces(edges, v if z == 0 else V + v)
                value += rate * edge if z == 0 else -rate * edge
            result.append(value)
        return result

    height = rows_of(chunk)
    sweeps(source, g, fg, extra, ((0, height),), p, inverse, lower, upper, cells)


def times(matrix, vector):
    result = []
    for a in range(V):
        total = matrix(a, 0) * vector[0]
        for b in range(1, V):
            total += matrix(a, b) * vector[b]
        result.append(total)
    return result


def plus(one, two):
    return [a + b for a, b in zip(one, two)]


def tiles(ref, c, kind):
    return [ref[c, kind * V + a, 0:V, :] for a in range(V)]


def rows(ref, c, kind):
    return lambda a, b: ref[c, kind * V + a, b : b + 1, :]


def unit(a):
    place = lax.broadcasted_iota(jnp.int32, (8, LANES), 0)
    return jnp.where(place == a, 1.0, 0.0).astype(F32)


def transfer(flags, lower, upper, blocks, group, forward):
    cells = blocks.shape[1] // V
    for c in range(2):
        p = 1 - flags[0] if c == 0 else flags[0]

        def ahead(z, current):
            result = times(lambda a, b: coefficient(lower, z, a, b, p), current)
            for a in range(V):
                forward[z * V + a] = result[a]
            return tuple(result)

        through = lax.fori_loop(0, cells, ahead, tuple(unit(a) for a in range(V)))

        def back(i, current):
            z = cells - 1 - i
            result = times(lambda a, b: coefficient(upper, z, a, b, p), current)
            for a in range(V):
                result[a] = result[a] + jnp.concatenate(
                    [forward[z * V + a], jnp.zeros((8, LANES), F32)], axis=0
                )
                blocks[c, z * V + a] = result[a]
            return tuple(result)

        start = tuple(
            jnp.concatenate([jnp.zeros((8, LANES), F32), unit(a)], axis=0) for a in range(V)
        )
        ends = lax.fori_loop(0, cells, back, start)
        for a in range(V):
            for kind, value in enumerate((ends[a][:V], ends[a][8 : 8 + V], through[a][:V])):
                group[pl.ds(((c * 3 + kind) * V + a) * V, V), :] = value
    group[6 * V * V :, :] = jnp.zeros((group.shape[0] - 6 * V * V, LANES), F32)


def merge_matrices(bit, levels, flags, mine, other, share, mats, merged, share_out, offset, new_offset):
    start, last = bit == 0, bit == levels - 1
    right = flags[3 + bit] == 1
    left = jnp.logical_not(right)
    nothing = jnp.zeros((V, LANES), F32)
    one = [unit(a)[:V] for a in range(V)]
    for c in range(2):
        kinds = 1 if last else 3
        at = lambda ref, kind: [ref[pl.ds(offset + ((c * kinds + kind) * V + a) * V, V), :] for a in range(V)]
        pick = lambda kind, own: [jnp.where(own, m, t) for m, t in zip(at(mine, kind), at(other, kind))]
        if start:
            own = [one, [nothing] * V, one]
        else:
            own = [tiles(share, c, kind) for kind in range(3)]
        found = [
            (1, pick(0, right)),
            (3, [jnp.where(right, x, nothing) for x in own[0]]),
            (4, [jnp.where(right, x, nothing) for x in own[1]]),
            (5, [jnp.where(right, nothing, x) for x in own[2]]),
        ]
        if not last:
            found += [(0, pick(2, right)), (2, pick(1, left))]
        for kind, values in found:
            for a in range(V):
                mats[c, kind * V + a, 0:V, :] = values[a]
        if last:
            continue
        p_left, g_left, h_right = pick(2, left), pick(0, left), pick(1, right)
        turned = times(rows(mats, c, 1), p_left)
        new = [plus(g_left, times(rows(mats, c, 2), turned))]
        if bit < levels - 2:
            new += [times(rows(mats, c, 2), h_right), times(rows(mats, c, 0), p_left)]
        for kind, values in enumerate(new):
            for a in range(V):
                merged[pl.ds(new_offset + ((c * len(new) + kind) * V + a) * V, V), :] = values[a]
        s0 = times(rows(mats, c, 3), p_left)
        s1 = times(rows(mats, c, 4), p_left)
        s1b = times(rows(mats, c, 5), turned)
        s2 = times(rows(mats, c, 5), h_right)
        for a in range(V):
            share_out[c, a, 0:V, :] = jnp.where(right, s0[a], own[0][a])
            share_out[c, V + a, 0:V, :] = jnp.where(right, s1[a], own[1][a] + s1b[a])
            share_out[c, 2 * V + a, 0:V, :] = jnp.where(right, own[2][a], s2[a])


def inflow_of(c, mats, f_left, g_right, known):
    back = plus(g_right, times(rows(mats, c, 1), f_left))
    from_left = times(rows(mats, c, 3), f_left)
    from_right = plus(times(rows(mats, c, 4), f_left), times(rows(mats, c, 5), back))
    total = from_left + from_right
    return back, total if known is None else plus(known, total)


def merge_all(part, bit, levels, flags, flows, other, *refs):
    share, known, mats, merged, share_out, inflow = (None, None, *refs) if bit == 0 else refs
    _, height, extra = part
    offset = packed_rows(2 * V, height, extra)
    new_offset = packed_rows(V, height, extra) if bit == levels - 2 else offset
    merge_matrices(bit, levels, flags, flows, other, share, mats, merged, share_out, offset, new_offset)
    merge_flows(part, bit, levels, flags, mats, flows, other, *([] if known is None else [known]), merged, inflow)


def merge_flows(part, bit, levels, flags, mats, flows, other, *refs):
    known, merged, inflow = (None, *refs) if bit == 0 else refs
    right, last_right = flags[3 + bit] == 1, flags[2 + levels] == 1
    last = bit == levels - 2
    c, height, extra = part

    def tile(t):
        at = lambda i: vector_rows(2 * V, i, t, height)
        mine = [flows[at(i), :] for i in range(2 * V)]
        theirs = [other[at(i), :] for i in range(2 * V)]
        f_left = [jnp.where(right, y, x) for x, y in zip(mine[:V], theirs[:V])]
        f_right = [jnp.where(right, x, y) for x, y in zip(mine[:V], theirs[:V])]
        g_left = [jnp.where(right, y, x) for x, y in zip(mine[V:], theirs[V:])]
        g_right = [jnp.where(right, x, y) for x, y in zip(mine[V:], theirs[V:])]
        before = None if known is None else [known[at(i), :] for i in range(2 * V)]
        back, total = inflow_of(c, mats, f_left, g_right, before)
        new_f = plus(f_right, times(rows(mats, c, 0), f_left))
        new_g = plus(g_left, times(rows(mats, c, 2), back))
        if last:
            for i in range(V):
                end = jnp.where(last_right, new_g[i], new_f[i])
                merged[vector_rows(V, i, t, height), :] = end
        else:
            for i, value in enumerate(new_f + new_g):
                merged[at(i), :] = value
        for i, value in enumerate(total):
            inflow[at(i), :] = value

    over_tiles(height, extra, tile)


def last_inflow(right, part, mats, ends, other, known, inflow):
    c, height, extra = part
    for t in range(height + (1 if extra else 0)):
        place = lambda i: vector_rows(V, i, t, height)
        mine = [ends[place(a), :] for a in range(V)]
        theirs = [other[place(a), :] for a in range(V)]
        f_left = [jnp.where(right, y, x) for x, y in zip(mine, theirs)]
        g_right = [jnp.where(right, x, y) for x, y in zip(mine, theirs)]
        before = [known[vector_rows(2 * V, i, t, height), :] for i in range(2 * V)]
        _, total = inflow_of(c, mats, f_left, g_right, before)
        for i, value in enumerate(total):
            inflow[i, t * 8 : t * 8 + 8, :] = jnp.broadcast_to(value, (8, LANES))


def corrected(c, z, a, first, last, g, blocks, inflow):
    total = g[z * V + a, first:last, :]
    for b in range(V):
        total += blocks[c, z * V + a, b : b + 1, :] * inflow[b]
        total += blocks[c, z * V + a, 8 + b : 9 + b, :] * inflow[V + b]
    return total


def correct(part, levels, flags, mats, ends, other, known, blocks, g, result, inflow):
    c = part[0]
    last_inflow(flags[2 + levels] == 1, part, mats, ends, other, known, inflow)
    height = g.shape[1]
    for first, last in ((0, 32), (32, height)) if height > 32 else ((0, height),):
        flow = tuple(inflow[i, first:last, :] for i in range(2 * V))

        def step(z, flow, first=first, last=last):
            for a in range(V):
                result[z * V + a, first:last, :] = corrected(c, z, a, first, last, g, blocks, flow)
            return flow

        lax.fori_loop(0, g.shape[0] // V, step, flow)


def correct_all(part, levels, flags, ends, other, share, known, blocks, g, result, mats, inflow):
    offset = packed_rows(V, *part[1:])
    merge_matrices(levels - 1, levels, flags, ends, other, share, mats, None, None, offset, 0)
    correct(part, levels, flags, mats, ends, other, known, blocks, g, result, inflow)


def finish(levels, flags, mats, ends, other, known, g, blocks, near, *refs):
    done, (out, inflow, held, sems) = refs[:-4], refs[-4:]
    right = flags[2 + levels] == 1
    p = flags[0]
    (first_row, last_row), last_extra = CHUNKS[-1]
    width, height = last_row - first_row, rows_of(CHUNKS[-1])
    part = (1, split_height(height, last_extra), last_extra)
    last_inflow(right, part, mats, ends, other, known, inflow)
    flow = tuple(inflow[i] for i in range(2 * V))

    def step(z, carry):
        for a in range(V):
            j = z * V + a
            row = j * 2 * NT
            held[pl.ds(row + 1 - p, NT, stride=2), :] = near[j, 0:NT, :]
            for ref, ((first, last), extra) in zip(done, CHUNKS):
                held[pl.ds(row + p + 2 * first, last - first, stride=2), :] = ref[j, 0 : last - first, :]
                if extra:
                    held[pl.ds(row + p + 2 * (NT - 1), 1), :] = ref[j, last - first : last - first + 1, :]
            value = corrected(1, z, a, 0, height, g, blocks, flow)
            held[pl.ds(row + p + 2 * first_row, width, stride=2), :] = value[:width]
            if last_extra:
                held[pl.ds(row + p + 2 * (NT - 1), 1), :] = value[width : width + 1]
        return carry

    parts = sems.shape[0]
    cells = g.shape[0] // V // parts
    size = held.shape[0] // parts
    copies = []
    for i in range(parts):
        lax.fori_loop(i * cells, (i + 1) * cells, step, 0)
        span = pl.ds(i * size, size)
        copies.append(pltpu.make_async_copy(held.at[span, :], out.at[span, :], sems.at[i]))
        copies[-1].start()
    for copy in copies:
        copy.wait()


def phase_tables(count):
    angle = 2.0 * math.pi * np.outer(np.arange(1, count + 1), np.arange(NT)) / NT
    cosine, sine = np.cos(angle), np.sin(angle)
    basis = np.zeros((PAD, 2 * count + 8), np.float32)
    basis[:NT, :count], basis[:NT, count : 2 * count], basis[:NT, 2 * count] = cosine.T, sine.T, 0.5
    turned = np.zeros((2, count + 8, 3, DEPTH), np.float32)
    turned[0, :count, :, :NT], turned[1, :count, :, :NT] = cosine[:, None], sine[:, None]
    turned[0, count, :, :NT] = 1.0
    return (2.0 / NT * basis).astype(np.float32), turned.reshape(2 * (count + 8), 3 * DEPTH)


def derivative_table():
    gap = np.arange(NT)[:, None] - np.arange(NT)[None, :]
    safe = np.where(gap == 0, 1.0, np.sin(np.pi * gap / NT))
    table = np.where(gap == 0, 0.0, 0.5 * (1.0 - 2.0 * np.mod(gap, 2)) / safe)
    wide = np.zeros((PAD, 3, DEPTH), np.float32)
    wide[:NT, :, :NT] = table[:, None]
    return wide.reshape(PAD, 3 * DEPTH)


COSTS = (0, 0, 6_000_000_000, 0)


def local(state, advect, viscous, inverse, lower, upper, blades, harmonic):
    cells = state.shape[0]
    count = harmonic.shape[0]
    segs, slabs = lax.axis_size("seg"), lax.axis_size("pitch")
    levels = segs.bit_length() - 1
    far_pairs = [(i, (i - 1) % slabs if i % 2 == 0 else (i + 1) % slabs) for i in range(slabs)]
    near_pairs = [(i, i ^ 1) for i in range(slabs)]
    to_far = lambda x: lax.ppermute(x, "pitch", far_pairs)
    to_level = lambda x, k: lax.ppermute(x, "seg", [(i, i ^ (1 << k)) for i in range(segs)])
    x_shape = (cells * V, PAD, LANES)

    slab, seg = lax.axis_index("pitch"), lax.axis_index("seg")
    side = slab % 2
    wrap = jnp.logical_or(slab == 0, slab == slabs - 1)
    bits = [(seg >> k) & 1 for k in range(levels)]
    run = Chain(
        jnp.stack(
            [side, wrap.astype(jnp.int32), (slab == 0).astype(jnp.int32), *bits]
        ).astype(jnp.int32)
    )
    flat = lambda x: x.transpose(0, 2, 3, 1, 4).reshape(cells * V * V * 2, LANES)
    inv, low, upp = flat(inverse.astype(F32)), flat(lower), flat(upper)
    st = state.transpose(0, 2, 3, 1, 4).reshape(cells * V * NT * 2, LANES)
    lead_rows, edge_rows = LEAD * V * NT, padded_even(V * NT * 2)
    held = pl.BlockSpec(memory_space=pltpu.VMEM)
    shapes = [(lead_rows, LANES), (edge_rows, LANES), (edge_rows, LANES), x_shape, x_shape]
    slab_out, first_cell, last_cell, xn, xf = pl.pallas_call(
        split_cells,
        out_shape=[jax.ShapeDtypeStruct(x, F32) for x in shapes],
        in_specs=[held],
        out_specs=[held] * 5,
        compiler_params=pltpu.CompilerParams(vmem_limit_bytes=16 * MB),
        name="split_cells",
    )(run.before(st))
    halo_near = lax.ppermute(xn, "pitch", near_pairs)
    slab_in = to_far(slab_out)
    from_left = lax.ppermute(last_cell, "seg", [(i, i + 1) for i in range(segs - 1)])
    from_right = lax.ppermute(first_cell, "seg", [(i + 1, i) for i in range(segs - 1)])

    basis, turned = phase_tables(count)
    table = derivative_table()
    wide_harmonic = jnp.broadcast_to(harmonic.astype(F32)[:, None], (count, LANES))

    rest = (cells - LEAD) * V
    chunk_shapes = [
        (rest * (last - first) + (padded_even(rest) if extra else 0), LANES)
        for (first, last), extra in CHUNKS
    ]
    adv = advect.transpose(0, 2, 1, 3).reshape(cells * V * 2, LANES)
    vis = viscous.transpose(0, 2, 1, 3).reshape(cells * V * 2, LANES)
    trig, base, *chunks = run(
        prepare, [(2 * count + 8, LANES), x_shape, *chunk_shapes],
        [xn, xf, wide_harmonic, basis, turned, adv, vis, table], scalars=[blades], name="prepare",
    )
    arrived = [slab_in]
    for chunk in chunks:
        if len(arrived) >= 2:
            chunk, arrived[-2] = lax.optimization_barrier((chunk, arrived[-2]))
        arrived.append(to_far(chunk))
    slab_in, *arrived = arrived

    edges = pltpu.VMEM((2 * V, PAD, LANES), F32)

    mats = []
    mats_shape = (2, 6 * V, 8, LANES)

    def solve_chunk(i):
        height, extra = rows_of(CHUNKS[i]), CHUNKS[i][1]
        tall = packed_rows(2 * V, split_height(height, extra), extra)
        return run(
            functools.partial(far_chunk, CHUNKS[i]),
            [(cells * V, height, LANES), (tall, LANES)],
            [base, lead, arrived[i], from_left, from_right, adv, vis, inv, low, upp],
            scratch=[edges], name="far_chunk",
        )

    class Exchange:
        def __init__(self, c, extra, g, flows, leads=False):
            self.part, self.leads = (c, split_height(g.shape[1], extra), extra), leads
            self.flows, self.known, self.solved, self.level = flows, [], g, 0
            self.scratch = [pltpu.VMEM((2 * V, g.shape[1], LANES), F32)]

        def step(self):
            k = self.level
            behind = k == levels - 2
            inflow = (packed_rows(2 * V, *self.part[1:]), LANES)
            tall = packed_rows(V if behind else 2 * V, *self.part[1:])
            other = to_level(self.flows, k)
            if self.leads:
                tall += padded_even((2 if behind else 6) * V * V)
                out = run(
                    functools.partial(merge_all, self.part, k, levels),
                    [mats_shape, (tall, LANES), (2, 3 * V, 8, LANES), inflow],
                    [self.flows, other, *self.known], name="merge_all",
                )
                mats.append(out[0])
                self.flows, self.known = out[1], out[2:]
            else:
                out = run(
                    functools.partial(merge_flows, self.part, k, levels), [(tall, LANES), inflow],
                    [mats[k], self.flows, other, *self.known], name="merge_flows",
                )
                self.flows, self.known = out[0], out[1:]
            self.level = k + 1

        def send(self):
            self.other = to_level(self.flows, levels - 1)

        def ahead_of(self, later):
            later.flows, self.other = lax.optimization_barrier((later.flows, self.other))

        def last(self):
            return [self.flows, self.other, *self.known]

        def correct(self):
            if self.leads:
                result, last = run(
                    functools.partial(correct_all, self.part, levels), [self.solved.shape, mats_shape],
                    [*self.last(), blocks, self.solved], scratch=self.scratch, name="correct_all",
                )
                mats.append(last)
                return result
            return run(
                functools.partial(correct, self.part, levels), [self.solved.shape],
                [mats[-1], *self.last(), blocks, self.solved], scratch=self.scratch, name="correct",
            )[0]

    base_near = run(
        near_base, [x_shape], [xn, xf, adv, vis, table, trig], name="near_base", flops=COSTS[0]
    )[0]
    blocks, group = run(
        transfer, [(2, cells * V, 16, LANES), (padded_even(6 * V * V), LANES)], [low, upp],
        scratch=[pltpu.VMEM((cells * V, 8, LANES), F32)], name="transfer", flops=COSTS[1],
    )
    lead = run(
        far_lead, [(LEAD * V, PAD, LANES)], [slab_in, trig, basis, turned],
        scratch=[pltpu.VMEM((V, PAD, LANES), F32)], name="far_lead", flops=COSTS[3],
    )[0]
    tall = packed_rows(2 * V, PAD // 8 - 1, True) + group.shape[0]
    first = Exchange(
        0,
        True,
        *run(
            near_cell, [x_shape, (tall, LANES)],
            [base_near, halo_near, from_left, from_right, adv, vis, inv, low, upp, group],
            scratch=[edges], name="near_cell", flops=COSTS[2],
        ),
        leads=True,
    )
    first.step()
    second = Exchange(1, CHUNKS[0][1], *solve_chunk(0))
    for k in range(1, levels - 1):
        first.step()
    first.send()
    second.step()
    third = Exchange(1, CHUNKS[1][1], *solve_chunk(1))
    third.step()
    for k in range(1, levels - 1):
        second.step()
    second.send()
    first.ahead_of(third)
    for k in range(1, levels - 1):
        third.step()
    near = first.correct()
    done = [second.correct()]
    g_last = third.solved
    third.send()
    small = [mats[-1], *third.last()]

    out = run(
        functools.partial(finish, levels), [st.shape], [*small, g_last, blocks, near, *done],
        out_specs=[pl.BlockSpec(memory_space=pltpu.HBM)],
        scratch=[
            pltpu.VMEM((2 * V, rows_of(CHUNKS[-1]), LANES), F32),
            pltpu.VMEM(st.shape, F32),
            pltpu.SemaphoreType.DMA((4,)),
        ],
        name="finish",
    )[0]
    return out.reshape(cells, V, NT, 2, LANES).transpose(0, 3, 1, 2, 4)


def solution(mesh):
    cell = P("seg", "pitch", None, None, None)
    return jax.shard_map(
        local,
        mesh=mesh,
        in_specs=(cell, P("seg", "pitch", None, None), P("seg", "pitch", None, None), cell, cell, cell, P(), P()),
        out_specs=cell,
        check_vma=False,
    )
```

```python
import functools
import math

import jax
import jax.numpy as jnp
import numpy as np
from jax import lax
from jax.experimental import pallas as pl
from jax.experimental.pallas import tpu as pltpu
from jax.sharding import PartitionSpec as P

F32 = jnp.float32
BF16 = jnp.bfloat16
V = 5
NT = 49
PAD = 56
DEPTH = 64
LANES = 128
LEAD = 4
MB = 1 << 20

CHUNKS = (((0, 32), False), ((32, 48), True))


def rows_of(chunk):
    (first, last), extra = chunk
    return last - first + (8 if extra else 0)


def padded_even(count):
    return (count + 7) // 8 * 8


class Chain:
    def __init__(self, flags):
        self.flags = flags

    def before(self, array):
        return lax.optimization_barrier((self.flags, array))[1]

    def after(self, array):
        self.flags, array = lax.optimization_barrier((self.flags, array))
        return array

    def __call__(self, body, out_shapes, arrays, scratch=(), vmem=16, name=None, grid=None, in_specs=None, out_specs=None, scalars=(), flops=1000):
        smem = pl.BlockSpec(memory_space=pltpu.SMEM)
        held = pl.BlockSpec(memory_space=pltpu.VMEM)
        extra = {} if grid is None else {"grid": grid}
        out = pl.pallas_call(
            body,
            out_shape=[jax.ShapeDtypeStruct(s, F32) for s in out_shapes],
            in_specs=[smem] * (1 + len(scalars)) + (in_specs or [held] * len(arrays)),
            out_specs=out_specs or [held] * len(out_shapes),
            scratch_shapes=list(scratch),
            compiler_params=pltpu.CompilerParams(vmem_limit_bytes=vmem * MB),
            cost_estimate=pl.CostEstimate(flops=flops, bytes_accessed=1000, transcendentals=0),
            name=name,
            **extra,
        )(self.flags, *scalars, *arrays)
        out = list(out)
        out[0] = self.after(out[0])
        return out


def coefficient(ref, z, a, b, p):
    return ref[pl.ds(((z * V + a) * V + b) * 2 + p, 1), :]


def split_left(matrix):
    high = matrix.astype(BF16).astype(F32)
    place = lax.broadcasted_iota(jnp.int32, matrix.shape, 1)
    return jnp.where(place < 2 * DEPTH, high, matrix - high).astype(BF16)


def lag_matrix(basis, turned, trig, sign):
    half = turned.shape[0] // 2
    count = (half - 4) // 8 * 8
    cosine, sine = turned[:half], turned[half:]
    turn, cross = trig[:count, :1], trig[count : 2 * count, :1] * sign
    right = jnp.concatenate(
        [
            turn * cosine[:count] + cross * sine[:count],
            turn * sine[:count] - cross * cosine[:count],
            cosine[count:],
        ],
        axis=0,
    )
    return jnp.dot(basis, right, preferred_element_type=F32, precision=lax.Precision.HIGHEST)


def over_instants(lefts, cells):
    whole = jnp.concatenate(cells, axis=1)
    if whole.shape[0] < DEPTH:
        whole = jnp.concatenate(
            [whole, jnp.zeros((DEPTH - whole.shape[0], whole.shape[1]), F32)], axis=0
        )
    high = whole.astype(BF16)
    low = (whole - high.astype(F32)).astype(BF16)
    right = jnp.concatenate([high, low, high], axis=0)
    products = [jnp.dot(left, right, preferred_element_type=F32) for left in lefts]
    return [[x[:, i * LANES : (i + 1) * LANES] for i in range(len(cells))] for x in products]


def split_cells(st, slab, first_cell, last_cell, xn, xf):
    p = lax.axis_index("pitch") % 2
    edge = first_cell.shape[0]
    zeros = jnp.zeros((8, LANES), F32)
    width = 4 * NT

    def step(i, carry):
        slab[pl.ds(i * width, width), :] = st[pl.ds(i * 2 * width + p, width, stride=2), :]
        return carry

    lax.fori_loop(0, LEAD * V // 4, step, 0)
    first_cell[...] = st[0:edge, :]
    last_cell[...] = st[st.shape[0] - edge :, :]

    def separate(z, carry):
        for v in range(V):
            j = z * V + v
            for out, q in ((xn, 1 - p), (xf, p)):
                out[j, PAD - 8 : PAD, :] = zeros
                out[j, 0:NT, :] = st[pl.ds(j * 2 * NT + q, NT, stride=2), :]
        return carry

    lax.fori_loop(0, xn.shape[0] // V, separate, 0)


def lags(blades, harmonic, trig):
    count = harmonic.shape[0]
    rotor = jnp.full(harmonic.shape, blades[0]).astype(F32)
    stator = jnp.full(harmonic.shape, blades[1]).astype(F32)
    turns = harmonic[...] * stator
    lag = (turns - rotor * jnp.floor(turns / rotor)) / rotor * (2.0 * math.pi)
    trig[0:count, :] = jnp.cos(lag)
    trig[count : 2 * count, :] = jnp.sin(lag)
    trig[2 * count : 2 * count + 8, :] = (stator / rotor / count)[:8]


def own_terms(z, x, other, advect, viscous, p, timing, above, below, base):
    for v in range(V):
        j = z * V + v
        total = viscous[pl.ds(j * 2 + p, 1), :] * (other[j] - 2.0 * x[j]) - timing[v]
        rate = advect[pl.ds(j * 2 + p, 1), :]
        if above and below:
            total += rate * (x[j - V] - x[j + V])
        else:
            total += rate * (x[j - V] if above else -x[j + V])
        base[j] = total


def timing_matrix(table, trig):
    return split_left(table[...] * trig[trig.shape[0] - 8 : trig.shape[0] - 7, :1])


def prepare(flags, blades, xn, xf, harmonic, basis, turned, advect, viscous, table, trig, base, *chunks):
    lags(blades, harmonic, trig)
    p, wrap = flags[0], flags[1]
    cells = xf.shape[0] // V
    sign = jnp.where(flags[2] == 1, 1.0, -1.0)
    lag = split_left(lag_matrix(basis[...], turned[...], trig[...], sign))
    derive = timing_matrix(table, trig)

    def one(z, above=True, below=True, sends=True):
        raw = [xf[z * V + v] for v in range(V)]
        timing, *lagged = over_instants([derive, lag] if sends else [derive], raw)
        own_terms(z, xf, xn, advect, viscous, p, timing, above, below, base)
        if not sends:
            return
        for v in range(V):
            value = jnp.where(wrap == 1, lagged[0][v], raw[v])
            j = (z - LEAD) * V + v
            for out, ((first, last), extra) in zip(chunks, CHUNKS):
                width = last - first
                out[pl.ds(pl.multiple_of(j * width, 8), width), :] = value[first:last]
                if extra:
                    out[pl.ds((cells - LEAD) * V * width + j, 1), :] = value[NT - 1 : NT]

    def early(z, carry):
        one(z, sends=False)
        return carry

    def late(z, carry):
        one(z)
        return carry

    one(0, above=False, sends=False)
    lax.fori_loop(1, LEAD, early, 0)
    one(LEAD)
    lax.fori_loop(LEAD + 1, cells - 1, late, 0, unroll=5)
    one(cells - 1, below=False)


def near_base(flags, xn, xf, advect, viscous, table, trig, base):
    p = 1 - flags[0]
    cells = xn.shape[0] // V
    derive = timing_matrix(table, trig)

    def one(z, above=True, below=True):
        (timing,) = over_instants([derive], [xn[z * V + v] for v in range(V)])
        own_terms(z, xn, xf, advect, viscous, p, timing, above, below, base)

    def inner(z, carry):
        one(z)
        return carry

    one(0, above=False)
    lax.fori_loop(1, cells - 1, inner, 0, unroll=7)
    one(cells - 1, below=False)


def split_height(rows_high, extra):
    return rows_high // 8 - (1 if extra else 0)


def packed_rows(count, height, extra):
    return count * height * 8 + (padded_even(count) if extra else 0)


def vector_rows(count, i, t, height):
    if isinstance(t, int) and t == height:
        return pl.ds(count * height * 8 + i, 1)
    return pl.ds(pl.multiple_of((i * height + t) * 8, 8), 8)


def over_tiles(height, extra, tile):
    lax.fori_loop(0, height, lambda t, carry: (tile(t), carry)[1], 0)
    if extra:
        tile(height)


def keep_tiles(ref, kind, values, first, last, height, extra):
    for a in range(V):
        for t in range(first // 8, last // 8):
            place = vector_rows(2 * V, kind + a, t, height)
            ref[place, :] = values[a][t * 8 - first : t * 8 - first + (1 if t == height else 8)]


def sweeps(source, g, fg, extra, spans, p, inverse, lower, upper, cells):
    height = split_height(g.shape[1], extra)
    for first, last in spans:
        nothing = tuple(jnp.zeros((last - first, LANES), F32) for _ in range(V))

        def ahead(z, current, first=first, last=last):
            right = source(z, first, last)
            result = []
            for a in range(V):
                total = coefficient(inverse, z, a, 0, p) * right[0]
                for b in range(1, V):
                    total += coefficient(inverse, z, a, b, p) * right[b]
                for b in range(V):
                    total += coefficient(lower, z, a, b, p) * current[b]
                g[z * V + a, first:last, :] = total
                result.append(total)
            return tuple(result)

        out = lax.fori_loop(1, cells - 1, ahead, ahead(0, nothing), unroll=2)
        out = ahead(cells - 1, out)
        keep_tiles(fg, 0, out, first, last, height, extra)

        def back(i, current, first=first, last=last):
            z = cells - 1 - i
            result = []
            for a in range(V):
                total = g[z * V + a, first:last, :]
                for b in range(V):
                    total += coefficient(upper, z, a, b, p) * current[b]
                g[z * V + a, first:last, :] = total
                result.append(total)
            return tuple(result)

        out = lax.fori_loop(0, cells, back, nothing, unroll=2)
        keep_tiles(fg, V, out, first, last, height, extra)


def take_edges(edges, from_left, from_right, p):
    skip = from_left.shape[0] - V * NT * 2
    for v in range(V):
        edges[v, PAD - 8 : PAD, :] = jnp.zeros((8, LANES), F32)
        edges[v, 0:NT, :] = from_left[pl.ds(skip + v * 2 * NT + p, NT, stride=2), :]
        edges[V + v, PAD - 8 : PAD, :] = jnp.zeros((8, LANES), F32)
        edges[V + v, 0:NT, :] = from_right[pl.ds(v * 2 * NT + p, NT, stride=2), :]


def edge_terms(z, cells, values, edges, advect, p, first, last):
    if not isinstance(z, int):
        return values
    return [
        value
        + (1.0 if z == 0 else -1.0)
        * advect[pl.ds((z * V + v) * 2 + p, 1), :]
        * edges[v if z == 0 else V + v, first:last, :]
        for v, value in enumerate(values)
    ]


def near_cell(
    flags, base, halo, from_left, from_right, advect, viscous, inverse, lower, upper, group,
    g, flows, edges,
):
    p = 1 - flags[0]
    cells = base.shape[0] // V
    take_edges(edges, from_left, from_right, p)

    def source(z, first, last):
        values = []
        for v in range(V):
            j = z * V + v
            values.append(base[j, first:last, :] + viscous[pl.ds(j * 2 + p, 1), :] * halo[j, first:last, :])
        return edge_terms(z, cells, values, edges, advect, p, first, last)

    sweeps(source, g, flows, True, ((0, 32), (32, PAD)), p, inverse, lower, upper, cells)
    flows[flows.shape[0] - group.shape[0] :, :] = group[...]


def far_lead(flags, slab, trig, basis, turned, lead, halo):
    wrap = flags[1]
    sign = jnp.where(flags[2] == 1, -1.0, 1.0)
    left = split_left(lag_matrix(basis[...], turned[...], trig[...], sign))
    for z in range(LEAD):
        for v in range(V):
            halo[v, PAD - 8 : PAD, :] = jnp.zeros((8, LANES), F32)
            halo[v, 0:NT, :] = slab[pl.ds((z * V + v) * NT, NT), :]
        raw = [halo[v] for v in range(V)]
        (lagged,) = over_instants([left], raw)
        for v in range(V):
            lead[z * V + v] = jnp.where(wrap == 1, lagged[v], raw[v])


def far_chunk(chunk, flags, base, lead, halo, from_left, from_right, advect, viscous, inverse, lower, upper, g, fg, edges):
    (first, last), extra = chunk
    width = last - first
    p = flags[0]
    cells = base.shape[0] // V
    top = lax.broadcasted_iota(jnp.int32, (8, LANES), 0) == 0
    take_edges(edges, from_left, from_right, p)

    def pieces(ref, j):
        value = ref[j, first:last, :]
        return jnp.concatenate([value, ref[j, PAD - 8 : PAD, :]], axis=0) if extra else value

    def source(z, start, stop):
        result = []
        for v in range(V):
            j = z * V + v
            h = jnp.maximum(z - LEAD, 0) * V + v
            arrived = halo[pl.ds(pl.multiple_of(h * width, 8), width), :]
            if extra:
                row = halo[pl.ds((cells - LEAD) * V * width + h, 1), :]
                arrived = jnp.concatenate([arrived, jnp.where(top, row, 0.0)], axis=0)
            early = pieces(lead, jnp.minimum(z, LEAD - 1) * V + v)
            arrived = jnp.where(z >= LEAD, arrived, early)
            value = pieces(base, j) + viscous[pl.ds(j * 2 + p, 1), :] * arrived
            if isinstance(z, int):
                rate = advect[pl.ds(j * 2 + p, 1), :]
                edge = pieces(edges, v if z == 0 else V + v)
                value += rate * edge if z == 0 else -rate * edge
            result.append(value)
        return result

    height = rows_of(chunk)
    sweeps(source, g, fg, extra, ((0, height),), p, inverse, lower, upper, cells)


def times(matrix, vector):
    result = []
    for a in range(V):
        total = matrix(a, 0) * vector[0]
        for b in range(1, V):
            total += matrix(a, b) * vector[b]
        result.append(total)
    return result


def plus(one, two):
    return [a + b for a, b in zip(one, two)]


def tiles(ref, c, kind):
    return [ref[c, kind * V + a, 0:V, :] for a in range(V)]


def rows(ref, c, kind):
    return lambda a, b: ref[c, kind * V + a, b : b + 1, :]


def unit(a):
    place = lax.broadcasted_iota(jnp.int32, (8, LANES), 0)
    return jnp.where(place == a, 1.0, 0.0).astype(F32)


def transfer(flags, lower, upper, blocks, group, forward):
    cells = blocks.shape[1] // V
    for c in range(2):
        p = 1 - flags[0] if c == 0 else flags[0]

        def ahead(z, current):
            result = times(lambda a, b: coefficient(lower, z, a, b, p), current)
            for a in range(V):
                forward[z * V + a] = result[a]
            return tuple(result)

        through = lax.fori_loop(0, cells, ahead, tuple(unit(a) for a in range(V)), unroll=4)

        def back(i, current):
            z = cells - 1 - i
            result = times(lambda a, b: coefficient(upper, z, a, b, p), current)
            for a in range(V):
                result[a] = result[a] + jnp.concatenate(
                    [forward[z * V + a], jnp.zeros((8, LANES), F32)], axis=0
                )
                blocks[c, z * V + a] = result[a]
            return tuple(result)

        start = tuple(
            jnp.concatenate([jnp.zeros((8, LANES), F32), unit(a)], axis=0) for a in range(V)
        )
        ends = lax.fori_loop(0, cells, back, start, unroll=4)
        for a in range(V):
            for kind, value in enumerate((ends[a][:V], ends[a][8 : 8 + V], through[a][:V])):
                group[pl.ds(((c * 3 + kind) * V + a) * V, V), :] = value
    group[6 * V * V :, :] = jnp.zeros((group.shape[0] - 6 * V * V, LANES), F32)


def merge_matrices(bit, levels, flags, mine, other, share, mats, merged, share_out, offset, new_offset):
    start, last = bit == 0, bit == levels - 1
    right = flags[3 + bit] == 1
    left = jnp.logical_not(right)
    nothing = jnp.zeros((V, LANES), F32)
    one = [unit(a)[:V] for a in range(V)]
    for c in range(2):
        kinds = 1 if last else 3
        at = lambda ref, kind: [ref[pl.ds(offset + ((c * kinds + kind) * V + a) * V, V), :] for a in range(V)]
        pick = lambda kind, own: [jnp.where(own, m, t) for m, t in zip(at(mine, kind), at(other, kind))]
        if start:
            own = [one, [nothing] * V, one]
        else:
            own = [tiles(share, c, kind) for kind in range(3)]
        found = [
            (1, pick(0, right)),
            (3, [jnp.where(right, x, nothing) for x in own[0]]),
            (4, [jnp.where(right, x, nothing) for x in own[1]]),
            (5, [jnp.where(right, nothing, x) for x in own[2]]),
        ]
        if not last:
            found += [(0, pick(2, right)), (2, pick(1, left))]
        for kind, values in found:
            for a in range(V):
                mats[c, kind * V + a, 0:V, :] = values[a]
        if last:
            continue
        p_left, g_left, h_right = pick(2, left), pick(0, left), pick(1, right)
        turned = times(rows(mats, c, 1), p_left)
        new = [plus(g_left, times(rows(mats, c, 2), turned))]
        if bit < levels - 2:
            new += [times(rows(mats, c, 2), h_right), times(rows(mats, c, 0), p_left)]
        for kind, values in enumerate(new):
            for a in range(V):
                merged[pl.ds(new_offset + ((c * len(new) + kind) * V + a) * V, V), :] = values[a]
        s0 = times(rows(mats, c, 3), p_left)
        s1 = times(rows(mats, c, 4), p_left)
        s1b = times(rows(mats, c, 5), turned)
        s2 = times(rows(mats, c, 5), h_right)
        for a in range(V):
            share_out[c, a, 0:V, :] = jnp.where(right, s0[a], own[0][a])
            share_out[c, V + a, 0:V, :] = jnp.where(right, s1[a], own[1][a] + s1b[a])
            share_out[c, 2 * V + a, 0:V, :] = jnp.where(right, own[2][a], s2[a])


def inflow_of(c, mats, f_left, g_right, known):
    back = plus(g_right, times(rows(mats, c, 1), f_left))
    from_left = times(rows(mats, c, 3), f_left)
    from_right = plus(times(rows(mats, c, 4), f_left), times(rows(mats, c, 5), back))
    total = from_left + from_right
    return back, total if known is None else plus(known, total)


def merge_all(part, bit, levels, flags, flows, other, *refs):
    share, known, mats, merged, share_out, inflow = (None, None, *refs) if bit == 0 else refs
    _, height, extra = part
    offset = packed_rows(2 * V, height, extra)
    new_offset = packed_rows(V, height, extra) if bit == levels - 2 else offset
    merge_matrices(bit, levels, flags, flows, other, share, mats, merged, share_out, offset, new_offset)
    merge_flows(part, bit, levels, flags, mats, flows, other, *([] if known is None else [known]), merged, inflow)


def merge_flows(part, bit, levels, flags, mats, flows, other, *refs):
    known, merged, inflow = (None, *refs) if bit == 0 else refs
    right, last_right = flags[3 + bit] == 1, flags[2 + levels] == 1
    last = bit == levels - 2
    c, height, extra = part

    def tile(t):
        at = lambda i: vector_rows(2 * V, i, t, height)
        mine = [flows[at(i), :] for i in range(2 * V)]
        theirs = [other[at(i), :] for i in range(2 * V)]
        f_left = [jnp.where(right, y, x) for x, y in zip(mine[:V], theirs[:V])]
        f_right = [jnp.where(right, x, y) for x, y in zip(mine[:V], theirs[:V])]
        g_left = [jnp.where(right, y, x) for x, y in zip(mine[V:], theirs[V:])]
        g_right = [jnp.where(right, x, y) for x, y in zip(mine[V:], theirs[V:])]
        before = None if known is None else [known[at(i), :] for i in range(2 * V)]
        back, total = inflow_of(c, mats, f_left, g_right, before)
        new_f = plus(f_right, times(rows(mats, c, 0), f_left))
        new_g = plus(g_left, times(rows(mats, c, 2), back))
        if last:
            for i in range(V):
                end = jnp.where(last_right, new_g[i], new_f[i])
                merged[vector_rows(V, i, t, height), :] = end
        else:
            for i, value in enumerate(new_f + new_g):
                merged[at(i), :] = value
        for i, value in enumerate(total):
            inflow[at(i), :] = value

    over_tiles(height, extra, tile)


def last_inflow(right, part, mats, ends, other, known, inflow):
    c, height, extra = part
    for t in range(height + (1 if extra else 0)):
        place = lambda i: vector_rows(V, i, t, height)
        mine = [ends[place(a), :] for a in range(V)]
        theirs = [other[place(a), :] for a in range(V)]
        f_left = [jnp.where(right, y, x) for x, y in zip(mine, theirs)]
        g_right = [jnp.where(right, x, y) for x, y in zip(mine, theirs)]
        before = [known[vector_rows(2 * V, i, t, height), :] for i in range(2 * V)]
        _, total = inflow_of(c, mats, f_left, g_right, before)
        for i, value in enumerate(total):
            inflow[i, t * 8 : t * 8 + 8, :] = jnp.broadcast_to(value, (8, LANES))


def corrected(c, z, a, first, last, g, blocks, inflow):
    total = g[z * V + a, first:last, :]
    for b in range(V):
        total += blocks[c, z * V + a, b : b + 1, :] * inflow[b]
        total += blocks[c, z * V + a, 8 + b : 9 + b, :] * inflow[V + b]
    return total


def correct(part, levels, flags, mats, ends, other, known, blocks, g, result, inflow):
    c = part[0]
    last_inflow(flags[2 + levels] == 1, part, mats, ends, other, known, inflow)
    height = g.shape[1]
    for first, last in ((0, 32), (32, height)) if height > 32 else ((0, height),):
        flow = tuple(inflow[i, first:last, :] for i in range(2 * V))

        def step(z, flow, first=first, last=last):
            for a in range(V):
                result[z * V + a, first:last, :] = corrected(c, z, a, first, last, g, blocks, flow)
            return flow

        lax.fori_loop(0, g.shape[0] // V, step, flow, unroll=2)


def correct_all(part, levels, flags, ends, other, share, known, blocks, g, result, mats, inflow):
    offset = packed_rows(V, *part[1:])
    merge_matrices(levels - 1, levels, flags, ends, other, share, mats, None, None, offset, 0)
    correct(part, levels, flags, mats, ends, other, known, blocks, g, result, inflow)


def finish(levels, flags, mats, ends, other, known, g, blocks, near, *refs):
    done, (out, inflow, held, sems) = refs[:-4], refs[-4:]
    right = flags[2 + levels] == 1
    p = flags[0]
    (first_row, last_row), last_extra = CHUNKS[-1]
    width, height = last_row - first_row, rows_of(CHUNKS[-1])
    part = (1, split_height(height, last_extra), last_extra)
    last_inflow(right, part, mats, ends, other, known, inflow)
    flow = tuple(inflow[i] for i in range(2 * V))

    def step(z, carry):
        for a in range(V):
            j = z * V + a
            row = j * 2 * NT
            held[pl.ds(row + 1 - p, NT, stride=2), :] = near[j, 0:NT, :]
            for ref, ((first, last), extra) in zip(done, CHUNKS):
                held[pl.ds(row + p + 2 * first, last - first, stride=2), :] = ref[j, 0 : last - first, :]
                if extra:
                    held[pl.ds(row + p + 2 * (NT - 1), 1), :] = ref[j, last - first : last - first + 1, :]
            value = corrected(1, z, a, 0, height, g, blocks, flow)
            held[pl.ds(row + p + 2 * first_row, width, stride=2), :] = value[:width]
            if last_extra:
                held[pl.ds(row + p + 2 * (NT - 1), 1), :] = value[width : width + 1]
        return carry

    parts = sems.shape[0]
    cells = g.shape[0] // V // parts
    size = held.shape[0] // parts
    copies = []
    for i in range(parts):
        lax.fori_loop(i * cells, (i + 1) * cells, step, 0, unroll=2)
        span = pl.ds(i * size, size)
        copies.append(pltpu.make_async_copy(held.at[span, :], out.at[span, :], sems.at[i]))
        copies[-1].start()
    for copy in copies:
        copy.wait()


def phase_tables(count):
    angle = 2.0 * math.pi * np.outer(np.arange(1, count + 1), np.arange(NT)) / NT
    cosine, sine = np.cos(angle), np.sin(angle)
    basis = np.zeros((PAD, 2 * count + 8), np.float32)
    basis[:NT, :count], basis[:NT, count : 2 * count], basis[:NT, 2 * count] = cosine.T, sine.T, 0.5
    turned = np.zeros((2, count + 8, 3, DEPTH), np.float32)
    turned[0, :count, :, :NT], turned[1, :count, :, :NT] = cosine[:, None], sine[:, None]
    turned[0, count, :, :NT] = 1.0
    return (2.0 / NT * basis).astype(np.float32), turned.reshape(2 * (count + 8), 3 * DEPTH)


def derivative_table():
    gap = np.arange(NT)[:, None] - np.arange(NT)[None, :]
    safe = np.where(gap == 0, 1.0, np.sin(np.pi * gap / NT))
    table = np.where(gap == 0, 0.0, 0.5 * (1.0 - 2.0 * np.mod(gap, 2)) / safe)
    wide = np.zeros((PAD, 3, DEPTH), np.float32)
    wide[:NT, :, :NT] = table[:, None]
    return wide.reshape(PAD, 3 * DEPTH)


COSTS = (0, 0, 6_000_000_000, 0)


def local(state, advect, viscous, inverse, lower, upper, blades, harmonic):
    cells = state.shape[0]
    count = harmonic.shape[0]
    segs, slabs = lax.axis_size("seg"), lax.axis_size("pitch")
    levels = segs.bit_length() - 1
    far_pairs = [(i, (i - 1) % slabs if i % 2 == 0 else (i + 1) % slabs) for i in range(slabs)]
    near_pairs = [(i, i ^ 1) for i in range(slabs)]
    to_far = lambda x: lax.ppermute(x, "pitch", far_pairs)
    to_level = lambda x, k: lax.ppermute(x, "seg", [(i, i ^ (1 << k)) for i in range(segs)])
    x_shape = (cells * V, PAD, LANES)

    slab, seg = lax.axis_index("pitch"), lax.axis_index("seg")
    side = slab % 2
    wrap = jnp.logical_or(slab == 0, slab == slabs - 1)
    bits = [(seg >> k) & 1 for k in range(levels)]
    run = Chain(
        jnp.stack(
            [side, wrap.astype(jnp.int32), (slab == 0).astype(jnp.int32), *bits]
        ).astype(jnp.int32)
    )
    flat = lambda x: x.transpose(0, 2, 3, 1, 4).reshape(cells * V * V * 2, LANES)
    inv, low, upp = flat(inverse.astype(F32)), flat(lower), flat(upper)
    st = state.transpose(0, 2, 3, 1, 4).reshape(cells * V * NT * 2, LANES)
    lead_rows, edge_rows = LEAD * V * NT, padded_even(V * NT * 2)
    held = pl.BlockSpec(memory_space=pltpu.VMEM)
    shapes = [(lead_rows, LANES), (edge_rows, LANES), (edge_rows, LANES), x_shape, x_shape]
    slab_out, first_cell, last_cell, xn, xf = pl.pallas_call(
        split_cells,
        out_shape=[jax.ShapeDtypeStruct(x, F32) for x in shapes],
        in_specs=[held],
        out_specs=[held] * 5,
        compiler_params=pltpu.CompilerParams(vmem_limit_bytes=16 * MB),
        name="split_cells",
    )(run.before(st))
    halo_near = lax.ppermute(xn, "pitch", near_pairs)
    slab_in = to_far(slab_out)
    from_left = lax.ppermute(last_cell, "seg", [(i, i + 1) for i in range(segs - 1)])
    from_right = lax.ppermute(first_cell, "seg", [(i + 1, i) for i in range(segs - 1)])

    basis, turned = phase_tables(count)
    table = derivative_table()
    wide_harmonic = jnp.broadcast_to(harmonic.astype(F32)[:, None], (count, LANES))

    rest = (cells - LEAD) * V
    chunk_shapes = [
        (rest * (last - first) + (padded_even(rest) if extra else 0), LANES)
        for (first, last), extra in CHUNKS
    ]
    adv = advect.transpose(0, 2, 1, 3).reshape(cells * V * 2, LANES)
    vis = viscous.transpose(0, 2, 1, 3).reshape(cells * V * 2, LANES)
    trig, base, *chunks = run(
        prepare, [(2 * count + 8, LANES), x_shape, *chunk_shapes],
        [xn, xf, wide_harmonic, basis, turned, adv, vis, table], scalars=[blades], name="prepare",
    )
    arrived = [slab_in]
    for chunk in chunks:
        if len(arrived) >= 2:
            chunk, arrived[-2] = lax.optimization_barrier((chunk, arrived[-2]))
        arrived.append(to_far(chunk))
    slab_in, *arrived = arrived

    edges = pltpu.VMEM((2 * V, PAD, LANES), F32)

    mats = []
    mats_shape = (2, 6 * V, 8, LANES)

    def solve_chunk(i):
        height, extra = rows_of(CHUNKS[i]), CHUNKS[i][1]
        tall = packed_rows(2 * V, split_height(height, extra), extra)
        return run(
            functools.partial(far_chunk, CHUNKS[i]),
            [(cells * V, height, LANES), (tall, LANES)],
            [base, lead, arrived[i], from_left, from_right, adv, vis, inv, low, upp],
            scratch=[edges], name="far_chunk",
        )

    class Exchange:
        def __init__(self, c, extra, g, flows, leads=False):
            self.part, self.leads = (c, split_height(g.shape[1], extra), extra), leads
            self.flows, self.known, self.solved, self.level = flows, [], g, 0
            self.scratch = [pltpu.VMEM((2 * V, g.shape[1], LANES), F32)]

        def step(self):
            k = self.level
            behind = k == levels - 2
            inflow = (packed_rows(2 * V, *self.part[1:]), LANES)
            tall = packed_rows(V if behind else 2 * V, *self.part[1:])
            other = to_level(self.flows, k)
            if self.leads:
                tall += padded_even((2 if behind else 6) * V * V)
                out = run(
                    functools.partial(merge_all, self.part, k, levels),
                    [mats_shape, (tall, LANES), (2, 3 * V, 8, LANES), inflow],
                    [self.flows, other, *self.known], name="merge_all",
                )
                mats.append(out[0])
                self.flows, self.known = out[1], out[2:]
            else:
                out = run(
                    functools.partial(merge_flows, self.part, k, levels), [(tall, LANES), inflow],
                    [mats[k], self.flows, other, *self.known], name="merge_flows",
                )
                self.flows, self.known = out[0], out[1:]
            self.level = k + 1

        def send(self):
            self.other = to_level(self.flows, levels - 1)

        def ahead_of(self, later):
            later.flows, self.other = lax.optimization_barrier((later.flows, self.other))

        def last(self):
            return [self.flows, self.other, *self.known]

        def correct(self):
            if self.leads:
                result, last = run(
                    functools.partial(correct_all, self.part, levels), [self.solved.shape, mats_shape],
                    [*self.last(), blocks, self.solved], scratch=self.scratch, name="correct_all",
                )
                mats.append(last)
                return result
            return run(
                functools.partial(correct, self.part, levels), [self.solved.shape],
                [mats[-1], *self.last(), blocks, self.solved], scratch=self.scratch, name="correct",
            )[0]

    base_near = run(
        near_base, [x_shape], [xn, xf, adv, vis, table, trig], name="near_base", flops=COSTS[0]
    )[0]
    blocks, group = run(
        transfer, [(2, cells * V, 16, LANES), (padded_even(6 * V * V), LANES)], [low, upp],
        scratch=[pltpu.VMEM((cells * V, 8, LANES), F32)], name="transfer", flops=COSTS[1],
    )
    lead = run(
        far_lead, [(LEAD * V, PAD, LANES)], [slab_in, trig, basis, turned],
        scratch=[pltpu.VMEM((V, PAD, LANES), F32)], name="far_lead", flops=COSTS[3],
    )[0]
    tall = packed_rows(2 * V, PAD // 8 - 1, True) + group.shape[0]
    first = Exchange(
        0,
        True,
        *run(
            near_cell, [x_shape, (tall, LANES)],
            [base_near, halo_near, from_left, from_right, adv, vis, inv, low, upp, group],
            scratch=[edges], name="near_cell", flops=COSTS[2],
        ),
        leads=True,
    )
    first.step()
    second = Exchange(1, CHUNKS[0][1], *solve_chunk(0))
    for k in range(1, levels - 1):
        first.step()
    first.send()
    second.step()
    third = Exchange(1, CHUNKS[1][1], *solve_chunk(1))
    third.step()
    for k in range(1, levels - 1):
        second.step()
    second.send()
    first.ahead_of(third)
    for k in range(1, levels - 1):
        third.step()
    near = first.correct()
    done = [second.correct()]
    g_last = third.solved
    third.send()
    small = [mats[-1], *third.last()]

    out = run(
        functools.partial(finish, levels), [st.shape], [*small, g_last, blocks, near, *done],
        out_specs=[pl.BlockSpec(memory_space=pltpu.HBM)],
        scratch=[
            pltpu.VMEM((2 * V, rows_of(CHUNKS[-1]), LANES), F32),
            pltpu.VMEM(st.shape, F32),
            pltpu.SemaphoreType.DMA((4,)),
        ],
        name="finish",
    )[0]
    return out.reshape(cells, V, NT, 2, LANES).transpose(0, 3, 1, 2, 4)


def solution(mesh):
    cell = P("seg", "pitch", None, None, None)
    return jax.shard_map(
        local,
        mesh=mesh,
        in_specs=(cell, P("seg", "pitch", None, None), P("seg", "pitch", None, None), cell, cell, cell, P(), P()),
        out_specs=cell,
        check_vma=False,
    )
```

```python
import functools
import math

import jax
import jax.numpy as jnp
import numpy as np
from jax import lax
from jax.experimental import pallas as pl
from jax.experimental.pallas import tpu as pltpu
from jax.sharding import PartitionSpec as P

F32 = jnp.float32
BF16 = jnp.bfloat16
V = 5
NT = 49
PAD = 56
DEPTH = 64
LANES = 128
LEAD = 4
MB = 1 << 20

CHUNKS = (((0, 32), False), ((32, 48), True))


def rows_of(chunk):
    (first, last), extra = chunk
    return last - first + (8 if extra else 0)


def padded_even(count):
    return (count + 7) // 8 * 8


class Chain:
    def __init__(self, flags):
        self.flags = flags

    def before(self, array):
        return lax.optimization_barrier((self.flags, array))[1]

    def after(self, array):
        self.flags, array = lax.optimization_barrier((self.flags, array))
        return array

    def __call__(self, body, out_shapes, arrays, scratch=(), vmem=16, name=None, grid=None, in_specs=None, out_specs=None, scalars=(), flops=1000):
        smem = pl.BlockSpec(memory_space=pltpu.SMEM)
        held = pl.BlockSpec(memory_space=pltpu.VMEM)
        extra = {} if grid is None else {"grid": grid}
        out = pl.pallas_call(
            body,
            out_shape=[jax.ShapeDtypeStruct(s, F32) for s in out_shapes],
            in_specs=[smem] * (1 + len(scalars)) + (in_specs or [held] * len(arrays)),
            out_specs=out_specs or [held] * len(out_shapes),
            scratch_shapes=list(scratch),
            compiler_params=pltpu.CompilerParams(vmem_limit_bytes=vmem * MB),
            cost_estimate=pl.CostEstimate(flops=flops, bytes_accessed=1000, transcendentals=0),
            name=name,
            **extra,
        )(self.flags, *scalars, *arrays)
        out = list(out)
        out[0] = self.after(out[0])
        return out


def coefficient(ref, z, a, b, p):
    return ref[pl.ds(((z * V + a) * V + b) * 2 + p, 1), :]


def split_left(matrix):
    high = matrix.astype(BF16).astype(F32)
    place = lax.broadcasted_iota(jnp.int32, matrix.shape, 1)
    return jnp.where(place < 2 * DEPTH, high, matrix - high).astype(BF16)


def lag_matrix(basis, turned, trig, sign):
    half = turned.shape[0] // 2
    count = (half - 4) // 8 * 8
    cosine, sine = turned[:half], turned[half:]
    turn, cross = trig[:count, :1], trig[count : 2 * count, :1] * sign
    right = jnp.concatenate(
        [
            turn * cosine[:count] + cross * sine[:count],
            turn * sine[:count] - cross * cosine[:count],
            cosine[count:],
        ],
        axis=0,
    )
    return jnp.dot(basis, right, preferred_element_type=F32, precision=lax.Precision.HIGHEST)


def over_instants(lefts, cells):
    whole = jnp.concatenate(cells, axis=1)
    if whole.shape[0] < DEPTH:
        whole = jnp.concatenate(
            [whole, jnp.zeros((DEPTH - whole.shape[0], whole.shape[1]), F32)], axis=0
        )
    high = whole.astype(BF16)
    low = (whole - high.astype(F32)).astype(BF16)
    right = jnp.concatenate([high, low, high], axis=0)
    products = [jnp.dot(left, right, preferred_element_type=F32) for left in lefts]
    return [[x[:, i * LANES : (i + 1) * LANES] for i in range(len(cells))] for x in products]


def split_cells(st, slab, first_cell, last_cell, xn, xf):
    p = lax.axis_index("pitch") % 2
    edge = first_cell.shape[0]
    zeros = jnp.zeros((8, LANES), F32)
    width = 4 * NT

    def step(i, carry):
        slab[pl.ds(i * width, width), :] = st[pl.ds(i * 2 * width + p, width, stride=2), :]
        return carry

    lax.fori_loop(0, LEAD * V // 4, step, 0)
    first_cell[...] = st[0:edge, :]
    last_cell[...] = st[st.shape[0] - edge :, :]

    def separate(z, carry):
        for v in range(V):
            j = z * V + v
            for out, q in ((xn, 1 - p), (xf, p)):
                out[j, PAD - 8 : PAD, :] = zeros
                out[j, 0:NT, :] = st[pl.ds(j * 2 * NT + q, NT, stride=2), :]
        return carry

    lax.fori_loop(0, xn.shape[0] // V, separate, 0)


def lags(blades, harmonic, trig):
    count = harmonic.shape[0]
    rotor = jnp.full(harmonic.shape, blades[0]).astype(F32)
    stator = jnp.full(harmonic.shape, blades[1]).astype(F32)
    turns = harmonic[...] * stator
    lag = (turns - rotor * jnp.floor(turns / rotor)) / rotor * (2.0 * math.pi)
    trig[0:count, :] = jnp.cos(lag)
    trig[count : 2 * count, :] = jnp.sin(lag)
    trig[2 * count : 2 * count + 8, :] = (stator / rotor / count)[:8]


def own_terms(z, x, other, advect, viscous, p, timing, above, below, base):
    for v in range(V):
        j = z * V + v
        total = viscous[pl.ds(j * 2 + p, 1), :] * (other[j] - 2.0 * x[j]) - timing[v]
        rate = advect[pl.ds(j * 2 + p, 1), :]
        if above and below:
            total += rate * (x[j - V] - x[j + V])
        else:
            total += rate * (x[j - V] if above else -x[j + V])
        base[j] = total


def timing_matrix(table, trig):
    return split_left(table[...] * trig[trig.shape[0] - 8 : trig.shape[0] - 7, :1])


def prepare(flags, blades, xn, xf, harmonic, basis, turned, advect, viscous, table, trig, base, *chunks):
    lags(blades, harmonic, trig)
    p, wrap = flags[0], flags[1]
    cells = xf.shape[0] // V
    sign = jnp.where(flags[2] == 1, 1.0, -1.0)
    lag = split_left(lag_matrix(basis[...], turned[...], trig[...], sign))
    derive = timing_matrix(table, trig)

    def one(z, above=True, below=True, sends=True):
        raw = [xf[z * V + v] for v in range(V)]
        timing, *lagged = over_instants([derive, lag] if sends else [derive], raw)
        own_terms(z, xf, xn, advect, viscous, p, timing, above, below, base)
        if not sends:
            return
        for v in range(V):
            value = jnp.where(wrap == 1, lagged[0][v], raw[v])
            j = (z - LEAD) * V + v
            for out, ((first, last), extra) in zip(chunks, CHUNKS):
                width = last - first
                out[pl.ds(pl.multiple_of(j * width, 8), width), :] = value[first:last]
                if extra:
                    out[pl.ds((cells - LEAD) * V * width + j, 1), :] = value[NT - 1 : NT]

    def early(z, carry):
        one(z, sends=False)
        return carry

    def late(z, carry):
        one(z)
        return carry

    one(0, above=False, sends=False)
    lax.fori_loop(1, LEAD, early, 0)
    one(LEAD)
    lax.fori_loop(LEAD + 1, cells - 1, late, 0, unroll=5)
    one(cells - 1, below=False)


def near_base(flags, xn, xf, advect, viscous, table, trig, base):
    p = 1 - flags[0]
    cells = xn.shape[0] // V
    derive = timing_matrix(table, trig)

    def one(z, above=True, below=True):
        (timing,) = over_instants([derive], [xn[z * V + v] for v in range(V)])
        own_terms(z, xn, xf, advect, viscous, p, timing, above, below, base)

    def inner(z, carry):
        one(z)
        return carry

    one(0, above=False)
    lax.fori_loop(1, cells - 1, inner, 0, unroll=7)
    one(cells - 1, below=False)


def split_height(rows_high, extra):
    return rows_high // 8 - (1 if extra else 0)


def packed_rows(count, height, extra):
    return count * height * 8 + (padded_even(count) if extra else 0)


def vector_rows(count, i, t, height):
    if isinstance(t, int) and t == height:
        return pl.ds(count * height * 8 + i, 1)
    return pl.ds(pl.multiple_of((i * height + t) * 8, 8), 8)


def over_tiles(height, extra, tile):
    lax.fori_loop(0, height, lambda t, carry: (tile(t), carry)[1], 0)
    if extra:
        tile(height)


def keep_tiles(ref, kind, values, first, last, height, extra):
    for a in range(V):
        for t in range(first // 8, last // 8):
            place = vector_rows(2 * V, kind + a, t, height)
            ref[place, :] = values[a][t * 8 - first : t * 8 - first + (1 if t == height else 8)]


def sweeps(source, g, fg, extra, spans, p, inverse, lower, upper, cells):
    height = split_height(g.shape[1], extra)
    for first, last in spans:
        nothing = tuple(jnp.zeros((last - first, LANES), F32) for _ in range(V))

        def ahead(z, current, first=first, last=last):
            right = source(z, first, last)
            result = []
            for a in range(V):
                total = coefficient(inverse, z, a, 0, p) * right[0]
                for b in range(1, V):
                    total += coefficient(inverse, z, a, b, p) * right[b]
                for b in range(V):
                    total += coefficient(lower, z, a, b, p) * current[b]
                g[z * V + a, first:last, :] = total
                result.append(total)
            return tuple(result)

        out = lax.fori_loop(1, cells - 1, ahead, ahead(0, nothing), unroll=2)
        out = ahead(cells - 1, out)
        keep_tiles(fg, 0, out, first, last, height, extra)

        def back(i, current, first=first, last=last):
            z = cells - 1 - i
            result = []
            for a in range(V):
                total = g[z * V + a, first:last, :]
                for b in range(V):
                    total += coefficient(upper, z, a, b, p) * current[b]
                g[z * V + a, first:last, :] = total
                result.append(total)
            return tuple(result)

        out = lax.fori_loop(0, cells, back, nothing, unroll=2)
        keep_tiles(fg, V, out, first, last, height, extra)


def take_edges(edges, from_left, from_right, p):
    skip = from_left.shape[0] - V * NT * 2
    for v in range(V):
        edges[v, PAD - 8 : PAD, :] = jnp.zeros((8, LANES), F32)
        edges[v, 0:NT, :] = from_left[pl.ds(skip + v * 2 * NT + p, NT, stride=2), :]
        edges[V + v, PAD - 8 : PAD, :] = jnp.zeros((8, LANES), F32)
        edges[V + v, 0:NT, :] = from_right[pl.ds(v * 2 * NT + p, NT, stride=2), :]


def edge_terms(z, cells, values, edges, advect, p, first, last):
    if not isinstance(z, int):
        return values
    return [
        value
        + (1.0 if z == 0 else -1.0)
        * advect[pl.ds((z * V + v) * 2 + p, 1), :]
        * edges[v if z == 0 else V + v, first:last, :]
        for v, value in enumerate(values)
    ]


def near_cell(
    flags, base, halo, from_left, from_right, advect, viscous, inverse, lower, upper, group,
    g, flows, edges,
):
    p = 1 - flags[0]
    cells = base.shape[0] // V
    take_edges(edges, from_left, from_right, p)

    def source(z, first, last):
        values = []
        for v in range(V):
            j = z * V + v
            values.append(base[j, first:last, :] + viscous[pl.ds(j * 2 + p, 1), :] * halo[j, first:last, :])
        return edge_terms(z, cells, values, edges, advect, p, first, last)

    sweeps(source, g, flows, True, ((0, 32), (32, PAD)), p, inverse, lower, upper, cells)
    flows[flows.shape[0] - group.shape[0] :, :] = group[...]


def far_lead(flags, slab, trig, basis, turned, lead, halo):
    wrap = flags[1]
    sign = jnp.where(flags[2] == 1, -1.0, 1.0)
    left = split_left(lag_matrix(basis[...], turned[...], trig[...], sign))
    for z in range(LEAD):
        for v in range(V):
            halo[v, PAD - 8 : PAD, :] = jnp.zeros((8, LANES), F32)
            halo[v, 0:NT, :] = slab[pl.ds((z * V + v) * NT, NT), :]
        raw = [halo[v] for v in range(V)]
        (lagged,) = over_instants([left], raw)
        for v in range(V):
            lead[z * V + v] = jnp.where(wrap == 1, lagged[v], raw[v])


def far_chunk(chunk, flags, base, lead, halo, from_left, from_right, advect, viscous, inverse, lower, upper, g, fg, edges):
    (first, last), extra = chunk
    width = last - first
    p = flags[0]
    cells = base.shape[0] // V
    top = lax.broadcasted_iota(jnp.int32, (8, LANES), 0) == 0
    take_edges(edges, from_left, from_right, p)

    def pieces(ref, j):
        value = ref[j, first:last, :]
        return jnp.concatenate([value, ref[j, PAD - 8 : PAD, :]], axis=0) if extra else value

    def source(z, start, stop):
        result = []
        for v in range(V):
            j = z * V + v
            h = jnp.maximum(z - LEAD, 0) * V + v
            arrived = halo[pl.ds(pl.multiple_of(h * width, 8), width), :]
            if extra:
                row = halo[pl.ds((cells - LEAD) * V * width + h, 1), :]
                arrived = jnp.concatenate([arrived, jnp.where(top, row, 0.0)], axis=0)
            early = pieces(lead, jnp.minimum(z, LEAD - 1) * V + v)
            arrived = jnp.where(z >= LEAD, arrived, early)
            value = pieces(base, j) + viscous[pl.ds(j * 2 + p, 1), :] * arrived
            if isinstance(z, int):
                rate = advect[pl.ds(j * 2 + p, 1), :]
                edge = pieces(edges, v if z == 0 else V + v)
                value += rate * edge if z == 0 else -rate * edge
            result.append(value)
        return result

    height = rows_of(chunk)
    sweeps(source, g, fg, extra, ((0, height),), p, inverse, lower, upper, cells)


def times(matrix, vector):
    result = []
    for a in range(V):
        total = matrix(a, 0) * vector[0]
        for b in range(1, V):
            total += matrix(a, b) * vector[b]
        result.append(total)
    return result


def plus(one, two):
    return [a + b for a, b in zip(one, two)]


def tiles(ref, c, kind):
    return [ref[c, kind * V + a, 0:V, :] for a in range(V)]


def rows(ref, c, kind):
    return lambda a, b: ref[c, kind * V + a, b : b + 1, :]


def unit(a):
    place = lax.broadcasted_iota(jnp.int32, (8, LANES), 0)
    return jnp.where(place == a, 1.0, 0.0).astype(F32)


def transfer(flags, lower, upper, blocks, group, forward):
    cells = blocks.shape[1] // V
    for c in range(2):
        p = 1 - flags[0] if c == 0 else flags[0]

        def ahead(z, current):
            result = times(lambda a, b: coefficient(lower, z, a, b, p), current)
            for a in range(V):
                forward[z * V + a] = result[a]
            return tuple(result)

        through = lax.fori_loop(0, cells, ahead, tuple(unit(a) for a in range(V)), unroll=4)

        def back(i, current):
            z = cells - 1 - i
            result = times(lambda a, b: coefficient(upper, z, a, b, p), current)
            for a in range(V):
                result[a] = result[a] + jnp.concatenate(
                    [forward[z * V + a], jnp.zeros((8, LANES), F32)], axis=0
                )
                blocks[c, z * V + a] = result[a]
            return tuple(result)

        start = tuple(
            jnp.concatenate([jnp.zeros((8, LANES), F32), unit(a)], axis=0) for a in range(V)
        )
        ends = lax.fori_loop(0, cells, back, start, unroll=4)
        for a in range(V):
            for kind, value in enumerate((ends[a][:V], ends[a][8 : 8 + V], through[a][:V])):
                group[pl.ds(((c * 3 + kind) * V + a) * V, V), :] = value
    group[6 * V * V :, :] = jnp.zeros((group.shape[0] - 6 * V * V, LANES), F32)


def merge_matrices(bit, levels, flags, mine, other, share, mats, merged, share_out, offset, new_offset):
    start, last = bit == 0, bit == levels - 1
    right = flags[3 + bit] == 1
    left = jnp.logical_not(right)
    nothing = jnp.zeros((V, LANES), F32)
    one = [unit(a)[:V] for a in range(V)]
    for c in range(2):
        kinds = 1 if last else 3
        at = lambda ref, kind: [ref[pl.ds(offset + ((c * kinds + kind) * V + a) * V, V), :] for a in range(V)]
        pick = lambda kind, own: [jnp.where(own, m, t) for m, t in zip(at(mine, kind), at(other, kind))]
        if start:
            own = [one, [nothing] * V, one]
        else:
            own = [tiles(share, c, kind) for kind in range(3)]
        found = [
            (1, pick(0, right)),
            (3, [jnp.where(right, x, nothing) for x in own[0]]),
            (4, [jnp.where(right, x, nothing) for x in own[1]]),
            (5, [jnp.where(right, nothing, x) for x in own[2]]),
        ]
        if not last:
            found += [(0, pick(2, right)), (2, pick(1, left))]
        for kind, values in found:
            for a in range(V):
                mats[c, kind * V + a, 0:V, :] = values[a]
        if last:
            continue
        p_left, g_left, h_right = pick(2, left), pick(0, left), pick(1, right)
        turned = times(rows(mats, c, 1), p_left)
        new = [plus(g_left, times(rows(mats, c, 2), turned))]
        if bit < levels - 2:
            new += [times(rows(mats, c, 2), h_right), times(rows(mats, c, 0), p_left)]
        for kind, values in enumerate(new):
            for a in range(V):
                merged[pl.ds(new_offset + ((c * len(new) + kind) * V + a) * V, V), :] = values[a]
        s0 = times(rows(mats, c, 3), p_left)
        s1 = times(rows(mats, c, 4), p_left)
        s1b = times(rows(mats, c, 5), turned)
        s2 = times(rows(mats, c, 5), h_right)
        for a in range(V):
            share_out[c, a, 0:V, :] = jnp.where(right, s0[a], own[0][a])
            share_out[c, V + a, 0:V, :] = jnp.where(right, s1[a], own[1][a] + s1b[a])
            share_out[c, 2 * V + a, 0:V, :] = jnp.where(right, own[2][a], s2[a])


def inflow_of(c, mats, f_left, g_right, known):
    back = plus(g_right, times(rows(mats, c, 1), f_left))
    from_left = times(rows(mats, c, 3), f_left)
    from_right = plus(times(rows(mats, c, 4), f_left), times(rows(mats, c, 5), back))
    total = from_left + from_right
    return back, total if known is None else plus(known, total)


def merge_all(part, bit, levels, flags, flows, other, *refs):
    share, known, mats, merged, share_out, inflow = (None, None, *refs) if bit == 0 else refs
    _, height, extra = part
    offset = packed_rows(2 * V, height, extra)
    new_offset = packed_rows(V, height, extra) if bit == levels - 2 else offset
    merge_matrices(bit, levels, flags, flows, other, share, mats, merged, share_out, offset, new_offset)
    merge_flows(part, bit, levels, flags, mats, flows, other, *([] if known is None else [known]), merged, inflow)


def merge_flows(part, bit, levels, flags, mats, flows, other, *refs):
    known, merged, inflow = (None, *refs) if bit == 0 else refs
    right, last_right = flags[3 + bit] == 1, flags[2 + levels] == 1
    last = bit == levels - 2
    c, height, extra = part

    def tile(t):
        at = lambda i: vector_rows(2 * V, i, t, height)
        mine = [flows[at(i), :] for i in range(2 * V)]
        theirs = [other[at(i), :] for i in range(2 * V)]
        f_left = [jnp.where(right, y, x) for x, y in zip(mine[:V], theirs[:V])]
        f_right = [jnp.where(right, x, y) for x, y in zip(mine[:V], theirs[:V])]
        g_left = [jnp.where(right, y, x) for x, y in zip(mine[V:], theirs[V:])]
        g_right = [jnp.where(right, x, y) for x, y in zip(mine[V:], theirs[V:])]
        before = None if known is None else [known[at(i), :] for i in range(2 * V)]
        back, total = inflow_of(c, mats, f_left, g_right, before)
        new_f = plus(f_right, times(rows(mats, c, 0), f_left))
        new_g = plus(g_left, times(rows(mats, c, 2), back))
        if last:
            for i in range(V):
                end = jnp.where(last_right, new_g[i], new_f[i])
                merged[vector_rows(V, i, t, height), :] = end
        else:
            for i, value in enumerate(new_f + new_g):
                merged[at(i), :] = value
        for i, value in enumerate(total):
            inflow[at(i), :] = value

    over_tiles(height, extra, tile)


def last_inflow(right, part, mats, ends, other, known, inflow):
    c, height, extra = part
    for t in range(height + (1 if extra else 0)):
        place = lambda i: vector_rows(V, i, t, height)
        mine = [ends[place(a), :] for a in range(V)]
        theirs = [other[place(a), :] for a in range(V)]
        f_left = [jnp.where(right, y, x) for x, y in zip(mine, theirs)]
        g_right = [jnp.where(right, x, y) for x, y in zip(mine, theirs)]
        before = [known[vector_rows(2 * V, i, t, height), :] for i in range(2 * V)]
        _, total = inflow_of(c, mats, f_left, g_right, before)
        for i, value in enumerate(total):
            inflow[i, t * 8 : t * 8 + 8, :] = jnp.broadcast_to(value, (8, LANES))


def corrected(c, z, a, first, last, g, blocks, inflow):
    total = g[z * V + a, first:last, :]
    for b in range(V):
        total += blocks[c, z * V + a, b : b + 1, :] * inflow[b]
        total += blocks[c, z * V + a, 8 + b : 9 + b, :] * inflow[V + b]
    return total


def correct(part, levels, flags, mats, ends, other, known, blocks, g, result, inflow):
    c = part[0]
    last_inflow(flags[2 + levels] == 1, part, mats, ends, other, known, inflow)
    height = g.shape[1]
    for first, last in ((0, 32), (32, height)) if height > 32 else ((0, height),):
        flow = tuple(inflow[i, first:last, :] for i in range(2 * V))

        def step(z, flow, first=first, last=last):
            for a in range(V):
                result[z * V + a, first:last, :] = corrected(c, z, a, first, last, g, blocks, flow)
            return flow

        lax.fori_loop(0, g.shape[0] // V, step, flow, unroll=2)


def correct_all(part, levels, flags, ends, other, share, known, blocks, g, result, mats, inflow):
    offset = packed_rows(V, *part[1:])
    merge_matrices(levels - 1, levels, flags, ends, other, share, mats, None, None, offset, 0)
    correct(part, levels, flags, mats, ends, other, known, blocks, g, result, inflow)


def finish(levels, flags, mats, blocks, near, *refs):
    count = len(CHUNKS)
    (out, held, sems), inflows = refs[4 * count : 4 * count + 3], refs[4 * count + 3 :]
    right = flags[2 + levels] == 1
    p = flags[0]
    chunks = []
    for i, ((first, last), extra) in enumerate(CHUNKS):
        ends, other, known, g = refs[4 * i : 4 * i + 4]
        height = g.shape[1]
        part = (1, split_height(height, extra), extra)
        last_inflow(right, part, mats, ends, other, known, inflows[i])
        chunks.append((first, last - first, height, extra, g, inflows[i]))
    flows = [tuple(inflow[i] for i in range(2 * V)) for *_, inflow in chunks]

    def step(z, carry):
        for a in range(V):
            j = z * V + a
            row = j * 2 * NT
            held[pl.ds(row + 1 - p, NT, stride=2), :] = near[j, 0:NT, :]
            for (first, width, height, extra, g, _), flow in zip(chunks, flows):
                value = corrected(1, z, a, 0, height, g, blocks, flow)
                held[pl.ds(row + p + 2 * first, width, stride=2), :] = value[:width]
                if extra:
                    held[pl.ds(row + p + 2 * (NT - 1), 1), :] = value[width : width + 1]
        return carry

    cells = near.shape[0] // V
    stops = [cells // 4, cells // 2, cells * 3 // 4, cells - 1, cells]
    copies, cell, row = [], 0, 0
    for i, stop in enumerate(stops):
        lax.fori_loop(cell, stop, step, 0, unroll=2 if (stop - cell) % 2 == 0 else 1)
        size = stop * V * NT * 2 // 8 * 8 - row
        span = pl.ds(row, size)
        copies.append(pltpu.make_async_copy(held.at[span, :], out.at[span, :], sems.at[i]))
        copies[-1].start()
        cell, row = stop, row + size
    for copy in copies:
        copy.wait()


def phase_tables(count):
    angle = 2.0 * math.pi * np.outer(np.arange(1, count + 1), np.arange(NT)) / NT
    cosine, sine = np.cos(angle), np.sin(angle)
    basis = np.zeros((PAD, 2 * count + 8), np.float32)
    basis[:NT, :count], basis[:NT, count : 2 * count], basis[:NT, 2 * count] = cosine.T, sine.T, 0.5
    turned = np.zeros((2, count + 8, 3, DEPTH), np.float32)
    turned[0, :count, :, :NT], turned[1, :count, :, :NT] = cosine[:, None], sine[:, None]
    turned[0, count, :, :NT] = 1.0
    return (2.0 / NT * basis).astype(np.float32), turned.reshape(2 * (count + 8), 3 * DEPTH)


def derivative_table():
    gap = np.arange(NT)[:, None] - np.arange(NT)[None, :]
    safe = np.where(gap == 0, 1.0, np.sin(np.pi * gap / NT))
    table = np.where(gap == 0, 0.0, 0.5 * (1.0 - 2.0 * np.mod(gap, 2)) / safe)
    wide = np.zeros((PAD, 3, DEPTH), np.float32)
    wide[:NT, :, :NT] = table[:, None]
    return wide.reshape(PAD, 3 * DEPTH)


COSTS = (0, 0, 6_000_000_000, 0)


def local(state, advect, viscous, inverse, lower, upper, blades, harmonic):
    cells = state.shape[0]
    count = harmonic.shape[0]
    segs, slabs = lax.axis_size("seg"), lax.axis_size("pitch")
    levels = segs.bit_length() - 1
    far_pairs = [(i, (i - 1) % slabs if i % 2 == 0 else (i + 1) % slabs) for i in range(slabs)]
    near_pairs = [(i, i ^ 1) for i in range(slabs)]
    to_far = lambda x: lax.ppermute(x, "pitch", far_pairs)
    to_level = lambda x, k: lax.ppermute(x, "seg", [(i, i ^ (1 << k)) for i in range(segs)])
    x_shape = (cells * V, PAD, LANES)

    slab, seg = lax.axis_index("pitch"), lax.axis_index("seg")
    side = slab % 2
    wrap = jnp.logical_or(slab == 0, slab == slabs - 1)
    bits = [(seg >> k) & 1 for k in range(levels)]
    run = Chain(
        jnp.stack(
            [side, wrap.astype(jnp.int32), (slab == 0).astype(jnp.int32), *bits]
        ).astype(jnp.int32)
    )
    flat = lambda x: x.transpose(0, 2, 3, 1, 4).reshape(cells * V * V * 2, LANES)
    inv, low, upp = flat(inverse.astype(F32)), flat(lower), flat(upper)
    st = state.transpose(0, 2, 3, 1, 4).reshape(cells * V * NT * 2, LANES)
    lead_rows, edge_rows = LEAD * V * NT, padded_even(V * NT * 2)
    held = pl.BlockSpec(memory_space=pltpu.VMEM)
    shapes = [(lead_rows, LANES), (edge_rows, LANES), (edge_rows, LANES), x_shape, x_shape]
    slab_out, first_cell, last_cell, xn, xf = pl.pallas_call(
        split_cells,
        out_shape=[jax.ShapeDtypeStruct(x, F32) for x in shapes],
        in_specs=[held],
        out_specs=[held] * 5,
        compiler_params=pltpu.CompilerParams(vmem_limit_bytes=16 * MB),
        name="split_cells",
    )(run.before(st))
    halo_near = lax.ppermute(xn, "pitch", near_pairs)
    slab_in = to_far(slab_out)
    from_left = lax.ppermute(last_cell, "seg", [(i, i + 1) for i in range(segs - 1)])
    from_right = lax.ppermute(first_cell, "seg", [(i + 1, i) for i in range(segs - 1)])

    basis, turned = phase_tables(count)
    table = derivative_table()
    wide_harmonic = jnp.broadcast_to(harmonic.astype(F32)[:, None], (count, LANES))

    rest = (cells - LEAD) * V
    chunk_shapes = [
        (rest * (last - first) + (padded_even(rest) if extra else 0), LANES)
        for (first, last), extra in CHUNKS
    ]
    adv = advect.transpose(0, 2, 1, 3).reshape(cells * V * 2, LANES)
    vis = viscous.transpose(0, 2, 1, 3).reshape(cells * V * 2, LANES)
    trig, base, *chunks = run(
        prepare, [(2 * count + 8, LANES), x_shape, *chunk_shapes],
        [xn, xf, wide_harmonic, basis, turned, adv, vis, table], scalars=[blades], name="prepare",
    )
    arrived = [slab_in]
    for chunk in chunks:
        if len(arrived) >= 2:
            chunk, arrived[-2] = lax.optimization_barrier((chunk, arrived[-2]))
        arrived.append(to_far(chunk))
    slab_in, *arrived = arrived

    edges = pltpu.VMEM((2 * V, PAD, LANES), F32)

    mats = []
    mats_shape = (2, 6 * V, 8, LANES)

    def solve_chunk(i):
        height, extra = rows_of(CHUNKS[i]), CHUNKS[i][1]
        tall = packed_rows(2 * V, split_height(height, extra), extra)
        return run(
            functools.partial(far_chunk, CHUNKS[i]),
            [(cells * V, height, LANES), (tall, LANES)],
            [base, lead, arrived[i], from_left, from_right, adv, vis, inv, low, upp],
            scratch=[edges], name="far_chunk",
        )

    class Exchange:
        def __init__(self, c, extra, g, flows, leads=False):
            self.part, self.leads = (c, split_height(g.shape[1], extra), extra), leads
            self.flows, self.known, self.solved, self.level = flows, [], g, 0
            self.scratch = [pltpu.VMEM((2 * V, g.shape[1], LANES), F32)]

        def step(self):
            k = self.level
            behind = k == levels - 2
            inflow = (packed_rows(2 * V, *self.part[1:]), LANES)
            tall = packed_rows(V if behind else 2 * V, *self.part[1:])
            other = to_level(self.flows, k)
            if self.leads:
                tall += padded_even((2 if behind else 6) * V * V)
                out = run(
                    functools.partial(merge_all, self.part, k, levels),
                    [mats_shape, (tall, LANES), (2, 3 * V, 8, LANES), inflow],
                    [self.flows, other, *self.known], name="merge_all",
                )
                mats.append(out[0])
                self.flows, self.known = out[1], out[2:]
            else:
                out = run(
                    functools.partial(merge_flows, self.part, k, levels), [(tall, LANES), inflow],
                    [mats[k], self.flows, other, *self.known], name="merge_flows",
                )
                self.flows, self.known = out[0], out[1:]
            self.level = k + 1

        def send(self):
            self.other = to_level(self.flows, levels - 1)

        def ahead_of(self, later):
            later.flows, self.other = lax.optimization_barrier((later.flows, self.other))

        def last(self):
            return [self.flows, self.other, *self.known]

        def correct(self):
            if self.leads:
                result, last = run(
                    functools.partial(correct_all, self.part, levels), [self.solved.shape, mats_shape],
                    [*self.last(), blocks, self.solved], scratch=self.scratch, name="correct_all",
                )
                mats.append(last)
                return result
            return run(
                functools.partial(correct, self.part, levels), [self.solved.shape],
                [mats[-1], *self.last(), blocks, self.solved], scratch=self.scratch, name="correct",
            )[0]

    base_near = run(
        near_base, [x_shape], [xn, xf, adv, vis, table, trig], name="near_base", flops=COSTS[0]
    )[0]
    blocks, group = run(
        transfer, [(2, cells * V, 16, LANES), (padded_even(6 * V * V), LANES)], [low, upp],
        scratch=[pltpu.VMEM((cells * V, 8, LANES), F32)], name="transfer", flops=COSTS[1],
    )
    lead = run(
        far_lead, [(LEAD * V, PAD, LANES)], [slab_in, trig, basis, turned],
        scratch=[pltpu.VMEM((V, PAD, LANES), F32)], name="far_lead", flops=COSTS[3],
    )[0]
    tall = packed_rows(2 * V, PAD // 8 - 1, True) + group.shape[0]
    first = Exchange(
        0,
        True,
        *run(
            near_cell, [x_shape, (tall, LANES)],
            [base_near, halo_near, from_left, from_right, adv, vis, inv, low, upp, group],
            scratch=[edges], name="near_cell", flops=COSTS[2],
        ),
        leads=True,
    )
    first.step()
    second = Exchange(1, CHUNKS[0][1], *solve_chunk(0))
    for k in range(1, levels - 1):
        first.step()
    first.send()
    second.step()
    third = Exchange(1, CHUNKS[1][1], *solve_chunk(1))
    third.step()
    for k in range(1, levels - 1):
        second.step()
    second.send()
    first.ahead_of(third)
    for k in range(1, levels - 1):
        third.step()
    near = first.correct()
    third.send()
    operands = [mats[-1], blocks, near]
    for item in (second, third):
        operands += [*item.last(), item.solved]
    out = run(
        functools.partial(finish, levels), [st.shape], operands,
        out_specs=[pl.BlockSpec(memory_space=pltpu.HBM)],
        scratch=[pltpu.VMEM(st.shape, F32), pltpu.SemaphoreType.DMA((5,))]
        + [pltpu.VMEM((2 * V, rows_of(chunk), LANES), F32) for chunk in CHUNKS],
        name="finish",
    )[0]
    return out.reshape(cells, V, NT, 2, LANES).transpose(0, 3, 1, 2, 4)


def solution(mesh):
    cell = P("seg", "pitch", None, None, None)
    return jax.shard_map(
        local,
        mesh=mesh,
        in_specs=(cell, P("seg", "pitch", None, None), P("seg", "pitch", None, None), cell, cell, cell, P(), P()),
        out_specs=cell,
        check_vma=False,
    )
```

```python
import functools
import math

import jax
import jax.numpy as jnp
import numpy as np
from jax import lax
from jax.experimental import pallas as pl
from jax.experimental.pallas import tpu as pltpu
from jax.sharding import PartitionSpec as P

F32 = jnp.float32
BF16 = jnp.bfloat16
V = 5
NT = 49
PAD = 56
DEPTH = 64
LANES = 128
LEAD = 4
MB = 1 << 20

CHUNKS = (((0, 32), False), ((32, 48), True))


def rows_of(chunk):
    (first, last), extra = chunk
    return last - first + (8 if extra else 0)


def padded_even(count):
    return (count + 7) // 8 * 8


class Chain:
    def __init__(self, flags):
        self.flags = flags

    def before(self, array):
        return lax.optimization_barrier((self.flags, array))[1]

    def after(self, array):
        self.flags, array = lax.optimization_barrier((self.flags, array))
        return array

    def __call__(self, body, out_shapes, arrays, scratch=(), vmem=16, name=None, grid=None, in_specs=None, out_specs=None, scalars=(), flops=1000):
        smem = pl.BlockSpec(memory_space=pltpu.SMEM)
        held = pl.BlockSpec(memory_space=pltpu.VMEM)
        extra = {} if grid is None else {"grid": grid}
        out = pl.pallas_call(
            body,
            out_shape=[jax.ShapeDtypeStruct(s, F32) for s in out_shapes],
            in_specs=[smem] * (1 + len(scalars)) + (in_specs or [held] * len(arrays)),
            out_specs=out_specs or [held] * len(out_shapes),
            scratch_shapes=list(scratch),
            compiler_params=pltpu.CompilerParams(vmem_limit_bytes=vmem * MB),
            cost_estimate=pl.CostEstimate(flops=flops, bytes_accessed=1000, transcendentals=0),
            name=name,
            **extra,
        )(self.flags, *scalars, *arrays)
        out = list(out)
        out[0] = self.after(out[0])
        return out


def coefficient(ref, z, a, b, p):
    return ref[pl.ds(((z * V + a) * V + b) * 2 + p, 1), :]


def split_left(matrix):
    high = matrix.astype(BF16).astype(F32)
    place = lax.broadcasted_iota(jnp.int32, matrix.shape, 1)
    return jnp.where(place < 2 * DEPTH, high, matrix - high).astype(BF16)


def lag_matrix(basis, turned, trig, sign):
    half = turned.shape[0] // 2
    count = (half - 4) // 8 * 8
    cosine, sine = turned[:half], turned[half:]
    turn, cross = trig[:count, :1], trig[count : 2 * count, :1] * sign
    right = jnp.concatenate(
        [
            turn * cosine[:count] + cross * sine[:count],
            turn * sine[:count] - cross * cosine[:count],
            cosine[count:],
        ],
        axis=0,
    )
    return jnp.dot(basis, right, preferred_element_type=F32, precision=lax.Precision.HIGHEST)


def over_instants(lefts, cells):
    whole = jnp.concatenate(cells, axis=1)
    if whole.shape[0] < DEPTH:
        whole = jnp.concatenate(
            [whole, jnp.zeros((DEPTH - whole.shape[0], whole.shape[1]), F32)], axis=0
        )
    high = whole.astype(BF16)
    low = (whole - high.astype(F32)).astype(BF16)
    right = jnp.concatenate([high, low, high], axis=0)
    products = [jnp.dot(left, right, preferred_element_type=F32) for left in lefts]
    return [[x[:, i * LANES : (i + 1) * LANES] for i in range(len(cells))] for x in products]


def take_rows(ref, start, store):
    store(0, NT - 1, ref[pl.ds(start, NT - 1, stride=2), :])
    store(NT - 1, NT, ref[pl.ds(start + 2 * (NT - 1), 1), :])


def split_cells(st, slab, first_cell, last_cell, xn, xf):
    p = lax.axis_index("pitch") % 2
    edge = first_cell.shape[0]
    zeros = jnp.zeros((8, LANES), F32)
    width = 4 * NT

    def step(i, carry):
        slab[pl.ds(i * width, width), :] = st[pl.ds(i * 2 * width + p, width, stride=2), :]
        return carry

    lax.fori_loop(0, LEAD * V // 4, step, 0)
    first_cell[...] = st[0:edge, :]
    last_cell[...] = st[st.shape[0] - edge :, :]

    def separate(z, carry):
        for v in range(V):
            j = z * V + v
            for out, q in ((xn, 1 - p), (xf, p)):
                out[j, PAD - 8 : PAD, :] = zeros

                def store(first, last, value, out=out, j=j):
                    out[j, first:last, :] = value

                take_rows(st, j * 2 * NT + q, store)
        return carry

    lax.fori_loop(0, xn.shape[0] // V, separate, 0)


def lags(blades, harmonic, trig):
    count = harmonic.shape[0]
    rotor = jnp.full(harmonic.shape, blades[0]).astype(F32)
    stator = jnp.full(harmonic.shape, blades[1]).astype(F32)
    turns = harmonic[...] * stator
    lag = (turns - rotor * jnp.floor(turns / rotor)) / rotor * (2.0 * math.pi)
    trig[0:count, :] = jnp.cos(lag)
    trig[count : 2 * count, :] = jnp.sin(lag)
    trig[2 * count : 2 * count + 8, :] = (stator / rotor / count)[:8]


def own_terms(z, x, other, advect, viscous, p, timing, above, below, base):
    for v in range(V):
        j = z * V + v
        total = viscous[pl.ds(j * 2 + p, 1), :] * (other[j] - 2.0 * x[j]) - timing[v]
        rate = advect[pl.ds(j * 2 + p, 1), :]
        if above and below:
            total += rate * (x[j - V] - x[j + V])
        else:
            total += rate * (x[j - V] if above else -x[j + V])
        base[j] = total


def timing_matrix(table, trig):
    return split_left(table[...] * trig[trig.shape[0] - 8 : trig.shape[0] - 7, :1])


def prepare(flags, blades, xn, xf, harmonic, basis, turned, advect, viscous, table, trig, base, *chunks):
    lags(blades, harmonic, trig)
    p, wrap = flags[0], flags[1]
    cells = xf.shape[0] // V
    sign = jnp.where(flags[2] == 1, 1.0, -1.0)
    lag = split_left(lag_matrix(basis[...], turned[...], trig[...], sign))
    derive = timing_matrix(table, trig)

    def one(z, above=True, below=True, sends=True):
        raw = [xf[z * V + v] for v in range(V)]
        timing, *lagged = over_instants([derive, lag] if sends else [derive], raw)
        own_terms(z, xf, xn, advect, viscous, p, timing, above, below, base)
        if not sends:
            return
        for v in range(V):
            value = jnp.where(wrap == 1, lagged[0][v], raw[v])
            j = (z - LEAD) * V + v
            for out, ((first, last), extra) in zip(chunks, CHUNKS):
                width = last - first
                out[pl.ds(pl.multiple_of(j * width, 8), width), :] = value[first:last]
                if extra:
                    out[pl.ds((cells - LEAD) * V * width + j, 1), :] = value[NT - 1 : NT]

    def early(z, carry):
        one(z, sends=False)
        return carry

    def late(z, carry):
        one(z)
        return carry

    one(0, above=False, sends=False)
    lax.fori_loop(1, LEAD, early, 0)
    one(LEAD)
    lax.fori_loop(LEAD + 1, cells - 1, late, 0, unroll=5)
    one(cells - 1, below=False)


def near_base(flags, xn, xf, advect, viscous, table, trig, base):
    p = 1 - flags[0]
    cells = xn.shape[0] // V
    derive = timing_matrix(table, trig)

    def one(z, above=True, below=True):
        (timing,) = over_instants([derive], [xn[z * V + v] for v in range(V)])
        own_terms(z, xn, xf, advect, viscous, p, timing, above, below, base)

    def inner(z, carry):
        one(z)
        return carry

    one(0, above=False)
    lax.fori_loop(1, cells - 1, inner, 0, unroll=7)
    one(cells - 1, below=False)


def split_height(rows_high, extra):
    return rows_high // 8 - (1 if extra else 0)


def packed_rows(count, height, extra):
    return count * height * 8 + (padded_even(count) if extra else 0)


def vector_rows(count, i, t, height):
    if isinstance(t, int) and t == height:
        return pl.ds(count * height * 8 + i, 1)
    return pl.ds(pl.multiple_of((i * height + t) * 8, 8), 8)


def over_tiles(height, extra, tile):
    lax.fori_loop(0, height, lambda t, carry: (tile(t), carry)[1], 0)
    if extra:
        tile(height)


def keep_tiles(ref, kind, values, first, last, height, extra):
    for a in range(V):
        for t in range(first // 8, last // 8):
            place = vector_rows(2 * V, kind + a, t, height)
            ref[place, :] = values[a][t * 8 - first : t * 8 - first + (1 if t == height else 8)]


def sweeps(source, g, fg, extra, spans, p, inverse, lower, upper, cells):
    height = split_height(g.shape[1], extra)
    for first, last in spans:
        nothing = tuple(jnp.zeros((last - first, LANES), F32) for _ in range(V))

        def ahead(z, current, first=first, last=last):
            right = source(z, first, last)
            result = []
            for a in range(V):
                total = coefficient(inverse, z, a, 0, p) * right[0]
                for b in range(1, V):
                    total += coefficient(inverse, z, a, b, p) * right[b]
                for b in range(V):
                    total += coefficient(lower, z, a, b, p) * current[b]
                g[z * V + a, first:last, :] = total
                result.append(total)
            return tuple(result)

        out = lax.fori_loop(1, cells - 1, ahead, ahead(0, nothing), unroll=2)
        out = ahead(cells - 1, out)
        keep_tiles(fg, 0, out, first, last, height, extra)

        def back(i, current, first=first, last=last):
            z = cells - 1 - i
            result = []
            for a in range(V):
                total = g[z * V + a, first:last, :]
                for b in range(V):
                    total += coefficient(upper, z, a, b, p) * current[b]
                g[z * V + a, first:last, :] = total
                result.append(total)
            return tuple(result)

        out = lax.fori_loop(0, cells, back, nothing, unroll=2)
        keep_tiles(fg, V, out, first, last, height, extra)


def take_edges(edges, from_left, from_right, p):
    skip = from_left.shape[0] - V * NT * 2
    for ref, offset, kind in ((from_left, skip, 0), (from_right, 0, V)):
        for v in range(V):
            edges[kind + v, PAD - 8 : PAD, :] = jnp.zeros((8, LANES), F32)

            def store(first, last, value, i=kind + v):
                edges[i, first:last, :] = value

            take_rows(ref, offset + v * 2 * NT + p, store)


def edge_terms(z, cells, values, edges, advect, p, first, last):
    if not isinstance(z, int):
        return values
    return [
        value
        + (1.0 if z == 0 else -1.0)
        * advect[pl.ds((z * V + v) * 2 + p, 1), :]
        * edges[v if z == 0 else V + v, first:last, :]
        for v, value in enumerate(values)
    ]


def near_cell(
    flags, base, halo, from_left, from_right, advect, viscous, inverse, lower, upper, group,
    g, flows, edges,
):
    p = 1 - flags[0]
    cells = base.shape[0] // V
    take_edges(edges, from_left, from_right, p)

    def source(z, first, last):
        values = []
        for v in range(V):
            j = z * V + v
            values.append(base[j, first:last, :] + viscous[pl.ds(j * 2 + p, 1), :] * halo[j, first:last, :])
        return edge_terms(z, cells, values, edges, advect, p, first, last)

    sweeps(source, g, flows, True, ((0, 32), (32, PAD)), p, inverse, lower, upper, cells)
    flows[flows.shape[0] - group.shape[0] :, :] = group[...]


def far_lead(flags, slab, trig, basis, turned, lead, halo):
    wrap = flags[1]
    sign = jnp.where(flags[2] == 1, -1.0, 1.0)
    left = split_left(lag_matrix(basis[...], turned[...], trig[...], sign))
    for z in range(LEAD):
        for v in range(V):
            halo[v, PAD - 8 : PAD, :] = jnp.zeros((8, LANES), F32)
            halo[v, 0:NT, :] = slab[pl.ds((z * V + v) * NT, NT), :]
        raw = [halo[v] for v in range(V)]
        (lagged,) = over_instants([left], raw)
        for v in range(V):
            lead[z * V + v] = jnp.where(wrap == 1, lagged[v], raw[v])


def far_chunk(chunk, flags, base, lead, halo, from_left, from_right, advect, viscous, inverse, lower, upper, g, fg, edges):
    (first, last), extra = chunk
    width = last - first
    p = flags[0]
    cells = base.shape[0] // V
    top = lax.broadcasted_iota(jnp.int32, (8, LANES), 0) == 0
    take_edges(edges, from_left, from_right, p)

    def pieces(ref, j):
        value = ref[j, first:last, :]
        return jnp.concatenate([value, ref[j, PAD - 8 : PAD, :]], axis=0) if extra else value

    def source(z, start, stop):
        result = []
        for v in range(V):
            j = z * V + v
            h = jnp.maximum(z - LEAD, 0) * V + v
            arrived = halo[pl.ds(pl.multiple_of(h * width, 8), width), :]
            if extra:
                row = halo[pl.ds((cells - LEAD) * V * width + h, 1), :]
                arrived = jnp.concatenate([arrived, jnp.where(top, row, 0.0)], axis=0)
            early = pieces(lead, jnp.minimum(z, LEAD - 1) * V + v)
            arrived = jnp.where(z >= LEAD, arrived, early)
            value = pieces(base, j) + viscous[pl.ds(j * 2 + p, 1), :] * arrived
            if isinstance(z, int):
                rate = advect[pl.ds(j * 2 + p, 1), :]
                edge = pieces(edges, v if z == 0 else V + v)
                value += rate * edge if z == 0 else -rate * edge
            result.append(value)
        return result

    height = rows_of(chunk)
    sweeps(source, g, fg, extra, ((0, height),), p, inverse, lower, upper, cells)


def times(matrix, vector):
    result = []
    for a in range(V):
        total = matrix(a, 0) * vector[0]
        for b in range(1, V):
            total += matrix(a, b) * vector[b]
        result.append(total)
    return result


def plus(one, two):
    return [a + b for a, b in zip(one, two)]


def tiles(ref, c, kind):
    return [ref[c, kind * V + a, 0:V, :] for a in range(V)]


def rows(ref, c, kind):
    return lambda a, b: ref[c, kind * V + a, b : b + 1, :]


def unit(a):
    place = lax.broadcasted_iota(jnp.int32, (8, LANES), 0)
    return jnp.where(place == a, 1.0, 0.0).astype(F32)


def transfer(flags, lower, upper, blocks, group, forward):
    cells = blocks.shape[1] // V
    for c in range(2):
        p = 1 - flags[0] if c == 0 else flags[0]

        def ahead(z, current):
            result = times(lambda a, b: coefficient(lower, z, a, b, p), current)
            for a in range(V):
                forward[z * V + a] = result[a]
            return tuple(result)

        through = lax.fori_loop(0, cells, ahead, tuple(unit(a) for a in range(V)), unroll=4)

        def back(i, current):
            z = cells - 1 - i
            result = times(lambda a, b: coefficient(upper, z, a, b, p), current)
            for a in range(V):
                result[a] = result[a] + jnp.concatenate(
                    [forward[z * V + a], jnp.zeros((8, LANES), F32)], axis=0
                )
                blocks[c, z * V + a] = result[a]
            return tuple(result)

        start = tuple(
            jnp.concatenate([jnp.zeros((8, LANES), F32), unit(a)], axis=0) for a in range(V)
        )
        ends = lax.fori_loop(0, cells, back, start, unroll=4)
        for a in range(V):
            for kind, value in enumerate((ends[a][:V], ends[a][8 : 8 + V], through[a][:V])):
                group[pl.ds(((c * 3 + kind) * V + a) * V, V), :] = value
    group[6 * V * V :, :] = jnp.zeros((group.shape[0] - 6 * V * V, LANES), F32)


def merge_matrices(bit, levels, flags, mine, other, share, mats, merged, share_out, offset, new_offset):
    start, last = bit == 0, bit == levels - 1
    right = flags[3 + bit] == 1
    left = jnp.logical_not(right)
    nothing = jnp.zeros((V, LANES), F32)
    one = [unit(a)[:V] for a in range(V)]
    for c in range(2):
        kinds = 1 if last else 3
        at = lambda ref, kind: [ref[pl.ds(offset + ((c * kinds + kind) * V + a) * V, V), :] for a in range(V)]
        pick = lambda kind, own: [jnp.where(own, m, t) for m, t in zip(at(mine, kind), at(other, kind))]
        if start:
            own = [one, [nothing] * V, one]
        else:
            own = [tiles(share, c, kind) for kind in range(3)]
        found = [
            (1, pick(0, right)),
            (3, [jnp.where(right, x, nothing) for x in own[0]]),
            (4, [jnp.where(right, x, nothing) for x in own[1]]),
            (5, [jnp.where(right, nothing, x) for x in own[2]]),
        ]
        if not last:
            found += [(0, pick(2, right)), (2, pick(1, left))]
        for kind, values in found:
            for a in range(V):
                mats[c, kind * V + a, 0:V, :] = values[a]
        if last:
            continue
        p_left, g_left, h_right = pick(2, left), pick(0, left), pick(1, right)
        turned = times(rows(mats, c, 1), p_left)
        new = [plus(g_left, times(rows(mats, c, 2), turned))]
        if bit < levels - 2:
            new += [times(rows(mats, c, 2), h_right), times(rows(mats, c, 0), p_left)]
        for kind, values in enumerate(new):
            for a in range(V):
                merged[pl.ds(new_offset + ((c * len(new) + kind) * V + a) * V, V), :] = values[a]
        s0 = times(rows(mats, c, 3), p_left)
        s1 = times(rows(mats, c, 4), p_left)
        s1b = times(rows(mats, c, 5), turned)
        s2 = times(rows(mats, c, 5), h_right)
        for a in range(V):
            share_out[c, a, 0:V, :] = jnp.where(right, s0[a], own[0][a])
            share_out[c, V + a, 0:V, :] = jnp.where(right, s1[a], own[1][a] + s1b[a])
            share_out[c, 2 * V + a, 0:V, :] = jnp.where(right, own[2][a], s2[a])


def inflow_of(c, mats, f_left, g_right, known):
    back = plus(g_right, times(rows(mats, c, 1), f_left))
    from_left = times(rows(mats, c, 3), f_left)
    from_right = plus(times(rows(mats, c, 4), f_left), times(rows(mats, c, 5), back))
    total = from_left + from_right
    return back, total if known is None else plus(known, total)


def merge_all(part, bit, levels, flags, flows, other, *refs):
    share, known, mats, merged, share_out, inflow = (None, None, *refs) if bit == 0 else refs
    _, height, extra = part
    offset = packed_rows(2 * V, height, extra)
    new_offset = packed_rows(V, height, extra) if bit == levels - 2 else offset
    merge_matrices(bit, levels, flags, flows, other, share, mats, merged, share_out, offset, new_offset)
    merge_flows(part, bit, levels, flags, mats, flows, other, *([] if known is None else [known]), merged, inflow)


def merge_flows(part, bit, levels, flags, mats, flows, other, *refs):
    known, merged, inflow = (None, *refs) if bit == 0 else refs
    right, last_right = flags[3 + bit] == 1, flags[2 + levels] == 1
    last = bit == levels - 2
    c, height, extra = part

    def tile(t):
        at = lambda i: vector_rows(2 * V, i, t, height)
        mine = [flows[at(i), :] for i in range(2 * V)]
        theirs = [other[at(i), :] for i in range(2 * V)]
        f_left = [jnp.where(right, y, x) for x, y in zip(mine[:V], theirs[:V])]
        f_right = [jnp.where(right, x, y) for x, y in zip(mine[:V], theirs[:V])]
        g_left = [jnp.where(right, y, x) for x, y in zip(mine[V:], theirs[V:])]
        g_right = [jnp.where(right, x, y) for x, y in zip(mine[V:], theirs[V:])]
        before = None if known is None else [known[at(i), :] for i in range(2 * V)]
        back, total = inflow_of(c, mats, f_left, g_right, before)
        new_f = plus(f_right, times(rows(mats, c, 0), f_left))
        new_g = plus(g_left, times(rows(mats, c, 2), back))
        if last:
            for i in range(V):
                end = jnp.where(last_right, new_g[i], new_f[i])
                merged[vector_rows(V, i, t, height), :] = end
        else:
            for i, value in enumerate(new_f + new_g):
                merged[at(i), :] = value
        for i, value in enumerate(total):
            inflow[at(i), :] = value

    over_tiles(height, extra, tile)


def last_inflow(right, part, mats, ends, other, known, inflow):
    c, height, extra = part
    for t in range(height + (1 if extra else 0)):
        place = lambda i: vector_rows(V, i, t, height)
        mine = [ends[place(a), :] for a in range(V)]
        theirs = [other[place(a), :] for a in range(V)]
        f_left = [jnp.where(right, y, x) for x, y in zip(mine, theirs)]
        g_right = [jnp.where(right, x, y) for x, y in zip(mine, theirs)]
        before = [known[vector_rows(2 * V, i, t, height), :] for i in range(2 * V)]
        _, total = inflow_of(c, mats, f_left, g_right, before)
        for i, value in enumerate(total):
            inflow[i, t * 8 : t * 8 + 8, :] = jnp.broadcast_to(value, (8, LANES))


def corrected(c, z, a, first, last, g, blocks, inflow):
    total = g[z * V + a, first:last, :]
    for b in range(V):
        total += blocks[c, z * V + a, b : b + 1, :] * inflow[b]
        total += blocks[c, z * V + a, 8 + b : 9 + b, :] * inflow[V + b]
    return total


def correct(part, levels, flags, mats, ends, other, known, blocks, g, result, inflow):
    c = part[0]
    last_inflow(flags[2 + levels] == 1, part, mats, ends, other, known, inflow)
    height = g.shape[1]
    for first, last in ((0, 32), (32, height)) if height > 32 else ((0, height),):
        flow = tuple(inflow[i, first:last, :] for i in range(2 * V))

        def step(z, flow, first=first, last=last):
            for a in range(V):
                result[z * V + a, first:last, :] = corrected(c, z, a, first, last, g, blocks, flow)
            return flow

        lax.fori_loop(0, g.shape[0] // V, step, flow, unroll=2)


def correct_all(part, levels, flags, ends, other, share, known, blocks, g, result, mats, inflow):
    offset = packed_rows(V, *part[1:])
    merge_matrices(levels - 1, levels, flags, ends, other, share, mats, None, None, offset, 0)
    correct(part, levels, flags, mats, ends, other, known, blocks, g, result, inflow)


def finish(levels, flags, mats, blocks, near, *refs):
    count = len(CHUNKS)
    (out, held, sems), inflows = refs[4 * count : 4 * count + 3], refs[4 * count + 3 :]
    right = flags[2 + levels] == 1
    p = flags[0]
    chunks = []
    for i, ((first, last), extra) in enumerate(CHUNKS):
        ends, other, known, g = refs[4 * i : 4 * i + 4]
        height = g.shape[1]
        part = (1, split_height(height, extra), extra)
        last_inflow(right, part, mats, ends, other, known, inflows[i])
        chunks.append((first, last - first, height, extra, g, inflows[i]))
    flows = [tuple(inflow[i] for i in range(2 * V)) for *_, inflow in chunks]

    def step(z, carry):
        for a in range(V):
            j = z * V + a
            row = j * 2 * NT
            held[pl.ds(row + 1 - p, NT - 1, stride=2), :] = near[j, 0 : NT - 1, :]
            held[pl.ds(row + 1 - p + 2 * (NT - 1), 1), :] = near[j, NT - 1 : NT, :]
            for (first, width, height, extra, g, _), flow in zip(chunks, flows):
                value = corrected(1, z, a, 0, height, g, blocks, flow)
                held[pl.ds(row + p + 2 * first, width, stride=2), :] = value[:width]
                if extra:
                    held[pl.ds(row + p + 2 * (NT - 1), 1), :] = value[width : width + 1]
        return carry

    cells = near.shape[0] // V
    stops = [cells // 4, cells // 2, cells * 3 // 4, cells - 1, cells]
    copies, cell, row = [], 0, 0
    for i, stop in enumerate(stops):
        lax.fori_loop(cell, stop, step, 0, unroll=2 if (stop - cell) % 2 == 0 else 1)
        size = stop * V * NT * 2 // 8 * 8 - row
        span = pl.ds(row, size)
        copies.append(pltpu.make_async_copy(held.at[span, :], out.at[span, :], sems.at[i]))
        copies[-1].start()
        cell, row = stop, row + size
    for copy in copies:
        copy.wait()


def phase_tables(count):
    angle = 2.0 * math.pi * np.outer(np.arange(1, count + 1), np.arange(NT)) / NT
    cosine, sine = np.cos(angle), np.sin(angle)
    basis = np.zeros((PAD, 2 * count + 8), np.float32)
    basis[:NT, :count], basis[:NT, count : 2 * count], basis[:NT, 2 * count] = cosine.T, sine.T, 0.5
    turned = np.zeros((2, count + 8, 3, DEPTH), np.float32)
    turned[0, :count, :, :NT], turned[1, :count, :, :NT] = cosine[:, None], sine[:, None]
    turned[0, count, :, :NT] = 1.0
    return (2.0 / NT * basis).astype(np.float32), turned.reshape(2 * (count + 8), 3 * DEPTH)


def derivative_table():
    gap = np.arange(NT)[:, None] - np.arange(NT)[None, :]
    safe = np.where(gap == 0, 1.0, np.sin(np.pi * gap / NT))
    table = np.where(gap == 0, 0.0, 0.5 * (1.0 - 2.0 * np.mod(gap, 2)) / safe)
    wide = np.zeros((PAD, 3, DEPTH), np.float32)
    wide[:NT, :, :NT] = table[:, None]
    return wide.reshape(PAD, 3 * DEPTH)


COSTS = (0, 0, 6_000_000_000, 0)


def local(state, advect, viscous, inverse, lower, upper, blades, harmonic):
    cells = state.shape[0]
    count = harmonic.shape[0]
    segs, slabs = lax.axis_size("seg"), lax.axis_size("pitch")
    levels = segs.bit_length() - 1
    far_pairs = [(i, (i - 1) % slabs if i % 2 == 0 else (i + 1) % slabs) for i in range(slabs)]
    near_pairs = [(i, i ^ 1) for i in range(slabs)]
    to_far = lambda x: lax.ppermute(x, "pitch", far_pairs)
    to_level = lambda x, k: lax.ppermute(x, "seg", [(i, i ^ (1 << k)) for i in range(segs)])
    x_shape = (cells * V, PAD, LANES)

    slab, seg = lax.axis_index("pitch"), lax.axis_index("seg")
    side = slab % 2
    wrap = jnp.logical_or(slab == 0, slab == slabs - 1)
    bits = [(seg >> k) & 1 for k in range(levels)]
    run = Chain(
        jnp.stack(
            [side, wrap.astype(jnp.int32), (slab == 0).astype(jnp.int32), *bits]
        ).astype(jnp.int32)
    )
    flat = lambda x: x.transpose(0, 2, 3, 1, 4).reshape(cells * V * V * 2, LANES)
    inv, low, upp = flat(inverse.astype(F32)), flat(lower), flat(upper)
    st = state.transpose(0, 2, 3, 1, 4).reshape(cells * V * NT * 2, LANES)
    lead_rows, edge_rows = LEAD * V * NT, padded_even(V * NT * 2)
    held = pl.BlockSpec(memory_space=pltpu.VMEM)
    shapes = [(lead_rows, LANES), (edge_rows, LANES), (edge_rows, LANES), x_shape, x_shape]
    slab_out, first_cell, last_cell, xn, xf = pl.pallas_call(
        split_cells,
        out_shape=[jax.ShapeDtypeStruct(x, F32) for x in shapes],
        in_specs=[held],
        out_specs=[held] * 5,
        compiler_params=pltpu.CompilerParams(vmem_limit_bytes=16 * MB),
        name="split_cells",
    )(run.before(st))
    halo_near = lax.ppermute(xn, "pitch", near_pairs)
    slab_in = to_far(slab_out)
    from_left = lax.ppermute(last_cell, "seg", [(i, i + 1) for i in range(segs - 1)])
    from_right = lax.ppermute(first_cell, "seg", [(i + 1, i) for i in range(segs - 1)])

    basis, turned = phase_tables(count)
    table = derivative_table()
    wide_harmonic = jnp.broadcast_to(harmonic.astype(F32)[:, None], (count, LANES))

    rest = (cells - LEAD) * V
    chunk_shapes = [
        (rest * (last - first) + (padded_even(rest) if extra else 0), LANES)
        for (first, last), extra in CHUNKS
    ]
    adv = advect.transpose(0, 2, 1, 3).reshape(cells * V * 2, LANES)
    vis = viscous.transpose(0, 2, 1, 3).reshape(cells * V * 2, LANES)
    trig, base, *chunks = run(
        prepare, [(2 * count + 8, LANES), x_shape, *chunk_shapes],
        [xn, xf, wide_harmonic, basis, turned, adv, vis, table], scalars=[blades], name="prepare",
    )
    arrived = [slab_in]
    for chunk in chunks:
        if len(arrived) >= 2:
            chunk, arrived[-2] = lax.optimization_barrier((chunk, arrived[-2]))
        arrived.append(to_far(chunk))
    slab_in, *arrived = arrived

    edges = pltpu.VMEM((2 * V, PAD, LANES), F32)

    mats = []
    mats_shape = (2, 6 * V, 8, LANES)

    def solve_chunk(i):
        height, extra = rows_of(CHUNKS[i]), CHUNKS[i][1]
        tall = packed_rows(2 * V, split_height(height, extra), extra)
        return run(
            functools.partial(far_chunk, CHUNKS[i]),
            [(cells * V, height, LANES), (tall, LANES)],
            [base, lead, arrived[i], from_left, from_right, adv, vis, inv, low, upp],
            scratch=[edges], name="far_chunk",
        )

    class Exchange:
        def __init__(self, c, extra, g, flows, leads=False):
            self.part, self.leads = (c, split_height(g.shape[1], extra), extra), leads
            self.flows, self.known, self.solved, self.level = flows, [], g, 0
            self.scratch = [pltpu.VMEM((2 * V, g.shape[1], LANES), F32)]

        def step(self):
            k = self.level
            behind = k == levels - 2
            inflow = (packed_rows(2 * V, *self.part[1:]), LANES)
            tall = packed_rows(V if behind else 2 * V, *self.part[1:])
            other = to_level(self.flows, k)
            if self.leads:
                tall += padded_even((2 if behind else 6) * V * V)
                out = run(
                    functools.partial(merge_all, self.part, k, levels),
                    [mats_shape, (tall, LANES), (2, 3 * V, 8, LANES), inflow],
                    [self.flows, other, *self.known], name="merge_all",
                )
                mats.append(out[0])
                self.flows, self.known = out[1], out[2:]
            else:
                out = run(
                    functools.partial(merge_flows, self.part, k, levels), [(tall, LANES), inflow],
                    [mats[k], self.flows, other, *self.known], name="merge_flows",
                )
                self.flows, self.known = out[0], out[1:]
            self.level = k + 1

        def send(self):
            self.other = to_level(self.flows, levels - 1)

        def ahead_of(self, later):
            later.flows, self.other = lax.optimization_barrier((later.flows, self.other))

        def last(self):
            return [self.flows, self.other, *self.known]

        def correct(self):
            if self.leads:
                result, last = run(
                    functools.partial(correct_all, self.part, levels), [self.solved.shape, mats_shape],
                    [*self.last(), blocks, self.solved], scratch=self.scratch, name="correct_all",
                )
                mats.append(last)
                return result
            return run(
                functools.partial(correct, self.part, levels), [self.solved.shape],
                [mats[-1], *self.last(), blocks, self.solved], scratch=self.scratch, name="correct",
            )[0]

    base_near = run(
        near_base, [x_shape], [xn, xf, adv, vis, table, trig], name="near_base", flops=COSTS[0]
    )[0]
    blocks, group = run(
        transfer, [(2, cells * V, 16, LANES), (padded_even(6 * V * V), LANES)], [low, upp],
        scratch=[pltpu.VMEM((cells * V, 8, LANES), F32)], name="transfer", flops=COSTS[1],
    )
    lead = run(
        far_lead, [(LEAD * V, PAD, LANES)], [slab_in, trig, basis, turned],
        scratch=[pltpu.VMEM((V, PAD, LANES), F32)], name="far_lead", flops=COSTS[3],
    )[0]
    tall = packed_rows(2 * V, PAD // 8 - 1, True) + group.shape[0]
    first = Exchange(
        0,
        True,
        *run(
            near_cell, [x_shape, (tall, LANES)],
            [base_near, halo_near, from_left, from_right, adv, vis, inv, low, upp, group],
            scratch=[edges], name="near_cell", flops=COSTS[2],
        ),
        leads=True,
    )
    first.step()
    second = Exchange(1, CHUNKS[0][1], *solve_chunk(0))
    for k in range(1, levels - 1):
        first.step()
    first.send()
    second.step()
    third = Exchange(1, CHUNKS[1][1], *solve_chunk(1))
    third.step()
    for k in range(1, levels - 1):
        second.step()
    second.send()
    first.ahead_of(third)
    for k in range(1, levels - 1):
        third.step()
    near = first.correct()
    third.send()
    operands = [mats[-1], blocks, near]
    for item in (second, third):
        operands += [*item.last(), item.solved]
    out = run(
        functools.partial(finish, levels), [st.shape], operands,
        out_specs=[pl.BlockSpec(memory_space=pltpu.HBM)],
        scratch=[pltpu.VMEM((st.shape[0] + 8, LANES), F32), pltpu.SemaphoreType.DMA((5,))]
        + [pltpu.VMEM((2 * V, rows_of(chunk), LANES), F32) for chunk in CHUNKS],
        name="finish",
    )[0]
    return out.reshape(cells, V, NT, 2, LANES).transpose(0, 3, 1, 2, 4)


def solution(mesh):
    cell = P("seg", "pitch", None, None, None)
    return jax.shard_map(
        local,
        mesh=mesh,
        in_specs=(cell, P("seg", "pitch", None, None), P("seg", "pitch", None, None), cell, cell, cell, P(), P()),
        out_specs=cell,
        check_vma=False,
    )
```

```python
import functools
import math

import jax
import jax.numpy as jnp
import numpy as np
from jax import lax
from jax.experimental import pallas as pl
from jax.experimental.pallas import tpu as pltpu
from jax.sharding import PartitionSpec as P

F32 = jnp.float32
BF16 = jnp.bfloat16
V = 5
NT = 49
PAD = 56
DEPTH = 64
LANES = 128
LEAD = 4
MB = 1 << 20

CHUNKS = (((0, 32), False), ((32, 48), True))


def rows_of(chunk):
    (first, last), extra = chunk
    return last - first + (8 if extra else 0)


def padded_even(count):
    return (count + 7) // 8 * 8


class Chain:
    def __init__(self, flags):
        self.flags = flags

    def before(self, array):
        return lax.optimization_barrier((self.flags, array))[1]

    def after(self, array):
        self.flags, array = lax.optimization_barrier((self.flags, array))
        return array

    def __call__(self, body, out_shapes, arrays, scratch=(), vmem=16, name=None, grid=None, in_specs=None, out_specs=None, scalars=(), flops=1000):
        smem = pl.BlockSpec(memory_space=pltpu.SMEM)
        held = pl.BlockSpec(memory_space=pltpu.VMEM)
        extra = {} if grid is None else {"grid": grid}
        out = pl.pallas_call(
            body,
            out_shape=[jax.ShapeDtypeStruct(s, F32) for s in out_shapes],
            in_specs=[smem] * (1 + len(scalars)) + (in_specs or [held] * len(arrays)),
            out_specs=out_specs or [held] * len(out_shapes),
            scratch_shapes=list(scratch),
            compiler_params=pltpu.CompilerParams(vmem_limit_bytes=vmem * MB),
            cost_estimate=pl.CostEstimate(flops=flops, bytes_accessed=1000, transcendentals=0),
            name=name,
            **extra,
        )(self.flags, *scalars, *arrays)
        out = list(out)
        out[0] = self.after(out[0])
        return out


def coefficient(ref, z, a, b, p):
    return ref[pl.ds(((z * V + a) * V + b) * 2 + p, 1), :]


def split_left(matrix):
    high = matrix.astype(BF16).astype(F32)
    place = lax.broadcasted_iota(jnp.int32, matrix.shape, 1)
    return jnp.where(place < 2 * DEPTH, high, matrix - high).astype(BF16)


def lag_matrix(basis, turned, trig, sign):
    half = turned.shape[0] // 2
    count = (half - 4) // 8 * 8
    cosine, sine = turned[:half], turned[half:]
    turn, cross = trig[:count, :1], trig[count : 2 * count, :1] * sign
    right = jnp.concatenate(
        [
            turn * cosine[:count] + cross * sine[:count],
            turn * sine[:count] - cross * cosine[:count],
            cosine[count:],
        ],
        axis=0,
    )
    return jnp.dot(basis, right, preferred_element_type=F32, precision=lax.Precision.HIGHEST)


def over_instants(lefts, cells):
    whole = jnp.concatenate(cells, axis=1)
    if whole.shape[0] < DEPTH:
        whole = jnp.concatenate(
            [whole, jnp.zeros((DEPTH - whole.shape[0], whole.shape[1]), F32)], axis=0
        )
    high = whole.astype(BF16)
    low = (whole - high.astype(F32)).astype(BF16)
    right = jnp.concatenate([high, low, high], axis=0)
    products = [jnp.dot(left, right, preferred_element_type=F32) for left in lefts]
    return [[x[:, i * LANES : (i + 1) * LANES] for i in range(len(cells))] for x in products]


def take_rows(ref, start, store):
    store(0, NT - 1, ref[pl.ds(start, NT - 1, stride=2), :])
    store(NT - 1, NT, ref[pl.ds(start + 2 * (NT - 1), 1), :])


def split_cells(st, slab, first_cell, last_cell, xn, xf):
    p = lax.axis_index("pitch") % 2
    edge = first_cell.shape[0]
    zeros = jnp.zeros((8, LANES), F32)
    width = 4 * NT

    def step(i, carry):
        slab[pl.ds(i * width, width), :] = st[pl.ds(i * 2 * width + p, width, stride=2), :]
        return carry

    lax.fori_loop(0, LEAD * V // 4, step, 0)
    first_cell[...] = st[0:edge, :]
    last_cell[...] = st[st.shape[0] - edge :, :]

    def separate(z, carry):
        for v in range(V):
            j = z * V + v
            for out, q in ((xn, 1 - p), (xf, p)):
                out[j, PAD - 8 : PAD, :] = zeros

                def store(first, last, value, out=out, j=j):
                    out[j, first:last, :] = value

                take_rows(st, j * 2 * NT + q, store)
        return carry

    lax.fori_loop(0, xn.shape[0] // V, separate, 0)


def lags(blades, harmonic, trig):
    count = harmonic.shape[0]
    rotor = jnp.full(harmonic.shape, blades[0]).astype(F32)
    stator = jnp.full(harmonic.shape, blades[1]).astype(F32)
    turns = harmonic[...] * stator
    lag = (turns - rotor * jnp.floor(turns / rotor)) / rotor * (2.0 * math.pi)
    trig[0:count, :] = jnp.cos(lag)
    trig[count : 2 * count, :] = jnp.sin(lag)
    trig[2 * count : 2 * count + 8, :] = (stator / rotor / count)[:8]


def own_terms(z, x, other, advect, viscous, p, timing, above, below, base):
    for v in range(V):
        j = z * V + v
        total = viscous[pl.ds(j * 2 + p, 1), :] * (other[j] - 2.0 * x[j]) - timing[v]
        rate = advect[pl.ds(j * 2 + p, 1), :]
        if above and below:
            total += rate * (x[j - V] - x[j + V])
        else:
            total += rate * (x[j - V] if above else -x[j + V])
        base[j] = total


def timing_matrix(table, trig):
    return split_left(table[...] * trig[trig.shape[0] - 8 : trig.shape[0] - 7, :1])


def prepare(flags, blades, xn, xf, harmonic, basis, turned, advect, viscous, table, trig, base, *chunks):
    lags(blades, harmonic, trig)
    p, wrap = flags[0], flags[1]
    cells = xf.shape[0] // V
    sign = jnp.where(flags[2] == 1, 1.0, -1.0)
    lag = split_left(lag_matrix(basis[...], turned[...], trig[...], sign))
    derive = timing_matrix(table, trig)

    def one(z, above=True, below=True, sends=True):
        raw = [xf[z * V + v] for v in range(V)]
        timing, *lagged = over_instants([derive, lag] if sends else [derive], raw)
        own_terms(z, xf, xn, advect, viscous, p, timing, above, below, base)
        if not sends:
            return
        for v in range(V):
            value = jnp.where(wrap == 1, lagged[0][v], raw[v])
            j = (z - LEAD) * V + v
            for out, ((first, last), extra) in zip(chunks, CHUNKS):
                width = last - first
                out[pl.ds(pl.multiple_of(j * width, 8), width), :] = value[first:last]
                if extra:
                    out[pl.ds((cells - LEAD) * V * width + j, 1), :] = value[NT - 1 : NT]

    def early(z, carry):
        one(z, sends=False)
        return carry

    def late(z, carry):
        one(z)
        return carry

    one(0, above=False, sends=False)
    lax.fori_loop(1, LEAD, early, 0)
    one(LEAD)
    lax.fori_loop(LEAD + 1, cells - 1, late, 0, unroll=5)
    one(cells - 1, below=False)


def near_base(flags, xn, xf, advect, viscous, table, trig, base):
    p = 1 - flags[0]
    cells = xn.shape[0] // V
    derive = timing_matrix(table, trig)

    def one(z, above=True, below=True):
        (timing,) = over_instants([derive], [xn[z * V + v] for v in range(V)])
        own_terms(z, xn, xf, advect, viscous, p, timing, above, below, base)

    def inner(z, carry):
        one(z)
        return carry

    one(0, above=False)
    lax.fori_loop(1, cells - 1, inner, 0, unroll=7)
    one(cells - 1, below=False)


def split_height(rows_high, extra):
    return rows_high // 8 - (1 if extra else 0)


def packed_rows(count, height, extra):
    return count * height * 8 + (padded_even(count) if extra else 0)


def vector_rows(count, i, t, height):
    if isinstance(t, int) and t == height:
        return pl.ds(count * height * 8 + i, 1)
    return pl.ds(pl.multiple_of((i * height + t) * 8, 8), 8)


def over_tiles(height, extra, tile):
    lax.fori_loop(0, height, lambda t, carry: (tile(t), carry)[1], 0)
    if extra:
        tile(height)


def keep_tiles(ref, kind, values, first, last, height, extra):
    for a in range(V):
        for t in range(first // 8, last // 8):
            place = vector_rows(2 * V, kind + a, t, height)
            ref[place, :] = values[a][t * 8 - first : t * 8 - first + (1 if t == height else 8)]


def sweeps(source, g, fg, extra, spans, p, inverse, lower, upper, cells):
    height = split_height(g.shape[1], extra)
    for first, last in spans:
        nothing = tuple(jnp.zeros((last - first, LANES), F32) for _ in range(V))

        def ahead(z, current, first=first, last=last):
            right = source(z, first, last)
            result = []
            for a in range(V):
                total = coefficient(inverse, z, a, 0, p) * right[0]
                for b in range(1, V):
                    total += coefficient(inverse, z, a, b, p) * right[b]
                for b in range(V):
                    total += coefficient(lower, z, a, b, p) * current[b]
                g[z * V + a, first:last, :] = total
                result.append(total)
            return tuple(result)

        out = lax.fori_loop(1, cells - 1, ahead, ahead(0, nothing), unroll=7)
        out = ahead(cells - 1, out)
        keep_tiles(fg, 0, out, first, last, height, extra)

        def back(i, current, first=first, last=last):
            z = cells - 1 - i
            result = []
            for a in range(V):
                total = g[z * V + a, first:last, :]
                for b in range(V):
                    total += coefficient(upper, z, a, b, p) * current[b]
                g[z * V + a, first:last, :] = total
                result.append(total)
            return tuple(result)

        out = lax.fori_loop(0, cells, back, nothing, unroll=4)
        keep_tiles(fg, V, out, first, last, height, extra)


def take_edges(edges, from_left, from_right, p):
    skip = from_left.shape[0] - V * NT * 2
    for ref, offset, kind in ((from_left, skip, 0), (from_right, 0, V)):
        for v in range(V):
            edges[kind + v, PAD - 8 : PAD, :] = jnp.zeros((8, LANES), F32)

            def store(first, last, value, i=kind + v):
                edges[i, first:last, :] = value

            take_rows(ref, offset + v * 2 * NT + p, store)


def edge_terms(z, cells, values, edges, advect, p, first, last):
    if not isinstance(z, int):
        return values
    return [
        value
        + (1.0 if z == 0 else -1.0)
        * advect[pl.ds((z * V + v) * 2 + p, 1), :]
        * edges[v if z == 0 else V + v, first:last, :]
        for v, value in enumerate(values)
    ]


def near_cell(
    flags, base, halo, from_left, from_right, advect, viscous, inverse, lower, upper, group,
    g, flows, edges,
):
    p = 1 - flags[0]
    cells = base.shape[0] // V
    take_edges(edges, from_left, from_right, p)

    def source(z, first, last):
        values = []
        for v in range(V):
            j = z * V + v
            values.append(base[j, first:last, :] + viscous[pl.ds(j * 2 + p, 1), :] * halo[j, first:last, :])
        return edge_terms(z, cells, values, edges, advect, p, first, last)

    sweeps(source, g, flows, True, ((0, 32), (32, PAD)), p, inverse, lower, upper, cells)
    flows[flows.shape[0] - group.shape[0] :, :] = group[...]


def far_lead(flags, slab, trig, basis, turned, lead, halo):
    wrap = flags[1]
    sign = jnp.where(flags[2] == 1, -1.0, 1.0)
    left = split_left(lag_matrix(basis[...], turned[...], trig[...], sign))
    for z in range(LEAD):
        for v in range(V):
            halo[v, PAD - 8 : PAD, :] = jnp.zeros((8, LANES), F32)
            halo[v, 0:NT, :] = slab[pl.ds((z * V + v) * NT, NT), :]
        raw = [halo[v] for v in range(V)]
        (lagged,) = over_instants([left], raw)
        for v in range(V):
            lead[z * V + v] = jnp.where(wrap == 1, lagged[v], raw[v])


def far_chunk(chunk, flags, base, lead, halo, from_left, from_right, advect, viscous, inverse, lower, upper, g, fg, edges):
    (first, last), extra = chunk
    width = last - first
    p = flags[0]
    cells = base.shape[0] // V
    top = lax.broadcasted_iota(jnp.int32, (8, LANES), 0) == 0
    take_edges(edges, from_left, from_right, p)

    def pieces(ref, j):
        value = ref[j, first:last, :]
        return jnp.concatenate([value, ref[j, PAD - 8 : PAD, :]], axis=0) if extra else value

    def source(z, start, stop):
        result = []
        for v in range(V):
            j = z * V + v
            h = jnp.maximum(z - LEAD, 0) * V + v
            arrived = halo[pl.ds(pl.multiple_of(h * width, 8), width), :]
            if extra:
                row = halo[pl.ds((cells - LEAD) * V * width + h, 1), :]
                arrived = jnp.concatenate([arrived, jnp.where(top, row, 0.0)], axis=0)
            early = pieces(lead, jnp.minimum(z, LEAD - 1) * V + v)
            arrived = jnp.where(z >= LEAD, arrived, early)
            value = pieces(base, j) + viscous[pl.ds(j * 2 + p, 1), :] * arrived
            if isinstance(z, int):
                rate = advect[pl.ds(j * 2 + p, 1), :]
                edge = pieces(edges, v if z == 0 else V + v)
                value += rate * edge if z == 0 else -rate * edge
            result.append(value)
        return result

    height = rows_of(chunk)
    sweeps(source, g, fg, extra, ((0, height),), p, inverse, lower, upper, cells)


def times(matrix, vector):
    result = []
    for a in range(V):
        total = matrix(a, 0) * vector[0]
        for b in range(1, V):
            total += matrix(a, b) * vector[b]
        result.append(total)
    return result


def plus(one, two):
    return [a + b for a, b in zip(one, two)]


def tiles(ref, c, kind):
    return [ref[c, kind * V + a, 0:V, :] for a in range(V)]


def rows(ref, c, kind):
    return lambda a, b: ref[c, kind * V + a, b : b + 1, :]


def unit(a):
    place = lax.broadcasted_iota(jnp.int32, (8, LANES), 0)
    return jnp.where(place == a, 1.0, 0.0).astype(F32)


def transfer(flags, lower, upper, blocks, group, forward):
    cells = blocks.shape[1] // V
    for c in range(2):
        p = 1 - flags[0] if c == 0 else flags[0]

        def ahead(z, current):
            result = times(lambda a, b: coefficient(lower, z, a, b, p), current)
            for a in range(V):
                forward[z * V + a] = result[a]
            return tuple(result)

        through = lax.fori_loop(0, cells, ahead, tuple(unit(a) for a in range(V)), unroll=4)

        def back(i, current):
            z = cells - 1 - i
            result = times(lambda a, b: coefficient(upper, z, a, b, p), current)
            for a in range(V):
                result[a] = result[a] + jnp.concatenate(
                    [forward[z * V + a], jnp.zeros((8, LANES), F32)], axis=0
                )
                blocks[c, z * V + a] = result[a]
            return tuple(result)

        start = tuple(
            jnp.concatenate([jnp.zeros((8, LANES), F32), unit(a)], axis=0) for a in range(V)
        )
        ends = lax.fori_loop(0, cells, back, start, unroll=4)
        for a in range(V):
            for kind, value in enumerate((ends[a][:V], ends[a][8 : 8 + V], through[a][:V])):
                group[pl.ds(((c * 3 + kind) * V + a) * V, V), :] = value
    group[6 * V * V :, :] = jnp.zeros((group.shape[0] - 6 * V * V, LANES), F32)


def merge_matrices(bit, levels, flags, mine, other, share, mats, merged, share_out, offset, new_offset):
    start, last = bit == 0, bit == levels - 1
    right = flags[3 + bit] == 1
    left = jnp.logical_not(right)
    nothing = jnp.zeros((V, LANES), F32)
    one = [unit(a)[:V] for a in range(V)]
    for c in range(2):
        kinds = 1 if last else 3
        at = lambda ref, kind: [ref[pl.ds(offset + ((c * kinds + kind) * V + a) * V, V), :] for a in range(V)]
        pick = lambda kind, own: [jnp.where(own, m, t) for m, t in zip(at(mine, kind), at(other, kind))]
        if start:
            own = [one, [nothing] * V, one]
        else:
            own = [tiles(share, c, kind) for kind in range(3)]
        found = [
            (1, pick(0, right)),
            (3, [jnp.where(right, x, nothing) for x in own[0]]),
            (4, [jnp.where(right, x, nothing) for x in own[1]]),
            (5, [jnp.where(right, nothing, x) for x in own[2]]),
        ]
        if not last:
            found += [(0, pick(2, right)), (2, pick(1, left))]
        for kind, values in found:
            for a in range(V):
                mats[c, kind * V + a, 0:V, :] = values[a]
        if last:
            continue
        p_left, g_left, h_right = pick(2, left), pick(0, left), pick(1, right)
        turned = times(rows(mats, c, 1), p_left)
        new = [plus(g_left, times(rows(mats, c, 2), turned))]
        if bit < levels - 2:
            new += [times(rows(mats, c, 2), h_right), times(rows(mats, c, 0), p_left)]
        for kind, values in enumerate(new):
            for a in range(V):
                merged[pl.ds(new_offset + ((c * len(new) + kind) * V + a) * V, V), :] = values[a]
        s0 = times(rows(mats, c, 3), p_left)
        s1 = times(rows(mats, c, 4), p_left)
        s1b = times(rows(mats, c, 5), turned)
        s2 = times(rows(mats, c, 5), h_right)
        for a in range(V):
            share_out[c, a, 0:V, :] = jnp.where(right, s0[a], own[0][a])
            share_out[c, V + a, 0:V, :] = jnp.where(right, s1[a], own[1][a] + s1b[a])
            share_out[c, 2 * V + a, 0:V, :] = jnp.where(right, own[2][a], s2[a])


def inflow_of(c, mats, f_left, g_right, known):
    back = plus(g_right, times(rows(mats, c, 1), f_left))
    from_left = times(rows(mats, c, 3), f_left)
    from_right = plus(times(rows(mats, c, 4), f_left), times(rows(mats, c, 5), back))
    total = from_left + from_right
    return back, total if known is None else plus(known, total)


def merge_all(part, bit, levels, flags, flows, other, *refs):
    share, known, mats, merged, share_out, inflow = (None, None, *refs) if bit == 0 else refs
    _, height, extra = part
    offset = packed_rows(2 * V, height, extra)
    new_offset = packed_rows(V, height, extra) if bit == levels - 2 else offset
    merge_matrices(bit, levels, flags, flows, other, share, mats, merged, share_out, offset, new_offset)
    merge_flows(part, bit, levels, flags, mats, flows, other, *([] if known is None else [known]), merged, inflow)


def merge_flows(part, bit, levels, flags, mats, flows, other, *refs):
    known, merged, inflow = (None, *refs) if bit == 0 else refs
    right, last_right = flags[3 + bit] == 1, flags[2 + levels] == 1
    last = bit == levels - 2
    c, height, extra = part

    def tile(t):
        at = lambda i: vector_rows(2 * V, i, t, height)
        mine = [flows[at(i), :] for i in range(2 * V)]
        theirs = [other[at(i), :] for i in range(2 * V)]
        f_left = [jnp.where(right, y, x) for x, y in zip(mine[:V], theirs[:V])]
        f_right = [jnp.where(right, x, y) for x, y in zip(mine[:V], theirs[:V])]
        g_left = [jnp.where(right, y, x) for x, y in zip(mine[V:], theirs[V:])]
        g_right = [jnp.where(right, x, y) for x, y in zip(mine[V:], theirs[V:])]
        before = None if known is None else [known[at(i), :] for i in range(2 * V)]
        back, total = inflow_of(c, mats, f_left, g_right, before)
        new_f = plus(f_right, times(rows(mats, c, 0), f_left))
        new_g = plus(g_left, times(rows(mats, c, 2), back))
        if last:
            for i in range(V):
                end = jnp.where(last_right, new_g[i], new_f[i])
                merged[vector_rows(V, i, t, height), :] = end
        else:
            for i, value in enumerate(new_f + new_g):
                merged[at(i), :] = value
        for i, value in enumerate(total):
            inflow[at(i), :] = value

    over_tiles(height, extra, tile)


def last_inflow(right, part, mats, ends, other, known, inflow):
    c, height, extra = part
    for t in range(height + (1 if extra else 0)):
        place = lambda i: vector_rows(V, i, t, height)
        mine = [ends[place(a), :] for a in range(V)]
        theirs = [other[place(a), :] for a in range(V)]
        f_left = [jnp.where(right, y, x) for x, y in zip(mine, theirs)]
        g_right = [jnp.where(right, x, y) for x, y in zip(mine, theirs)]
        before = [known[vector_rows(2 * V, i, t, height), :] for i in range(2 * V)]
        _, total = inflow_of(c, mats, f_left, g_right, before)
        for i, value in enumerate(total):
            inflow[i, t * 8 : t * 8 + 8, :] = jnp.broadcast_to(value, (8, LANES))


def corrected(c, z, a, first, last, g, blocks, inflow):
    total = g[z * V + a, first:last, :]
    for b in range(V):
        total += blocks[c, z * V + a, b : b + 1, :] * inflow[b]
        total += blocks[c, z * V + a, 8 + b : 9 + b, :] * inflow[V + b]
    return total


def correct(part, levels, flags, mats, ends, other, known, blocks, g, result, inflow):
    c = part[0]
    last_inflow(flags[2 + levels] == 1, part, mats, ends, other, known, inflow)
    height = g.shape[1]
    for first, last in ((0, 32), (32, height)) if height > 32 else ((0, height),):
        flow = tuple(inflow[i, first:last, :] for i in range(2 * V))

        def step(z, flow, first=first, last=last):
            for a in range(V):
                result[z * V + a, first:last, :] = corrected(c, z, a, first, last, g, blocks, flow)
            return flow

        lax.fori_loop(0, g.shape[0] // V, step, flow, unroll=4)


def correct_all(part, levels, flags, ends, other, share, known, blocks, g, result, mats, inflow):
    offset = packed_rows(V, *part[1:])
    merge_matrices(levels - 1, levels, flags, ends, other, share, mats, None, None, offset, 0)
    correct(part, levels, flags, mats, ends, other, known, blocks, g, result, inflow)


def finish(levels, flags, mats, blocks, near, *refs):
    count = len(CHUNKS)
    (out, held, sems), inflows = refs[4 * count : 4 * count + 3], refs[4 * count + 3 :]
    right = flags[2 + levels] == 1
    p = flags[0]
    chunks = []
    for i, ((first, last), extra) in enumerate(CHUNKS):
        ends, other, known, g = refs[4 * i : 4 * i + 4]
        height = g.shape[1]
        part = (1, split_height(height, extra), extra)
        last_inflow(right, part, mats, ends, other, known, inflows[i])
        chunks.append((first, last - first, height, extra, g, inflows[i]))
    flows = [tuple(inflow[i] for i in range(2 * V)) for *_, inflow in chunks]

    def step(z, carry):
        for a in range(V):
            j = z * V + a
            row = j * 2 * NT
            held[pl.ds(row + 1 - p, NT - 1, stride=2), :] = near[j, 0 : NT - 1, :]
            held[pl.ds(row + 1 - p + 2 * (NT - 1), 1), :] = near[j, NT - 1 : NT, :]
            for (first, width, height, extra, g, _), flow in zip(chunks, flows):
                value = corrected(1, z, a, 0, height, g, blocks, flow)
                held[pl.ds(row + p + 2 * first, width, stride=2), :] = value[:width]
                if extra:
                    held[pl.ds(row + p + 2 * (NT - 1), 1), :] = value[width : width + 1]
        return carry

    cells = near.shape[0] // V
    stops = [cells // 4, cells // 2, cells * 3 // 4, cells - 1, cells]
    copies, cell, row = [], 0, 0
    for i, stop in enumerate(stops):
        lax.fori_loop(cell, stop, step, 0, unroll=4 if (stop - cell) % 4 == 0 else 1)
        size = stop * V * NT * 2 // 8 * 8 - row
        span = pl.ds(row, size)
        copies.append(pltpu.make_async_copy(held.at[span, :], out.at[span, :], sems.at[i]))
        copies[-1].start()
        cell, row = stop, row + size
    for copy in copies:
        copy.wait()


def phase_tables(count):
    angle = 2.0 * math.pi * np.outer(np.arange(1, count + 1), np.arange(NT)) / NT
    cosine, sine = np.cos(angle), np.sin(angle)
    basis = np.zeros((PAD, 2 * count + 8), np.float32)
    basis[:NT, :count], basis[:NT, count : 2 * count], basis[:NT, 2 * count] = cosine.T, sine.T, 0.5
    turned = np.zeros((2, count + 8, 3, DEPTH), np.float32)
    turned[0, :count, :, :NT], turned[1, :count, :, :NT] = cosine[:, None], sine[:, None]
    turned[0, count, :, :NT] = 1.0
    return (2.0 / NT * basis).astype(np.float32), turned.reshape(2 * (count + 8), 3 * DEPTH)


def derivative_table():
    gap = np.arange(NT)[:, None] - np.arange(NT)[None, :]
    safe = np.where(gap == 0, 1.0, np.sin(np.pi * gap / NT))
    table = np.where(gap == 0, 0.0, 0.5 * (1.0 - 2.0 * np.mod(gap, 2)) / safe)
    wide = np.zeros((PAD, 3, DEPTH), np.float32)
    wide[:NT, :, :NT] = table[:, None]
    return wide.reshape(PAD, 3 * DEPTH)


COSTS = (0, 0, 6_000_000_000, 0)


def local(state, advect, viscous, inverse, lower, upper, blades, harmonic):
    cells = state.shape[0]
    count = harmonic.shape[0]
    segs, slabs = lax.axis_size("seg"), lax.axis_size("pitch")
    levels = segs.bit_length() - 1
    far_pairs = [(i, (i - 1) % slabs if i % 2 == 0 else (i + 1) % slabs) for i in range(slabs)]
    near_pairs = [(i, i ^ 1) for i in range(slabs)]
    to_far = lambda x: lax.ppermute(x, "pitch", far_pairs)
    to_level = lambda x, k: lax.ppermute(x, "seg", [(i, i ^ (1 << k)) for i in range(segs)])
    x_shape = (cells * V, PAD, LANES)

    slab, seg = lax.axis_index("pitch"), lax.axis_index("seg")
    side = slab % 2
    wrap = jnp.logical_or(slab == 0, slab == slabs - 1)
    bits = [(seg >> k) & 1 for k in range(levels)]
    run = Chain(
        jnp.stack(
            [side, wrap.astype(jnp.int32), (slab == 0).astype(jnp.int32), *bits]
        ).astype(jnp.int32)
    )
    flat = lambda x: x.transpose(0, 2, 3, 1, 4).reshape(cells * V * V * 2, LANES)
    inv, low, upp = flat(inverse.astype(F32)), flat(lower), flat(upper)
    st = state.transpose(0, 2, 3, 1, 4).reshape(cells * V * NT * 2, LANES)
    lead_rows, edge_rows = LEAD * V * NT, padded_even(V * NT * 2)
    held = pl.BlockSpec(memory_space=pltpu.VMEM)
    shapes = [(lead_rows, LANES), (edge_rows, LANES), (edge_rows, LANES), x_shape, x_shape]
    slab_out, first_cell, last_cell, xn, xf = pl.pallas_call(
        split_cells,
        out_shape=[jax.ShapeDtypeStruct(x, F32) for x in shapes],
        in_specs=[held],
        out_specs=[held] * 5,
        compiler_params=pltpu.CompilerParams(vmem_limit_bytes=16 * MB),
        name="split_cells",
    )(run.before(st))
    halo_near = lax.ppermute(xn, "pitch", near_pairs)
    slab_in = to_far(slab_out)
    from_left = lax.ppermute(last_cell, "seg", [(i, i + 1) for i in range(segs - 1)])
    from_right = lax.ppermute(first_cell, "seg", [(i + 1, i) for i in range(segs - 1)])

    basis, turned = phase_tables(count)
    table = derivative_table()
    wide_harmonic = jnp.broadcast_to(harmonic.astype(F32)[:, None], (count, LANES))

    rest = (cells - LEAD) * V
    chunk_shapes = [
        (rest * (last - first) + (padded_even(rest) if extra else 0), LANES)
        for (first, last), extra in CHUNKS
    ]
    adv = advect.transpose(0, 2, 1, 3).reshape(cells * V * 2, LANES)
    vis = viscous.transpose(0, 2, 1, 3).reshape(cells * V * 2, LANES)
    trig, base, *chunks = run(
        prepare, [(2 * count + 8, LANES), x_shape, *chunk_shapes],
        [xn, xf, wide_harmonic, basis, turned, adv, vis, table], scalars=[blades], name="prepare",
    )
    arrived = [slab_in]
    for chunk in chunks:
        if len(arrived) >= 2:
            chunk, arrived[-2] = lax.optimization_barrier((chunk, arrived[-2]))
        arrived.append(to_far(chunk))
    slab_in, *arrived = arrived

    edges = pltpu.VMEM((2 * V, PAD, LANES), F32)

    mats = []
    mats_shape = (2, 6 * V, 8, LANES)

    def solve_chunk(i):
        height, extra = rows_of(CHUNKS[i]), CHUNKS[i][1]
        tall = packed_rows(2 * V, split_height(height, extra), extra)
        return run(
            functools.partial(far_chunk, CHUNKS[i]),
            [(cells * V, height, LANES), (tall, LANES)],
            [base, lead, arrived[i], from_left, from_right, adv, vis, inv, low, upp],
            scratch=[edges], name="far_chunk",
        )

    class Exchange:
        def __init__(self, c, extra, g, flows, leads=False):
            self.part, self.leads = (c, split_height(g.shape[1], extra), extra), leads
            self.flows, self.known, self.solved, self.level = flows, [], g, 0
            self.scratch = [pltpu.VMEM((2 * V, g.shape[1], LANES), F32)]

        def step(self):
            k = self.level
            behind = k == levels - 2
            inflow = (packed_rows(2 * V, *self.part[1:]), LANES)
            tall = packed_rows(V if behind else 2 * V, *self.part[1:])
            other = to_level(self.flows, k)
            if self.leads:
                tall += padded_even((2 if behind else 6) * V * V)
                out = run(
                    functools.partial(merge_all, self.part, k, levels),
                    [mats_shape, (tall, LANES), (2, 3 * V, 8, LANES), inflow],
                    [self.flows, other, *self.known], name="merge_all",
                )
                mats.append(out[0])
                self.flows, self.known = out[1], out[2:]
            else:
                out = run(
                    functools.partial(merge_flows, self.part, k, levels), [(tall, LANES), inflow],
                    [mats[k], self.flows, other, *self.known], name="merge_flows",
                )
                self.flows, self.known = out[0], out[1:]
            self.level = k + 1

        def send(self):
            self.other = to_level(self.flows, levels - 1)

        def ahead_of(self, later):
            later.flows, self.other = lax.optimization_barrier((later.flows, self.other))

        def last(self):
            return [self.flows, self.other, *self.known]

        def correct(self):
            if self.leads:
                result, last = run(
                    functools.partial(correct_all, self.part, levels), [self.solved.shape, mats_shape],
                    [*self.last(), blocks, self.solved], scratch=self.scratch, name="correct_all",
                )
                mats.append(last)
                return result
            return run(
                functools.partial(correct, self.part, levels), [self.solved.shape],
                [mats[-1], *self.last(), blocks, self.solved], scratch=self.scratch, name="correct",
            )[0]

    base_near = run(
        near_base, [x_shape], [xn, xf, adv, vis, table, trig], name="near_base", flops=COSTS[0]
    )[0]
    blocks, group = run(
        transfer, [(2, cells * V, 16, LANES), (padded_even(6 * V * V), LANES)], [low, upp],
        scratch=[pltpu.VMEM((cells * V, 8, LANES), F32)], name="transfer", flops=COSTS[1],
    )
    lead = run(
        far_lead, [(LEAD * V, PAD, LANES)], [slab_in, trig, basis, turned],
        scratch=[pltpu.VMEM((V, PAD, LANES), F32)], name="far_lead", flops=COSTS[3],
    )[0]
    tall = packed_rows(2 * V, PAD // 8 - 1, True) + group.shape[0]
    first = Exchange(
        0,
        True,
        *run(
            near_cell, [x_shape, (tall, LANES)],
            [base_near, halo_near, from_left, from_right, adv, vis, inv, low, upp, group],
            scratch=[edges], name="near_cell", flops=COSTS[2],
        ),
        leads=True,
    )
    first.step()
    second = Exchange(1, CHUNKS[0][1], *solve_chunk(0))
    for k in range(1, levels - 1):
        first.step()
    first.send()
    second.step()
    third = Exchange(1, CHUNKS[1][1], *solve_chunk(1))
    third.step()
    for k in range(1, levels - 1):
        second.step()
    second.send()
    first.ahead_of(third)
    for k in range(1, levels - 1):
        third.step()
    near = first.correct()
    third.send()
    operands = [mats[-1], blocks, near]
    for item in (second, third):
        operands += [*item.last(), item.solved]
    out = run(
        functools.partial(finish, levels), [st.shape], operands,
        out_specs=[pl.BlockSpec(memory_space=pltpu.HBM)],
        scratch=[pltpu.VMEM((st.shape[0] + 8, LANES), F32), pltpu.SemaphoreType.DMA((5,))]
        + [pltpu.VMEM((2 * V, rows_of(chunk), LANES), F32) for chunk in CHUNKS],
        name="finish",
    )[0]
    return out.reshape(cells, V, NT, 2, LANES).transpose(0, 3, 1, 2, 4)


def solution(mesh):
    cell = P("seg", "pitch", None, None, None)
    return jax.shard_map(
        local,
        mesh=mesh,
        in_specs=(cell, P("seg", "pitch", None, None), P("seg", "pitch", None, None), cell, cell, cell, P(), P()),
        out_specs=cell,
        check_vma=False,
    )
```
